128 devices in a mesh: dp: 16 (over y, z), tensor: 8 (over x, core).
Axes of the slice: x: 4, y: 4, z: 4, core: 2. Of those that a mesh axis runs over, the one named last changes fastest.
Arguments:
- tokens: bfloat16 [256, 32, 8192], P('dp', None, 'tensor'), may hold values from -6 to 6
- destinations: int32 [256], P('dp'), may hold values from 0 to 255, as said below
- counts: int32 [256], P('dp'), may hold values from 1 to 32, as said below
- sequence_job_ids: int32 [256], P('dp'), may hold values from 0 to 15, as said below
- job_owner_slot: int32 [16], replicated, may hold values from 0 to 15, each once
- rank_per_job: int32 [16], replicated, may hold values from 8 to 128, as said below
- weight: bfloat16 [8192, 8192], P('tensor'), may hold values from -0.0625 to 0.0625
- input_factor_table: bfloat16 [16, 8192, 128], P('dp', 'tensor'), may hold values from -0.0625 to 0.0625
- output_factor_table: bfloat16 [16, 128, 8192], P('dp', None, 'tensor'), may hold values from -0.5 to 0.5
- cotangent: bfloat16 [256, 32, 8192], P('dp', None, 'tensor'), may hold values from -3 to 3
Outputs:
- output: bfloat16 [256, 32, 8192], P('dp', None, 'tensor')
- input_factor_gradient: float32 [16, 8192, 128], P('dp', 'tensor')
- output_factor_gradient: float32 [16, 128, 8192], P('dp', None, 'tensor')
The draws below stay inside these ranges and needn't reach their ends.
Inputs may be any that keep to these rules, and one draw needn't show every extreme that they name: destinations is a permutation of all sequence slots; each device sends at most one sequence to one device and receives exactly 16. `sequence_job_ids`: in the packed layout the 16 sequences of one dp index name one job at most 2 times, and some job exactly 2 times. `counts`: some sequence is full. `rank_per_job`: multiples of 8; some job has rank 8 and some rank 128.
All inputs are finite; a program needn't handle non-finite values.
Results may differ from the reference program's by a relative error of at most 0.0075.
Values may be sent and summed in bfloat16 or wider, within the bound.
A program may use at most 192 MiB of HBM per device.

```python
import jax
import jax.numpy as jnp
from jax import lax

MODEL_WIDTH = 8192
MAX_RANK = 128
SEQ = 32
SLOTS = 16
ADAPTER_JOBS = 16
SEQS = 256


def shared_layout(key):
    keys = jax.random.split(jax.random.fold_in(key, 101), 6)
    dp_count = SEQS // SLOTS
    shifts = jax.random.permutation(keys[0], dp_count)[:SLOTS]
    sigma = jax.random.permutation(keys[1], SLOTS)
    devices = jnp.arange(dp_count, dtype=jnp.int32)[:, None]
    targets = ((devices + shifts[None, :]) % dp_count * SLOTS + sigma[None, :]).reshape(-1).astype(jnp.int32)
    popular = jax.random.permutation(keys[2], ADAPTER_JOBS).astype(jnp.int32) * 4096
    noise = jax.random.randint(keys[3], (dp_count, ADAPTER_JOBS), 0, 65536)
    scores = (noise + popular[None, :]) * ADAPTER_JOBS + jnp.arange(ADAPTER_JOBS, dtype=jnp.int32)[None, :]
    picked = lax.top_k(scores, SLOTS)[1].astype(jnp.int32)
    doubles = jax.random.randint(keys[4], (dp_count, 1), 1, min(4, SLOTS // 2) + 1)
    places = jnp.arange(SLOTS, dtype=jnp.int32)[None, :]
    limit = SLOTS - doubles
    index_map = jnp.where(places < limit, places, places - limit)
    chosen = jnp.take_along_axis(picked, index_map, 1)
    shuffle = jax.random.randint(keys[5], (dp_count, SLOTS), 0, 1 << 20) * SLOTS + places
    order = jnp.argsort(shuffle, axis=1)
    chosen = jnp.take_along_axis(chosen, order, 1).reshape(-1).astype(jnp.int32)
    return (targets, chosen[targets])


def draw_destinations(key, part):
    targets, source_jobs = shared_layout(key)
    return targets


def draw_sequence_job_ids(key, part):
    targets, source_jobs = shared_layout(key)
    return source_jobs


def draw_counts(key, part):
    key = jax.random.fold_in(key, 7)
    first, second = jax.random.split(key)
    values = jax.random.randint(first, (SEQS,), 1, SEQ + 1)
    full_index = jax.random.randint(second, (), 0, SEQS)
    return jnp.where(jnp.arange(SEQS) == full_index, SEQ, values).astype(jnp.int32)


def draw_rank_per_job(key, part):
    key = jax.random.fold_in(key, 11)
    first, second, third = jax.random.split(key, 3)
    values = jax.random.randint(first, (ADAPTER_JOBS,), 1, MAX_RANK // 8 + 1) * 8
    top_index = jax.random.randint(second, (), 0, ADAPTER_JOBS)
    low_index = (top_index + 1 + jax.random.randint(third, (), 0, ADAPTER_JOBS - 1)) % ADAPTER_JOBS
    places = jnp.arange(ADAPTER_JOBS)
    values = jnp.where(places == top_index, MAX_RANK, values)
    values = jnp.where(places == low_index, 8, values)
    return values.astype(jnp.int32)


def shard_levels(own_key, extent, cuts, smallest, largest):
    loudness = 1.0
    for position, shards_of in cuts:
        draws = jax.random.uniform(jax.random.fold_in(jax.random.fold_in(own_key, 6), position), (shards_of,), jnp.float32, smallest / len(cuts), largest / len(cuts))
        loudness = loudness * jnp.repeat(jnp.exp(draws), extent[position] // shards_of).reshape((-1,) + (1,) * (len(extent) - 1 - position))
    return loudness


def centred(own_key, shape, spread, bound, cuts=(), kind=jnp.bfloat16):
    values = jax.random.normal(own_key, shape, jnp.float32) * spread
    if len(cuts) > 0:
        values = shard_levels(own_key, shape, cuts, -0.22, 0.18) * values
    return jnp.clip(values, min=-bound, max=bound).astype(kind)


def setup_inputs(seed: int = 0) -> dict:
    key_of = jax.random.split(jax.random.key(seed), 11)
    return {
        "tokens": centred(key_of[0], (SEQS, SEQ, MODEL_WIDTH), 1.0, 6.0, ((0, 16), (2, 8))),
        "destinations": draw_destinations(jax.random.fold_in(key_of[10], 71), 0),
        "counts": draw_counts(jax.random.fold_in(key_of[10], 71), 0),
        "sequence_job_ids": draw_sequence_job_ids(jax.random.fold_in(key_of[10], 71), 0),
        "job_owner_slot": jax.random.permutation(key_of[4], ADAPTER_JOBS).astype(jnp.int32),
        "rank_per_job": draw_rank_per_job(jax.random.fold_in(key_of[10], 71), 0),
        "weight": centred(key_of[6], (MODEL_WIDTH, MODEL_WIDTH), MODEL_WIDTH ** -0.5, 0.0625, ((0, 8),)),
        "input_factor_table": centred(key_of[7], (ADAPTER_JOBS, MODEL_WIDTH, MAX_RANK), MODEL_WIDTH ** -0.5, 0.0625, ((0, 16), (1, 8))),
        "output_factor_table": centred(key_of[8], (ADAPTER_JOBS, MAX_RANK, MODEL_WIDTH), MAX_RANK ** -0.5, 0.5, ((0, 16), (2, 8))),
        "cotangent": centred(key_of[9], (SEQS, SEQ, MODEL_WIDTH), 0.5, 3.0, ((0, 16), (2, 8))),
    }


def reference(tokens, destinations, counts, sequence_job_ids, job_owner_slot, rank_per_job, weight, input_factor_table, output_factor_table, cotangent):
    source_of = jnp.zeros((SEQS,), jnp.int32).at[destinations].set(jnp.arange(SEQS, dtype=jnp.int32))
    placed = tokens[source_of]
    live_count = counts[source_of]
    job_here = sequence_job_ids[source_of]
    live_mask = jnp.arange(SEQ)[None, :] < live_count[:, None]
    masked_factor = jnp.where(live_mask[:, :, None], placed, jnp.zeros((), jnp.bfloat16))
    token_rows = masked_factor.reshape(SEQS * SEQ, MODEL_WIDTH)
    base_out = jnp.dot(token_rows, weight, preferred_element_type=jnp.float32)
    owning_slot = job_owner_slot[job_here].astype(jnp.int32)
    single_job_rank = rank_per_job[job_here].astype(jnp.int32)
    factor_pair = 32.0 / single_job_rank.astype(jnp.float32)

    def loop_step_body(totals, seq_item):
        total_a, total_b = totals
        seq_rows, seq_cot, owner_slot_index, rank_value, factor = seq_item
        rank_limit_mask = jnp.arange(MAX_RANK) < rank_value
        input_matrix = jnp.where(rank_limit_mask[None, :], input_factor_table[owner_slot_index], jnp.zeros((), jnp.bfloat16))
        output_matrix = jnp.where(rank_limit_mask[:, None], output_factor_table[owner_slot_index], jnp.zeros((), jnp.bfloat16))
        lowrank = jnp.dot(seq_rows, input_matrix, preferred_element_type=jnp.float32).astype(jnp.bfloat16)
        adapter_item = (factor * jnp.dot(lowrank, output_matrix, preferred_element_type=jnp.float32)).astype(jnp.bfloat16)
        upgrad = (factor * jnp.dot(seq_cot, output_matrix.T, preferred_element_type=jnp.float32)).astype(jnp.bfloat16)
        piece_a = jnp.dot(seq_rows.T, upgrad, preferred_element_type=jnp.float32) / SEQ
        piece_b = factor * jnp.dot(lowrank.T, seq_cot, preferred_element_type=jnp.float32) / SEQ
        return (total_a.at[owner_slot_index].add(piece_a), total_b.at[owner_slot_index].add(piece_b)), adapter_item

    start_offset = (jnp.zeros((ADAPTER_JOBS, MODEL_WIDTH, MAX_RANK), jnp.float32), jnp.zeros((ADAPTER_JOBS, MAX_RANK, MODEL_WIDTH), jnp.float32))
    (input_factor_gradient, output_factor_gradient), adapter_item = lax.scan(loop_step_body, start_offset, (masked_factor, cotangent, owning_slot, single_job_rank, factor_pair))
    output = (base_out.reshape(SEQS, SEQ, MODEL_WIDTH) + adapter_item.astype(jnp.float32)).astype(jnp.bfloat16)
    return output, input_factor_gradient, output_factor_gradient
```

```python
import jax
import jax.numpy as jnp
from jax import lax
from jax.sharding import PartitionSpec as P


def on_device(
    tokens,
    destinations,
    counts,
    sequence_job_ids,
    job_owner_slot,
    rank_per_job,
    weight,
    input_factor_table,
    output_factor_table,
    cotangent,
):
    slot_count, seq_len, local_width = tokens.shape
    dp_count = lax.axis_size("dp")
    here_index = lax.axis_index("dp")
    job_count = job_owner_slot.shape[0]
    max_rank = input_factor_table.shape[2]
    places = jnp.arange(slot_count, dtype=jnp.int32)
    owners = jnp.arange(dp_count, dtype=jnp.int32)

    outbound = (destinations // slot_count)[None, :] == owners[:, None]
    facts = jnp.stack([destinations % slot_count, counts, sequence_job_ids], 1)
    facts_out = jnp.sum(jnp.where(outbound[:, :, None], facts[None], 0), 1)
    facts_in = lax.all_to_all(facts_out, "dp", split_axis=0, concat_axis=0, tiled=True)
    send_tokens = jnp.einsum(
        "gq,qlm->glm", outbound.astype(jnp.bfloat16), tokens, preferred_element_type=jnp.float32
    ).astype(jnp.bfloat16)
    arrived = lax.all_to_all(send_tokens, "dp", split_axis=0, concat_axis=0, tiled=True)

    slot_hot = facts_in[None, :, 0] == places[:, None]
    live_count = jnp.sum(jnp.where(slot_hot, facts_in[None, :, 1], 0), 1)
    job_here = jnp.sum(jnp.where(slot_hot, facts_in[None, :, 2], 0), 1)
    placed = jnp.einsum(
        "qp,pld->qld", slot_hot.astype(jnp.bfloat16), arrived, preferred_element_type=jnp.float32
    ).astype(jnp.bfloat16)
    live_mask = jnp.arange(seq_len)[None, :] < live_count[:, None]
    masked = jnp.where(live_mask[:, :, None], placed, jnp.zeros((), jnp.bfloat16))

    job_hot = job_here[:, None] == jnp.arange(job_count, dtype=jnp.int32)[None, :]
    owner_here = jnp.sum(jnp.where(job_hot, job_owner_slot[None, :], 0), 1)
    earlier = (owner_here[:, None] == owner_here[None, :]) & (places[None, :] < places[:, None])
    turn = jnp.sum(earlier.astype(jnp.int32), 1)
    lanes = jnp.arange(2 * dp_count, dtype=jnp.int32)
    lane_hot = ((owner_here * 2 + turn)[None, :] == lanes[:, None]).astype(jnp.bfloat16)
    both = jnp.stack([masked, cotangent])
    to_owner = jnp.einsum(
        "jq,bqld->jbld", lane_hot, both, preferred_element_type=jnp.float32
    ).astype(jnp.bfloat16)
    to_owner = to_owner.reshape(dp_count, 2, 2, seq_len, local_width)
    at_owner = lax.all_to_all(to_owner, "dp", split_axis=0, concat_axis=0, tiled=True)
    rows = dp_count * 2 * seq_len
    rows_x = at_owner[:, :, 0].reshape(rows, local_width)
    rows_c = at_owner[:, :, 1].reshape(rows, local_width)

    rank = jnp.sum(jnp.where(job_owner_slot == here_index, rank_per_job, 0))
    factor = 32.0 / rank.astype(jnp.float32)
    rank_mask = jnp.arange(max_rank, dtype=jnp.int32) < rank
    a_mine = jnp.where(rank_mask[None, :], input_factor_table[0], jnp.zeros((), jnp.bfloat16))
    b_mine = jnp.where(rank_mask[:, None], output_factor_table[0], jnp.zeros((), jnp.bfloat16))
    down_part = jnp.dot(rows_x, a_mine, preferred_element_type=jnp.float32)
    back_part = jnp.einsum("nc,rc->nr", rows_c, b_mine, preferred_element_type=jnp.float32)
    sums = lax.psum(jnp.concatenate([down_part, back_part], 1), "tensor")
    lowrank = sums[:, :max_rank].astype(jnp.bfloat16)
    upgrad = (factor * sums[:, max_rank:]).astype(jnp.bfloat16)

    adapter_rows = (factor * jnp.dot(lowrank, b_mine, preferred_element_type=jnp.float32)).astype(
        jnp.bfloat16
    )
    adapter_back = lax.all_to_all(
        adapter_rows.reshape(dp_count, 2, seq_len, local_width),
        "dp",
        split_axis=0,
        concat_axis=0,
        tiled=True,
    ).reshape(2 * dp_count, seq_len, local_width)
    adapter = jnp.einsum("jq,jld->qld", lane_hot, adapter_back, preferred_element_type=jnp.float32)

    input_factor_gradient = (
        jnp.einsum("nd,nr->dr", rows_x, upgrad, preferred_element_type=jnp.float32) / seq_len
    )
    output_factor_gradient = (
        factor * jnp.einsum("nr,nc->rc", lowrank, rows_c, preferred_element_type=jnp.float32) / seq_len
    )

    token_rows = masked.reshape(slot_count * seq_len, local_width)
    partial_out = jnp.dot(token_rows, weight, preferred_element_type=jnp.float32).astype(jnp.bfloat16)
    base_out = lax.psum_scatter(partial_out, "tensor", scatter_dimension=1, tiled=True)
    output = (
        base_out.reshape(slot_count, seq_len, local_width).astype(jnp.float32) + adapter
    ).astype(jnp.bfloat16)
    return output, input_factor_gradient[None], output_factor_gradient[None]


def solution(mesh):
    in_specs = (
        P("dp", None, "tensor"),
        P("dp"),
        P("dp"),
        P("dp"),
        P(),
        P(),
        P("tensor", None),
        P("dp", "tensor", None),
        P("dp", None, "tensor"),
        P("dp", None, "tensor"),
    )
    out_specs = (P("dp", None, "tensor"), P("dp", "tensor", None), P("dp", None, "tensor"))
    return jax.shard_map(
        on_device, mesh=mesh, in_specs=in_specs, out_specs=out_specs, check_vma=False
    )
```

```python
import jax
import jax.numpy as jnp
from jax import lax
from jax.experimental import pallas as pl
from jax.experimental.pallas import tpu as pltpu
from jax.sharding import PartitionSpec as P

BF = jnp.bfloat16
F32 = jnp.float32
RING = 4
DP = RING * RING
TENSOR = 2 * RING
TILE = 256
W_SLOTS = 3
BLOCK_ORDER = ((2, 1), (2, 0), (1, 1), (1, 0), (3, 1), (3, 0), (0, 1), (0, 0))


def mm(a, b):
    return jnp.dot(a, b, preferred_element_type=F32)


def kernel(
    inverse_ref,
    factor_ref,
    rank_ref,
    facts_ref,
    tok_ref,
    cot_ref,
    a_ref,
    b_ref,
    w_ref,
    out_ref,
    ga_ref,
    gb_ref,
    tok_s,
    tok_r,
    facts_r,
    place_hot,
    lane_hot,
    slot_hot,
    xs,
    x_s,
    x_r,
    c_s,
    c_r,
    fa,
    fb,
    wbuf,
    sib_s,
    sib_r,
    hold,
    hop_s,
    hop_r,
    ring_s,
    ring_r,
    part_s,
    part_r,
    ranks,
    ad_s,
    ad_r,
    g_own,
    g_s,
    g_r,
    w_sem,
    facts_ss,
    facts_rs,
    tok_ss,
    tok_rs,
    fac_ss,
    fac_rs,
    c_ss,
    c_rs,
    x_ss,
    x_rs,
    sib_ss,
    sib_rs,
    hop_ss,
    hop_rs,
    ring_ss,
    ring_rs,
    part_ss,
    part_rs,
    gath_ss,
    gath_rs,
    ad_ss,
    ad_rs,
    g_ss,
    g_rs,
):
    seq_len = tok_ref.shape[1]
    width = tok_ref.shape[2]
    rows = DP * seq_len
    half = rows // 2
    me = lax.axis_index("dp")
    t = lax.axis_index("tensor")
    y, z = me // RING, me % RING
    x, c = t // 2, t % 2
    own_side = (y + z) % 2
    own_job = jnp.where(own_side == 0, z // 2, y // 2)
    tiles = width // TILE

    def remote(src, dst, send, recv, **where):
        return pltpu.make_async_remote_copy(
            src_ref=src,
            dst_ref=dst,
            send_sem=send,
            recv_sem=recv,
            device_id=where,
            device_id_type=pl.DeviceIdType.MESH,
        )

    def along(side, k):
        return ((y + k) % RING) * RING + z if side == 0 else y * RING + (z + k) % RING

    def owner_of(side, job):
        first = y * RING + 2 * job + y % 2
        second = (2 * job + (z + 1) % 2) * RING + z
        return jnp.where(side == 0, first, second)

    def owner_ring(k):
        return jnp.where(own_side == 0, y * RING + (z + k) % RING, ((y + k) % RING) * RING + z)

    def w_copy(i):
        ahead, other = BLOCK_ORDER[i]
        block = ((x + ahead) % RING) * 2 + (1 - c if other else c)
        columns = pl.ds(pl.multiple_of(block * width, width), width)
        return pltpu.make_async_copy(w_ref.at[:, columns], wbuf.at[i % W_SLOTS], w_sem.at[i % W_SLOTS])

    for i in range(W_SLOTS):
        w_copy(i).start()

    barrier = pltpu.get_barrier_semaphore()
    for k in range(1, DP):
        pl.semaphore_signal(
            barrier, inc=1, device_id={"dp": (me + k) % DP}, device_id_type=pl.DeviceIdType.MESH
        )
    for k in range(1, TENSOR):
        pl.semaphore_signal(
            barrier, inc=1, device_id={"tensor": (t + k) % TENSOR}, device_id_type=pl.DeviceIdType.MESH
        )

    for k in range(1, DP):
        tok_s[k - 1] = tok_ref[inverse_ref[(me + k) % DP]]
    tok_r[me] = tok_ref[inverse_ref[me]]
    facts_r[me] = facts_ref[me]
    my_rank = rank_ref[me]
    fa[own_side, own_job] = jnp.where(
        lax.broadcasted_iota(jnp.int32, a_ref.shape[1:], 1) < my_rank, a_ref[0].astype(F32), 0.0
    ).astype(BF)
    fb[own_side, own_job] = jnp.where(
        lax.broadcasted_iota(jnp.int32, b_ref.shape[1:], 0) < my_rank, b_ref[0].astype(F32), 0.0
    ).astype(BF)

    pl.semaphore_wait(barrier, DP - 1 + TENSOR - 1)

    def facts_copy(k):
        to = (me + k) % DP
        return remote(facts_ref.at[to], facts_r.at[me], facts_ss.at[k - 1], facts_rs.at[k - 1], dp=to)

    def tok_copy(k):
        return remote(
            tok_s.at[k - 1], tok_r.at[me], tok_ss.at[k - 1], tok_rs.at[k - 1], dp=(me + k) % DP
        )

    def fac_copy(k, n):
        held = (fa, fb)[n].at[own_side, own_job]
        return remote(held, held, fac_ss.at[k - 1, n], fac_rs.at[own_side, own_job, n], dp=owner_ring(k))

    def fac_wait(side, job, n):
        held = (fa, fb)[n].at[side, job]
        remote(held, held, fac_ss.at[0, n], fac_rs.at[side, job, n], dp=me).wait_recv()

    for k in range(1, DP):
        facts_copy(k).start()
    for k in range(1, DP):
        tok_copy(k).start()
    for k in range(1, RING):
        fac_copy(k, 1).start()
        fac_copy(k, 0).start()

    for k in range(1, DP):
        facts_copy(k).wait_recv()
    slot_c = facts_r[:, 0, :].astype(F32)
    live_c = facts_r[:, 1, :].astype(F32)
    base_c = facts_r[:, 2, :].astype(F32)

    def iota(shape, axis):
        return lax.broadcasted_iota(jnp.int32, shape, axis)

    square = (DP, 128)
    diagonal = iota(square, 0) == iota(square, 1)
    slot_l = jnp.sum(jnp.where(diagonal, slot_c, 0.0), 0, keepdims=True)
    base_l = jnp.sum(jnp.where(diagonal, base_c, 0.0), 0, keepdims=True)
    earlier = (base_l == base_c) & (slot_l < slot_c) & (iota(square, 1) < DP)
    turn_c = jnp.sum(jnp.where(earlier, 1.0, 0.0), 1, keepdims=True)
    lane_c = base_c + turn_c
    lane_l = jnp.sum(jnp.where(diagonal, lane_c, 0.0), 0, keepdims=True)
    wide = (DP, rows)
    seq_of = iota(wide, 1) // seq_len
    slot_1, live_1, lane_1 = slot_c[:, :1], live_c[:, :1], lane_c[:, :1]
    in_slot = slot_1 == seq_of.astype(F32)
    in_order = iota(wide, 0) == seq_of
    position = (iota((1, rows), 1) % seq_len).astype(F32)
    lane_row = jnp.sum(jnp.where(in_slot, lane_1, 0.0), 0, keepdims=True) * seq_len + position
    slot_row = jnp.sum(jnp.where(in_order, slot_1, 0.0), 0, keepdims=True) * seq_len + position
    live_row = jnp.sum(jnp.where(in_order, live_1, 0.0), 0, keepdims=True)
    slot_row = jnp.where(position < live_row, slot_row, -1.0)

    @pl.loop(0, 2 * rows // 128)
    def _(n):
        at = pl.ds(pl.multiple_of(n * 128, 128), 128)
        row = (iota((128, rows), 0) + n * 128).astype(F32)
        lane_hot[at, :] = jnp.where(row == lane_row, 1.0, 0.0).astype(BF)

    def lanes(source, send, recv, send_sem, recv_sem, start):
        def copy(side, k):
            place = y if side == 0 else z
            return remote(
                send.at[side, k - 1],
                recv.at[side, :, place],
                send_sem.at[side, k - 1],
                recv_sem.at[side, k - 1],
                dp=along(side, k),
            )

        if start:
            for k in (2, 1, 3, 0):
                for side in range(2):
                    place = y if side == 0 else z
                    first = (side * RING + (place + k) % RING) * 128
                    hot = lane_hot[pl.ds(pl.multiple_of(first, 128), 128), :]
                    for n in range(tiles // 2):
                        columns = slice(n * 2 * TILE, (n + 1) * 2 * TILE)
                        block = mm(hot, source[:, columns]).astype(BF)
                        for job in range(2):
                            piece = block[job * 64 : (job + 1) * 64]
                            if k == 0:
                                recv[side, job, place, :, columns] = piece
                            else:
                                send[side, k - 1, job, :, columns] = piece
                    if k > 0:
                        copy(side, k).start()
        return copy

    c_copy = lanes(cot_ref, c_s, c_r, c_ss, c_rs, True)

    @pl.loop(0, rows // 128)
    def _(n):
        at = pl.ds(pl.multiple_of(n * 128, 128), 128)
        row = (iota((128, rows), 0) + n * 128).astype(F32)
        place_hot[at, :] = jnp.where(row == slot_row, 1.0, 0.0).astype(BF)

    @pl.loop(0, rows // 128)
    def _(n):
        at = pl.ds(pl.multiple_of(n * 128, 128), 128)
        row = iota((128, 128), 0) + n * 128
        mine = jnp.where(slot_l == (row // seq_len).astype(F32), lane_l, 0.0)
        target = jnp.sum(mine, 1, keepdims=True) * seq_len + (row % seq_len).astype(F32)[:, :1]
        slot_hot[at, :] = jnp.where(iota((128, 2 * rows), 1).astype(F32) == target, 1.0, 0.0).astype(BF)

    for k in range(1, DP):
        tok_copy(k).wait_recv()
    for n in range(tiles // 2):
        columns = slice(n * 2 * TILE, (n + 1) * 2 * TILE)
        landed = tok_r[:, :, columns].reshape(rows, 2 * TILE)
        xs[:, columns] = mm(place_hot[...], landed).astype(BF)
    x_copy = lanes(xs, x_s, x_r, x_ss, x_rs, True)

    def block(i, put):
        w_copy(i).wait()

        @pl.loop(0, tiles)
        def _(n):
            columns = pl.ds(pl.multiple_of(n * TILE, TILE), TILE)
            put(columns, mm(xs[...], wbuf[i % W_SLOTS, :, columns]))

        if i + W_SLOTS < len(BLOCK_ORDER):
            w_copy(i + W_SLOTS).start()

    def sib_copy(j):
        return remote(
            sib_s.at[j % 2], sib_r.at[j], sib_ss.at[j % 2], sib_rs.at[j], tensor=x * 2 + (1 - c)
        )

    def other_block(j):
        if j >= 2:
            sib_copy(j - 2).wait_send()

        def put(columns, value):
            sib_s[j % 2, :, columns] = value.astype(BF)

        block(2 * j, put)
        sib_copy(j).start()

    def my_block(j, slot):
        def put(columns, value):
            hold[slot, :, columns] = value

        block(2 * j + 1, put)

    right, left = ((x + 1) % RING) * 2 + c, ((x + 3) % RING) * 2 + c
    upper, lower = slice(0, half), slice(half, rows)

    def hop_copy(way):
        return remote(
            hop_s.at[way], hop_r.at[way], hop_ss.at[way], hop_rs.at[way], tensor=(right, left)[way]
        )

    def ring_copy(way, part):
        return remote(
            ring_s.at[way, part],
            ring_r.at[way, part],
            ring_ss.at[way, part],
            ring_rs.at[way, part],
            tensor=(right, left)[way],
        )

    parts = (upper, lower)
    other_block(0)
    my_block(0, 0)
    other_block(1)
    sib_copy(0).wait_recv()
    for way in range(2):
        hop_s[way] = (hold[0, parts[way]] + sib_r[0, parts[way]].astype(F32)).astype(BF)
        hop_copy(way).start()
    my_block(1, 1)
    other_block(2)
    sib_copy(1).wait_recv()
    ring_s[0, 1] = (hold[1, lower] + sib_r[1, lower].astype(F32)).astype(BF)
    ring_copy(0, 1).start()
    my_block(2, 0)
    other_block(3)
    sib_copy(2).wait_recv()
    ring_s[1, 0] = (hold[0, upper] + sib_r[2, upper].astype(F32)).astype(BF)
    ring_copy(1, 0).start()
    my_block(3, 2)

    def part_copy(kind, k):
        to = (t + k) % TENSOR
        return remote(
            part_s.at[kind, to],
            part_r.at[kind, k],
            part_ss.at[kind, k - 1],
            part_rs.at[kind, k - 1],
            tensor=to,
        )

    def gath_copy(kind, k):
        to = (t + k) % TENSOR
        held = ranks.at[kind, t]
        return remote(held, held, gath_ss.at[kind, k - 1], gath_rs.at[kind, k - 1], tensor=to)

    def served(ref, side, job):
        return ref[side, job].reshape(RING * 64, width)

    def send_parts(kind, make):
        for side in range(2):
            for job in range(2):
                value = make(side, job)
                for piece in range(2):
                    part_s[kind, side * 4 + job * 2 + piece] = value[piece * 128 : (piece + 1) * 128].astype(
                        BF
                    )
        for k in range(1, TENSOR):
            part_copy(kind, k).start()
        part_r[kind, 0] = part_s[kind, t]

    def sum_parts(kind, scale):
        for k in range(1, TENSOR):
            part_copy(kind, k).wait_recv()
        total = part_r[kind, 0].astype(F32)
        for k in range(1, TENSOR):
            total = total + part_r[kind, k].astype(F32)
        ranks[kind, t] = (total if scale is None else total * scale).astype(BF)
        for k in range(1, TENSOR):
            gath_copy(kind, k).start()

    def gathered(kind):
        for k in range(1, TENSOR):
            frm = (t + TENSOR - k) % TENSOR
            held = ranks.at[kind, frm]
            remote(held, held, gath_ss.at[kind, k - 1], gath_rs.at[kind, k - 1], tensor=t).wait_recv()

    others = ((own_side, 1 - own_job), (1 - own_side, 0), (1 - own_side, 1))
    for side, job in others:
        for n in (1, 0):
            fac_wait(side, job, n)
    for side in range(2):
        for k in range(1, RING):
            c_copy(side, k).wait_recv()
    send_parts(
        1,
        lambda side, job: lax.dot_general(
            served(c_r, side, job), fb[side, job], (((1,), (1,)), ((), ())), preferred_element_type=F32
        ),
    )

    hop_copy(0).wait_recv()
    sib_copy(3).wait_recv()
    ring_s[0, 0] = (
        hold[1, upper] + sib_r[1, upper].astype(F32) + hop_r[0].astype(F32)
    ).astype(BF)
    ring_copy(0, 0).start()
    hop_copy(1).wait_recv()
    ring_s[1, 1] = (
        hold[0, lower] + sib_r[2, lower].astype(F32) + hop_r[1].astype(F32)
    ).astype(BF)
    ring_copy(1, 1).start()

    for side in range(2):
        for k in range(1, RING):
            x_copy(side, k).wait_recv()
    send_parts(0, lambda side, job: mm(served(x_r, side, job), fa[side, job]))
    my_factor = factor_ref[owner_of(t // 4, (t // 2) % 2)]
    sum_parts(1, my_factor)
    sum_parts(0, None)

    def g_copy(n, which):
        side, job = others[which]
        k = jnp.where(
            side == 0,
            (z - (2 * job + y % 2) + RING) % RING,
            (y - (2 * job + (z + 1) % 2) + RING) % RING,
        )
        return remote(
            g_s.at[n, which], g_r.at[n, k - 1], g_ss.at[n, which], g_rs.at[n, k - 1], dp=owner_of(side, job)
        )

    def g_wait(n, k):
        remote(g_s.at[n, 0], g_r.at[n, k - 1], g_ss.at[n, 0], g_rs.at[n, k - 1], dp=me).wait_recv()

    def gradient(n, rank_rows, row_ref):
        for which, (side, job) in enumerate(others + ((own_side, own_job),)):
            turned = rank_rows(side, job).astype(F32).T.astype(BF)
            value = mm(turned, row_ref[side, job].reshape(RING * 64, width)) * (1.0 / seq_len)
            if n == 1:
                value = value * factor_ref[owner_of(side, job)]
            if which < 3:
                g_s[n, which] = value.astype(BF)
                g_copy(n, which).start()
            else:
                g_own[n] = value

    def rank_rows(kind):
        def load(side, job):
            at = pl.ds(side * 4 + job * 2, 2)
            return ranks[kind, at].reshape(RING * 64, ranks.shape[3])

        return load

    gathered(1)
    gradient(0, rank_rows(1), x_r)

    gathered(0)
    def ad_copy(side, k):
        place = y if side == 0 else z
        return remote(
            ad_s.at[side, :, (place + k) % RING],
            ad_r.at[side, place],
            ad_ss.at[side, k - 1],
            ad_rs.at[side, k - 1],
            dp=along(side, k),
        )

    for side in range(2):
        place = y if side == 0 else z
        for job in range(2):
            scale = factor_ref[owner_of(side, job)]
            value = (mm(rank_rows(0)(side, job), fb[side, job]) * scale).astype(BF)
            ad_s[side, job] = value.reshape(RING, 64, width)
        for k in (2, 1, 3):
            ad_copy(side, k).start()
        ad_r[side, place] = ad_s[side, :, place]
    gradient(1, rank_rows(0), c_r)

    for way in range(2):
        for part in range(2):
            ring_copy(way, part).wait_recv()
    for part in range(2):
        hold[2, parts[part]] = (
            hold[2, parts[part]]
            + sib_r[3, parts[part]].astype(F32)
            + ring_r[0, part].astype(F32)
            + ring_r[1, part].astype(F32)
        )
    for side in range(2):
        for k in range(1, RING):
            ad_copy(side, k).wait_recv()

    for n in range(tiles // 2):
        columns = slice(n * 2 * TILE, (n + 1) * 2 * TILE)
        back = ad_r[:, :, :, :, columns].reshape(2 * rows, 2 * TILE)
        out_ref[:, columns] = (hold[2, :, columns] + mm(slot_hot[...], back)).astype(BF)

    for n, g_ref in ((0, ga_ref), (1, gb_ref)):
        for k in range(1, RING):
            g_wait(n, k)
        total = g_own[n]
        for k in range(1, RING):
            total = total + g_r[n, k - 1].astype(F32)
        g_ref[...] = total

    for k in range(1, DP):
        facts_copy(k).wait_send()
        tok_copy(k).wait_send()
    for k in range(1, RING):
        for n in range(2):
            fac_copy(k, n).wait_send()
        for side in range(2):
            c_copy(side, k).wait_send()
            x_copy(side, k).wait_send()
            ad_copy(side, k).wait_send()
    for j in (2, 3):
        sib_copy(j).wait_send()
    for way in range(2):
        hop_copy(way).wait_send()
        for part in range(2):
            ring_copy(way, part).wait_send()
    for kind in range(2):
        for k in range(1, TENSOR):
            part_copy(kind, k).wait_send()
            gath_copy(kind, k).wait_send()
    for n in range(2):
        for which in range(3):
            g_copy(n, which).wait_send()


def on_device(
    tokens,
    destinations,
    counts,
    sequence_job_ids,
    job_owner_slot,
    rank_per_job,
    weight,
    input_factor_table,
    output_factor_table,
    cotangent,
):
    slot_count, seq_len, width = tokens.shape
    max_rank = input_factor_table.shape[2]
    rows = slot_count * seq_len
    devices = jnp.arange(DP, dtype=jnp.int32)

    outbound = (destinations // slot_count)[None, :] == devices[:, None]
    inverse = jnp.sum(jnp.where(outbound, jnp.arange(slot_count, dtype=jnp.int32)[None, :], 0), 1)
    job_hot = sequence_job_ids[:, None] == jnp.arange(job_owner_slot.shape[0], dtype=jnp.int32)[None, :]
    owner = jnp.sum(jnp.where(job_hot, job_owner_slot[None, :], 0), 1)
    oy, oz = owner // RING, owner % RING
    lane_base = jnp.where((oy + oz) % 2 == 0, oy * 4 + oz // 2 * 2, 2 * RING * 2 + oz * 4 + oy // 2 * 2)
    facts = jnp.stack([destinations % slot_count, counts, lane_base] + [jnp.zeros_like(counts)] * 5, 1)
    facts_out = jnp.sum(jnp.where(outbound[:, :, None], facts[None], 0), 1)
    facts_out = jnp.broadcast_to(facts_out[:, :, None], (DP, 8, 128))
    rank_by_owner = jnp.sum(
        jnp.where(job_owner_slot[None, :] == devices[:, None], rank_per_job[None, :], 0), 1
    )
    factor_by_owner = 32.0 / rank_by_owner.astype(F32)

    vmem = pl.BlockSpec(memory_space=pltpu.VMEM)
    smem = pl.BlockSpec(memory_space=pltpu.SMEM)
    dma = pltpu.SemaphoreType.DMA
    served = (2, 2, RING, 64, width)
    out, ga, gb = pl.pallas_call(
        kernel,
        out_shape=(
            jax.ShapeDtypeStruct((rows, width), BF),
            jax.ShapeDtypeStruct((max_rank, width), F32),
            jax.ShapeDtypeStruct((max_rank, width), F32),
        ),
        in_specs=[smem] * 3 + [vmem] * 5 + [pl.BlockSpec(memory_space=pl.ANY)],
        out_specs=(vmem,) * 3,
        scratch_shapes=[
            pltpu.VMEM((DP - 1, seq_len, width), BF),
            pltpu.VMEM((DP, seq_len, width), BF),
            pltpu.VMEM((DP, 8, 128), jnp.int32),
            pltpu.VMEM((rows, rows), BF),
            pltpu.VMEM((2 * rows, rows), BF),
            pltpu.VMEM((rows, 2 * rows), BF),
            pltpu.VMEM((rows, width), BF),
            pltpu.VMEM((2, RING - 1, 2, 64, width), BF),
            pltpu.VMEM(served, BF),
            pltpu.VMEM((2, RING - 1, 2, 64, width), BF),
            pltpu.VMEM(served, BF),
            pltpu.VMEM((2, 2, width, max_rank), BF),
            pltpu.VMEM((2, 2, max_rank, width), BF),
            pltpu.VMEM((W_SLOTS, width, width), BF),
            pltpu.VMEM((2, rows, width), BF),
            pltpu.VMEM((4, rows, width), BF),
            pltpu.VMEM((3, rows, width), F32),
            pltpu.VMEM((2, rows // 2, width), BF),
            pltpu.VMEM((2, rows // 2, width), BF),
            pltpu.VMEM((2, 2, rows // 2, width), BF),
            pltpu.VMEM((2, 2, rows // 2, width), BF),
            pltpu.VMEM((2, TENSOR, 128, max_rank), BF),
            pltpu.VMEM((2, TENSOR, 128, max_rank), BF),
            pltpu.VMEM((2, TENSOR, 128, max_rank), BF),
            pltpu.VMEM(served, BF),
            pltpu.VMEM((2, RING, 2, 64, width), BF),
            pltpu.VMEM((2, max_rank, width), F32),
            pltpu.VMEM((2, 3, max_rank, width), BF),
            pltpu.VMEM((2, 3, max_rank, width), BF),
            dma((W_SLOTS,)),
            dma((DP - 1,)),
            dma((DP - 1,)),
            dma((DP - 1,)),
            dma((DP - 1,)),
            dma((RING - 1, 2)),
            dma((2, 2, 2)),
            dma((2, RING - 1)),
            dma((2, RING - 1)),
            dma((2, RING - 1)),
            dma((2, RING - 1)),
            dma((2,)),
            dma((4,)),
            dma((2,)),
            dma((2,)),
            dma((2, 2)),
            dma((2, 2)),
            dma((2, TENSOR - 1)),
            dma((2, TENSOR - 1)),
            dma((2, TENSOR - 1)),
            dma((2, TENSOR - 1)),
            dma((2, RING - 1)),
            dma((2, RING - 1)),
            dma((2, 3)),
            dma((2, 3)),
        ],
        compiler_params=pltpu.CompilerParams(
            collective_id=0, has_side_effects=True, vmem_limit_bytes=58 * 2**20
        ),
    )(
        inverse,
        factor_by_owner,
        rank_by_owner,
        facts_out,
        tokens,
        cotangent.reshape(rows, width),
        input_factor_table,
        output_factor_table,
        weight,
    )
    return out.reshape(slot_count, seq_len, width), ga.T[None], gb[None]


def solution(mesh):
    in_specs = (
        P("dp", None, "tensor"),
        P("dp"),
        P("dp"),
        P("dp"),
        P(),
        P(),
        P("tensor", None),
        P("dp", "tensor", None),
        P("dp", None, "tensor"),
        P("dp", None, "tensor"),
    )
    out_specs = (P("dp", None, "tensor"), P("dp", "tensor", None), P("dp", None, "tensor"))
    return jax.shard_map(
        on_device, mesh=mesh, in_specs=in_specs, out_specs=out_specs, check_vma=False
    )
```

```python
import jax
import jax.numpy as jnp
from jax import lax
from jax.experimental import pallas as pl
from jax.experimental.pallas import tpu as pltpu
from jax.sharding import PartitionSpec as P

BF = jnp.bfloat16
F32 = jnp.float32
RING = 4
DP = RING * RING
TENSOR = 2 * RING
TILE = 256
W_SLOTS = 3
BLOCK_ORDER = ((2, 1), (2, 0), (1, 1), (1, 0), (3, 1), (3, 0), (0, 1), (0, 0))


def mm(a, b):
    return jnp.dot(a, b, preferred_element_type=F32)


def kernel(
    dest_ref,
    count_ref,
    job_ref,
    owner_ref,
    rank_ref,
    tok_ref,
    cot_ref,
    a_ref,
    b_ref,
    w_ref,
    out_ref,
    ga_ref,
    gb_ref,
    tok_v,
    cot_v,
    a_v,
    b_v,
    out_v,
    tok_s,
    tok_r,
    facts_s,
    facts_r,
    place_hot,
    x_hot,
    c_hot,
    slot_hot,
    xs,
    x_s,
    x_r,
    c_s,
    c_r,
    fa,
    fb,
    wbuf,
    sib_s,
    sib_r,
    hold,
    hop_s,
    hop_r,
    ring_s,
    ring_r,
    part_s,
    part_r,
    ranks,
    ad_s,
    ad_r,
    g_own,
    g_s,
    g_r,
    in_sem,
    out_sem,
    w_sem,
    facts_ss,
    facts_rs,
    tok_ss,
    tok_rs,
    fac_ss,
    fac_rs,
    c_ss,
    c_rs,
    x_ss,
    x_rs,
    sib_ss,
    sib_rs,
    hop_ss,
    hop_rs,
    ring_ss,
    ring_rs,
    part_ss,
    part_rs,
    gath_ss,
    gath_rs,
    ad_ss,
    ad_rs,
    g_ss,
    g_rs,
):
    seq_len, width = tok_ref.shape[1:]
    rows = DP * seq_len
    half = rows // 2
    me = lax.axis_index("dp")
    t = lax.axis_index("tensor")
    y, z = me // RING, me % RING
    x, c = t // 2, t % 2
    own_side = (y + z) % 2
    own_job = jnp.where(own_side == 0, z // 2, y // 2)
    others = ((own_side, 1 - own_job), (1 - own_side, 0), (1 - own_side, 1))
    tiles = width // TILE
    wide_half = width // 2
    column_halves = (slice(0, wide_half), slice(wide_half, width))

    def remote(src, dst, send, recv, **where):
        return pltpu.make_async_remote_copy(
            src_ref=src,
            dst_ref=dst,
            send_sem=send,
            recv_sem=recv,
            device_id=where,
            device_id_type=pl.DeviceIdType.MESH,
        )

    def iota(shape, axis):
        return lax.broadcasted_iota(jnp.int32, shape, axis)

    def along(side, k):
        return ((y + k) % RING) * RING + z if side == 0 else y * RING + (z + k) % RING

    def owner_of(side, job):
        first = y * RING + 2 * job + y % 2
        second = (2 * job + (z + 1) % 2) * RING + z
        return jnp.where(side == 0, first, second)

    def owner_ring(k):
        return jnp.where(own_side == 0, y * RING + (z + k) % RING, ((y + k) % RING) * RING + z)

    def rank_at(owner):
        total = jnp.int32(0)
        for j in range(DP):
            total = total + jnp.where(owner_ref[j] == owner, rank_ref[j], 0)
        return total

    def factor_at(owner, columns):
        return 32.0 / jnp.full((1, columns), rank_at(owner).astype(F32), F32)

    loads = [
        pltpu.make_async_copy(src, dst, in_sem.at[n])
        for n, (src, dst) in enumerate(((tok_ref, tok_v), (a_ref, a_v), (b_ref, b_v), (cot_ref, cot_v)))
    ]
    for load in loads:
        load.start()

    barrier = pltpu.get_barrier_semaphore()
    for k in range(1, DP):
        pl.semaphore_signal(
            barrier, inc=1, device_id={"dp": (me + k) % DP}, device_id_type=pl.DeviceIdType.MESH
        )
    for k in range(1, TENSOR):
        pl.semaphore_signal(
            barrier, inc=1, device_id={"tensor": (t + k) % TENSOR}, device_id_type=pl.DeviceIdType.MESH
        )

    def w_copy(i):
        ahead, other = BLOCK_ORDER[i]
        block = ((x + ahead) % RING) * 2 + (1 - c if other else c)
        columns = pl.ds(pl.multiple_of(block * width, width), width)
        return pltpu.make_async_copy(w_ref.at[:, columns], wbuf.at[i % W_SLOTS], w_sem.at[i % W_SLOTS])

    for i in range(W_SLOTS):
        w_copy(i).start()

    target = [lax.shift_right_logical(dest_ref[i], 4) for i in range(DP)]
    chosen = []
    for k in range(DP):
        to = (me + k) % DP
        index = jnp.int32(0)
        for i in range(DP):
            index = jnp.where(target[i] == to, i, index)
        chosen.append(index)
        owner = owner_ref[job_ref[index]]
        oy, oz = lax.shift_right_logical(owner, 2), owner & 3
        base = jnp.where(
            ((oy + oz) & 1) == 0,
            oy * 4 + lax.shift_right_logical(oz, 1) * 2,
            4 * RING + oz * 4 + lax.shift_right_logical(oy, 1) * 2,
        )
        row = iota((8, 128), 0)
        tile = jnp.where(row == 0, dest_ref[index] & 15, jnp.where(row == 1, count_ref[index], base))
        if k == 0:
            facts_r[me] = tile
        else:
            facts_s[k - 1] = tile

    loads[0].wait()
    for k in range(1, DP):
        tok_s[k - 1] = tok_v[chosen[k]]
    tok_r[me] = tok_v[chosen[0]]

    pl.semaphore_wait(barrier, DP - 1 + TENSOR - 1)

    def facts_copy(k):
        return remote(
            facts_s.at[k - 1], facts_r.at[me], facts_ss.at[k - 1], facts_rs.at[k - 1], dp=(me + k) % DP
        )

    def tok_copy(h, k):
        columns = column_halves[h]
        return remote(
            tok_s.at[k - 1, :, columns],
            tok_r.at[me, :, columns],
            tok_ss.at[h, k - 1],
            tok_rs.at[h, k - 1],
            dp=(me + k) % DP,
        )

    def fac_copy(k, n):
        held = (fa, fb)[n].at[own_side, own_job]
        return remote(held, held, fac_ss.at[k - 1, n], fac_rs.at[own_side, own_job, n], dp=owner_ring(k))

    def fac_wait(n):
        for side, job in others:
            held = (fa, fb)[n].at[side, job]
            remote(held, held, fac_ss.at[0, n], fac_rs.at[side, job, n], dp=me).wait_recv()

    for k in range(1, DP):
        facts_copy(k).start()
    for h in range(2):
        for k in range(1, DP):
            tok_copy(h, k).start()
    my_rank = rank_at(me)
    loads[1].wait()
    fa[own_side, own_job] = jnp.where(
        iota(a_v.shape[1:], 1) < my_rank, a_v[0].astype(F32), 0.0
    ).astype(BF)
    for k in range(1, RING):
        fac_copy(k, 0).start()
    loads[2].wait()
    fb[own_side, own_job] = jnp.where(
        iota(b_v.shape[1:], 0) < my_rank, b_v[0].astype(F32), 0.0
    ).astype(BF)

    for k in range(1, DP):
        facts_copy(k).wait_recv()
    slot_c = facts_r[:, 0, :].astype(F32)
    live_c = facts_r[:, 1, :].astype(F32)
    base_c = facts_r[:, 2, :].astype(F32)
    square = (DP, 128)
    diagonal = iota(square, 0) == iota(square, 1)
    slot_l = jnp.sum(jnp.where(diagonal, slot_c, 0.0), 0, keepdims=True)
    base_l = jnp.sum(jnp.where(diagonal, base_c, 0.0), 0, keepdims=True)
    earlier = (base_l == base_c) & (slot_l < slot_c) & (iota(square, 1) < DP)
    turn_c = jnp.sum(jnp.where(earlier, 1.0, 0.0), 1, keepdims=True)
    lane_c = base_c + turn_c
    lane_l = jnp.sum(jnp.where(diagonal, lane_c, 0.0), 0, keepdims=True)
    wide = (DP, rows)
    seq_of = iota(wide, 1) // seq_len
    slot_1, live_1, lane_1 = slot_c[:, :1], live_c[:, :1], lane_c[:, :1]
    in_slot = slot_1 == seq_of.astype(F32)
    in_order = iota(wide, 0) == seq_of
    position = (iota((1, rows), 1) % seq_len).astype(F32)

    def spread(where, value):
        return jnp.sum(jnp.where(where, value, 0.0), 0, keepdims=True)

    live = position < spread(in_order, live_1)
    c_row = spread(in_slot, lane_1) * seq_len + position
    x_row = jnp.where(live, spread(in_order, lane_1) * seq_len + position, -1.0)
    slot_row = jnp.where(live, spread(in_order, slot_1) * seq_len + position, -1.0)

    def build(hot, wanted):
        @pl.loop(0, hot.shape[0] // 128)
        def _(n):
            at = pl.ds(pl.multiple_of(n * 128, 128), 128)
            row = (iota((128, rows), 0) + n * 128).astype(F32)
            hot[at, :] = jnp.where(row == wanted, 1.0, 0.0).astype(BF)

    build(x_hot, x_row)
    build(place_hot, slot_row)
    build(c_hot, c_row)

    lane_shape = (2, RING, 2, 64)

    def lane_copy(send, recv, send_sem, recv_sem, h, side, k):
        place = y if side == 0 else z
        columns = column_halves[h]
        return remote(
            send.at[side, (place + k) % RING, :, :, columns],
            recv.at[side, :, place, :, columns],
            send_sem.at[h, side, k - 1],
            recv_sem.at[h, side, k - 1],
            dp=along(side, k),
        )

    def x_copy(h, side, k):
        return lane_copy(x_s, x_r, x_ss, x_rs, h, side, k)

    def c_copy(h, side, k):
        return lane_copy(c_s, c_r, c_ss, c_rs, h, side, k)

    def make_lanes(hot, source, send, columns):
        for n in range(columns.start, columns.stop, TILE):
            at = slice(n, n + TILE)
            send[:, :, :, :, at] = mm(hot[...], source(at)).astype(BF).reshape(lane_shape + (TILE,))

    def keep_lanes(send, recv):
        for side in range(2):
            place = y if side == 0 else z
            recv[side, :, place] = send[side, place]

    loads[3].wait()
    for columns in column_halves:
        make_lanes(c_hot, lambda at: cot_v[:, at], c_s, columns)

    def landed(at):
        return tok_r[:, :, at].reshape(rows, at.stop - at.start)

    for h, columns in enumerate(column_halves):
        for k in range(1, DP):
            tok_copy(h, k).wait_recv()
        make_lanes(x_hot, landed, x_s, columns)
        for k in (2, 1, 3):
            for side in range(2):
                x_copy(h, side, k).start()
        for n in range(columns.start, columns.stop, TILE):
            at = slice(n, n + TILE)
            xs[:, at] = mm(place_hot[...], landed(at)).astype(BF)

    for k in range(1, RING):
        fac_copy(k, 1).start()
    for h in range(2):
        for k in (2, 1, 3):
            for side in range(2):
                c_copy(h, side, k).start()

    def block(i, put):
        w_copy(i).wait()

        @pl.loop(0, tiles)
        def _(n):
            columns = pl.ds(pl.multiple_of(n * TILE, TILE), TILE)
            put(columns, mm(xs[...], wbuf[i % W_SLOTS, :, columns]))

        if i + W_SLOTS < len(BLOCK_ORDER):
            w_copy(i + W_SLOTS).start()

    def sib_copy(j):
        return remote(
            sib_s.at[j % 2], sib_r.at[j], sib_ss.at[j % 2], sib_rs.at[j], tensor=x * 2 + (1 - c)
        )

    def other_block(j):
        if j >= 2:
            sib_copy(j - 2).wait_send()

        def put(columns, value):
            sib_s[j % 2, :, columns] = value.astype(BF)

        block(2 * j, put)
        sib_copy(j).start()

    def my_block(j, slot):
        def put(columns, value):
            hold[slot, :, columns] = value

        block(2 * j + 1, put)

    right, left = ((x + 1) % RING) * 2 + c, ((x + 3) % RING) * 2 + c
    parts = (slice(0, half), slice(half, rows))

    def hop_copy(way):
        return remote(
            hop_s.at[way], hop_r.at[way], hop_ss.at[way], hop_rs.at[way], tensor=(right, left)[way]
        )

    def ring_copy(way, part):
        return remote(
            ring_s.at[way, part],
            ring_r.at[way, part],
            ring_ss.at[way, part],
            ring_rs.at[way, part],
            tensor=(right, left)[way],
        )

    other_block(0)
    my_block(0, 0)
    other_block(1)
    sib_copy(0).wait_recv()
    for way in range(2):
        hop_s[way] = (hold[0, parts[way]] + sib_r[0, parts[way]].astype(F32)).astype(BF)
        hop_copy(way).start()
    my_block(1, 1)
    other_block(2)
    my_block(2, 0)
    other_block(3)
    my_block(3, 2)

    def part_copy(kind, k):
        to = (t + k) % TENSOR
        return remote(
            part_s.at[kind, to],
            part_r.at[kind, k],
            part_ss.at[kind, k - 1],
            part_rs.at[kind, k - 1],
            tensor=to,
        )

    def gath_copy(kind, k):
        to = (t + k) % TENSOR
        held = ranks.at[kind, t]
        return remote(held, held, gath_ss.at[kind, k - 1], gath_rs.at[kind, k - 1], tensor=to)

    def served(ref, side, job):
        return ref[side, job].reshape(RING * 64, width)

    def send_parts(kind, make):
        for side in range(2):
            for job in range(2):
                value = make(side, job)
                for piece in range(2):
                    part_s[kind, side * 4 + job * 2 + piece] = value[piece * 128 : (piece + 1) * 128].astype(
                        BF
                    )
        for k in range(1, TENSOR):
            part_copy(kind, k).start()
        part_r[kind, 0] = part_s[kind, t]

    def sum_parts(kind, scale):
        for k in range(1, TENSOR):
            part_copy(kind, k).wait_recv()
        total = part_r[kind, 0].astype(F32)
        for k in range(1, TENSOR):
            total = total + part_r[kind, k].astype(F32)
        ranks[kind, t] = (total if scale is None else total * scale).astype(BF)
        for k in range(1, TENSOR):
            gath_copy(kind, k).start()

    def gathered(kind):
        for k in range(1, TENSOR):
            frm = (t + TENSOR - k) % TENSOR
            held = ranks.at[kind, frm]
            remote(held, held, gath_ss.at[kind, k - 1], gath_rs.at[kind, k - 1], tensor=t).wait_recv()

    def rank_rows(kind, side, job):
        return ranks[kind, pl.ds(side * 4 + job * 2, 2)].reshape(RING * 64, ranks.shape[3])

    keep_lanes(x_s, x_r)
    keep_lanes(c_s, c_r)
    fac_wait(0)
    for h in range(2):
        for side in range(2):
            for k in range(1, RING):
                x_copy(h, side, k).wait_recv()
    send_parts(0, lambda side, job: mm(served(x_r, side, job), fa[side, job]))

    sib_copy(1).wait_recv()
    ring_s[0, 1] = (hold[1, parts[1]] + sib_r[1, parts[1]].astype(F32)).astype(BF)
    sib_copy(2).wait_recv()
    ring_s[1, 0] = (hold[0, parts[0]] + sib_r[2, parts[0]].astype(F32)).astype(BF)
    sum_parts(0, None)
    ring_copy(0, 1).start()
    ring_copy(1, 0).start()

    @pl.loop(0, rows // 128)
    def _(n):
        at = pl.ds(pl.multiple_of(n * 128, 128), 128)
        row = iota((128, 128), 0) + n * 128
        mine = jnp.where(slot_l == (row // seq_len).astype(F32), lane_l, 0.0)
        place = jnp.sum(mine, 1, keepdims=True) * seq_len + (row % seq_len).astype(F32)[:, :1]
        slot_hot[at, :] = jnp.where(iota((128, 2 * rows), 1).astype(F32) == place, 1.0, 0.0).astype(BF)

    def ad_copy(side, k):
        place = y if side == 0 else z
        return remote(
            ad_s.at[side, :, (place + k) % RING],
            ad_r.at[side, place],
            ad_ss.at[side, k - 1],
            ad_rs.at[side, k - 1],
            dp=along(side, k),
        )

    fac_wait(1)
    gathered(0)
    for side in range(2):
        place = y if side == 0 else z
        for job in range(2):
            value = mm(rank_rows(0, side, job), fb[side, job]) * factor_at(owner_of(side, job), width)
            ad_s[side, job] = value.astype(BF).reshape(RING, 64, width)
        for k in (2, 1, 3):
            ad_copy(side, k).start()
        ad_r[side, place] = ad_s[side, :, place]

    for h in range(2):
        for side in range(2):
            for k in range(1, RING):
                c_copy(h, side, k).wait_recv()
    send_parts(
        1,
        lambda side, job: lax.dot_general(
            served(c_r, side, job), fb[side, job], (((1,), (1,)), ((), ())), preferred_element_type=F32
        ),
    )

    def g_copy(n, which):
        side, job = others[which]
        k = jnp.where(
            side == 0,
            (z - (2 * job + y % 2) + RING) % RING,
            (y - (2 * job + (z + 1) % 2) + RING) % RING,
        )
        return remote(
            g_s.at[n, which], g_r.at[n, k - 1], g_ss.at[n, which], g_rs.at[n, k - 1], dp=owner_of(side, job)
        )

    def g_wait(n, k):
        remote(g_s.at[n, 0], g_r.at[n, k - 1], g_ss.at[n, 0], g_rs.at[n, k - 1], dp=me).wait_recv()

    def gradient(n, kind, row_ref):
        for which, (side, job) in enumerate(others + ((own_side, own_job),)):
            turned = rank_rows(kind, side, job).astype(F32).T.astype(BF)
            value = mm(turned, row_ref[side, job].reshape(RING * 64, width)) * (1.0 / seq_len)
            if n == 1:
                value = value * factor_at(owner_of(side, job), width)
            if which < 3:
                g_s[n, which] = value.astype(BF)
                g_copy(n, which).start()
            else:
                g_own[n] = value

    gradient(1, 0, c_r)

    hop_copy(0).wait_recv()
    ring_s[0, 0] = (
        hold[1, parts[0]] + sib_r[1, parts[0]].astype(F32) + hop_r[0].astype(F32)
    ).astype(BF)
    hop_copy(1).wait_recv()
    ring_s[1, 1] = (
        hold[0, parts[1]] + sib_r[2, parts[1]].astype(F32) + hop_r[1].astype(F32)
    ).astype(BF)
    sum_parts(1, factor_at(owner_of(t // 4, (t // 2) % 2), ranks.shape[3]))
    ring_copy(0, 0).start()
    ring_copy(1, 1).start()
    gathered(1)
    gradient(0, 1, x_r)

    sib_copy(3).wait_recv()
    for side in range(2):
        for k in range(1, RING):
            ad_copy(side, k).wait_recv()
    for n in range(tiles):
        at = slice(n * TILE, (n + 1) * TILE)
        back = ad_r[:, :, :, :, at].reshape(2 * rows, TILE)
        hold[2, :, at] = hold[2, :, at] + sib_r[3, :, at].astype(F32) + mm(slot_hot[...], back)
    for part in (1, 0):
        ring_copy(0, part).wait_recv()
        ring_copy(1, 1 - part).wait_recv()
    for part in range(2):
        out_v[parts[part]] = (
            hold[2, parts[part]] + ring_r[0, part].astype(F32) + ring_r[1, part].astype(F32)
        ).astype(BF)
    stores = [pltpu.make_async_copy(out_v, out_ref, out_sem.at[2])]
    stores[0].start()

    for n, g_ref in ((1, gb_ref), (0, ga_ref)):
        for k in range(1, RING):
            g_wait(n, k)
        total = g_own[n]
        for k in range(1, RING):
            total = total + g_r[n, k - 1].astype(F32)
        g_own[n] = total
        stores.append(pltpu.make_async_copy(g_own.at[n], g_ref, out_sem.at[n]))
        stores[-1].start()

    for k in range(1, DP):
        facts_copy(k).wait_send()
        for h in range(2):
            tok_copy(h, k).wait_send()
    for k in range(1, RING):
        for n in range(2):
            fac_copy(k, n).wait_send()
        for side in range(2):
            for h in range(2):
                c_copy(h, side, k).wait_send()
                x_copy(h, side, k).wait_send()
            ad_copy(side, k).wait_send()
    for j in (2, 3):
        sib_copy(j).wait_send()
    for way in range(2):
        hop_copy(way).wait_send()
        for part in range(2):
            ring_copy(way, part).wait_send()
    for kind in range(2):
        for k in range(1, TENSOR):
            part_copy(kind, k).wait_send()
            gath_copy(kind, k).wait_send()
    for n in range(2):
        for which in range(3):
            g_copy(n, which).wait_send()
    for store in stores:
        store.wait()


def finish(out_ref, gb_ref, ga_ref, out_to, gb_to, ga_to, sem):
    stores = [
        pltpu.make_async_copy(out_ref, out_to, sem.at[0]),
        pltpu.make_async_copy(gb_ref, gb_to, sem.at[1]),
    ]
    for store in stores:
        store.start()
    ga_to[...] = ga_ref[...].T
    for store in stores:
        store.wait()


def on_device(
    tokens,
    destinations,
    counts,
    sequence_job_ids,
    job_owner_slot,
    rank_per_job,
    weight,
    input_factor_table,
    output_factor_table,
    cotangent,
):
    slot_count, seq_len, width = tokens.shape
    max_rank = input_factor_table.shape[2]
    rows = slot_count * seq_len
    anywhere = pl.BlockSpec(memory_space=pl.ANY)
    vmem = pl.BlockSpec(memory_space=pltpu.VMEM)
    smem = pl.BlockSpec(memory_space=pltpu.SMEM)
    dma = pltpu.SemaphoreType.DMA
    served = (2, 2, RING, 64, width)
    lanes = (2, RING, 2, 64, width)
    out, ga, gb = pl.pallas_call(
        kernel,
        out_shape=(
            jax.ShapeDtypeStruct((rows, width), BF),
            jax.ShapeDtypeStruct((max_rank, width), F32),
            jax.ShapeDtypeStruct((max_rank, width), F32),
        ),
        in_specs=[smem] * 5 + [anywhere] * 5,
        out_specs=(anywhere,) * 3,
        scratch_shapes=[
            pltpu.VMEM(tokens.shape, BF),
            pltpu.VMEM((rows, width), BF),
            pltpu.VMEM(input_factor_table.shape, BF),
            pltpu.VMEM(output_factor_table.shape, BF),
            pltpu.VMEM((rows, width), BF),
            pltpu.VMEM((DP - 1, seq_len, width), BF),
            pltpu.VMEM((DP, seq_len, width), BF),
            pltpu.VMEM((DP - 1, 8, 128), jnp.int32),
            pltpu.VMEM((DP, 8, 128), jnp.int32),
            pltpu.VMEM((rows, rows), BF),
            pltpu.VMEM((2 * rows, rows), BF),
            pltpu.VMEM((2 * rows, rows), BF),
            pltpu.VMEM((rows, 2 * rows), BF),
            pltpu.VMEM((rows, width), BF),
            pltpu.VMEM(lanes, BF),
            pltpu.VMEM(served, BF),
            pltpu.VMEM(lanes, BF),
            pltpu.VMEM(served, BF),
            pltpu.VMEM((2, 2, width, max_rank), BF),
            pltpu.VMEM((2, 2, max_rank, width), BF),
            pltpu.VMEM((W_SLOTS, width, width), BF),
            pltpu.VMEM((2, rows, width), BF),
            pltpu.VMEM((4, rows, width), BF),
            pltpu.VMEM((3, rows, width), F32),
            pltpu.VMEM((2, rows // 2, width), BF),
            pltpu.VMEM((2, rows // 2, width), BF),
            pltpu.VMEM((2, 2, rows // 2, width), BF),
            pltpu.VMEM((2, 2, rows // 2, width), BF),
            pltpu.VMEM((2, TENSOR, 128, max_rank), BF),
            pltpu.VMEM((2, TENSOR, 128, max_rank), BF),
            pltpu.VMEM((2, TENSOR, 128, max_rank), BF),
            pltpu.VMEM(served, BF),
            pltpu.VMEM(lanes, BF),
            pltpu.VMEM((2, max_rank, width), F32),
            pltpu.VMEM((2, 3, max_rank, width), BF),
            pltpu.VMEM((2, 3, max_rank, width), BF),
            dma((4,)),
            dma((3,)),
            dma((W_SLOTS,)),
            dma((DP - 1,)),
            dma((DP - 1,)),
            dma((2, DP - 1)),
            dma((2, DP - 1)),
            dma((RING - 1, 2)),
            dma((2, 2, 2)),
            dma((2, 2, RING - 1)),
            dma((2, 2, RING - 1)),
            dma((2, 2, RING - 1)),
            dma((2, 2, RING - 1)),
            dma((2,)),
            dma((4,)),
            dma((2,)),
            dma((2,)),
            dma((2, 2)),
            dma((2, 2)),
            dma((2, TENSOR - 1)),
            dma((2, TENSOR - 1)),
            dma((2, TENSOR - 1)),
            dma((2, TENSOR - 1)),
            dma((2, RING - 1)),
            dma((2, RING - 1)),
            dma((2, 3)),
            dma((2, 3)),
        ],
        compiler_params=pltpu.CompilerParams(
            collective_id=0, has_side_effects=True, vmem_limit_bytes=58 * 2**20
        ),
    )(
        destinations,
        counts,
        sequence_job_ids,
        job_owner_slot,
        rank_per_job,
        tokens,
        cotangent.reshape(rows, width),
        input_factor_table,
        output_factor_table,
        weight,
    )
    out, gb, ga = pl.pallas_call(
        finish,
        out_shape=(
            jax.ShapeDtypeStruct((rows, width), BF),
            jax.ShapeDtypeStruct((max_rank, width), F32),
            jax.ShapeDtypeStruct((width, max_rank), F32),
        ),
        in_specs=[anywhere, anywhere, vmem],
        out_specs=(anywhere, anywhere, vmem),
        scratch_shapes=[dma((2,))],
    )(out, gb, ga)
    return out.reshape(slot_count, seq_len, width), ga[None], gb[None]


def solution(mesh):
    in_specs = (
        P("dp", None, "tensor"),
        P("dp"),
        P("dp"),
        P("dp"),
        P(),
        P(),
        P("tensor", None),
        P("dp", "tensor", None),
        P("dp", None, "tensor"),
        P("dp", None, "tensor"),
    )
    out_specs = (P("dp", None, "tensor"), P("dp", "tensor", None), P("dp", None, "tensor"))
    return jax.shard_map(
        on_device, mesh=mesh, in_specs=in_specs, out_specs=out_specs, check_vma=False
    )
```

```python
import jax
import jax.numpy as jnp
from jax import lax
from jax.experimental import pallas as pl
from jax.experimental.pallas import tpu as pltpu
from jax.sharding import PartitionSpec as P

BF = jnp.bfloat16
F32 = jnp.float32
RING = 4
DP = RING * RING
TENSOR = 2 * RING
TILE = 256
W_SLOTS = 3
BLOCK_ORDER = ((2, 1), (2, 0), (1, 1), (1, 0), (3, 1), (3, 0), (0, 1), (0, 0))


def mm(a, b):
    return jnp.dot(a, b, preferred_element_type=F32)


def kernel(
    dest_ref,
    count_ref,
    job_ref,
    owner_ref,
    rank_ref,
    tok_ref,
    cot_ref,
    a_ref,
    b_ref,
    w_ref,
    out_ref,
    ga_ref,
    gb_ref,
    tok_v,
    cot_v,
    a_v,
    b_v,
    out_v,
    tok_s,
    tok_r,
    facts_s,
    facts_r,
    place_hot,
    x_hot,
    c_hot,
    slot_hot,
    xs,
    x_s,
    x_r,
    c_s,
    c_r,
    fa,
    fb,
    wbuf,
    sib_s,
    sib_r,
    hold,
    hop_s,
    hop_r,
    ring_s,
    ring_r,
    part_s,
    part_r,
    ranks,
    ad_s,
    ad_r,
    g_own,
    g_s,
    g_r,
    in_sem,
    out_sem,
    w_sem,
    facts_ss,
    facts_rs,
    tok_ss,
    tok_rs,
    fac_ss,
    fac_rs,
    c_ss,
    c_rs,
    x_ss,
    x_rs,
    sib_ss,
    sib_rs,
    hop_ss,
    hop_rs,
    ring_ss,
    ring_rs,
    part_ss,
    part_rs,
    gath_ss,
    gath_rs,
    ad_ss,
    ad_rs,
    g_ss,
    g_rs,
):
    seq_len, width = tok_ref.shape[1:]
    rows = DP * seq_len
    half = rows // 2
    me = lax.axis_index("dp")
    t = lax.axis_index("tensor")
    y, z = me // RING, me % RING
    x, c = t // 2, t % 2
    own_side = (y + z) % 2
    own_job = jnp.where(own_side == 0, z // 2, y // 2)
    others = ((own_side, 1 - own_job), (1 - own_side, 0), (1 - own_side, 1))
    tiles = width // TILE
    wide_half = width // 2
    column_halves = (slice(0, wide_half), slice(wide_half, width))

    def remote(src, dst, send, recv, **where):
        return pltpu.make_async_remote_copy(
            src_ref=src,
            dst_ref=dst,
            send_sem=send,
            recv_sem=recv,
            device_id=where,
            device_id_type=pl.DeviceIdType.MESH,
        )

    def iota(shape, axis):
        return lax.broadcasted_iota(jnp.int32, shape, axis)

    def along(side, k):
        return ((y + k) % RING) * RING + z if side == 0 else y * RING + (z + k) % RING

    def owner_of(side, job):
        first = y * RING + 2 * job + y % 2
        second = (2 * job + (z + 1) % 2) * RING + z
        return jnp.where(side == 0, first, second)

    def owner_ring(k):
        return jnp.where(own_side == 0, y * RING + (z + k) % RING, ((y + k) % RING) * RING + z)

    def mid_ring(k):
        return jnp.where(own_side == 1, y * RING + (z + k) % RING, ((y + k) % RING) * RING + z)

    def mid_job(k):
        return jnp.where(own_side == 1, (z + k) % RING, (y + k) % RING) // 2

    def rank_at(owner):
        total = jnp.int32(0)
        for j in range(DP):
            total = total + jnp.where(owner_ref[j] == owner, rank_ref[j], 0)
        return total

    def factor_at(owner, columns):
        return 32.0 / jnp.full((1, columns), rank_at(owner).astype(F32), F32)

    loads = [
        pltpu.make_async_copy(src, dst, in_sem.at[n])
        for n, (src, dst) in enumerate(((tok_ref, tok_v), (a_ref, a_v), (b_ref, b_v), (cot_ref, cot_v)))
    ]
    for load in loads:
        load.start()

    barrier = pltpu.get_barrier_semaphore()
    for k in range(1, DP):
        pl.semaphore_signal(
            barrier, inc=1, device_id={"dp": (me + k) % DP}, device_id_type=pl.DeviceIdType.MESH
        )
    for k in range(1, TENSOR):
        pl.semaphore_signal(
            barrier, inc=1, device_id={"tensor": (t + k) % TENSOR}, device_id_type=pl.DeviceIdType.MESH
        )

    def w_copy(i):
        ahead, other = BLOCK_ORDER[i]
        block = ((x + ahead) % RING) * 2 + (1 - c if other else c)
        columns = pl.ds(pl.multiple_of(block * width, width), width)
        return pltpu.make_async_copy(w_ref.at[:, columns], wbuf.at[i % W_SLOTS], w_sem.at[i % W_SLOTS])

    for i in range(W_SLOTS):
        w_copy(i).start()

    target = [lax.shift_right_logical(dest_ref[i], 4) for i in range(DP)]
    chosen = []
    for k in range(DP):
        to = (me + k) % DP
        index = jnp.int32(0)
        for i in range(DP):
            index = jnp.where(target[i] == to, i, index)
        chosen.append(index)
        owner = owner_ref[job_ref[index]]
        oy, oz = lax.shift_right_logical(owner, 2), owner & 3
        base = jnp.where(
            ((oy + oz) & 1) == 0,
            oy * 4 + lax.shift_right_logical(oz, 1) * 2,
            4 * RING + oz * 4 + lax.shift_right_logical(oy, 1) * 2,
        )
        row = iota((8, 128), 0)
        tile = jnp.where(row == 0, dest_ref[index] & 15, jnp.where(row == 1, count_ref[index], base))
        if k == 0:
            facts_r[me] = tile
        else:
            facts_s[k - 1] = tile

    loads[0].wait()
    for k in range(1, DP):
        tok_s[k - 1] = tok_v[chosen[k]]
    tok_r[me] = tok_v[chosen[0]]

    pl.semaphore_wait(barrier, DP - 1 + TENSOR - 1)

    def facts_copy(k):
        return remote(
            facts_s.at[k - 1], facts_r.at[me], facts_ss.at[k - 1], facts_rs.at[k - 1], dp=(me + k) % DP
        )

    def tok_copy(h, k):
        columns = column_halves[h]
        return remote(
            tok_s.at[k - 1, :, columns],
            tok_r.at[me, :, columns],
            tok_ss.at[h, k - 1],
            tok_rs.at[h, k - 1],
            dp=(me + k) % DP,
        )

    def fac_copy(k, n):
        held = (fa, fb)[n].at[own_side, own_job]
        return remote(held, held, fac_ss.at[k - 1, n], fac_rs.at[own_side, own_job, n], dp=owner_ring(k))

    def fac_wait(n, which):
        for side, job in which:
            held = (fa, fb)[n].at[side, job]
            remote(held, held, fac_ss.at[0, n], fac_rs.at[side, job, n], dp=me).wait_recv()

    def fac_relay(n):
        side, job = 1 - own_side, mid_job((RING - 1, 1)[n])
        held = (fa, fb)[n].at[side, job]
        return remote(held, held, fac_ss.at[1, n], fac_rs.at[side, job, n], dp=mid_ring((1, RING - 1)[n]))

    for k in range(1, DP):
        facts_copy(k).start()
    for h in range(2):
        for k in range(1, DP):
            tok_copy(h, k).start()
    my_rank = rank_at(me)
    loads[1].wait()
    fa[own_side, own_job] = jnp.where(
        iota(a_v.shape[1:], 1) < my_rank, a_v[0].astype(F32), 0.0
    ).astype(BF)
    for k in (1, RING - 1):
        fac_copy(k, 0).start()
    loads[2].wait()
    fb[own_side, own_job] = jnp.where(
        iota(b_v.shape[1:], 0) < my_rank, b_v[0].astype(F32), 0.0
    ).astype(BF)
    for k in (1, RING - 1):
        fac_copy(k, 1).start()

    for k in range(1, DP):
        facts_copy(k).wait_recv()
    slot_c = facts_r[:, 0, :].astype(F32)
    live_c = facts_r[:, 1, :].astype(F32)
    base_c = facts_r[:, 2, :].astype(F32)
    square = (DP, 128)
    diagonal = iota(square, 0) == iota(square, 1)
    slot_l = jnp.sum(jnp.where(diagonal, slot_c, 0.0), 0, keepdims=True)
    base_l = jnp.sum(jnp.where(diagonal, base_c, 0.0), 0, keepdims=True)
    earlier = (base_l == base_c) & (slot_l < slot_c) & (iota(square, 1) < DP)
    turn_c = jnp.sum(jnp.where(earlier, 1.0, 0.0), 1, keepdims=True)
    lane_c = base_c + turn_c
    lane_l = jnp.sum(jnp.where(diagonal, lane_c, 0.0), 0, keepdims=True)
    wide = (DP, rows)
    seq_of = iota(wide, 1) // seq_len
    slot_1, live_1, lane_1 = slot_c[:, :1], live_c[:, :1], lane_c[:, :1]
    in_slot = slot_1 == seq_of.astype(F32)
    in_order = iota(wide, 0) == seq_of
    position = (iota((1, rows), 1) % seq_len).astype(F32)

    def spread(where, value):
        return jnp.sum(jnp.where(where, value, 0.0), 0, keepdims=True)

    live = position < spread(in_order, live_1)
    c_row = spread(in_slot, lane_1) * seq_len + position
    x_row = jnp.where(live, spread(in_order, lane_1) * seq_len + position, -1.0)
    slot_row = jnp.where(live, spread(in_order, slot_1) * seq_len + position, -1.0)

    def build(hot, wanted):
        @pl.loop(0, hot.shape[0] // 128)
        def _(n):
            at = pl.ds(pl.multiple_of(n * 128, 128), 128)
            row = (iota((128, rows), 0) + n * 128).astype(F32)
            hot[at, :] = jnp.where(row == wanted, 1.0, 0.0).astype(BF)

    build(x_hot, x_row)
    build(place_hot, slot_row)
    build(c_hot, c_row)

    lane_shape = (2, RING, 2, 64)

    def lane_copy(send, recv, send_sem, recv_sem, h, side, k):
        place = y if side == 0 else z
        columns = column_halves[h]
        return remote(
            send.at[side, (place + k) % RING, :, :, columns],
            recv.at[side, :, place, :, columns],
            send_sem.at[h, side, k - 1],
            recv_sem.at[h, side, k - 1],
            dp=along(side, k),
        )

    def x_copy(h, side, k):
        return lane_copy(x_s, x_r, x_ss, x_rs, h, side, k)

    def c_copy(h, side, k):
        return lane_copy(c_s, c_r, c_ss, c_rs, h, side, k)

    def make_lanes(hot, source, send, columns):
        for n in range(columns.start, columns.stop, TILE):
            at = slice(n, n + TILE)
            send[:, :, :, :, at] = mm(hot[...], source(at)).astype(BF).reshape(lane_shape + (TILE,))

    def keep_lanes(send, recv):
        for side in range(2):
            place = y if side == 0 else z
            recv[side, :, place] = send[side, place]

    loads[3].wait()
    for columns in column_halves:
        make_lanes(c_hot, lambda at: cot_v[:, at], c_s, columns)

    def landed(at):
        return tok_r[:, :, at].reshape(rows, at.stop - at.start)

    for h, columns in enumerate(column_halves):
        for k in range(1, DP):
            tok_copy(h, k).wait_recv()
        make_lanes(x_hot, landed, x_s, columns)
        for k in (2, 1, 3):
            for side in range(2):
                x_copy(h, side, k).start()
        for n in range(columns.start, columns.stop, TILE):
            at = slice(n, n + TILE)
            xs[:, at] = mm(place_hot[...], landed(at)).astype(BF)

    for n in range(2):
        fac_wait(n, others[1:])
        fac_relay(n).start()
    for h in range(2):
        for k in (2, 1, 3):
            for side in range(2):
                c_copy(h, side, k).start()

    def block(i, put):
        w_copy(i).wait()

        @pl.loop(0, tiles)
        def _(n):
            columns = pl.ds(pl.multiple_of(n * TILE, TILE), TILE)
            put(columns, mm(xs[...], wbuf[i % W_SLOTS, :, columns]))

        if i + W_SLOTS < len(BLOCK_ORDER):
            w_copy(i + W_SLOTS).start()

    def sib_copy(j):
        return remote(
            sib_s.at[j % 2], sib_r.at[j], sib_ss.at[j % 2], sib_rs.at[j], tensor=x * 2 + (1 - c)
        )

    def other_block(j):
        if j >= 2:
            sib_copy(j - 2).wait_send()

        def put(columns, value):
            sib_s[j % 2, :, columns] = value.astype(BF)

        block(2 * j, put)
        sib_copy(j).start()

    def my_block(j, slot):
        def put(columns, value):
            hold[slot, :, columns] = value

        block(2 * j + 1, put)

    right, left = ((x + 1) % RING) * 2 + c, ((x + 3) % RING) * 2 + c
    parts = (slice(0, half), slice(half, rows))

    def hop_copy(way):
        return remote(
            hop_s.at[way], hop_r.at[way], hop_ss.at[way], hop_rs.at[way], tensor=(right, left)[way]
        )

    def ring_copy(way, part):
        return remote(
            ring_s.at[way, part],
            ring_r.at[way, part],
            ring_ss.at[way, part],
            ring_rs.at[way, part],
            tensor=(right, left)[way],
        )

    other_block(0)
    my_block(0, 0)
    other_block(1)
    sib_copy(0).wait_recv()
    for way in range(2):
        hop_s[way] = (hold[0, parts[way]] + sib_r[0, parts[way]].astype(F32)).astype(BF)
        hop_copy(way).start()
    my_block(1, 1)
    other_block(2)
    my_block(2, 0)
    other_block(3)
    my_block(3, 2)

    def part_copy(kind, k):
        to = (t + k) % TENSOR
        return remote(
            part_s.at[kind, to],
            part_r.at[kind, k],
            part_ss.at[kind, k - 1],
            part_rs.at[kind, k - 1],
            tensor=to,
        )

    def gath_copy(kind, k):
        to = (t + k) % TENSOR
        held = ranks.at[kind, t]
        return remote(held, held, gath_ss.at[kind, k - 1], gath_rs.at[kind, k - 1], tensor=to)

    def served(ref, side, job):
        return ref[side, job].reshape(RING * 64, width)

    def send_parts(kind, make):
        for side in range(2):
            for job in range(2):
                value = make(side, job)
                for piece in range(2):
                    part_s[kind, side * 4 + job * 2 + piece] = value[piece * 128 : (piece + 1) * 128].astype(
                        BF
                    )
        for k in range(1, TENSOR):
            part_copy(kind, k).start()
        part_r[kind, 0] = part_s[kind, t]

    def sum_parts(kind, scale):
        for k in range(1, TENSOR):
            part_copy(kind, k).wait_recv()
        total = part_r[kind, 0].astype(F32)
        for k in range(1, TENSOR):
            total = total + part_r[kind, k].astype(F32)
        ranks[kind, t] = (total if scale is None else total * scale).astype(BF)
        for k in range(1, TENSOR):
            gath_copy(kind, k).start()

    def gathered(kind):
        for k in range(1, TENSOR):
            frm = (t + TENSOR - k) % TENSOR
            held = ranks.at[kind, frm]
            remote(held, held, gath_ss.at[kind, k - 1], gath_rs.at[kind, k - 1], tensor=t).wait_recv()

    def rank_rows(kind, side, job):
        return ranks[kind, pl.ds(side * 4 + job * 2, 2)].reshape(RING * 64, ranks.shape[3])

    keep_lanes(x_s, x_r)
    keep_lanes(c_s, c_r)
    fac_wait(0, others[:1])
    for h in range(2):
        for side in range(2):
            for k in range(1, RING):
                x_copy(h, side, k).wait_recv()
    send_parts(0, lambda side, job: mm(served(x_r, side, job), fa[side, job]))

    sib_copy(1).wait_recv()
    ring_s[0, 1] = (hold[1, parts[1]] + sib_r[1, parts[1]].astype(F32)).astype(BF)
    sib_copy(2).wait_recv()
    ring_s[1, 0] = (hold[0, parts[0]] + sib_r[2, parts[0]].astype(F32)).astype(BF)
    sum_parts(0, None)
    ring_copy(0, 1).start()
    ring_copy(1, 0).start()

    @pl.loop(0, rows // 128)
    def _(n):
        at = pl.ds(pl.multiple_of(n * 128, 128), 128)
        row = iota((128, 128), 0) + n * 128
        mine = jnp.where(slot_l == (row // seq_len).astype(F32), lane_l, 0.0)
        place = jnp.sum(mine, 1, keepdims=True) * seq_len + (row % seq_len).astype(F32)[:, :1]
        slot_hot[at, :] = jnp.where(iota((128, 2 * rows), 1).astype(F32) == place, 1.0, 0.0).astype(BF)

    def ad_copy(side, k):
        place = y if side == 0 else z
        return remote(
            ad_s.at[side, :, (place + k) % RING],
            ad_r.at[side, place],
            ad_ss.at[side, k - 1],
            ad_rs.at[side, k - 1],
            dp=along(side, k),
        )

    fac_wait(1, others[:1])
    gathered(0)
    for side in range(2):
        place = y if side == 0 else z
        for job in range(2):
            value = mm(rank_rows(0, side, job), fb[side, job]) * factor_at(owner_of(side, job), width)
            ad_s[side, job] = value.astype(BF).reshape(RING, 64, width)
        for k in (2, 1, 3):
            ad_copy(side, k).start()
        ad_r[side, place] = ad_s[side, :, place]

    hop_copy(0).wait_recv()
    ring_s[0, 0] = (
        hold[1, parts[0]] + sib_r[1, parts[0]].astype(F32) + hop_r[0].astype(F32)
    ).astype(BF)
    hop_copy(1).wait_recv()
    ring_s[1, 1] = (
        hold[0, parts[1]] + sib_r[2, parts[1]].astype(F32) + hop_r[1].astype(F32)
    ).astype(BF)
    ring_copy(0, 0).start()
    ring_copy(1, 1).start()

    for h in range(2):
        for side in range(2):
            for k in range(1, RING):
                c_copy(h, side, k).wait_recv()
    send_parts(
        1,
        lambda side, job: lax.dot_general(
            served(c_r, side, job), fb[side, job], (((1,), (1,)), ((), ())), preferred_element_type=F32
        ),
    )

    def g_copy(n, which):
        side, job = others[which]
        k = jnp.where(
            side == 0,
            (z - (2 * job + y % 2) + RING) % RING,
            (y - (2 * job + (z + 1) % 2) + RING) % RING,
        )
        return remote(
            g_s.at[n, which], g_r.at[n, k - 1], g_ss.at[n, which], g_rs.at[n, k - 1], dp=owner_of(side, job)
        )

    def g_wait(n, k):
        remote(g_s.at[n, 0], g_r.at[n, k - 1], g_ss.at[n, 0], g_rs.at[n, k - 1], dp=me).wait_recv()

    def gradient(n, kind, row_ref):
        for which, (side, job) in enumerate(others + ((own_side, own_job),)):
            turned = rank_rows(kind, side, job).astype(F32).T.astype(BF)
            value = mm(turned, row_ref[side, job].reshape(RING * 64, width)) * (1.0 / seq_len)
            if n == 1:
                value = value * factor_at(owner_of(side, job), width)
            if which < 3:
                g_s[n, which] = value.astype(BF)
                g_copy(n, which).start()
            else:
                g_own[n] = value

    gradient(1, 0, c_r)

    sum_parts(1, factor_at(owner_of(t // 4, (t // 2) % 2), ranks.shape[3]))
    gathered(1)
    gradient(0, 1, x_r)

    sib_copy(3).wait_recv()
    for side in range(2):
        for k in range(1, RING):
            ad_copy(side, k).wait_recv()
    for n in range(tiles):
        at = slice(n * TILE, (n + 1) * TILE)
        back = ad_r[:, :, :, :, at].reshape(2 * rows, TILE)
        hold[2, :, at] = hold[2, :, at] + sib_r[3, :, at].astype(F32) + mm(slot_hot[...], back)
    for part in (1, 0):
        ring_copy(0, part).wait_recv()
        ring_copy(1, 1 - part).wait_recv()
    for part in range(2):
        out_v[parts[part]] = (
            hold[2, parts[part]] + ring_r[0, part].astype(F32) + ring_r[1, part].astype(F32)
        ).astype(BF)
    stores = [pltpu.make_async_copy(out_v, out_ref, out_sem.at[2])]
    stores[0].start()

    for n, g_ref in ((1, gb_ref), (0, ga_ref)):
        for k in range(1, RING):
            g_wait(n, k)
        total = g_own[n]
        for k in range(1, RING):
            total = total + g_r[n, k - 1].astype(F32)
        g_own[n] = total
        stores.append(pltpu.make_async_copy(g_own.at[n], g_ref, out_sem.at[n]))
        stores[-1].start()

    for k in range(1, DP):
        facts_copy(k).wait_send()
        for h in range(2):
            tok_copy(h, k).wait_send()
    for n in range(2):
        for k in (1, RING - 1):
            fac_copy(k, n).wait_send()
        fac_relay(n).wait_send()
    for k in range(1, RING):
        for side in range(2):
            for h in range(2):
                c_copy(h, side, k).wait_send()
                x_copy(h, side, k).wait_send()
            ad_copy(side, k).wait_send()
    for j in (2, 3):
        sib_copy(j).wait_send()
    for way in range(2):
        hop_copy(way).wait_send()
        for part in range(2):
            ring_copy(way, part).wait_send()
    for kind in range(2):
        for k in range(1, TENSOR):
            part_copy(kind, k).wait_send()
            gath_copy(kind, k).wait_send()
    for n in range(2):
        for which in range(3):
            g_copy(n, which).wait_send()
    for store in stores:
        store.wait()


def finish(out_ref, gb_ref, ga_ref, out_to, gb_to, ga_to, out_v, gb_v, ga_v, turned_v, sem):
    names = ((ga_ref, ga_v, turned_v, ga_to), (gb_ref, gb_v, gb_v, gb_to), (out_ref, out_v, out_v, out_to))
    loads = [pltpu.make_async_copy(src, held, sem.at[0, n]) for n, (src, held, _, _) in enumerate(names)]
    stores = [pltpu.make_async_copy(held, dst, sem.at[1, n]) for n, (_, _, held, dst) in enumerate(names)]
    for load in loads:
        load.start()
    loads[0].wait()
    turned_v[...] = ga_v[...].T
    stores[0].start()
    for n in (1, 2):
        loads[n].wait()
        stores[n].start()
    for store in stores:
        store.wait()


def on_device(
    tokens,
    destinations,
    counts,
    sequence_job_ids,
    job_owner_slot,
    rank_per_job,
    weight,
    input_factor_table,
    output_factor_table,
    cotangent,
):
    slot_count, seq_len, width = tokens.shape
    max_rank = input_factor_table.shape[2]
    rows = slot_count * seq_len
    anywhere = pl.BlockSpec(memory_space=pl.ANY)
    smem = pl.BlockSpec(memory_space=pltpu.SMEM)
    dma = pltpu.SemaphoreType.DMA
    served = (2, 2, RING, 64, width)
    lanes = (2, RING, 2, 64, width)
    out, ga, gb = pl.pallas_call(
        kernel,
        out_shape=(
            jax.ShapeDtypeStruct((rows, width), BF),
            jax.ShapeDtypeStruct((max_rank, width), F32),
            jax.ShapeDtypeStruct((max_rank, width), F32),
        ),
        in_specs=[smem] * 5 + [anywhere] * 5,
        out_specs=(anywhere,) * 3,
        scratch_shapes=[
            pltpu.VMEM(tokens.shape, BF),
            pltpu.VMEM((rows, width), BF),
            pltpu.VMEM(input_factor_table.shape, BF),
            pltpu.VMEM(output_factor_table.shape, BF),
            pltpu.VMEM((rows, width), BF),
            pltpu.VMEM((DP - 1, seq_len, width), BF),
            pltpu.VMEM((DP, seq_len, width), BF),
            pltpu.VMEM((DP - 1, 8, 128), jnp.int32),
            pltpu.VMEM((DP, 8, 128), jnp.int32),
            pltpu.VMEM((rows, rows), BF),
            pltpu.VMEM((2 * rows, rows), BF),
            pltpu.VMEM((2 * rows, rows), BF),
            pltpu.VMEM((rows, 2 * rows), BF),
            pltpu.VMEM((rows, width), BF),
            pltpu.VMEM(lanes, BF),
            pltpu.VMEM(served, BF),
            pltpu.VMEM(lanes, BF),
            pltpu.VMEM(served, BF),
            pltpu.VMEM((2, 2, width, max_rank), BF),
            pltpu.VMEM((2, 2, max_rank, width), BF),
            pltpu.VMEM((W_SLOTS, width, width), BF),
            pltpu.VMEM((2, rows, width), BF),
            pltpu.VMEM((4, rows, width), BF),
            pltpu.VMEM((3, rows, width), F32),
            pltpu.VMEM((2, rows // 2, width), BF),
            pltpu.VMEM((2, rows // 2, width), BF),
            pltpu.VMEM((2, 2, rows // 2, width), BF),
            pltpu.VMEM((2, 2, rows // 2, width), BF),
            pltpu.VMEM((2, TENSOR, 128, max_rank), BF),
            pltpu.VMEM((2, TENSOR, 128, max_rank), BF),
            pltpu.VMEM((2, TENSOR, 128, max_rank), BF),
            pltpu.VMEM(served, BF),
            pltpu.VMEM(lanes, BF),
            pltpu.VMEM((2, max_rank, width), F32),
            pltpu.VMEM((2, 3, max_rank, width), BF),
            pltpu.VMEM((2, 3, max_rank, width), BF),
            dma((4,)),
            dma((3,)),
            dma((W_SLOTS,)),
            dma((DP - 1,)),
            dma((DP - 1,)),
            dma((2, DP - 1)),
            dma((2, DP - 1)),
            dma((RING - 1, 2)),
            dma((2, 2, 2)),
            dma((2, 2, RING - 1)),
            dma((2, 2, RING - 1)),
            dma((2, 2, RING - 1)),
            dma((2, 2, RING - 1)),
            dma((2,)),
            dma((4,)),
            dma((2,)),
            dma((2,)),
            dma((2, 2)),
            dma((2, 2)),
            dma((2, TENSOR - 1)),
            dma((2, TENSOR - 1)),
            dma((2, TENSOR - 1)),
            dma((2, TENSOR - 1)),
            dma((2, RING - 1)),
            dma((2, RING - 1)),
            dma((2, 3)),
            dma((2, 3)),
        ],
        compiler_params=pltpu.CompilerParams(
            collective_id=0, has_side_effects=True, vmem_limit_bytes=58 * 2**20
        ),
    )(
        destinations,
        counts,
        sequence_job_ids,
        job_owner_slot,
        rank_per_job,
        tokens,
        cotangent.reshape(rows, width),
        input_factor_table,
        output_factor_table,
        weight,
    )
    out, gb, ga = pl.pallas_call(
        finish,
        out_shape=(
            jax.ShapeDtypeStruct((rows, width), BF),
            jax.ShapeDtypeStruct((max_rank, width), F32),
            jax.ShapeDtypeStruct((width, max_rank), F32),
        ),
        in_specs=[anywhere] * 3,
        out_specs=(anywhere,) * 3,
        scratch_shapes=[
            pltpu.VMEM((rows, width), BF),
            pltpu.VMEM((max_rank, width), F32),
            pltpu.VMEM((max_rank, width), F32),
            pltpu.VMEM((width, max_rank), F32),
            dma((2, 3)),
        ],
    )(out, gb, ga)
    return out.reshape(slot_count, seq_len, width), ga[None], gb[None]


def solution(mesh):
    in_specs = (
        P("dp", None, "tensor"),
        P("dp"),
        P("dp"),
        P("dp"),
        P(),
        P(),
        P("tensor", None),
        P("dp", "tensor", None),
        P("dp", None, "tensor"),
        P("dp", None, "tensor"),
    )
    out_specs = (P("dp", None, "tensor"), P("dp", "tensor", None), P("dp", None, "tensor"))
    return jax.shard_map(
        on_device, mesh=mesh, in_specs=in_specs, out_specs=out_specs, check_vma=False
    )
```

```python
import jax
import jax.numpy as jnp
from jax import lax
from jax.experimental import pallas as pl
from jax.experimental.pallas import tpu as pltpu
from jax.sharding import PartitionSpec as P

BF = jnp.bfloat16
F32 = jnp.float32
RING = 4
DP = RING * RING
TENSOR = 2 * RING
TILE = 256
W_SLOTS = 3
BLOCK_ORDER = ((2, 1), (2, 0), (1, 1), (1, 0), (3, 1), (3, 0), (0, 1), (0, 0))


def mm(a, b):
    return jnp.dot(a, b, preferred_element_type=F32)


def kernel(
    dest_ref,
    count_ref,
    job_ref,
    owner_ref,
    rank_ref,
    tok_ref,
    cot_ref,
    a_ref,
    b_ref,
    w_ref,
    out_ref,
    ga_ref,
    gb_ref,
    tok_v,
    cot_v,
    a_v,
    b_v,
    out_v,
    tok_s,
    tok_r,
    facts_s,
    facts_r,
    place_hot,
    x_hot,
    c_hot,
    slot_hot,
    xs,
    x_s,
    x_r,
    c_s,
    c_r,
    fa,
    fb,
    wbuf,
    sib_s,
    sib_r,
    hold,
    hop_s,
    hop_r,
    ring_s,
    ring_r,
    part_s,
    part_r,
    ranks,
    ad_s,
    ad_r,
    g_own,
    g_s,
    g_r,
    in_sem,
    out_sem,
    w_sem,
    facts_ss,
    facts_rs,
    tok_ss,
    tok_rs,
    fac_ss,
    fac_rs,
    c_ss,
    c_rs,
    x_ss,
    x_rs,
    sib_ss,
    sib_rs,
    hop_ss,
    hop_rs,
    ring_ss,
    ring_rs,
    part_ss,
    part_rs,
    gath_ss,
    gath_rs,
    ad_ss,
    ad_rs,
    g_ss,
    g_rs,
):
    seq_len, width = tok_ref.shape[1:]
    rows = DP * seq_len
    half = rows // 2
    me = lax.axis_index("dp")
    t = lax.axis_index("tensor")
    y, z = me // RING, me % RING
    x, c = t // 2, t % 2
    own_side = (y + z) % 2
    own_job = jnp.where(own_side == 0, z // 2, y // 2)
    others = ((own_side, 1 - own_job), (1 - own_side, 0), (1 - own_side, 1))
    tiles = width // TILE
    wide_half = width // 2
    column_halves = (slice(0, wide_half), slice(wide_half, width))

    def remote(src, dst, send, recv, **where):
        return pltpu.make_async_remote_copy(
            src_ref=src,
            dst_ref=dst,
            send_sem=send,
            recv_sem=recv,
            device_id=where,
            device_id_type=pl.DeviceIdType.MESH,
        )

    def iota(shape, axis):
        return lax.broadcasted_iota(jnp.int32, shape, axis)

    def along(side, k):
        return ((y + k) % RING) * RING + z if side == 0 else y * RING + (z + k) % RING

    def owner_of(side, job):
        first = y * RING + 2 * job + y % 2
        second = (2 * job + (z + 1) % 2) * RING + z
        return jnp.where(side == 0, first, second)

    def owner_ring(k):
        return jnp.where(own_side == 0, y * RING + (z + k) % RING, ((y + k) % RING) * RING + z)

    def mid_ring(k):
        return jnp.where(own_side == 1, y * RING + (z + k) % RING, ((y + k) % RING) * RING + z)

    def mid_job(k):
        return jnp.where(own_side == 1, (z + k) % RING, (y + k) % RING) // 2

    def rank_at(owner):
        total = jnp.int32(0)
        for j in range(DP):
            total = total + jnp.where(owner_ref[j] == owner, rank_ref[j], 0)
        return total

    def factor_at(owner, columns):
        return 32.0 / jnp.full((1, columns), rank_at(owner).astype(F32), F32)

    loads = [
        pltpu.make_async_copy(src, dst, in_sem.at[n])
        for n, (src, dst) in enumerate(((tok_ref, tok_v), (a_ref, a_v), (b_ref, b_v), (cot_ref, cot_v)))
    ]
    for load in loads:
        load.start()

    barrier = pltpu.get_barrier_semaphore()
    for k in range(1, DP):
        pl.semaphore_signal(
            barrier, inc=1, device_id={"dp": (me + k) % DP}, device_id_type=pl.DeviceIdType.MESH
        )
    for k in range(1, TENSOR):
        pl.semaphore_signal(
            barrier, inc=1, device_id={"tensor": (t + k) % TENSOR}, device_id_type=pl.DeviceIdType.MESH
        )

    def w_copy(i):
        ahead, other = BLOCK_ORDER[i]
        block = ((x + ahead) % RING) * 2 + (1 - c if other else c)
        columns = pl.ds(pl.multiple_of(block * width, width), width)
        return pltpu.make_async_copy(w_ref.at[:, columns], wbuf.at[i % W_SLOTS], w_sem.at[i % W_SLOTS])

    for i in range(W_SLOTS):
        w_copy(i).start()

    target = [lax.shift_right_logical(dest_ref[i], 4) for i in range(DP)]
    chosen = []
    for k in range(DP):
        to = (me + k) % DP
        index = jnp.int32(0)
        for i in range(DP):
            index = jnp.where(target[i] == to, i, index)
        chosen.append(index)
        owner = owner_ref[job_ref[index]]
        oy, oz = lax.shift_right_logical(owner, 2), owner & 3
        base = jnp.where(
            ((oy + oz) & 1) == 0,
            oy * 4 + lax.shift_right_logical(oz, 1) * 2,
            4 * RING + oz * 4 + lax.shift_right_logical(oy, 1) * 2,
        )
        row = iota((8, 128), 0)
        tile = jnp.where(row == 0, dest_ref[index] & 15, jnp.where(row == 1, count_ref[index], base))
        if k == 0:
            facts_r[me] = tile
        else:
            facts_s[k - 1] = tile

    loads[0].wait()
    for k in range(1, DP):
        tok_s[k - 1] = tok_v[chosen[k]]
    tok_r[me] = tok_v[chosen[0]]

    pl.semaphore_wait(barrier, DP - 1 + TENSOR - 1)

    def facts_copy(k):
        return remote(
            facts_s.at[k - 1], facts_r.at[me], facts_ss.at[k - 1], facts_rs.at[k - 1], dp=(me + k) % DP
        )

    def tok_copy(h, k):
        columns = column_halves[h]
        return remote(
            tok_s.at[k - 1, :, columns],
            tok_r.at[me, :, columns],
            tok_ss.at[h, k - 1],
            tok_rs.at[h, k - 1],
            dp=(me + k) % DP,
        )

    def fac_copy(k, n):
        held = (fa, fb)[n].at[own_side, own_job]
        return remote(held, held, fac_ss.at[k - 1, n], fac_rs.at[own_side, own_job, n], dp=owner_ring(k))

    def fac_wait(n, which):
        for side, job in which:
            held = (fa, fb)[n].at[side, job]
            remote(held, held, fac_ss.at[0, n], fac_rs.at[side, job, n], dp=me).wait_recv()

    def fac_relay(n):
        side, job = 1 - own_side, mid_job((RING - 1, 1)[n])
        held = (fa, fb)[n].at[side, job]
        return remote(held, held, fac_ss.at[1, n], fac_rs.at[side, job, n], dp=mid_ring((1, RING - 1)[n]))

    for k in range(1, DP):
        facts_copy(k).start()
    for h in range(2):
        for k in range(1, DP):
            tok_copy(h, k).start()
    my_rank = rank_at(me)
    loads[1].wait()
    fa[own_side, own_job] = jnp.where(
        iota(a_v.shape[1:], 1) < my_rank, a_v[0].astype(F32), 0.0
    ).astype(BF)
    for k in (1, RING - 1):
        fac_copy(k, 0).start()
    loads[2].wait()
    fb[own_side, own_job] = jnp.where(
        iota(b_v.shape[1:], 0) < my_rank, b_v[0].astype(F32), 0.0
    ).astype(BF)

    for k in range(1, DP):
        facts_copy(k).wait_recv()
    slot_c = facts_r[:, 0, :].astype(F32)
    live_c = facts_r[:, 1, :].astype(F32)
    base_c = facts_r[:, 2, :].astype(F32)
    square = (DP, 128)
    diagonal = iota(square, 0) == iota(square, 1)
    slot_l = jnp.sum(jnp.where(diagonal, slot_c, 0.0), 0, keepdims=True)
    base_l = jnp.sum(jnp.where(diagonal, base_c, 0.0), 0, keepdims=True)
    earlier = (base_l == base_c) & (slot_l < slot_c) & (iota(square, 1) < DP)
    turn_c = jnp.sum(jnp.where(earlier, 1.0, 0.0), 1, keepdims=True)
    lane_c = base_c + turn_c
    lane_l = jnp.sum(jnp.where(diagonal, lane_c, 0.0), 0, keepdims=True)
    wide = (DP, rows)
    seq_of = iota(wide, 1) // seq_len
    slot_1, live_1, lane_1 = slot_c[:, :1], live_c[:, :1], lane_c[:, :1]
    in_slot = slot_1 == seq_of.astype(F32)
    in_order = iota(wide, 0) == seq_of
    position = (iota((1, rows), 1) % seq_len).astype(F32)

    def spread(where, value):
        return jnp.sum(jnp.where(where, value, 0.0), 0, keepdims=True)

    live = position < spread(in_order, live_1)
    c_row = spread(in_slot, lane_1) * seq_len + position
    x_row = jnp.where(live, spread(in_order, lane_1) * seq_len + position, -1.0)
    slot_row = jnp.where(live, spread(in_order, slot_1) * seq_len + position, -1.0)

    def build(hot, wanted):
        @pl.loop(0, hot.shape[0] // 128)
        def _(n):
            at = pl.ds(pl.multiple_of(n * 128, 128), 128)
            row = (iota((128, rows), 0) + n * 128).astype(F32)
            hot[at, :] = jnp.where(row == wanted, 1.0, 0.0).astype(BF)

    build(x_hot, x_row)
    build(place_hot, slot_row)
    build(c_hot, c_row)

    lane_shape = (2, RING, 2, 64)

    def lane_copy(send, recv, send_sem, recv_sem, h, side, k):
        place = y if side == 0 else z
        columns = column_halves[h]
        return remote(
            send.at[side, (place + k) % RING, :, :, columns],
            recv.at[side, :, place, :, columns],
            send_sem.at[h, side, k - 1],
            recv_sem.at[h, side, k - 1],
            dp=along(side, k),
        )

    def x_copy(h, side, k):
        return lane_copy(x_s, x_r, x_ss, x_rs, h, side, k)

    def c_copy(h, side, k):
        return lane_copy(c_s, c_r, c_ss, c_rs, h, side, k)

    def make_lanes(hot, source, send, columns):
        for n in range(columns.start, columns.stop, TILE):
            at = slice(n, n + TILE)
            send[:, :, :, :, at] = mm(hot[...], source(at)).astype(BF).reshape(lane_shape + (TILE,))

    def keep_lanes(send, recv):
        for side in range(2):
            place = y if side == 0 else z
            recv[side, :, place] = send[side, place]

    loads[3].wait()
    for columns in column_halves:
        make_lanes(c_hot, lambda at: cot_v[:, at], c_s, columns)

    def landed(at):
        return tok_r[:, :, at].reshape(rows, at.stop - at.start)

    for h, columns in enumerate(column_halves):
        for k in range(1, DP):
            tok_copy(h, k).wait_recv()
        make_lanes(x_hot, landed, x_s, columns)
        for k in (2, 1, 3):
            for side in range(2):
                x_copy(h, side, k).start()
        for n in range(columns.start, columns.stop, TILE):
            at = slice(n, n + TILE)
            xs[:, at] = mm(place_hot[...], landed(at)).astype(BF)

    for k in (1, RING - 1):
        fac_copy(k, 1).start()
    for h in range(2):
        for k in (2, 1, 3):
            for side in range(2):
                c_copy(h, side, k).start()

    def block(i, put):
        w_copy(i).wait()

        @pl.loop(0, tiles)
        def _(n):
            columns = pl.ds(pl.multiple_of(n * TILE, TILE), TILE)
            put(columns, mm(xs[...], wbuf[i % W_SLOTS, :, columns]))

        if i + W_SLOTS < len(BLOCK_ORDER):
            w_copy(i + W_SLOTS).start()

    def sib_copy(j):
        return remote(
            sib_s.at[j % 2], sib_r.at[j], sib_ss.at[j % 2], sib_rs.at[j], tensor=x * 2 + (1 - c)
        )

    def other_block(j):
        if j >= 2:
            sib_copy(j - 2).wait_send()

        def put(columns, value):
            sib_s[j % 2, :, columns] = value.astype(BF)

        block(2 * j, put)
        sib_copy(j).start()

    def my_block(j, slot):
        def put(columns, value):
            hold[slot, :, columns] = value

        block(2 * j + 1, put)

    right, left = ((x + 1) % RING) * 2 + c, ((x + 3) % RING) * 2 + c
    parts = (slice(0, half), slice(half, rows))

    def hop_copy(way):
        return remote(
            hop_s.at[way], hop_r.at[way], hop_ss.at[way], hop_rs.at[way], tensor=(right, left)[way]
        )

    def ring_copy(way, part):
        return remote(
            ring_s.at[way, part],
            ring_r.at[way, part],
            ring_ss.at[way, part],
            ring_rs.at[way, part],
            tensor=(right, left)[way],
        )

    other_block(0)
    my_block(0, 0)
    other_block(1)
    sib_copy(0).wait_recv()
    for way in range(2):
        hop_s[way] = (hold[0, parts[way]] + sib_r[0, parts[way]].astype(F32)).astype(BF)
        hop_copy(way).start()
    fac_wait(0, others[1:])
    fac_relay(0).start()
    my_block(1, 1)
    other_block(2)
    sib_copy(1).wait_recv()
    ring_s[0, 1] = (hold[1, parts[1]] + sib_r[1, parts[1]].astype(F32)).astype(BF)
    ring_copy(0, 1).start()
    my_block(2, 0)
    other_block(3)
    sib_copy(2).wait_recv()
    ring_s[1, 0] = (hold[0, parts[0]] + sib_r[2, parts[0]].astype(F32)).astype(BF)
    ring_copy(1, 0).start()
    my_block(3, 2)

    def part_copy(kind, k):
        to = (t + k) % TENSOR
        return remote(
            part_s.at[kind, to],
            part_r.at[kind, k],
            part_ss.at[kind, k - 1],
            part_rs.at[kind, k - 1],
            tensor=to,
        )

    def gath_copy(kind, k):
        to = (t + k) % TENSOR
        held = ranks.at[kind, t]
        return remote(held, held, gath_ss.at[kind, k - 1], gath_rs.at[kind, k - 1], tensor=to)

    def served(ref, side, job):
        return ref[side, job].reshape(RING * 64, width)

    def send_parts(kind, make):
        for side in range(2):
            for job in range(2):
                value = make(side, job)
                for piece in range(2):
                    part_s[kind, side * 4 + job * 2 + piece] = value[piece * 128 : (piece + 1) * 128].astype(
                        BF
                    )
        for k in range(1, TENSOR):
            part_copy(kind, k).start()
        part_r[kind, 0] = part_s[kind, t]

    def sum_parts(kind, scale):
        for k in range(1, TENSOR):
            part_copy(kind, k).wait_recv()
        total = part_r[kind, 0].astype(F32)
        for k in range(1, TENSOR):
            total = total + part_r[kind, k].astype(F32)
        ranks[kind, t] = (total if scale is None else total * scale).astype(BF)
        for k in range(1, TENSOR):
            gath_copy(kind, k).start()

    def gathered(kind):
        for k in range(1, TENSOR):
            frm = (t + TENSOR - k) % TENSOR
            held = ranks.at[kind, frm]
            remote(held, held, gath_ss.at[kind, k - 1], gath_rs.at[kind, k - 1], tensor=t).wait_recv()

    def rank_rows(kind, side, job):
        return ranks[kind, pl.ds(side * 4 + job * 2, 2)].reshape(RING * 64, ranks.shape[3])

    keep_lanes(x_s, x_r)
    keep_lanes(c_s, c_r)
    fac_wait(0, others[:1])
    for h in range(2):
        for side in range(2):
            for k in range(1, RING):
                x_copy(h, side, k).wait_recv()
    send_parts(0, lambda side, job: mm(served(x_r, side, job), fa[side, job]))

    fac_wait(1, others[1:])
    fac_relay(1).start()
    sum_parts(0, None)

    hop_copy(0).wait_recv()
    ring_s[0, 0] = (
        hold[1, parts[0]] + sib_r[1, parts[0]].astype(F32) + hop_r[0].astype(F32)
    ).astype(BF)
    hop_copy(1).wait_recv()
    ring_s[1, 1] = (
        hold[0, parts[1]] + sib_r[2, parts[1]].astype(F32) + hop_r[1].astype(F32)
    ).astype(BF)
    ring_copy(0, 0).start()
    ring_copy(1, 1).start()

    @pl.loop(0, rows // 128)
    def _(n):
        at = pl.ds(pl.multiple_of(n * 128, 128), 128)
        row = iota((128, 128), 0) + n * 128
        mine = jnp.where(slot_l == (row // seq_len).astype(F32), lane_l, 0.0)
        place = jnp.sum(mine, 1, keepdims=True) * seq_len + (row % seq_len).astype(F32)[:, :1]
        slot_hot[at, :] = jnp.where(iota((128, 2 * rows), 1).astype(F32) == place, 1.0, 0.0).astype(BF)

    def ad_copy(side, k):
        place = y if side == 0 else z
        return remote(
            ad_s.at[side, :, (place + k) % RING],
            ad_r.at[side, place],
            ad_ss.at[side, k - 1],
            ad_rs.at[side, k - 1],
            dp=along(side, k),
        )

    fac_wait(1, others[:1])
    gathered(0)
    for side in range(2):
        place = y if side == 0 else z
        for job in range(2):
            value = mm(rank_rows(0, side, job), fb[side, job]) * factor_at(owner_of(side, job), width)
            ad_s[side, job] = value.astype(BF).reshape(RING, 64, width)
        for k in (2, 1, 3):
            ad_copy(side, k).start()
        ad_r[side, place] = ad_s[side, :, place]

    for h in range(2):
        for side in range(2):
            for k in range(1, RING):
                c_copy(h, side, k).wait_recv()
    send_parts(
        1,
        lambda side, job: lax.dot_general(
            served(c_r, side, job), fb[side, job], (((1,), (1,)), ((), ())), preferred_element_type=F32
        ),
    )

    def g_copy(n, which):
        side, job = others[which]
        k = jnp.where(
            side == 0,
            (z - (2 * job + y % 2) + RING) % RING,
            (y - (2 * job + (z + 1) % 2) + RING) % RING,
        )
        return remote(
            g_s.at[n, which], g_r.at[n, k - 1], g_ss.at[n, which], g_rs.at[n, k - 1], dp=owner_of(side, job)
        )

    def g_wait(n, k):
        remote(g_s.at[n, 0], g_r.at[n, k - 1], g_ss.at[n, 0], g_rs.at[n, k - 1], dp=me).wait_recv()

    def gradient(n, kind, row_ref):
        for which, (side, job) in enumerate(others + ((own_side, own_job),)):
            turned = rank_rows(kind, side, job).astype(F32).T.astype(BF)
            value = mm(turned, row_ref[side, job].reshape(RING * 64, width)) * (1.0 / seq_len)
            if n == 1:
                value = value * factor_at(owner_of(side, job), width)
            if which < 3:
                g_s[n, which] = value.astype(BF)
                g_copy(n, which).start()
            else:
                g_own[n] = value

    gradient(1, 0, c_r)

    sum_parts(1, factor_at(owner_of(t // 4, (t // 2) % 2), ranks.shape[3]))
    gathered(1)
    gradient(0, 1, x_r)

    sib_copy(3).wait_recv()
    for side in range(2):
        for k in range(1, RING):
            ad_copy(side, k).wait_recv()
    for n in range(tiles):
        at = slice(n * TILE, (n + 1) * TILE)
        back = ad_r[:, :, :, :, at].reshape(2 * rows, TILE)
        hold[2, :, at] = hold[2, :, at] + sib_r[3, :, at].astype(F32) + mm(slot_hot[...], back)
    for part in (1, 0):
        ring_copy(0, part).wait_recv()
        ring_copy(1, 1 - part).wait_recv()
    for part in range(2):
        out_v[parts[part]] = (
            hold[2, parts[part]] + ring_r[0, part].astype(F32) + ring_r[1, part].astype(F32)
        ).astype(BF)
    stores = [pltpu.make_async_copy(out_v, out_ref, out_sem.at[2])]
    stores[0].start()

    for n, g_ref in ((1, gb_ref), (0, ga_ref)):
        for k in range(1, RING):
            g_wait(n, k)
        total = g_own[n]
        for k in range(1, RING):
            total = total + g_r[n, k - 1].astype(F32)
        g_own[n] = total
        stores.append(pltpu.make_async_copy(g_own.at[n], g_ref, out_sem.at[n]))
        stores[-1].start()

    for k in range(1, DP):
        facts_copy(k).wait_send()
        for h in range(2):
            tok_copy(h, k).wait_send()
    for n in range(2):
        for k in (1, RING - 1):
            fac_copy(k, n).wait_send()
        fac_relay(n).wait_send()
    for k in range(1, RING):
        for side in range(2):
            for h in range(2):
                c_copy(h, side, k).wait_send()
                x_copy(h, side, k).wait_send()
            ad_copy(side, k).wait_send()
    for j in (2, 3):
        sib_copy(j).wait_send()
    for way in range(2):
        hop_copy(way).wait_send()
        for part in range(2):
            ring_copy(way, part).wait_send()
    for kind in range(2):
        for k in range(1, TENSOR):
            part_copy(kind, k).wait_send()
            gath_copy(kind, k).wait_send()
    for n in range(2):
        for which in range(3):
            g_copy(n, which).wait_send()
    for store in stores:
        store.wait()


def finish(out_ref, gb_ref, ga_ref, out_to, gb_to, ga_to, out_v, gb_v, ga_v, turned_v, sem):
    names = ((ga_ref, ga_v, turned_v, ga_to), (gb_ref, gb_v, gb_v, gb_to), (out_ref, out_v, out_v, out_to))
    loads = [pltpu.make_async_copy(src, held, sem.at[0, n]) for n, (src, held, _, _) in enumerate(names)]
    stores = [pltpu.make_async_copy(held, dst, sem.at[1, n]) for n, (_, _, held, dst) in enumerate(names)]
    for load in loads:
        load.start()
    loads[0].wait()
    turned_v[...] = ga_v[...].T
    stores[0].start()
    for n in (1, 2):
        loads[n].wait()
        stores[n].start()
    for store in stores:
        store.wait()


def on_device(
    tokens,
    destinations,
    counts,
    sequence_job_ids,
    job_owner_slot,
    rank_per_job,
    weight,
    input_factor_table,
    output_factor_table,
    cotangent,
):
    slot_count, seq_len, width = tokens.shape
    max_rank = input_factor_table.shape[2]
    rows = slot_count * seq_len
    anywhere = pl.BlockSpec(memory_space=pl.ANY)
    smem = pl.BlockSpec(memory_space=pltpu.SMEM)
    dma = pltpu.SemaphoreType.DMA
    served = (2, 2, RING, 64, width)
    lanes = (2, RING, 2, 64, width)
    out, ga, gb = pl.pallas_call(
        kernel,
        out_shape=(
            jax.ShapeDtypeStruct((rows, width), BF),
            jax.ShapeDtypeStruct((max_rank, width), F32),
            jax.ShapeDtypeStruct((max_rank, width), F32),
        ),
        in_specs=[smem] * 5 + [anywhere] * 5,
        out_specs=(anywhere,) * 3,
        scratch_shapes=[
            pltpu.VMEM(tokens.shape, BF),
            pltpu.VMEM((rows, width), BF),
            pltpu.VMEM(input_factor_table.shape, BF),
            pltpu.VMEM(output_factor_table.shape, BF),
            pltpu.VMEM((rows, width), BF),
            pltpu.VMEM((DP - 1, seq_len, width), BF),
            pltpu.VMEM((DP, seq_len, width), BF),
            pltpu.VMEM((DP - 1, 8, 128), jnp.int32),
            pltpu.VMEM((DP, 8, 128), jnp.int32),
            pltpu.VMEM((rows, rows), BF),
            pltpu.VMEM((2 * rows, rows), BF),
            pltpu.VMEM((2 * rows, rows), BF),
            pltpu.VMEM((rows, 2 * rows), BF),
            pltpu.VMEM((rows, width), BF),
            pltpu.VMEM(lanes, BF),
            pltpu.VMEM(served, BF),
            pltpu.VMEM(lanes, BF),
            pltpu.VMEM(served, BF),
            pltpu.VMEM((2, 2, width, max_rank), BF),
            pltpu.VMEM((2, 2, max_rank, width), BF),
            pltpu.VMEM((W_SLOTS, width, width), BF),
            pltpu.VMEM((2, rows, width), BF),
            pltpu.VMEM((4, rows, width), BF),
            pltpu.VMEM((3, rows, width), F32),
            pltpu.VMEM((2, rows // 2, width), BF),
            pltpu.VMEM((2, rows // 2, width), BF),
            pltpu.VMEM((2, 2, rows // 2, width), BF),
            pltpu.VMEM((2, 2, rows // 2, width), BF),
            pltpu.VMEM((2, TENSOR, 128, max_rank), BF),
            pltpu.VMEM((2, TENSOR, 128, max_rank), BF),
            pltpu.VMEM((2, TENSOR, 128, max_rank), BF),
            pltpu.VMEM(served, BF),
            pltpu.VMEM(lanes, BF),
            pltpu.VMEM((2, max_rank, width), F32),
            pltpu.VMEM((2, 3, max_rank, width), BF),
            pltpu.VMEM((2, 3, max_rank, width), BF),
            dma((4,)),
            dma((3,)),
            dma((W_SLOTS,)),
            dma((DP - 1,)),
            dma((DP - 1,)),
            dma((2, DP - 1)),
            dma((2, DP - 1)),
            dma((RING - 1, 2)),
            dma((2, 2, 2)),
            dma((2, 2, RING - 1)),
            dma((2, 2, RING - 1)),
            dma((2, 2, RING - 1)),
            dma((2, 2, RING - 1)),
            dma((2,)),
            dma((4,)),
            dma((2,)),
            dma((2,)),
            dma((2, 2)),
            dma((2, 2)),
            dma((2, TENSOR - 1)),
            dma((2, TENSOR - 1)),
            dma((2, TENSOR - 1)),
            dma((2, TENSOR - 1)),
            dma((2, RING - 1)),
            dma((2, RING - 1)),
            dma((2, 3)),
            dma((2, 3)),
        ],
        compiler_params=pltpu.CompilerParams(
            collective_id=0, has_side_effects=True, vmem_limit_bytes=58 * 2**20
        ),
    )(
        destinations,
        counts,
        sequence_job_ids,
        job_owner_slot,
        rank_per_job,
        tokens,
        cotangent.reshape(rows, width),
        input_factor_table,
        output_factor_table,
        weight,
    )
    out, gb, ga = pl.pallas_call(
        finish,
        out_shape=(
            jax.ShapeDtypeStruct((rows, width), BF),
            jax.ShapeDtypeStruct((max_rank, width), F32),
            jax.ShapeDtypeStruct((width, max_rank), F32),
        ),
        in_specs=[anywhere] * 3,
        out_specs=(anywhere,) * 3,
        scratch_shapes=[
            pltpu.VMEM((rows, width), BF),
            pltpu.VMEM((max_rank, width), F32),
            pltpu.VMEM((max_rank, width), F32),
            pltpu.VMEM((width, max_rank), F32),
            dma((2, 3)),
        ],
    )(out, gb, ga)
    return out.reshape(slot_count, seq_len, width), ga[None], gb[None]


def solution(mesh):
    in_specs = (
        P("dp", None, "tensor"),
        P("dp"),
        P("dp"),
        P("dp"),
        P(),
        P(),
        P("tensor", None),
        P("dp", "tensor", None),
        P("dp", None, "tensor"),
        P("dp", None, "tensor"),
    )
    out_specs = (P("dp", None, "tensor"), P("dp", "tensor", None), P("dp", None, "tensor"))
    return jax.shard_map(
        on_device, mesh=mesh, in_specs=in_specs, out_specs=out_specs, check_vma=False
    )
```

```python
import jax
import jax.numpy as jnp
from jax import lax
from jax.experimental import pallas as pl
from jax.experimental.pallas import tpu as pltpu
from jax.sharding import PartitionSpec as P

BF = jnp.bfloat16
F32 = jnp.float32
RING = 4
DP = RING * RING
TENSOR = 2 * RING
TILE = 256
W_SLOTS = 3
BLOCK_ORDER = ((2, 1), (2, 0), (1, 1), (1, 0), (3, 1), (3, 0), (0, 1), (0, 0))


def mm(a, b):
    return jnp.dot(a, b, preferred_element_type=F32)


def kernel(
    dest_ref,
    count_ref,
    job_ref,
    owner_ref,
    rank_ref,
    tok_ref,
    cot_ref,
    a_ref,
    b_ref,
    w_ref,
    out_ref,
    ga_ref,
    gb_ref,
    tok_v,
    cot_v,
    a_v,
    b_v,
    out_v,
    tok_s,
    tok_r,
    facts_s,
    facts_r,
    place_hot,
    x_hot,
    c_hot,
    slot_hot,
    xs,
    x_s,
    x_r,
    c_s,
    c_r,
    fa,
    fb,
    wbuf,
    sib_s,
    sib_r,
    hold,
    hop_s,
    hop_r,
    ring_s,
    ring_r,
    part_s,
    part_r,
    ranks,
    ad_s,
    ad_r,
    g_own,
    g_s,
    g_r,
    in_sem,
    out_sem,
    w_sem,
    facts_ss,
    facts_rs,
    tok_ss,
    tok_rs,
    fac_ss,
    fac_rs,
    c_ss,
    c_rs,
    x_ss,
    x_rs,
    sib_ss,
    sib_rs,
    hop_ss,
    hop_rs,
    ring_ss,
    ring_rs,
    part_ss,
    part_rs,
    gath_ss,
    gath_rs,
    ad_ss,
    ad_rs,
    g_ss,
    g_rs,
):
    seq_len, width = tok_ref.shape[1:]
    rows = DP * seq_len
    half = rows // 2
    me = lax.axis_index("dp")
    t = lax.axis_index("tensor")
    y, z = me // RING, me % RING
    x, c = t // 2, t % 2
    own_side = (y + z) % 2
    own_job = jnp.where(own_side == 0, z // 2, y // 2)
    others = ((own_side, 1 - own_job), (1 - own_side, 0), (1 - own_side, 1))
    tiles = width // TILE
    wide_half = width // 2
    column_halves = (slice(0, wide_half), slice(wide_half, width))

    def remote(src, dst, send, recv, **where):
        return pltpu.make_async_remote_copy(
            src_ref=src,
            dst_ref=dst,
            send_sem=send,
            recv_sem=recv,
            device_id=where,
            device_id_type=pl.DeviceIdType.MESH,
        )

    def iota(shape, axis):
        return lax.broadcasted_iota(jnp.int32, shape, axis)

    def along(side, k):
        return ((y + k) % RING) * RING + z if side == 0 else y * RING + (z + k) % RING

    def owner_of(side, job):
        first = y * RING + 2 * job + y % 2
        second = (2 * job + (z + 1) % 2) * RING + z
        return jnp.where(side == 0, first, second)

    def owner_ring(k):
        return jnp.where(own_side == 0, y * RING + (z + k) % RING, ((y + k) % RING) * RING + z)

    def rank_at(owner):
        total = jnp.int32(0)
        for j in range(DP):
            total = total + jnp.where(owner_ref[j] == owner, rank_ref[j], 0)
        return total

    def factor_at(owner, columns):
        return 32.0 / jnp.full((1, columns), rank_at(owner).astype(F32), F32)

    loads = [
        pltpu.make_async_copy(src, dst, in_sem.at[n])
        for n, (src, dst) in enumerate(((tok_ref, tok_v), (a_ref, a_v), (b_ref, b_v), (cot_ref, cot_v)))
    ]
    for load in loads:
        load.start()

    barrier = pltpu.get_barrier_semaphore()
    for k in range(1, DP):
        pl.semaphore_signal(
            barrier, inc=1, device_id={"dp": (me + k) % DP}, device_id_type=pl.DeviceIdType.MESH
        )
    for k in range(1, TENSOR):
        pl.semaphore_signal(
            barrier, inc=1, device_id={"tensor": (t + k) % TENSOR}, device_id_type=pl.DeviceIdType.MESH
        )

    def w_copy(i):
        ahead, other = BLOCK_ORDER[i]
        block = ((x + ahead) % RING) * 2 + (1 - c if other else c)
        columns = pl.ds(pl.multiple_of(block * width, width), width)
        return pltpu.make_async_copy(w_ref.at[:, columns], wbuf.at[i % W_SLOTS], w_sem.at[i % W_SLOTS])

    for i in range(W_SLOTS):
        w_copy(i).start()

    target = [lax.shift_right_logical(dest_ref[i], 4) for i in range(DP)]
    chosen = []
    for k in range(DP):
        to = (me + k) % DP
        index = jnp.int32(0)
        for i in range(DP):
            index = jnp.where(target[i] == to, i, index)
        chosen.append(index)
        owner = owner_ref[job_ref[index]]
        oy, oz = lax.shift_right_logical(owner, 2), owner & 3
        base = jnp.where(
            ((oy + oz) & 1) == 0,
            oy * 4 + lax.shift_right_logical(oz, 1) * 2,
            4 * RING + oz * 4 + lax.shift_right_logical(oy, 1) * 2,
        )
        row = iota((8, 128), 0)
        tile = jnp.where(row == 0, dest_ref[index] & 15, jnp.where(row == 1, count_ref[index], base))
        if k == 0:
            facts_r[me] = tile
        else:
            facts_s[k - 1] = tile

    loads[0].wait()
    for k in range(1, DP):
        tok_s[k - 1] = tok_v[chosen[k]]
    tok_r[me] = tok_v[chosen[0]]

    pl.semaphore_wait(barrier, DP - 1 + TENSOR - 1)

    def facts_copy(k):
        return remote(
            facts_s.at[k - 1], facts_r.at[me], facts_ss.at[k - 1], facts_rs.at[k - 1], dp=(me + k) % DP
        )

    def tok_copy(h, k):
        columns = column_halves[h]
        return remote(
            tok_s.at[k - 1, :, columns],
            tok_r.at[me, :, columns],
            tok_ss.at[h, k - 1],
            tok_rs.at[h, k - 1],
            dp=(me + k) % DP,
        )

    def fac_copy(k, n):
        held = (fa, fb)[n].at[own_side, own_job]
        return remote(held, held, fac_ss.at[k - 1, n], fac_rs.at[own_side, own_job, n], dp=owner_ring(k))

    def fac_wait(n):
        for side, job in others:
            held = (fa, fb)[n].at[side, job]
            remote(held, held, fac_ss.at[0, n], fac_rs.at[side, job, n], dp=me).wait_recv()

    for k in range(1, DP):
        facts_copy(k).start()
    for h in range(2):
        for k in range(1, DP):
            tok_copy(h, k).start()
    my_rank = rank_at(me)
    loads[1].wait()
    fa[own_side, own_job] = jnp.where(
        iota(a_v.shape[1:], 1) < my_rank, a_v[0].astype(F32), 0.0
    ).astype(BF)
    for k in range(1, RING):
        fac_copy(k, 0).start()
    loads[2].wait()
    fb[own_side, own_job] = jnp.where(
        iota(b_v.shape[1:], 0) < my_rank, b_v[0].astype(F32), 0.0
    ).astype(BF)

    for k in range(1, DP):
        facts_copy(k).wait_recv()
    slot_c = facts_r[:, 0, :].astype(F32)
    live_c = facts_r[:, 1, :].astype(F32)
    base_c = facts_r[:, 2, :].astype(F32)
    square = (DP, 128)
    diagonal = iota(square, 0) == iota(square, 1)
    slot_l = jnp.sum(jnp.where(diagonal, slot_c, 0.0), 0, keepdims=True)
    base_l = jnp.sum(jnp.where(diagonal, base_c, 0.0), 0, keepdims=True)
    earlier = (base_l == base_c) & (slot_l < slot_c) & (iota(square, 1) < DP)
    turn_c = jnp.sum(jnp.where(earlier, 1.0, 0.0), 1, keepdims=True)
    lane_c = base_c + turn_c
    lane_l = jnp.sum(jnp.where(diagonal, lane_c, 0.0), 0, keepdims=True)
    wide = (DP, rows)
    seq_of = iota(wide, 1) // seq_len
    slot_1, live_1, lane_1 = slot_c[:, :1], live_c[:, :1], lane_c[:, :1]
    in_slot = slot_1 == seq_of.astype(F32)
    in_order = iota(wide, 0) == seq_of
    position = (iota((1, rows), 1) % seq_len).astype(F32)

    def spread(where, value):
        return jnp.sum(jnp.where(where, value, 0.0), 0, keepdims=True)

    live = position < spread(in_order, live_1)
    c_row = spread(in_slot, lane_1) * seq_len + position
    x_row = jnp.where(live, spread(in_order, lane_1) * seq_len + position, -1.0)
    slot_row = jnp.where(live, spread(in_order, slot_1) * seq_len + position, -1.0)

    def build(hot, wanted):
        @pl.loop(0, hot.shape[0] // 128)
        def _(n):
            at = pl.ds(pl.multiple_of(n * 128, 128), 128)
            row = (iota((128, rows), 0) + n * 128).astype(F32)
            hot[at, :] = jnp.where(row == wanted, 1.0, 0.0).astype(BF)

    build(x_hot, x_row)
    build(place_hot, slot_row)
    build(c_hot, c_row)

    lane_shape = (2, RING, 2, 64)

    def lane_copy(send, recv, send_sem, recv_sem, h, side, k):
        place = y if side == 0 else z
        columns = column_halves[h]
        return remote(
            send.at[side, (place + k) % RING, :, :, columns],
            recv.at[side, :, place, :, columns],
            send_sem.at[h, side, k - 1],
            recv_sem.at[h, side, k - 1],
            dp=along(side, k),
        )

    def x_copy(h, side, k):
        return lane_copy(x_s, x_r, x_ss, x_rs, h, side, k)

    def c_copy(h, side, k):
        return lane_copy(c_s, c_r, c_ss, c_rs, h, side, k)

    def make_lanes(hot, source, send, columns):
        for n in range(columns.start, columns.stop, TILE):
            at = slice(n, n + TILE)
            send[:, :, :, :, at] = mm(hot[...], source(at)).astype(BF).reshape(lane_shape + (TILE,))

    def keep_lanes(send, recv):
        for side in range(2):
            place = y if side == 0 else z
            recv[side, :, place] = send[side, place]

    loads[3].wait()
    for columns in column_halves:
        make_lanes(c_hot, lambda at: cot_v[:, at], c_s, columns)

    def landed(at):
        return tok_r[:, :, at].reshape(rows, at.stop - at.start)

    for h, columns in enumerate(column_halves):
        for k in range(1, DP):
            tok_copy(h, k).wait_recv()
        make_lanes(x_hot, landed, x_s, columns)
        for k in (2, 1, 3):
            for side in range(2):
                x_copy(h, side, k).start()
        for n in range(columns.start, columns.stop, TILE):
            at = slice(n, n + TILE)
            xs[:, at] = mm(place_hot[...], landed(at)).astype(BF)

    for k in range(1, RING):
        fac_copy(k, 1).start()
    for h in range(2):
        for k in (2, 1, 3):
            for side in range(2):
                c_copy(h, side, k).start()

    def block(i, put):
        w_copy(i).wait()

        @pl.loop(0, tiles)
        def _(n):
            columns = pl.ds(pl.multiple_of(n * TILE, TILE), TILE)
            put(columns, mm(xs[...], wbuf[i % W_SLOTS, :, columns]))

        if i + W_SLOTS < len(BLOCK_ORDER):
            w_copy(i + W_SLOTS).start()

    def sib_copy(j):
        return remote(
            sib_s.at[j % 2], sib_r.at[j], sib_ss.at[j % 2], sib_rs.at[j], tensor=x * 2 + (1 - c)
        )

    def other_block(j):
        if j >= 2:
            sib_copy(j - 2).wait_send()

        def put(columns, value):
            sib_s[j % 2, :, columns] = value.astype(BF)

        block(2 * j, put)
        sib_copy(j).start()

    def my_block(j, slot):
        def put(columns, value):
            hold[slot, :, columns] = value

        block(2 * j + 1, put)

    right, left = ((x + 1) % RING) * 2 + c, ((x + 3) % RING) * 2 + c
    parts = (slice(0, half), slice(half, rows))

    def hop_copy(way):
        return remote(
            hop_s.at[way], hop_r.at[way], hop_ss.at[way], hop_rs.at[way], tensor=(right, left)[way]
        )

    def ring_copy(way, part):
        return remote(
            ring_s.at[way, part],
            ring_r.at[way, part],
            ring_ss.at[way, part],
            ring_rs.at[way, part],
            tensor=(right, left)[way],
        )

    other_block(0)
    my_block(0, 0)
    other_block(1)
    sib_copy(0).wait_recv()
    for way in range(2):
        hop_s[way] = (hold[0, parts[way]] + sib_r[0, parts[way]].astype(F32)).astype(BF)
        hop_copy(way).start()
    my_block(1, 1)

    def part_copy(kind, k):
        to = (t + k) % TENSOR
        return remote(
            part_s.at[kind, to],
            part_r.at[kind, k],
            part_ss.at[kind, k - 1],
            part_rs.at[kind, k - 1],
            tensor=to,
        )

    def gath_copy(kind, k):
        to = (t + k) % TENSOR
        held = ranks.at[kind, t]
        return remote(held, held, gath_ss.at[kind, k - 1], gath_rs.at[kind, k - 1], tensor=to)

    def served(ref, side, job):
        return ref[side, job].reshape(RING * 64, width)

    def send_parts(kind, make):
        for side in range(2):
            for job in range(2):
                value = make(side, job)
                for piece in range(2):
                    part_s[kind, side * 4 + job * 2 + piece] = value[piece * 128 : (piece + 1) * 128].astype(
                        BF
                    )
        for k in range(1, TENSOR):
            part_copy(kind, k).start()
        part_r[kind, 0] = part_s[kind, t]

    def sum_parts(kind, scale):
        for k in range(1, TENSOR):
            part_copy(kind, k).wait_recv()
        total = part_r[kind, 0].astype(F32)
        for k in range(1, TENSOR):
            total = total + part_r[kind, k].astype(F32)
        ranks[kind, t] = (total if scale is None else total * scale).astype(BF)
        for k in range(1, TENSOR):
            gath_copy(kind, k).start()

    def gathered(kind):
        for k in range(1, TENSOR):
            frm = (t + TENSOR - k) % TENSOR
            held = ranks.at[kind, frm]
            remote(held, held, gath_ss.at[kind, k - 1], gath_rs.at[kind, k - 1], tensor=t).wait_recv()

    def rank_rows(kind, side, job):
        return ranks[kind, pl.ds(side * 4 + job * 2, 2)].reshape(RING * 64, ranks.shape[3])

    keep_lanes(x_s, x_r)
    keep_lanes(c_s, c_r)
    fac_wait(0)
    for h in range(2):
        for side in range(2):
            for k in range(1, RING):
                x_copy(h, side, k).wait_recv()
    send_parts(0, lambda side, job: mm(served(x_r, side, job), fa[side, job]))

    other_block(2)
    my_block(2, 0)
    sum_parts(0, None)
    sib_copy(1).wait_recv()
    ring_s[0, 1] = (hold[1, parts[1]] + sib_r[1, parts[1]].astype(F32)).astype(BF)
    ring_copy(0, 1).start()
    other_block(3)
    sib_copy(2).wait_recv()
    ring_s[1, 0] = (hold[0, parts[0]] + sib_r[2, parts[0]].astype(F32)).astype(BF)
    ring_copy(1, 0).start()
    my_block(3, 2)

    def ad_copy(side, k):
        place = y if side == 0 else z
        return remote(
            ad_s.at[side, :, (place + k) % RING],
            ad_r.at[side, place],
            ad_ss.at[side, k - 1],
            ad_rs.at[side, k - 1],
            dp=along(side, k),
        )

    fac_wait(1)
    gathered(0)
    for side in range(2):
        place = y if side == 0 else z
        for job in range(2):
            value = mm(rank_rows(0, side, job), fb[side, job]) * factor_at(owner_of(side, job), width)
            ad_s[side, job] = value.astype(BF).reshape(RING, 64, width)
        for k in (2, 1, 3):
            ad_copy(side, k).start()
        ad_r[side, place] = ad_s[side, :, place]

    for h in range(2):
        for side in range(2):
            for k in range(1, RING):
                c_copy(h, side, k).wait_recv()
    send_parts(
        1,
        lambda side, job: lax.dot_general(
            served(c_r, side, job), fb[side, job], (((1,), (1,)), ((), ())), preferred_element_type=F32
        ),
    )

    def g_copy(n, which):
        side, job = others[which]
        k = jnp.where(
            side == 0,
            (z - (2 * job + y % 2) + RING) % RING,
            (y - (2 * job + (z + 1) % 2) + RING) % RING,
        )
        return remote(
            g_s.at[n, which], g_r.at[n, k - 1], g_ss.at[n, which], g_rs.at[n, k - 1], dp=owner_of(side, job)
        )

    def g_wait(n, k):
        remote(g_s.at[n, 0], g_r.at[n, k - 1], g_ss.at[n, 0], g_rs.at[n, k - 1], dp=me).wait_recv()

    def gradient(n, kind, row_ref):
        for which, (side, job) in enumerate(others + ((own_side, own_job),)):
            turned = rank_rows(kind, side, job).astype(F32).T.astype(BF)
            value = mm(turned, row_ref[side, job].reshape(RING * 64, width)) * (1.0 / seq_len)
            if n == 1:
                value = value * factor_at(owner_of(side, job), width)
            if which < 3:
                g_s[n, which] = value.astype(BF)
                g_copy(n, which).start()
            else:
                g_own[n] = value

    gradient(1, 0, c_r)

    @pl.loop(0, rows // 128)
    def _(n):
        at = pl.ds(pl.multiple_of(n * 128, 128), 128)
        row = iota((128, 128), 0) + n * 128
        mine = jnp.where(slot_l == (row // seq_len).astype(F32), lane_l, 0.0)
        place = jnp.sum(mine, 1, keepdims=True) * seq_len + (row % seq_len).astype(F32)[:, :1]
        slot_hot[at, :] = jnp.where(iota((128, 2 * rows), 1).astype(F32) == place, 1.0, 0.0).astype(BF)

    hop_copy(0).wait_recv()
    ring_s[0, 0] = (
        hold[1, parts[0]] + sib_r[1, parts[0]].astype(F32) + hop_r[0].astype(F32)
    ).astype(BF)
    hop_copy(1).wait_recv()
    ring_s[1, 1] = (
        hold[0, parts[1]] + sib_r[2, parts[1]].astype(F32) + hop_r[1].astype(F32)
    ).astype(BF)
    sum_parts(1, factor_at(owner_of(t // 4, (t // 2) % 2), ranks.shape[3]))
    ring_copy(0, 0).start()
    ring_copy(1, 1).start()
    gathered(1)
    gradient(0, 1, x_r)

    sib_copy(3).wait_recv()
    for side in range(2):
        for k in range(1, RING):
            ad_copy(side, k).wait_recv()
    for n in range(tiles):
        at = slice(n * TILE, (n + 1) * TILE)
        back = ad_r[:, :, :, :, at].reshape(2 * rows, TILE)
        hold[2, :, at] = hold[2, :, at] + sib_r[3, :, at].astype(F32) + mm(slot_hot[...], back)
    for part in (1, 0):
        ring_copy(0, part).wait_recv()
        ring_copy(1, 1 - part).wait_recv()
    for part in range(2):
        out_v[parts[part]] = (
            hold[2, parts[part]] + ring_r[0, part].astype(F32) + ring_r[1, part].astype(F32)
        ).astype(BF)
    stores = [pltpu.make_async_copy(out_v, out_ref, out_sem.at[2])]
    stores[0].start()

    for n, g_ref in ((1, gb_ref), (0, ga_ref)):
        for k in range(1, RING):
            g_wait(n, k)
        total = g_own[n]
        for k in range(1, RING):
            total = total + g_r[n, k - 1].astype(F32)
        g_own[n] = total
        stores.append(pltpu.make_async_copy(g_own.at[n], g_ref, out_sem.at[n]))
        stores[-1].start()

    for k in range(1, DP):
        facts_copy(k).wait_send()
        for h in range(2):
            tok_copy(h, k).wait_send()
    for k in range(1, RING):
        for n in range(2):
            fac_copy(k, n).wait_send()
        for side in range(2):
            for h in range(2):
                c_copy(h, side, k).wait_send()
                x_copy(h, side, k).wait_send()
            ad_copy(side, k).wait_send()
    for j in (2, 3):
        sib_copy(j).wait_send()
    for way in range(2):
        hop_copy(way).wait_send()
        for part in range(2):
            ring_copy(way, part).wait_send()
    for kind in range(2):
        for k in range(1, TENSOR):
            part_copy(kind, k).wait_send()
            gath_copy(kind, k).wait_send()
    for n in range(2):
        for which in range(3):
            g_copy(n, which).wait_send()
    for store in stores:
        store.wait()


def finish(out_ref, gb_ref, ga_ref, out_to, gb_to, ga_to, out_v, gb_v, ga_v, turned_v, sem):
    names = ((ga_ref, ga_v, turned_v, ga_to), (gb_ref, gb_v, gb_v, gb_to), (out_ref, out_v, out_v, out_to))
    loads = [pltpu.make_async_copy(src, held, sem.at[0, n]) for n, (src, held, _, _) in enumerate(names)]
    stores = [pltpu.make_async_copy(held, dst, sem.at[1, n]) for n, (_, _, held, dst) in enumerate(names)]
    for load in loads:
        load.start()
    loads[0].wait()
    turned_v[...] = ga_v[...].T
    stores[0].start()
    for n in (1, 2):
        loads[n].wait()
        stores[n].start()
    for store in stores:
        store.wait()


def on_device(
    tokens,
    destinations,
    counts,
    sequence_job_ids,
    job_owner_slot,
    rank_per_job,
    weight,
    input_factor_table,
    output_factor_table,
    cotangent,
):
    slot_count, seq_len, width = tokens.shape
    max_rank = input_factor_table.shape[2]
    rows = slot_count * seq_len
    anywhere = pl.BlockSpec(memory_space=pl.ANY)
    smem = pl.BlockSpec(memory_space=pltpu.SMEM)
    dma = pltpu.SemaphoreType.DMA
    served = (2, 2, RING, 64, width)
    lanes = (2, RING, 2, 64, width)
    out, ga, gb = pl.pallas_call(
        kernel,
        out_shape=(
            jax.ShapeDtypeStruct((rows, width), BF),
            jax.ShapeDtypeStruct((max_rank, width), F32),
            jax.ShapeDtypeStruct((max_rank, width), F32),
        ),
        in_specs=[smem] * 5 + [anywhere] * 5,
        out_specs=(anywhere,) * 3,
        scratch_shapes=[
            pltpu.VMEM(tokens.shape, BF),
            pltpu.VMEM((rows, width), BF),
            pltpu.VMEM(input_factor_table.shape, BF),
            pltpu.VMEM(output_factor_table.shape, BF),
            pltpu.VMEM((rows, width), BF),
            pltpu.VMEM((DP - 1, seq_len, width), BF),
            pltpu.VMEM((DP, seq_len, width), BF),
            pltpu.VMEM((DP - 1, 8, 128), jnp.int32),
            pltpu.VMEM((DP, 8, 128), jnp.int32),
            pltpu.VMEM((rows, rows), BF),
            pltpu.VMEM((2 * rows, rows), BF),
            pltpu.VMEM((2 * rows, rows), BF),
            pltpu.VMEM((rows, 2 * rows), BF),
            pltpu.VMEM((rows, width), BF),
            pltpu.VMEM(lanes, BF),
            pltpu.VMEM(served, BF),
            pltpu.VMEM(lanes, BF),
            pltpu.VMEM(served, BF),
            pltpu.VMEM((2, 2, width, max_rank), BF),
            pltpu.VMEM((2, 2, max_rank, width), BF),
            pltpu.VMEM((W_SLOTS, width, width), BF),
            pltpu.VMEM((2, rows, width), BF),
            pltpu.VMEM((4, rows, width), BF),
            pltpu.VMEM((3, rows, width), F32),
            pltpu.VMEM((2, rows // 2, width), BF),
            pltpu.VMEM((2, rows // 2, width), BF),
            pltpu.VMEM((2, 2, rows // 2, width), BF),
            pltpu.VMEM((2, 2, rows // 2, width), BF),
            pltpu.VMEM((2, TENSOR, 128, max_rank), BF),
            pltpu.VMEM((2, TENSOR, 128, max_rank), BF),
            pltpu.VMEM((2, TENSOR, 128, max_rank), BF),
            pltpu.VMEM(served, BF),
            pltpu.VMEM(lanes, BF),
            pltpu.VMEM((2, max_rank, width), F32),
            pltpu.VMEM((2, 3, max_rank, width), BF),
            pltpu.VMEM((2, 3, max_rank, width), BF),
            dma((4,)),
            dma((3,)),
            dma((W_SLOTS,)),
            dma((DP - 1,)),
            dma((DP - 1,)),
            dma((2, DP - 1)),
            dma((2, DP - 1)),
            dma((RING - 1, 2)),
            dma((2, 2, 2)),
            dma((2, 2, RING - 1)),
            dma((2, 2, RING - 1)),
            dma((2, 2, RING - 1)),
            dma((2, 2, RING - 1)),
            dma((2,)),
            dma((4,)),
            dma((2,)),
            dma((2,)),
            dma((2, 2)),
            dma((2, 2)),
            dma((2, TENSOR - 1)),
            dma((2, TENSOR - 1)),
            dma((2, TENSOR - 1)),
            dma((2, TENSOR - 1)),
            dma((2, RING - 1)),
            dma((2, RING - 1)),
            dma((2, 3)),
            dma((2, 3)),
        ],
        compiler_params=pltpu.CompilerParams(
            collective_id=0, has_side_effects=True, vmem_limit_bytes=58 * 2**20
        ),
    )(
        destinations,
        counts,
        sequence_job_ids,
        job_owner_slot,
        rank_per_job,
        tokens,
        cotangent.reshape(rows, width),
        input_factor_table,
        output_factor_table,
        weight,
    )
    out, gb, ga = pl.pallas_call(
        finish,
        out_shape=(
            jax.ShapeDtypeStruct((rows, width), BF),
            jax.ShapeDtypeStruct((max_rank, width), F32),
            jax.ShapeDtypeStruct((width, max_rank), F32),
        ),
        in_specs=[anywhere] * 3,
        out_specs=(anywhere,) * 3,
        scratch_shapes=[
            pltpu.VMEM((rows, width), BF),
            pltpu.VMEM((max_rank, width), F32),
            pltpu.VMEM((max_rank, width), F32),
            pltpu.VMEM((width, max_rank), F32),
            dma((2, 3)),
        ],
    )(out, gb, ga)
    return out.reshape(slot_count, seq_len, width), ga[None], gb[None]


def solution(mesh):
    in_specs = (
        P("dp", None, "tensor"),
        P("dp"),
        P("dp"),
        P("dp"),
        P(),
        P(),
        P("tensor", None),
        P("dp", "tensor", None),
        P("dp", None, "tensor"),
        P("dp", None, "tensor"),
    )
    out_specs = (P("dp", None, "tensor"), P("dp", "tensor", None), P("dp", None, "tensor"))
    return jax.shard_map(
        on_device, mesh=mesh, in_specs=in_specs, out_specs=out_specs, check_vma=False
    )
```

```python
import jax
import jax.numpy as jnp
from jax import lax
from jax.experimental import pallas as pl
from jax.experimental.pallas import tpu as pltpu
from jax.sharding import PartitionSpec as P

BF = jnp.bfloat16
F32 = jnp.float32
RING = 4
DP = RING * RING
TENSOR = 2 * RING
TILE = 256
W_SLOTS = 3
MOVE, PLACE = (0, 0, -1, 1), (0, 1, 1, 0)
BOTH = slice(0, 2)
MESSAGES = ((2, 2), (2, 3), (3, 2), (3, 3), (2, BOTH), (3, BOTH), (BOTH, 2), (BOTH, 3))
BLOCK_ORDER = ((2, 1), (2, 0), (1, 1), (1, 0), (3, 1), (3, 0), (0, 1), (0, 0))


def mm(a, b):
    return jnp.dot(a, b, preferred_element_type=F32)


def kernel(
    dest_ref,
    count_ref,
    job_ref,
    owner_ref,
    rank_ref,
    tok_ref,
    cot_ref,
    a_ref,
    b_ref,
    w_ref,
    out_ref,
    ga_ref,
    gb_ref,
    tok_v,
    cot_v,
    a_v,
    b_v,
    out_v,
    tok_s,
    tok_r,
    facts_s,
    facts_r,
    place_hot,
    x_hot,
    c_hot,
    slot_hot,
    xs,
    x_s,
    x_r,
    c_s,
    c_r,
    fa,
    fb,
    wbuf,
    sib_s,
    sib_r,
    hold,
    hop_s,
    hop_r,
    ring_s,
    ring_r,
    part_s,
    part_r,
    ranks,
    ad_s,
    ad_r,
    g_own,
    g_s,
    g_r,
    in_sem,
    out_sem,
    w_sem,
    facts_ss,
    facts_rs,
    tok_ss,
    tok_rs,
    fac_ss,
    fac_rs,
    c_ss,
    c_rs,
    x_ss,
    x_rs,
    sib_ss,
    sib_rs,
    hop_ss,
    hop_rs,
    ring_ss,
    ring_rs,
    part_ss,
    part_rs,
    gath_ss,
    gath_rs,
    ad_ss,
    ad_rs,
    g_ss,
    g_rs,
):
    seq_len, width = tok_ref.shape[1:]
    rows = DP * seq_len
    half = rows // 2
    me = lax.axis_index("dp")
    t = lax.axis_index("tensor")
    y, z = me // RING, me % RING
    x, c = t // 2, t % 2
    odd = (y + z) % 2
    ahead = 1 - 2 * odd
    others = ((1 - odd, 1 - odd), (odd, 1 - odd), (1 - odd, odd))
    tiles = width // TILE
    wide_half = width // 2
    column_halves = (slice(0, wide_half), slice(wide_half, width))

    def remote(src, dst, send, recv, **where):
        return pltpu.make_async_remote_copy(
            src_ref=src,
            dst_ref=dst,
            send_sem=send,
            recv_sem=recv,
            device_id=where,
            device_id_type=pl.DeviceIdType.MESH,
        )

    def iota(shape, axis):
        return lax.broadcasted_iota(jnp.int32, shape, axis)

    def near(dy, dz):
        return (y + dy + RING) % RING * RING + (z + dz + RING) % RING

    def owner_of(i, j):
        first, second = (y - i + RING) % RING, (z - j + RING) % RING
        shift = (first + second) % 2
        return (first + shift) % RING * RING + (second + shift) % RING

    def rank_at(owner):
        total = jnp.int32(0)
        for j in range(DP):
            total = total + jnp.where(owner_ref[j] == owner, rank_ref[j], 0)
        return total

    def factor_at(owner, columns):
        return 32.0 / jnp.full((1, columns), rank_at(owner).astype(F32), F32)

    loads = [
        pltpu.make_async_copy(src, dst, in_sem.at[n])
        for n, (src, dst) in enumerate(((tok_ref, tok_v), (a_ref, a_v), (b_ref, b_v), (cot_ref, cot_v)))
    ]
    for load in loads:
        load.start()

    barrier = pltpu.get_barrier_semaphore()
    for k in range(1, DP):
        pl.semaphore_signal(
            barrier, inc=1, device_id={"dp": (me + k) % DP}, device_id_type=pl.DeviceIdType.MESH
        )
    for k in range(1, TENSOR):
        pl.semaphore_signal(
            barrier, inc=1, device_id={"tensor": (t + k) % TENSOR}, device_id_type=pl.DeviceIdType.MESH
        )

    def w_copy(i):
        ahead, other = BLOCK_ORDER[i]
        block = ((x + ahead) % RING) * 2 + (1 - c if other else c)
        columns = pl.ds(pl.multiple_of(block * width, width), width)
        return pltpu.make_async_copy(w_ref.at[:, columns], wbuf.at[i % W_SLOTS], w_sem.at[i % W_SLOTS])

    for i in range(W_SLOTS):
        w_copy(i).start()

    target = [lax.shift_right_logical(dest_ref[i], 4) for i in range(DP)]
    chosen = []
    for k in range(DP):
        to = (me + k) % DP
        index = jnp.int32(0)
        for i in range(DP):
            index = jnp.where(target[i] == to, i, index)
        chosen.append(index)
        owner = owner_ref[job_ref[index]]
        oy, oz = lax.shift_right_logical(owner, 2), owner & 3
        shift = (oy + oz) & 1
        dy, dz = (to // RING + RING - oy + shift) & 3, (to % RING + RING - oz + shift) & 3
        base = (dy * RING + dz) * 2
        row = iota((8, 128), 0)
        tile = jnp.where(row == 0, dest_ref[index] & 15, jnp.where(row == 1, count_ref[index], base))
        if k == 0:
            facts_r[me] = tile
        else:
            facts_s[k - 1] = tile

    loads[0].wait()
    for k in range(1, DP):
        tok_s[k - 1] = tok_v[chosen[k]]
    tok_r[me] = tok_v[chosen[0]]

    pl.semaphore_wait(barrier, DP - 1 + TENSOR - 1)

    def facts_copy(k):
        return remote(
            facts_s.at[k - 1], facts_r.at[me], facts_ss.at[k - 1], facts_rs.at[k - 1], dp=(me + k) % DP
        )

    def tok_copy(h, k):
        columns = column_halves[h]
        return remote(
            tok_s.at[k - 1, :, columns],
            tok_r.at[me, :, columns],
            tok_ss.at[h, k - 1],
            tok_rs.at[h, k - 1],
            dp=(me + k) % DP,
        )

    def fac_copy(axis, n):
        table = (fa, fb)[n]
        there = ((1 - odd, odd), (odd, 1 - odd))[axis]
        to = (near(ahead, 0), near(0, ahead))[axis]
        return remote(
            table.at[odd, odd], table.at[there], fac_ss.at[axis, n], fac_rs.at[there + (n,)], dp=to
        )

    def fac_wait(n, which):
        for there in which:
            held = (fa, fb)[n].at[there]
            remote(held, held, fac_ss.at[0, n], fac_rs.at[there + (n,)], dp=me).wait_recv()

    def fac_relay(n):
        table = (fa, fb)[n]
        here = ((odd, 1 - odd), (1 - odd, odd))[n]
        to = (near(0, -ahead), near(-ahead, 0))[n]
        return remote(table.at[here], table.at[odd, odd], fac_ss.at[2, n], fac_rs.at[odd, odd, n], dp=to)

    for k in range(1, DP):
        facts_copy(k).start()
    for h in range(2):
        for k in range(1, DP):
            tok_copy(h, k).start()
    my_rank = rank_at(me)
    loads[1].wait()
    fa[odd, odd] = jnp.where(
        iota(a_v.shape[1:], 1) < my_rank, a_v[0].astype(F32), 0.0
    ).astype(BF)
    for axis in range(2):
        fac_copy(axis, 0).start()
    loads[2].wait()
    fb[odd, odd] = jnp.where(
        iota(b_v.shape[1:], 0) < my_rank, b_v[0].astype(F32), 0.0
    ).astype(BF)

    for k in range(1, DP):
        facts_copy(k).wait_recv()
    slot_c = facts_r[:, 0, :].astype(F32)
    live_c = facts_r[:, 1, :].astype(F32)
    base_c = facts_r[:, 2, :].astype(F32)
    square = (DP, 128)
    diagonal = iota(square, 0) == iota(square, 1)
    slot_l = jnp.sum(jnp.where(diagonal, slot_c, 0.0), 0, keepdims=True)
    base_l = jnp.sum(jnp.where(diagonal, base_c, 0.0), 0, keepdims=True)
    earlier = (base_l == base_c) & (slot_l < slot_c) & (iota(square, 1) < DP)
    turn_c = jnp.sum(jnp.where(earlier, 1.0, 0.0), 1, keepdims=True)
    lane_c = base_c + turn_c
    lane_l = jnp.sum(jnp.where(diagonal, lane_c, 0.0), 0, keepdims=True)
    wide = (DP, rows)
    seq_of = iota(wide, 1) // seq_len
    slot_1, live_1, lane_1 = slot_c[:, :1], live_c[:, :1], lane_c[:, :1]
    in_slot = slot_1 == seq_of.astype(F32)
    in_order = iota(wide, 0) == seq_of
    position = (iota((1, rows), 1) % seq_len).astype(F32)

    def spread(where, value):
        return jnp.sum(jnp.where(where, value, 0.0), 0, keepdims=True)

    live = position < spread(in_order, live_1)
    c_row = spread(in_slot, lane_1) * seq_len + position
    x_row = jnp.where(live, spread(in_order, lane_1) * seq_len + position, -1.0)
    slot_row = jnp.where(live, spread(in_order, slot_1) * seq_len + position, -1.0)

    def build(hot, wanted):
        @pl.loop(0, hot.shape[0] // 128)
        def _(n):
            at = pl.ds(pl.multiple_of(n * 128, 128), 128)
            row = (iota((128, rows), 0) + n * 128).astype(F32)
            hot[at, :] = jnp.where(row == wanted, 1.0, 0.0).astype(BF)

    build(x_hot, x_row)
    build(place_hot, slot_row)
    build(c_hot, c_row)

    lane_shape = (RING, RING, 2 * seq_len)

    def lane_place(dy, dz):
        row = PLACE[dy] if dy != BOTH else BOTH
        column = PLACE[dz] if dz != BOTH else BOTH
        return row, column, (dy != BOTH) * 2 + (dz != BOTH)

    def lane_move(dy, dz):
        return (MOVE[dy] if dy != BOTH else 0, MOVE[dz] if dz != BOTH else 0)

    def x_copy(h, m):
        message, columns = MESSAGES[m], column_halves[h]
        return remote(
            x_s.at[message + (slice(None), columns)],
            x_r.at[lane_place(*message) + (slice(None), columns)],
            x_ss.at[h, m],
            x_rs.at[h, m],
            dp=near(*lane_move(*message)),
        )

    def c_copy(m):
        message = MESSAGES[m]
        return remote(
            c_s.at[message],
            c_r.at[lane_place(*message)],
            c_ss.at[m],
            c_rs.at[m],
            dp=near(*lane_move(*message)),
        )

    def make_lanes(hot, source, send, columns):
        for n in range(columns.start, columns.stop, TILE):
            at = slice(n, n + TILE)
            send[:, :, :, at] = mm(hot[...], source(at)).astype(BF).reshape(lane_shape + (TILE,))

    loads[3].wait()
    for columns in column_halves:
        make_lanes(c_hot, lambda at: cot_v[:, at], c_s, columns)

    def landed(at):
        return tok_r[:, :, at].reshape(rows, at.stop - at.start)

    for h, columns in enumerate(column_halves):
        for k in range(1, DP):
            tok_copy(h, k).wait_recv()
        make_lanes(x_hot, landed, x_s, columns)
        for m in range(len(MESSAGES)):
            x_copy(h, m).start()
        for n in range(columns.start, columns.stop, TILE):
            at = slice(n, n + TILE)
            xs[:, at] = mm(place_hot[...], landed(at)).astype(BF)

    for axis in range(2):
        fac_copy(axis, 1).start()
    for m in range(len(MESSAGES)):
        c_copy(m).start()

    def block(i, put):
        w_copy(i).wait()

        @pl.loop(0, tiles)
        def _(n):
            columns = pl.ds(pl.multiple_of(n * TILE, TILE), TILE)
            put(columns, mm(xs[...], wbuf[i % W_SLOTS, :, columns]))

        if i + W_SLOTS < len(BLOCK_ORDER):
            w_copy(i + W_SLOTS).start()

    def sib_copy(j):
        return remote(
            sib_s.at[j % 2], sib_r.at[j], sib_ss.at[j % 2], sib_rs.at[j], tensor=x * 2 + (1 - c)
        )

    def other_block(j):
        if j >= 2:
            sib_copy(j - 2).wait_send()

        def put(columns, value):
            sib_s[j % 2, :, columns] = value.astype(BF)

        block(2 * j, put)
        sib_copy(j).start()

    def my_block(j, slot):
        def put(columns, value):
            hold[slot, :, columns] = value

        block(2 * j + 1, put)

    right, left = ((x + 1) % RING) * 2 + c, ((x + 3) % RING) * 2 + c
    parts = (slice(0, half), slice(half, rows))

    def hop_copy(way):
        return remote(
            hop_s.at[way], hop_r.at[way], hop_ss.at[way], hop_rs.at[way], tensor=(right, left)[way]
        )

    def ring_copy(way, part):
        return remote(
            ring_s.at[way, part],
            ring_r.at[way, part],
            ring_ss.at[way, part],
            ring_rs.at[way, part],
            tensor=(right, left)[way],
        )

    other_block(0)
    my_block(0, 0)
    other_block(1)
    sib_copy(0).wait_recv()
    for way in range(2):
        hop_s[way] = (hold[0, parts[way]] + sib_r[0, parts[way]].astype(F32)).astype(BF)
        hop_copy(way).start()
    fac_wait(0, others[1:])
    fac_relay(0).start()
    my_block(1, 1)

    def part_copy(kind, k):
        to = (t + k) % TENSOR
        return remote(
            part_s.at[kind, to],
            part_r.at[kind, k],
            part_ss.at[kind, k - 1],
            part_rs.at[kind, k - 1],
            tensor=to,
        )

    def gath_copy(kind, k):
        to = (t + k) % TENSOR
        held = ranks.at[kind, t]
        return remote(held, held, gath_ss.at[kind, k - 1], gath_rs.at[kind, k - 1], tensor=to)

    def served(ref, side, job):
        return ref[side, job].reshape(RING * 64, width)

    def send_parts(kind, make):
        for side in range(2):
            for job in range(2):
                value = make(side, job)
                for piece in range(2):
                    part_s[kind, side * 4 + job * 2 + piece] = value[piece * 128 : (piece + 1) * 128].astype(
                        BF
                    )
        for k in range(1, TENSOR):
            part_copy(kind, k).start()
        part_r[kind, 0] = part_s[kind, t]

    def sum_parts(kind, scale):
        for k in range(1, TENSOR):
            part_copy(kind, k).wait_recv()
        total = part_r[kind, 0].astype(F32)
        for k in range(1, TENSOR):
            total = total + part_r[kind, k].astype(F32)
        ranks[kind, t] = (total if scale is None else total * scale).astype(BF)
        for k in range(1, TENSOR):
            gath_copy(kind, k).start()

    def gathered(kind):
        for k in range(1, TENSOR):
            frm = (t + TENSOR - k) % TENSOR
            held = ranks.at[kind, frm]
            remote(held, held, gath_ss.at[kind, k - 1], gath_rs.at[kind, k - 1], tensor=t).wait_recv()

    def rank_rows(kind, side, job):
        return ranks[kind, pl.ds(side * 4 + job * 2, 2)].reshape(RING * 64, ranks.shape[3])

    x_r[:, :, 0] = x_s[BOTH, BOTH]
    c_r[:, :, 0] = c_s[BOTH, BOTH]
    fac_wait(0, others[:1])
    for h in range(2):
        for m in range(len(MESSAGES)):
            x_copy(h, m).wait_recv()
    send_parts(0, lambda side, job: mm(served(x_r, side, job), fa[side, job]))

    other_block(2)
    my_block(2, 0)
    fac_wait(1, others[1:])
    fac_relay(1).start()
    sum_parts(0, None)
    sib_copy(1).wait_recv()
    ring_s[0, 1] = (hold[1, parts[1]] + sib_r[1, parts[1]].astype(F32)).astype(BF)
    ring_copy(0, 1).start()
    other_block(3)
    sib_copy(2).wait_recv()
    ring_s[1, 0] = (hold[0, parts[0]] + sib_r[2, parts[0]].astype(F32)).astype(BF)
    ring_copy(1, 0).start()
    my_block(3, 2)

    def ad_copy(m):
        message = MESSAGES[m]
        dy, dz = lane_move(*message)
        return remote(
            ad_s.at[lane_place(*message)],
            ad_r.at[message],
            ad_ss.at[m],
            ad_rs.at[m],
            dp=near(-dy, -dz),
        )

    fac_wait(1, others[:1])
    gathered(0)
    for i in range(2):
        for j in range(2):
            value = mm(rank_rows(0, i, j), fb[i, j]) * factor_at(owner_of(i, j), width)
            ad_s[i, j] = value.astype(BF).reshape(RING, 64, width)
    for m in range(len(MESSAGES)):
        ad_copy(m).start()
    ad_r[BOTH, BOTH] = ad_s[:, :, 0]

    for m in range(len(MESSAGES)):
        c_copy(m).wait_recv()
    send_parts(
        1,
        lambda side, job: lax.dot_general(
            served(c_r, side, job), fb[side, job], (((1,), (1,)), ((), ())), preferred_element_type=F32
        ),
    )

    def g_copy(n, which):
        to = (near(-ahead, -ahead), near(ahead, 0), near(0, ahead))[which]
        return remote(
            g_s.at[n, which], g_r.at[n, which], g_ss.at[n, which], g_rs.at[n, which], dp=to
        )

    def g_wait(n, k):
        remote(g_s.at[n, k], g_r.at[n, k], g_ss.at[n, k], g_rs.at[n, k], dp=me).wait_recv()

    def gradient(n, kind, row_ref):
        for which, (side, job) in enumerate(others + ((odd, odd),)):
            turned = rank_rows(kind, side, job).astype(F32).T.astype(BF)
            value = mm(turned, row_ref[side, job].reshape(RING * 64, width)) * (1.0 / seq_len)
            if n == 1:
                value = value * factor_at(owner_of(side, job), width)
            if which < 3:
                g_s[n, which] = value.astype(BF)
                g_copy(n, which).start()
            else:
                g_own[n] = value

    gradient(1, 0, c_r)

    @pl.loop(0, rows // 128)
    def _(n):
        at = pl.ds(pl.multiple_of(n * 128, 128), 128)
        row = iota((128, 128), 0) + n * 128
        mine = jnp.where(slot_l == (row // seq_len).astype(F32), lane_l, 0.0)
        place = jnp.sum(mine, 1, keepdims=True) * seq_len + (row % seq_len).astype(F32)[:, :1]
        slot_hot[at, :] = jnp.where(iota((128, 2 * rows), 1).astype(F32) == place, 1.0, 0.0).astype(BF)

    hop_copy(0).wait_recv()
    ring_s[0, 0] = (
        hold[1, parts[0]] + sib_r[1, parts[0]].astype(F32) + hop_r[0].astype(F32)
    ).astype(BF)
    hop_copy(1).wait_recv()
    ring_s[1, 1] = (
        hold[0, parts[1]] + sib_r[2, parts[1]].astype(F32) + hop_r[1].astype(F32)
    ).astype(BF)
    sum_parts(1, factor_at(owner_of(t // 4, (t // 2) % 2), ranks.shape[3]))
    ring_copy(0, 0).start()
    ring_copy(1, 1).start()
    gathered(1)
    gradient(0, 1, x_r)

    sib_copy(3).wait_recv()
    for m in range(len(MESSAGES)):
        ad_copy(m).wait_recv()
    for n in range(tiles):
        at = slice(n * TILE, (n + 1) * TILE)
        back = ad_r[:, :, :, at].reshape(2 * rows, TILE)
        hold[2, :, at] = hold[2, :, at] + sib_r[3, :, at].astype(F32) + mm(slot_hot[...], back)
    for part in (1, 0):
        ring_copy(0, part).wait_recv()
        ring_copy(1, 1 - part).wait_recv()
    for part in range(2):
        out_v[parts[part]] = (
            hold[2, parts[part]] + ring_r[0, part].astype(F32) + ring_r[1, part].astype(F32)
        ).astype(BF)
    stores = [pltpu.make_async_copy(out_v, out_ref, out_sem.at[2])]
    stores[0].start()

    for n, g_ref in ((1, gb_ref), (0, ga_ref)):
        total = g_own[n]
        for k in range(3):
            g_wait(n, k)
            total = total + g_r[n, k].astype(F32)
        g_own[n] = total
        stores.append(pltpu.make_async_copy(g_own.at[n], g_ref, out_sem.at[n]))
        stores[-1].start()

    for k in range(1, DP):
        facts_copy(k).wait_send()
        for h in range(2):
            tok_copy(h, k).wait_send()
    for n in range(2):
        for axis in range(2):
            fac_copy(axis, n).wait_send()
        fac_relay(n).wait_send()
    for m in range(len(MESSAGES)):
        for h in range(2):
            x_copy(h, m).wait_send()
        c_copy(m).wait_send()
        ad_copy(m).wait_send()
    for j in (2, 3):
        sib_copy(j).wait_send()
    for way in range(2):
        hop_copy(way).wait_send()
        for part in range(2):
            ring_copy(way, part).wait_send()
    for kind in range(2):
        for k in range(1, TENSOR):
            part_copy(kind, k).wait_send()
            gath_copy(kind, k).wait_send()
    for n in range(2):
        for which in range(3):
            g_copy(n, which).wait_send()
    for store in stores:
        store.wait()


def finish(out_ref, gb_ref, ga_ref, out_to, gb_to, ga_to, out_v, gb_v, ga_v, turned_v, sem):
    names = ((ga_ref, ga_v, turned_v, ga_to), (gb_ref, gb_v, gb_v, gb_to), (out_ref, out_v, out_v, out_to))
    loads = [pltpu.make_async_copy(src, held, sem.at[0, n]) for n, (src, held, _, _) in enumerate(names)]
    stores = [pltpu.make_async_copy(held, dst, sem.at[1, n]) for n, (_, _, held, dst) in enumerate(names)]
    for load in loads:
        load.start()
    loads[0].wait()
    turned_v[...] = ga_v[...].T
    stores[0].start()
    for n in (1, 2):
        loads[n].wait()
        stores[n].start()
    for store in stores:
        store.wait()


def on_device(
    tokens,
    destinations,
    counts,
    sequence_job_ids,
    job_owner_slot,
    rank_per_job,
    weight,
    input_factor_table,
    output_factor_table,
    cotangent,
):
    slot_count, seq_len, width = tokens.shape
    max_rank = input_factor_table.shape[2]
    rows = slot_count * seq_len
    anywhere = pl.BlockSpec(memory_space=pl.ANY)
    smem = pl.BlockSpec(memory_space=pltpu.SMEM)
    dma = pltpu.SemaphoreType.DMA
    served = (2, 2, RING, 64, width)
    lanes = (RING, RING, 64, width)
    out, ga, gb = pl.pallas_call(
        kernel,
        out_shape=(
            jax.ShapeDtypeStruct((rows, width), BF),
            jax.ShapeDtypeStruct((max_rank, width), F32),
            jax.ShapeDtypeStruct((max_rank, width), F32),
        ),
        in_specs=[smem] * 5 + [anywhere] * 5,
        out_specs=(anywhere,) * 3,
        scratch_shapes=[
            pltpu.VMEM(tokens.shape, BF),
            pltpu.VMEM((rows, width), BF),
            pltpu.VMEM(input_factor_table.shape, BF),
            pltpu.VMEM(output_factor_table.shape, BF),
            pltpu.VMEM((rows, width), BF),
            pltpu.VMEM((DP - 1, seq_len, width), BF),
            pltpu.VMEM((DP, seq_len, width), BF),
            pltpu.VMEM((DP - 1, 8, 128), jnp.int32),
            pltpu.VMEM((DP, 8, 128), jnp.int32),
            pltpu.VMEM((rows, rows), BF),
            pltpu.VMEM((2 * rows, rows), BF),
            pltpu.VMEM((2 * rows, rows), BF),
            pltpu.VMEM((rows, 2 * rows), BF),
            pltpu.VMEM((rows, width), BF),
            pltpu.VMEM(lanes, BF),
            pltpu.VMEM(served, BF),
            pltpu.VMEM(lanes, BF),
            pltpu.VMEM(served, BF),
            pltpu.VMEM((2, 2, width, max_rank), BF),
            pltpu.VMEM((2, 2, max_rank, width), BF),
            pltpu.VMEM((W_SLOTS, width, width), BF),
            pltpu.VMEM((2, rows, width), BF),
            pltpu.VMEM((4, rows, width), BF),
            pltpu.VMEM((3, rows, width), F32),
            pltpu.VMEM((2, rows // 2, width), BF),
            pltpu.VMEM((2, rows // 2, width), BF),
            pltpu.VMEM((2, 2, rows // 2, width), BF),
            pltpu.VMEM((2, 2, rows // 2, width), BF),
            pltpu.VMEM((2, TENSOR, 128, max_rank), BF),
            pltpu.VMEM((2, TENSOR, 128, max_rank), BF),
            pltpu.VMEM((2, TENSOR, 128, max_rank), BF),
            pltpu.VMEM(served, BF),
            pltpu.VMEM(lanes, BF),
            pltpu.VMEM((2, max_rank, width), F32),
            pltpu.VMEM((2, 3, max_rank, width), BF),
            pltpu.VMEM((2, 3, max_rank, width), BF),
            dma((4,)),
            dma((3,)),
            dma((W_SLOTS,)),
            dma((DP - 1,)),
            dma((DP - 1,)),
            dma((2, DP - 1)),
            dma((2, DP - 1)),
            dma((3, 2)),
            dma((2, 2, 2)),
            dma((8,)),
            dma((8,)),
            dma((2, 8)),
            dma((2, 8)),
            dma((2,)),
            dma((4,)),
            dma((2,)),
            dma((2,)),
            dma((2, 2)),
            dma((2, 2)),
            dma((2, TENSOR - 1)),
            dma((2, TENSOR - 1)),
            dma((2, TENSOR - 1)),
            dma((2, TENSOR - 1)),
            dma((8,)),
            dma((8,)),
            dma((2, 3)),
            dma((2, 3)),
        ],
        compiler_params=pltpu.CompilerParams(
            collective_id=0, has_side_effects=True, vmem_limit_bytes=58 * 2**20
        ),
    )(
        destinations,
        counts,
        sequence_job_ids,
        job_owner_slot,
        rank_per_job,
        tokens,
        cotangent.reshape(rows, width),
        input_factor_table,
        output_factor_table,
        weight,
    )
    out, gb, ga = pl.pallas_call(
        finish,
        out_shape=(
            jax.ShapeDtypeStruct((rows, width), BF),
            jax.ShapeDtypeStruct((max_rank, width), F32),
            jax.ShapeDtypeStruct((width, max_rank), F32),
        ),
        in_specs=[anywhere] * 3,
        out_specs=(anywhere,) * 3,
        scratch_shapes=[
            pltpu.VMEM((rows, width), BF),
            pltpu.VMEM((max_rank, width), F32),
            pltpu.VMEM((max_rank, width), F32),
            pltpu.VMEM((width, max_rank), F32),
            dma((2, 3)),
        ],
    )(out, gb, ga)
    return out.reshape(slot_count, seq_len, width), ga[None], gb[None]


def solution(mesh):
    in_specs = (
        P("dp", None, "tensor"),
        P("dp"),
        P("dp"),
        P("dp"),
        P(),
        P(),
        P("tensor", None),
        P("dp", "tensor", None),
        P("dp", None, "tensor"),
        P("dp", None, "tensor"),
    )
    out_specs = (P("dp", None, "tensor"), P("dp", "tensor", None), P("dp", None, "tensor"))
    return jax.shard_map(
        on_device, mesh=mesh, in_specs=in_specs, out_specs=out_specs, check_vma=False
    )
```

```python
import jax
import jax.numpy as jnp
from jax import lax
from jax.experimental import pallas as pl
from jax.experimental.pallas import tpu as pltpu
from jax.sharding import PartitionSpec as P

BF = jnp.bfloat16
F32 = jnp.float32
RING = 4
DP = RING * RING
TENSOR = 2 * RING
TILE = 256
W_SLOTS = 3
MOVE, PLACE = (0, 0, -1, 1), (0, 1, 1, 0)
BOTH = slice(0, 2)
MESSAGES = ((2, 2), (2, 3), (3, 2), (3, 3), (2, BOTH), (3, BOTH), (BOTH, 2), (BOTH, 3))


def mm(a, b):
    return jnp.dot(a, b, preferred_element_type=F32)


def kernel(
    dest_ref,
    count_ref,
    job_ref,
    owner_ref,
    rank_ref,
    tok_ref,
    cot_ref,
    a_ref,
    b_ref,
    w_ref,
    out_ref,
    ga_ref,
    gb_ref,
    tok_v,
    cot_v,
    a_v,
    b_v,
    out_v,
    tok_s,
    tok_r,
    facts_s,
    facts_r,
    place_hot,
    x_hot,
    c_hot,
    slot_hot,
    xs,
    x_s,
    x_r,
    c_s,
    c_r,
    fa,
    fb,
    wbuf,
    sib_s,
    sib_r,
    hold,
    hop_s,
    hop_r,
    ring_s,
    ring_r,
    part_s,
    part_r,
    ranks,
    ad_s,
    ad_r,
    g_own,
    g_s,
    g_r,
    in_sem,
    out_sem,
    w_sem,
    facts_ss,
    facts_rs,
    tok_ss,
    tok_rs,
    fac_ss,
    fac_rs,
    c_ss,
    c_rs,
    x_ss,
    x_rs,
    sib_ss,
    sib_rs,
    hop_ss,
    hop_rs,
    ring_ss,
    ring_rs,
    part_ss,
    part_rs,
    gath_ss,
    gath_rs,
    ad_ss,
    ad_rs,
    g_ss,
    g_rs,
):
    seq_len, width = tok_ref.shape[1:]
    rows = DP * seq_len
    half = rows // 2
    me = lax.axis_index("dp")
    t = lax.axis_index("tensor")
    y, z = me // RING, me % RING
    x, c = t // 2, t % 2
    odd = (y + z) % 2
    ahead = 1 - 2 * odd
    others = ((1 - odd, 1 - odd), (odd, 1 - odd), (1 - odd, odd))
    tiles = width // TILE
    wide_half = width // 2

    def remote(src, dst, send, recv, **where):
        return pltpu.make_async_remote_copy(
            src_ref=src,
            dst_ref=dst,
            send_sem=send,
            recv_sem=recv,
            device_id=where,
            device_id_type=pl.DeviceIdType.MESH,
        )

    def iota(shape, axis):
        return lax.broadcasted_iota(jnp.int32, shape, axis)

    def near(dy, dz):
        return (y + dy + RING) % RING * RING + (z + dz + RING) % RING

    def owner_of(i, j):
        first, second = (y - i + RING) % RING, (z - j + RING) % RING
        shift = (first + second) % 2
        return (first + shift) % RING * RING + (second + shift) % RING

    def rank_at(owner):
        total = jnp.int32(0)
        for j in range(DP):
            total = total + jnp.where(owner_ref[j] == owner, rank_ref[j], 0)
        return total

    def factor_at(owner, columns):
        return 32.0 / jnp.full((1, columns), rank_at(owner).astype(F32), F32)

    def span(start, size):
        return pl.ds(pl.multiple_of(start, size), size)

    loads = [
        pltpu.make_async_copy(src, dst, in_sem.at[n])
        for n, (src, dst) in enumerate(((tok_ref, tok_v), (a_ref, a_v), (b_ref, b_v), (cot_ref, cot_v)))
    ]
    for load in loads:
        load.start()

    barrier = pltpu.get_barrier_semaphore()

    @pl.loop(1, DP)
    def _(k):
        pl.semaphore_signal(
            barrier, inc=1, device_id={"dp": (me + k) % DP}, device_id_type=pl.DeviceIdType.MESH
        )

    @pl.loop(1, TENSOR)
    def _(k):
        pl.semaphore_signal(
            barrier, inc=1, device_id={"tensor": (t + k) % TENSOR}, device_id_type=pl.DeviceIdType.MESH
        )

    def w_copy(i):
        j = i // 2
        block = (x + jnp.where(j == 0, 2, jnp.where(j == 1, 1, jnp.where(j == 2, 3, 0)))) % RING * 2
        block = block + (c + 1 - i % 2) % 2
        return pltpu.make_async_copy(
            w_ref.at[:, span(block * width, width)], wbuf.at[i % W_SLOTS], w_sem.at[i % W_SLOTS]
        )

    for i in range(W_SLOTS):
        w_copy(jnp.int32(i)).start()

    loads[0].wait()

    @pl.loop(0, DP)
    def _(k):
        to = (me + k) % DP
        index = jnp.int32(0)
        for i in range(DP):
            index = jnp.where(lax.shift_right_logical(dest_ref[i], 4) == to, i, index)
        owner = owner_ref[job_ref[index]]
        oy, oz = lax.shift_right_logical(owner, 2), owner & 3
        shift = (oy + oz) & 1
        dy, dz = (to // RING + RING - oy + shift) & 3, (to % RING + RING - oz + shift) & 3
        base = (dy * RING + dz) * 2
        row = iota((8, 128), 0)
        facts_s[k] = jnp.where(
            row == 0, dest_ref[index] & 15, jnp.where(row == 1, count_ref[index], base)
        )
        tok_s[k] = tok_v[index]

    tok_r[me] = tok_s[0]
    facts_r[me] = facts_s[0]

    pl.semaphore_wait(barrier, DP - 1 + TENSOR - 1)

    def facts_copy(k):
        return remote(
            facts_s.at[k], facts_r.at[me], facts_ss.at[k - 1], facts_rs.at[k - 1], dp=(me + k) % DP
        )

    def tok_copy(h, k):
        columns = span(h * wide_half, wide_half)
        return remote(
            tok_s.at[k, :, columns],
            tok_r.at[me, :, columns],
            tok_ss.at[h, k - 1],
            tok_rs.at[h, k - 1],
            dp=(me + k) % DP,
        )

    def fac_copy(axis, n):
        table = (fa, fb)[n]
        there = ((1 - odd, odd), (odd, 1 - odd))[axis]
        to = (near(ahead, 0), near(0, ahead))[axis]
        return remote(
            table.at[odd, odd], table.at[there], fac_ss.at[axis, n], fac_rs.at[there + (n,)], dp=to
        )

    def fac_wait(n, which):
        for there in which:
            held = (fa, fb)[n].at[there]
            remote(held, held, fac_ss.at[0, n], fac_rs.at[there + (n,)], dp=me).wait_recv()

    def fac_relay(n):
        table = (fa, fb)[n]
        here = ((odd, 1 - odd), (1 - odd, odd))[n]
        to = (near(0, -ahead), near(-ahead, 0))[n]
        return remote(table.at[here], table.at[odd, odd], fac_ss.at[2, n], fac_rs.at[odd, odd, n], dp=to)

    @pl.loop(1, DP)
    def _(k):
        facts_copy(k).start()

    @pl.loop(0, 2)
    def _(h):
        @pl.loop(1, DP)
        def _(k):
            tok_copy(h, k).start()

    my_rank = rank_at(me)
    loads[1].wait()

    @pl.loop(0, width // 128)
    def _(n):
        at = span(n * 128, 128)
        kept = iota((128, a_v.shape[2]), 1) < my_rank
        fa[odd, odd, at, :] = jnp.where(kept, a_v[0, at, :].astype(F32), 0.0).astype(BF)

    for axis in range(2):
        fac_copy(axis, 0).start()
    loads[2].wait()

    @pl.loop(0, width // 128)
    def _(n):
        at = span(n * 128, 128)
        kept = iota((b_v.shape[1], 128), 0) < my_rank
        fb[odd, odd, :, at] = jnp.where(kept, b_v[0, :, at].astype(F32), 0.0).astype(BF)

    @pl.loop(1, DP)
    def _(k):
        facts_copy(k).wait_recv()

    slot_c = facts_r[:, 0, :].astype(F32)
    live_c = facts_r[:, 1, :].astype(F32)
    base_c = facts_r[:, 2, :].astype(F32)
    square = (DP, 128)
    diagonal = iota(square, 0) == iota(square, 1)
    slot_l = jnp.sum(jnp.where(diagonal, slot_c, 0.0), 0, keepdims=True)
    base_l = jnp.sum(jnp.where(diagonal, base_c, 0.0), 0, keepdims=True)
    earlier = (base_l == base_c) & (slot_l < slot_c) & (iota(square, 1) < DP)
    turn_c = jnp.sum(jnp.where(earlier, 1.0, 0.0), 1, keepdims=True)
    lane_c = base_c + turn_c
    lane_l = jnp.sum(jnp.where(diagonal, lane_c, 0.0), 0, keepdims=True)
    wide = (DP, rows)
    seq_of = iota(wide, 1) // seq_len
    slot_1, live_1, lane_1 = slot_c[:, :1], live_c[:, :1], lane_c[:, :1]
    in_slot = slot_1 == seq_of.astype(F32)
    in_order = iota(wide, 0) == seq_of
    position = (iota((1, rows), 1) % seq_len).astype(F32)

    def spread(where, value):
        return jnp.sum(jnp.where(where, value, 0.0), 0, keepdims=True)

    live = position < spread(in_order, live_1)
    c_row = spread(in_slot, lane_1) * seq_len + position
    x_row = jnp.where(live, spread(in_order, lane_1) * seq_len + position, -1.0)
    slot_row = jnp.where(live, spread(in_order, slot_1) * seq_len + position, -1.0)

    def build(hot, wanted):
        @pl.loop(0, hot.shape[0] // 64)
        def _(n):
            row = (iota((64, rows), 0) + n * 64).astype(F32)
            hot[span(n * 64, 64), :] = jnp.where(row == wanted, 1.0, 0.0).astype(BF)

    build(x_hot, x_row)
    build(place_hot, slot_row)
    build(c_hot, c_row)

    lane_shape = (RING, RING, 2 * seq_len)

    def lane_place(dy, dz):
        row = PLACE[dy] if dy != BOTH else BOTH
        column = PLACE[dz] if dz != BOTH else BOTH
        return row, column, (dy != BOTH) * 2 + (dz != BOTH)

    def lane_move(dy, dz):
        return (MOVE[dy] if dy != BOTH else 0, MOVE[dz] if dz != BOTH else 0)

    def x_copy(h, m):
        message, columns = MESSAGES[m], span(h * wide_half, wide_half)
        return remote(
            x_s.at[message + (slice(None), columns)],
            x_r.at[lane_place(*message) + (slice(None), columns)],
            x_ss.at[h, m],
            x_rs.at[h, m],
            dp=near(*lane_move(*message)),
        )

    def c_copy(m):
        message = MESSAGES[m]
        return remote(
            c_s.at[message],
            c_r.at[lane_place(*message)],
            c_ss.at[m],
            c_rs.at[m],
            dp=near(*lane_move(*message)),
        )

    loads[3].wait()

    @pl.loop(0, tiles)
    def _(n):
        at = span(n * TILE, TILE)
        c_s[:, :, :, at] = mm(c_hot[...], cot_v[:, at]).astype(BF).reshape(lane_shape + (TILE,))

    @pl.loop(0, 2)
    def _(h):
        @pl.loop(1, DP)
        def _(k):
            tok_copy(h, k).wait_recv()

        @pl.loop(0, tiles // 2)
        def _(n):
            at = span(h * wide_half + n * TILE, TILE)
            landed = tok_r[:, :, at].reshape(rows, TILE)
            x_s[:, :, :, at] = mm(x_hot[...], landed).astype(BF).reshape(lane_shape + (TILE,))

        for m in range(len(MESSAGES)):
            x_copy(h, m).start()

        @pl.loop(0, tiles // 2)
        def _(n):
            at = span(h * wide_half + n * TILE, TILE)
            xs[:, at] = mm(place_hot[...], tok_r[:, :, at].reshape(rows, TILE)).astype(BF)

    for axis in range(2):
        fac_copy(axis, 1).start()
    for m in range(len(MESSAGES)):
        c_copy(m).start()
    x_r[:, :, 0] = x_s[BOTH, BOTH]
    c_r[:, :, 0] = c_s[BOTH, BOTH]

    def sib_copy(j):
        return remote(
            sib_s.at[j % 2], sib_r.at[j], sib_ss.at[j % 2], sib_rs.at[j], tensor=x * 2 + (1 - c)
        )

    right, left = ((x + 1) % RING) * 2 + c, ((x + 3) % RING) * 2 + c

    def hop_copy(way):
        return remote(
            hop_s.at[way], hop_r.at[way], hop_ss.at[way], hop_rs.at[way], tensor=(right, left)[way]
        )

    def ring_copy(way, part):
        return remote(
            ring_s.at[way, part],
            ring_r.at[way, part],
            ring_ss.at[way, part],
            ring_rs.at[way, part],
            tensor=(right, left)[way],
        )

    def half_rows(part, put):
        @pl.loop(0, half // 32)
        def _(n):
            put(span(part * half + n * 32, 32), span(n * 32, 32))

    def send_hop(way):
        def put(at, to):
            hop_s[way, to] = (hold[0, at] + sib_r[0, at].astype(F32)).astype(BF)

        half_rows(way, put)
        hop_copy(way).start()

    def send_ring(way, part):
        def put(at, to):
            value = hold[1 - way, at] + sib_r[1 + way, at].astype(F32)
            if way == part:
                value = value + hop_r[way, to].astype(F32)
            ring_s[way, part, to] = value.astype(BF)

        half_rows(part, put)
        ring_copy(way, part).start()

    def part_copy(kind, k):
        to = (t + k) % TENSOR
        return remote(
            part_s.at[kind, to],
            part_r.at[kind, k],
            part_ss.at[kind, k - 1],
            part_rs.at[kind, k - 1],
            tensor=to,
        )

    def gath_copy(kind, k):
        to = (t + k) % TENSOR
        held = ranks.at[kind, t]
        return remote(held, held, gath_ss.at[kind, k - 1], gath_rs.at[kind, k - 1], tensor=to)

    def served(ref, i, j):
        return ref[i, j].reshape(RING * 64, width)

    def send_parts(kind, make):
        @pl.loop(0, 4)
        def _(q):
            value = make(q // 2, q % 2).astype(BF)
            part_s[kind, 2 * q] = value[:128]
            part_s[kind, 2 * q + 1] = value[128:]

        @pl.loop(1, TENSOR)
        def _(k):
            part_copy(kind, k).start()

        part_r[kind, 0] = part_s[kind, t]

    def sum_parts(kind, scale):
        @pl.loop(1, TENSOR)
        def _(k):
            part_copy(kind, k).wait_recv()

        total = part_r[kind, 0].astype(F32)
        for k in range(1, TENSOR):
            total = total + part_r[kind, k].astype(F32)
        ranks[kind, t] = (total if scale is None else total * scale).astype(BF)

        @pl.loop(1, TENSOR)
        def _(k):
            gath_copy(kind, k).start()

    def gathered(kind):
        @pl.loop(1, TENSOR)
        def _(k):
            held = ranks.at[kind, (t + TENSOR - k) % TENSOR]
            remote(held, held, gath_ss.at[kind, k - 1], gath_rs.at[kind, k - 1], tensor=t).wait_recv()

    def rank_rows(kind, i, j):
        return ranks[kind, pl.ds(i * 4 + j * 2, 2)].reshape(RING * 64, ranks.shape[3])

    @pl.loop(0, 4)
    def _(j):
        w_copy(2 * j).wait()

        @pl.when(j >= 2)
        def _():
            sib_copy(j - 2).wait_send()

        @pl.loop(0, tiles)
        def _(n):
            at = span(n * TILE, TILE)
            sib_s[j % 2, :, at] = mm(xs[...], wbuf[(2 * j) % W_SLOTS, :, at]).astype(BF)

        sib_copy(j).start()

        @pl.when(2 * j + W_SLOTS < 8)
        def _():
            w_copy(2 * j + W_SLOTS).start()

        @pl.when(j == 1)
        def _():
            sib_copy(0).wait_recv()
            send_hop(0)
            send_hop(1)
            fac_wait(0, others[1:])
            fac_relay(0).start()

        @pl.when(j == 3)
        def _():
            sib_copy(2).wait_recv()
            send_ring(1, 0)

        w_copy(2 * j + 1).wait()

        @pl.loop(0, tiles)
        def _(n):
            at = span(n * TILE, TILE)
            hold[jnp.where(j == 3, 2, j % 2), :, at] = mm(xs[...], wbuf[(2 * j + 1) % W_SLOTS, :, at])

        @pl.when(2 * j + 1 + W_SLOTS < 8)
        def _():
            w_copy(2 * j + 1 + W_SLOTS).start()

        @pl.when(j == 1)
        def _():
            fac_wait(0, others[:1])

            @pl.loop(0, 2)
            def _(h):
                for m in range(len(MESSAGES)):
                    x_copy(h, m).wait_recv()

            send_parts(0, lambda i, k: mm(served(x_r, i, k), fa[i, k]))

        @pl.when(j == 2)
        def _():
            fac_wait(1, others[1:])
            fac_relay(1).start()
            sum_parts(0, None)
            sib_copy(1).wait_recv()
            send_ring(0, 1)

    def ad_copy(m):
        message = MESSAGES[m]
        dy, dz = lane_move(*message)
        return remote(
            ad_s.at[lane_place(*message)],
            ad_r.at[message],
            ad_ss.at[m],
            ad_rs.at[m],
            dp=near(-dy, -dz),
        )

    fac_wait(1, others[:1])
    gathered(0)

    @pl.loop(0, 4)
    def _(q):
        i, j = q // 2, q % 2
        value = mm(rank_rows(0, i, j), fb[i, j]) * factor_at(owner_of(i, j), width)
        ad_s[i, j] = value.astype(BF).reshape(RING, 64, width)

    for m in range(len(MESSAGES)):
        ad_copy(m).start()
    ad_r[BOTH, BOTH] = ad_s[:, :, 0]

    for m in range(len(MESSAGES)):
        c_copy(m).wait_recv()
    send_parts(
        1,
        lambda i, j: lax.dot_general(
            served(c_r, i, j), fb[i, j], (((1,), (1,)), ((), ())), preferred_element_type=F32
        ),
    )

    def g_copy(n, which):
        dy = jnp.where(which == 0, -ahead, jnp.where(which == 1, ahead, 0))
        dz = jnp.where(which == 0, -ahead, jnp.where(which == 1, 0, ahead))
        return remote(
            g_s.at[n, which],
            g_r.at[n, which],
            g_ss.at[n, which],
            g_rs.at[n, which],
            dp=near(dy, dz),
        )

    def gradient(n, kind, row_ref):
        @pl.loop(0, 4)
        def _(which):
            i = jnp.where((which == 1) | (which == 3), odd, 1 - odd)
            j = jnp.where(which >= 2, odd, 1 - odd)
            turned = rank_rows(kind, i, j).astype(F32).T.astype(BF)
            value = mm(turned, served(row_ref, i, j)) * (1.0 / seq_len)
            if n == 1:
                value = value * factor_at(owner_of(i, j), width)
            g_own[n] = value
            g_s[n, which] = value.astype(BF)

            @pl.when(which < 3)
            def _():
                g_copy(n, which).start()

    gradient(1, 0, c_r)

    @pl.loop(0, rows // 64)
    def _(n):
        row = iota((64, 128), 0) + n * 64
        mine = jnp.where(slot_l == (row // seq_len).astype(F32), lane_l, 0.0)
        place = jnp.sum(mine, 1, keepdims=True) * seq_len + (row % seq_len).astype(F32)[:, :1]
        slot_hot[span(n * 64, 64), :] = jnp.where(
            iota((64, 2 * rows), 1).astype(F32) == place, 1.0, 0.0
        ).astype(BF)

    sum_parts(1, factor_at(owner_of(t // 4, (t // 2) % 2), ranks.shape[3]))
    for way in range(2):
        hop_copy(way).wait_recv()
        send_ring(way, way)
    gathered(1)
    gradient(0, 1, x_r)

    sib_copy(3).wait_recv()
    for m in range(len(MESSAGES)):
        ad_copy(m).wait_recv()

    @pl.loop(0, tiles)
    def _(n):
        at = span(n * TILE, TILE)
        back = ad_r[:, :, :, at].reshape(2 * rows, TILE)
        hold[2, :, at] = hold[2, :, at] + sib_r[3, :, at].astype(F32) + mm(slot_hot[...], back)

    for way in range(2):
        for part in range(2):
            ring_copy(way, part).wait_recv()

    for part in range(2):

        def put(at, to):
            out_v[at] = (
                hold[2, at] + ring_r[0, part, to].astype(F32) + ring_r[1, part, to].astype(F32)
            ).astype(BF)

        half_rows(part, put)
    stores = [pltpu.make_async_copy(out_v, out_ref, out_sem.at[2])]
    stores[0].start()

    for n, g_ref in ((1, gb_ref), (0, ga_ref)):

        @pl.loop(0, 3)
        def _(which):
            remote(
                g_s.at[n, which], g_r.at[n, which], g_ss.at[n, which], g_rs.at[n, which], dp=me
            ).wait_recv()

        @pl.loop(0, g_own.shape[1] // 32)
        def _(k):
            at = span(k * 32, 32)
            total = g_own[n, at]
            for which in range(3):
                total = total + g_r[n, which, at].astype(F32)
            g_own[n, at] = total

        stores.append(pltpu.make_async_copy(g_own.at[n], g_ref, out_sem.at[n]))
        stores[-1].start()

    @pl.loop(1, DP)
    def _(k):
        facts_copy(k).wait_send()
        tok_copy(0, k).wait_send()
        tok_copy(1, k).wait_send()

    for n in range(2):
        for axis in range(2):
            fac_copy(axis, n).wait_send()
        fac_relay(n).wait_send()
    for m in range(len(MESSAGES)):
        for h in range(2):
            x_copy(h, m).wait_send()
        c_copy(m).wait_send()
        ad_copy(m).wait_send()
    for j in (2, 3):
        sib_copy(j).wait_send()
    for way in range(2):
        hop_copy(way).wait_send()
        for part in range(2):
            ring_copy(way, part).wait_send()
    for kind in range(2):

        @pl.loop(1, TENSOR)
        def _(k):
            part_copy(kind, k).wait_send()
            gath_copy(kind, k).wait_send()

        @pl.loop(0, 3)
        def _(which):
            g_copy(kind, which).wait_send()

    for store in stores:
        store.wait()


def finish(out_ref, gb_ref, ga_ref, out_to, gb_to, ga_to, out_v, gb_v, ga_v, turned_v, sem):
    names = ((ga_ref, ga_v, turned_v, ga_to), (gb_ref, gb_v, gb_v, gb_to), (out_ref, out_v, out_v, out_to))
    loads = [pltpu.make_async_copy(src, held, sem.at[0, n]) for n, (src, held, _, _) in enumerate(names)]
    stores = [pltpu.make_async_copy(held, dst, sem.at[1, n]) for n, (_, _, held, dst) in enumerate(names)]
    for load in loads:
        load.start()
    loads[0].wait()
    turned_v[...] = ga_v[...].T
    stores[0].start()
    for n in (1, 2):
        loads[n].wait()
        stores[n].start()
    for store in stores:
        store.wait()


def on_device(
    tokens,
    destinations,
    counts,
    sequence_job_ids,
    job_owner_slot,
    rank_per_job,
    weight,
    input_factor_table,
    output_factor_table,
    cotangent,
):
    slot_count, seq_len, width = tokens.shape
    max_rank = input_factor_table.shape[2]
    rows = slot_count * seq_len
    anywhere = pl.BlockSpec(memory_space=pl.ANY)
    smem = pl.BlockSpec(memory_space=pltpu.SMEM)
    dma = pltpu.SemaphoreType.DMA
    served = (2, 2, RING, 64, width)
    lanes = (RING, RING, 64, width)
    out, ga, gb = pl.pallas_call(
        kernel,
        out_shape=(
            jax.ShapeDtypeStruct((rows, width), BF),
            jax.ShapeDtypeStruct((max_rank, width), F32),
            jax.ShapeDtypeStruct((max_rank, width), F32),
        ),
        in_specs=[smem] * 5 + [anywhere] * 5,
        out_specs=(anywhere,) * 3,
        scratch_shapes=[
            pltpu.VMEM(tokens.shape, BF),
            pltpu.VMEM((rows, width), BF),
            pltpu.VMEM(input_factor_table.shape, BF),
            pltpu.VMEM(output_factor_table.shape, BF),
            pltpu.VMEM((rows, width), BF),
            pltpu.VMEM((DP, seq_len, width), BF),
            pltpu.VMEM((DP, seq_len, width), BF),
            pltpu.VMEM((DP, 8, 128), jnp.int32),
            pltpu.VMEM((DP, 8, 128), jnp.int32),
            pltpu.VMEM((rows, rows), BF),
            pltpu.VMEM((2 * rows, rows), BF),
            pltpu.VMEM((2 * rows, rows), BF),
            pltpu.VMEM((rows, 2 * rows), BF),
            pltpu.VMEM((rows, width), BF),
            pltpu.VMEM(lanes, BF),
            pltpu.VMEM(served, BF),
            pltpu.VMEM(lanes, BF),
            pltpu.VMEM(served, BF),
            pltpu.VMEM((2, 2, width, max_rank), BF),
            pltpu.VMEM((2, 2, max_rank, width), BF),
            pltpu.VMEM((W_SLOTS, width, width), BF),
            pltpu.VMEM((2, rows, width), BF),
            pltpu.VMEM((4, rows, width), BF),
            pltpu.VMEM((3, rows, width), F32),
            pltpu.VMEM((2, rows // 2, width), BF),
            pltpu.VMEM((2, rows // 2, width), BF),
            pltpu.VMEM((2, 2, rows // 2, width), BF),
            pltpu.VMEM((2, 2, rows // 2, width), BF),
            pltpu.VMEM((2, TENSOR, 128, max_rank), BF),
            pltpu.VMEM((2, TENSOR, 128, max_rank), BF),
            pltpu.VMEM((2, TENSOR, 128, max_rank), BF),
            pltpu.VMEM(served, BF),
            pltpu.VMEM(lanes, BF),
            pltpu.VMEM((2, max_rank, width), F32),
            pltpu.VMEM((2, 4, max_rank, width), BF),
            pltpu.VMEM((2, 3, max_rank, width), BF),
            dma((4,)),
            dma((3,)),
            dma((W_SLOTS,)),
            dma((DP - 1,)),
            dma((DP - 1,)),
            dma((2, DP - 1)),
            dma((2, DP - 1)),
            dma((3, 2)),
            dma((2, 2, 2)),
            dma((8,)),
            dma((8,)),
            dma((2, 8)),
            dma((2, 8)),
            dma((2,)),
            dma((4,)),
            dma((2,)),
            dma((2,)),
            dma((2, 2)),
            dma((2, 2)),
            dma((2, TENSOR - 1)),
            dma((2, TENSOR - 1)),
            dma((2, TENSOR - 1)),
            dma((2, TENSOR - 1)),
            dma((8,)),
            dma((8,)),
            dma((2, 3)),
            dma((2, 3)),
        ],
        compiler_params=pltpu.CompilerParams(
            collective_id=0, has_side_effects=True, vmem_limit_bytes=58 * 2**20
        ),
    )(
        destinations,
        counts,
        sequence_job_ids,
        job_owner_slot,
        rank_per_job,
        tokens,
        cotangent.reshape(rows, width),
        input_factor_table,
        output_factor_table,
        weight,
    )
    out, gb, ga = pl.pallas_call(
        finish,
        out_shape=(
            jax.ShapeDtypeStruct((rows, width), BF),
            jax.ShapeDtypeStruct((max_rank, width), F32),
            jax.ShapeDtypeStruct((width, max_rank), F32),
        ),
        in_specs=[anywhere] * 3,
        out_specs=(anywhere,) * 3,
        scratch_shapes=[
            pltpu.VMEM((rows, width), BF),
            pltpu.VMEM((max_rank, width), F32),
            pltpu.VMEM((max_rank, width), F32),
            pltpu.VMEM((width, max_rank), F32),
            dma((2, 3)),
        ],
    )(out, gb, ga)
    return out.reshape(slot_count, seq_len, width), ga[None], gb[None]


def solution(mesh):
    in_specs = (
        P("dp", None, "tensor"),
        P("dp"),
        P("dp"),
        P("dp"),
        P(),
        P(),
        P("tensor", None),
        P("dp", "tensor", None),
        P("dp", None, "tensor"),
        P("dp", None, "tensor"),
    )
    out_specs = (P("dp", None, "tensor"), P("dp", "tensor", None), P("dp", None, "tensor"))
    return jax.shard_map(
        on_device, mesh=mesh, in_specs=in_specs, out_specs=out_specs, check_vma=False
    )
```

```python
import jax
import jax.numpy as jnp
from jax import lax
from jax.experimental import pallas as pl
from jax.experimental.pallas import tpu as pltpu
from jax.sharding import PartitionSpec as P

BF = jnp.bfloat16
F32 = jnp.float32
RING = 4
DP = RING * RING
TENSOR = 2 * RING
TILE = 256
W_SLOTS = 4
MOVE, PLACE = (0, 0, -1, 1), (0, 1, 1, 0)
BOTH = slice(0, 2)
MESSAGES = ((2, 2), (2, 3), (3, 2), (3, 3), (2, BOTH), (3, BOTH), (BOTH, 2), (BOTH, 3))


def mm(a, b):
    return jnp.dot(a, b, preferred_element_type=F32)


def kernel(
    dest_ref,
    count_ref,
    job_ref,
    owner_ref,
    rank_ref,
    tok_ref,
    cot_ref,
    a_ref,
    b_ref,
    w_ref,
    out_ref,
    ga_ref,
    gb_ref,
    tok_v,
    cot_v,
    a_v,
    b_v,
    out_v,
    tok_s,
    tok_r,
    facts_s,
    facts_r,
    place_hot,
    x_hot,
    c_hot,
    slot_hot,
    xs,
    x_s,
    x_r,
    c_s,
    c_r,
    fa,
    fb,
    wbuf,
    sib_s,
    sib_r,
    hold,
    hop_s,
    hop_r,
    ring_s,
    ring_r,
    part_s,
    part_r,
    ranks,
    ad_s,
    ad_r,
    g_own,
    g_s,
    g_r,
    in_sem,
    out_sem,
    w_sem,
    facts_ss,
    facts_rs,
    tok_ss,
    tok_rs,
    fac_ss,
    fac_rs,
    c_ss,
    c_rs,
    x_ss,
    x_rs,
    sib_ss,
    sib_rs,
    hop_ss,
    hop_rs,
    ring_ss,
    ring_rs,
    part_ss,
    part_rs,
    gath_ss,
    gath_rs,
    ad_ss,
    ad_rs,
    g_ss,
    g_rs,
):
    seq_len, width = tok_ref.shape[1:]
    rows = DP * seq_len
    half = rows // 2
    me = lax.axis_index("dp")
    t = lax.axis_index("tensor")
    y, z = me // RING, me % RING
    x, c = t // 2, t % 2
    odd = (y + z) % 2
    ahead = 1 - 2 * odd
    others = ((1 - odd, 1 - odd), (odd, 1 - odd), (1 - odd, odd))
    tiles = width // TILE
    wide_half = width // 2

    def remote(src, dst, send, recv, **where):
        return pltpu.make_async_remote_copy(
            src_ref=src,
            dst_ref=dst,
            send_sem=send,
            recv_sem=recv,
            device_id=where,
            device_id_type=pl.DeviceIdType.MESH,
        )

    def iota(shape, axis):
        return lax.broadcasted_iota(jnp.int32, shape, axis)

    def near(dy, dz):
        return (y + dy + RING) % RING * RING + (z + dz + RING) % RING

    def owner_of(i, j):
        first, second = (y - i + RING) % RING, (z - j + RING) % RING
        shift = (first + second) % 2
        return (first + shift) % RING * RING + (second + shift) % RING

    def rank_at(owner):
        total = jnp.int32(0)
        for j in range(DP):
            total = total + jnp.where(owner_ref[j] == owner, rank_ref[j], 0)
        return total

    def factor_at(owner, columns):
        return 32.0 / jnp.full((1, columns), rank_at(owner).astype(F32), F32)

    def span(start, size):
        return pl.ds(pl.multiple_of(start, size), size)

    loads = [
        pltpu.make_async_copy(src, dst, in_sem.at[n])
        for n, (src, dst) in enumerate(((tok_ref, tok_v), (a_ref, a_v), (b_ref, b_v), (cot_ref, cot_v)))
    ]
    for load in loads:
        load.start()

    barrier = pltpu.get_barrier_semaphore()

    @pl.loop(1, DP)
    def _(k):
        pl.semaphore_signal(
            barrier, inc=1, device_id={"dp": (me + k) % DP}, device_id_type=pl.DeviceIdType.MESH
        )

    @pl.loop(1, TENSOR)
    def _(k):
        pl.semaphore_signal(
            barrier, inc=1, device_id={"tensor": (t + k) % TENSOR}, device_id_type=pl.DeviceIdType.MESH
        )

    def w_copy(i):
        j = i // 2
        block = (x + jnp.where(j == 0, 2, jnp.where(j == 1, 1, jnp.where(j == 2, 3, 0)))) % RING * 2
        block = block + (c + 1 - i % 2) % 2
        return pltpu.make_async_copy(
            w_ref.at[:, span(block * width, width)], wbuf.at[i % W_SLOTS], w_sem.at[i % W_SLOTS]
        )

    for i in range(W_SLOTS):
        w_copy(jnp.int32(i)).start()

    loads[0].wait()

    @pl.loop(0, DP)
    def _(k):
        to = (me + k) % DP
        index = jnp.int32(0)
        for i in range(DP):
            index = jnp.where(lax.shift_right_logical(dest_ref[i], 4) == to, i, index)
        owner = owner_ref[job_ref[index]]
        oy, oz = lax.shift_right_logical(owner, 2), owner & 3
        shift = (oy + oz) & 1
        dy, dz = (to // RING + RING - oy + shift) & 3, (to % RING + RING - oz + shift) & 3
        base = (dy * RING + dz) * 2
        row = iota((8, 128), 0)
        facts_s[k] = jnp.where(
            row == 0, dest_ref[index] & 15, jnp.where(row == 1, count_ref[index], base)
        )
        tok_s[k] = tok_v[index]

    tok_r[me] = tok_s[0]
    facts_r[me] = facts_s[0]

    pl.semaphore_wait(barrier, DP - 1 + TENSOR - 1)

    def facts_copy(k):
        return remote(
            facts_s.at[k], facts_r.at[me], facts_ss.at[k - 1], facts_rs.at[k - 1], dp=(me + k) % DP
        )

    def tok_copy(h, k):
        columns = span(h * wide_half, wide_half)
        return remote(
            tok_s.at[k, :, columns],
            tok_r.at[me, :, columns],
            tok_ss.at[h, k - 1],
            tok_rs.at[h, k - 1],
            dp=(me + k) % DP,
        )

    def fac_copy(axis, n):
        table = (fa, fb)[n]
        there = ((1 - odd, odd), (odd, 1 - odd))[axis]
        to = (near(ahead, 0), near(0, ahead))[axis]
        return remote(
            table.at[odd, odd], table.at[there], fac_ss.at[axis, n], fac_rs.at[there + (n,)], dp=to
        )

    def fac_wait(n, which):
        for there in which:
            held = (fa, fb)[n].at[there]
            remote(held, held, fac_ss.at[0, n], fac_rs.at[there + (n,)], dp=me).wait_recv()

    def fac_relay(n):
        table = (fa, fb)[n]
        here = ((odd, 1 - odd), (1 - odd, odd))[n]
        to = (near(0, -ahead), near(-ahead, 0))[n]
        return remote(table.at[here], table.at[odd, odd], fac_ss.at[2, n], fac_rs.at[odd, odd, n], dp=to)

    @pl.loop(1, DP)
    def _(k):
        facts_copy(k).start()

    @pl.loop(0, 2)
    def _(h):
        @pl.loop(1, DP)
        def _(k):
            tok_copy(h, k).start()

    my_rank = rank_at(me)
    loads[1].wait()

    @pl.loop(0, width // 128)
    def _(n):
        at = span(n * 128, 128)
        kept = iota((128, a_v.shape[2]), 1) < my_rank
        fa[odd, odd, at, :] = jnp.where(kept, a_v[0, at, :].astype(F32), 0.0).astype(BF)

    for axis in range(2):
        fac_copy(axis, 0).start()
    loads[2].wait()

    @pl.loop(0, width // 128)
    def _(n):
        at = span(n * 128, 128)
        kept = iota((b_v.shape[1], 128), 0) < my_rank
        fb[odd, odd, :, at] = jnp.where(kept, b_v[0, :, at].astype(F32), 0.0).astype(BF)

    for axis in range(2):
        fac_copy(axis, 1).start()

    @pl.loop(1, DP)
    def _(k):
        facts_copy(k).wait_recv()

    slot_c = facts_r[:, 0, :].astype(F32)
    live_c = facts_r[:, 1, :].astype(F32)
    base_c = facts_r[:, 2, :].astype(F32)
    square = (DP, 128)
    diagonal = iota(square, 0) == iota(square, 1)
    slot_l = jnp.sum(jnp.where(diagonal, slot_c, 0.0), 0, keepdims=True)
    base_l = jnp.sum(jnp.where(diagonal, base_c, 0.0), 0, keepdims=True)
    earlier = (base_l == base_c) & (slot_l < slot_c) & (iota(square, 1) < DP)
    turn_c = jnp.sum(jnp.where(earlier, 1.0, 0.0), 1, keepdims=True)
    lane_c = base_c + turn_c
    lane_l = jnp.sum(jnp.where(diagonal, lane_c, 0.0), 0, keepdims=True)
    wide = (DP, rows)
    seq_of = iota(wide, 1) // seq_len
    slot_1, live_1, lane_1 = slot_c[:, :1], live_c[:, :1], lane_c[:, :1]
    in_slot = slot_1 == seq_of.astype(F32)
    in_order = iota(wide, 0) == seq_of
    position = (iota((1, rows), 1) % seq_len).astype(F32)

    def spread(where, value):
        return jnp.sum(jnp.where(where, value, 0.0), 0, keepdims=True)

    live = position < spread(in_order, live_1)
    c_row = spread(in_slot, lane_1) * seq_len + position
    x_row = jnp.where(live, spread(in_order, lane_1) * seq_len + position, -1.0)
    slot_row = jnp.where(live, spread(in_order, slot_1) * seq_len + position, -1.0)

    def build(hot, wanted):
        @pl.loop(0, hot.shape[0] // 64)
        def _(n):
            row = (iota((64, rows), 0) + n * 64).astype(F32)
            hot[span(n * 64, 64), :] = jnp.where(row == wanted, 1.0, 0.0).astype(BF)

    build(c_hot, c_row)

    lane_shape = (RING, RING, 2 * seq_len)

    def lane_place(dy, dz):
        row = PLACE[dy] if dy != BOTH else BOTH
        column = PLACE[dz] if dz != BOTH else BOTH
        return row, column, (dy != BOTH) * 2 + (dz != BOTH)

    def lane_move(dy, dz):
        return (MOVE[dy] if dy != BOTH else 0, MOVE[dz] if dz != BOTH else 0)

    def x_copy(h, m):
        message, columns = MESSAGES[m], span(h * wide_half, wide_half)
        return remote(
            x_s.at[message + (slice(None), columns)],
            x_r.at[lane_place(*message) + (slice(None), columns)],
            x_ss.at[h, m],
            x_rs.at[h, m],
            dp=near(*lane_move(*message)),
        )

    def c_copy(m):
        message = MESSAGES[m]
        return remote(
            c_s.at[message],
            c_r.at[lane_place(*message)],
            c_ss.at[m],
            c_rs.at[m],
            dp=near(*lane_move(*message)),
        )

    loads[3].wait()

    @pl.loop(0, tiles)
    def _(n):
        at = span(n * TILE, TILE)
        c_s[:, :, :, at] = mm(c_hot[...], cot_v[:, at]).astype(BF).reshape(lane_shape + (TILE,))

    for m in range(len(MESSAGES)):
        c_copy(m).start()
    build(x_hot, x_row)
    build(place_hot, slot_row)

    @pl.loop(0, rows // 64)
    def _(n):
        row = iota((64, 128), 0) + n * 64
        mine = jnp.where(slot_l == (row // seq_len).astype(F32), lane_l, 0.0)
        place = jnp.sum(mine, 1, keepdims=True) * seq_len + (row % seq_len).astype(F32)[:, :1]
        slot_hot[span(n * 64, 64), :] = jnp.where(
            iota((64, 2 * rows), 1).astype(F32) == place, 1.0, 0.0
        ).astype(BF)

    @pl.loop(0, 2)
    def _(h):
        @pl.loop(1, DP)
        def _(k):
            tok_copy(h, k).wait_recv()

        @pl.loop(0, tiles // 2)
        def _(n):
            at = span(h * wide_half + n * TILE, TILE)
            landed = tok_r[:, :, at].reshape(rows, TILE)
            x_s[:, :, :, at] = mm(x_hot[...], landed).astype(BF).reshape(lane_shape + (TILE,))

        for m in range(len(MESSAGES)):
            x_copy(h, m).start()

        @pl.loop(0, tiles // 2)
        def _(n):
            at = span(h * wide_half + n * TILE, TILE)
            xs[:, at] = mm(place_hot[...], tok_r[:, :, at].reshape(rows, TILE)).astype(BF)

    x_r[:, :, 0] = x_s[BOTH, BOTH]
    c_r[:, :, 0] = c_s[BOTH, BOTH]

    def sib_copy(j):
        return remote(
            sib_s.at[j % 2], sib_r.at[j], sib_ss.at[j % 2], sib_rs.at[j], tensor=x * 2 + (1 - c)
        )

    right, left = ((x + 1) % RING) * 2 + c, ((x + 3) % RING) * 2 + c

    def hop_copy(way):
        return remote(
            hop_s.at[way], hop_r.at[way], hop_ss.at[way], hop_rs.at[way], tensor=(right, left)[way]
        )

    def ring_copy(way, part):
        return remote(
            ring_s.at[way, part],
            ring_r.at[way, part],
            ring_ss.at[way, part],
            ring_rs.at[way, part],
            tensor=(right, left)[way],
        )

    def half_rows(part, put):
        @pl.loop(0, half // 32)
        def _(n):
            put(span(part * half + n * 32, 32), span(n * 32, 32))

    def send_hop(way):
        def put(at, to):
            hop_s[way, to] = (hold[0, at] + sib_r[0, at].astype(F32)).astype(BF)

        half_rows(way, put)
        hop_copy(way).start()

    def send_ring(way, part):
        def put(at, to):
            value = hold[1 - way, at] + sib_r[1 + way, at].astype(F32)
            if way == part:
                value = value + hop_r[way, to].astype(F32)
            ring_s[way, part, to] = value.astype(BF)

        half_rows(part, put)
        ring_copy(way, part).start()

    def part_copy(kind, k):
        to = (t + k) % TENSOR
        return remote(
            part_s.at[kind, to],
            part_r.at[kind, k],
            part_ss.at[kind, k - 1],
            part_rs.at[kind, k - 1],
            tensor=to,
        )

    def gath_copy(kind, k):
        to = (t + k) % TENSOR
        held = ranks.at[kind, t]
        return remote(held, held, gath_ss.at[kind, k - 1], gath_rs.at[kind, k - 1], tensor=to)

    def served(ref, i, j):
        return ref[i, j].reshape(RING * 64, width)

    def send_parts(kind, make):
        @pl.loop(0, 4)
        def _(q):
            value = make(q // 2, q % 2).astype(BF)
            part_s[kind, 2 * q] = value[:128]
            part_s[kind, 2 * q + 1] = value[128:]

        @pl.loop(1, TENSOR)
        def _(k):
            part_copy(kind, k).start()

        part_r[kind, 0] = part_s[kind, t]

    def sum_parts(kind, scale):
        @pl.loop(1, TENSOR)
        def _(k):
            part_copy(kind, k).wait_recv()

        total = part_r[kind, 0].astype(F32)
        for k in range(1, TENSOR):
            total = total + part_r[kind, k].astype(F32)
        ranks[kind, t] = (total if scale is None else total * scale).astype(BF)

        @pl.loop(1, TENSOR)
        def _(k):
            gath_copy(kind, k).start()

    def gathered(kind):
        @pl.loop(1, TENSOR)
        def _(k):
            held = ranks.at[kind, (t + TENSOR - k) % TENSOR]
            remote(held, held, gath_ss.at[kind, k - 1], gath_rs.at[kind, k - 1], tensor=t).wait_recv()

    def rank_rows(kind, i, j):
        return ranks[kind, pl.ds(i * 4 + j * 2, 2)].reshape(RING * 64, ranks.shape[3])

    @pl.loop(0, 4)
    def _(j):
        w_copy(2 * j).wait()

        @pl.when(j >= 2)
        def _():
            sib_copy(j - 2).wait_send()

        @pl.loop(0, tiles)
        def _(n):
            at = span(n * TILE, TILE)
            sib_s[j % 2, :, at] = mm(xs[...], wbuf[(2 * j) % W_SLOTS, :, at]).astype(BF)

        sib_copy(j).start()

        @pl.when(2 * j + W_SLOTS < 8)
        def _():
            w_copy(2 * j + W_SLOTS).start()

        @pl.when(j == 1)
        def _():
            sib_copy(0).wait_recv()
            send_hop(0)
            send_hop(1)
            for n in (1, 0):
                fac_wait(n, others[1:])
                fac_relay(n).start()

        @pl.when(j == 3)
        def _():
            sib_copy(2).wait_recv()
            send_ring(1, 0)

        w_copy(2 * j + 1).wait()

        @pl.loop(0, tiles)
        def _(n):
            at = span(n * TILE, TILE)
            hold[jnp.where(j == 3, 2, j % 2), :, at] = mm(xs[...], wbuf[(2 * j + 1) % W_SLOTS, :, at])

        @pl.when(2 * j + 1 + W_SLOTS < 8)
        def _():
            w_copy(2 * j + 1 + W_SLOTS).start()

        @pl.when(j == 1)
        def _():
            fac_wait(1, others[:1])
            for m in range(len(MESSAGES)):
                c_copy(m).wait_recv()
            send_parts(
                1,
                lambda i, k: lax.dot_general(
                    served(c_r, i, k), fb[i, k], (((1,), (1,)), ((), ())), preferred_element_type=F32
                ),
            )

        @pl.when(j == 2)
        def _():
            sum_parts(1, factor_at(owner_of(t // 4, (t // 2) % 2), ranks.shape[3]))
            fac_wait(0, others[:1])

            @pl.loop(0, 2)
            def _(h):
                for m in range(len(MESSAGES)):
                    x_copy(h, m).wait_recv()

            send_parts(0, lambda i, k: mm(served(x_r, i, k), fa[i, k]))
            sib_copy(1).wait_recv()
            send_ring(0, 1)

    def ad_copy(m):
        message = MESSAGES[m]
        dy, dz = lane_move(*message)
        return remote(
            ad_s.at[lane_place(*message)],
            ad_r.at[message],
            ad_ss.at[m],
            ad_rs.at[m],
            dp=near(-dy, -dz),
        )

    def g_copy(n, which):
        dy = jnp.where(which == 0, -ahead, jnp.where(which == 1, ahead, 0))
        dz = jnp.where(which == 0, -ahead, jnp.where(which == 1, 0, ahead))
        return remote(
            g_s.at[n, which],
            g_r.at[n, which],
            g_ss.at[n, which],
            g_rs.at[n, which],
            dp=near(dy, dz),
        )

    def gradient(n, kind, row_ref):
        @pl.loop(0, 4)
        def _(which):
            i = jnp.where((which == 1) | (which == 3), odd, 1 - odd)
            j = jnp.where(which >= 2, odd, 1 - odd)
            turned = rank_rows(kind, i, j).astype(F32).T.astype(BF)
            value = mm(turned, served(row_ref, i, j)) * (1.0 / seq_len)
            if n == 1:
                value = value * factor_at(owner_of(i, j), width)
            g_own[n] = value
            g_s[n, which] = value.astype(BF)

            @pl.when(which < 3)
            def _():
                g_copy(n, which).start()

    sum_parts(0, None)
    for way in range(2):
        hop_copy(way).wait_recv()
        send_ring(way, way)
    gathered(1)
    gradient(0, 1, x_r)

    gathered(0)

    @pl.loop(0, 4)
    def _(q):
        i, j = q // 2, q % 2
        value = mm(rank_rows(0, i, j), fb[i, j]) * factor_at(owner_of(i, j), width)
        ad_s[i, j] = value.astype(BF).reshape(RING, 64, width)

    for m in range(len(MESSAGES)):
        ad_copy(m).start()
    ad_r[BOTH, BOTH] = ad_s[:, :, 0]

    gradient(1, 0, c_r)

    sib_copy(3).wait_recv()
    for m in range(len(MESSAGES)):
        ad_copy(m).wait_recv()

    @pl.loop(0, tiles)
    def _(n):
        at = span(n * TILE, TILE)
        back = ad_r[:, :, :, at].reshape(2 * rows, TILE)
        hold[2, :, at] = hold[2, :, at] + sib_r[3, :, at].astype(F32) + mm(slot_hot[...], back)

    for way in range(2):
        for part in range(2):
            ring_copy(way, part).wait_recv()

    for part in range(2):

        def put(at, to):
            out_v[at] = (
                hold[2, at] + ring_r[0, part, to].astype(F32) + ring_r[1, part, to].astype(F32)
            ).astype(BF)

        half_rows(part, put)
    stores = [pltpu.make_async_copy(out_v, out_ref, out_sem.at[2])]
    stores[0].start()

    for n, g_ref in ((0, ga_ref), (1, gb_ref)):

        @pl.loop(0, 3)
        def _(which):
            remote(
                g_s.at[n, which], g_r.at[n, which], g_ss.at[n, which], g_rs.at[n, which], dp=me
            ).wait_recv()

        @pl.loop(0, g_own.shape[1] // 32)
        def _(k):
            at = span(k * 32, 32)
            total = g_own[n, at]
            for which in range(3):
                total = total + g_r[n, which, at].astype(F32)
            g_own[n, at] = total

        stores.append(pltpu.make_async_copy(g_own.at[n], g_ref, out_sem.at[n]))
        stores[-1].start()

    @pl.loop(1, DP)
    def _(k):
        facts_copy(k).wait_send()
        tok_copy(0, k).wait_send()
        tok_copy(1, k).wait_send()

    for n in range(2):
        for axis in range(2):
            fac_copy(axis, n).wait_send()
        fac_relay(n).wait_send()
    for m in range(len(MESSAGES)):
        for h in range(2):
            x_copy(h, m).wait_send()
        c_copy(m).wait_send()
        ad_copy(m).wait_send()
    for j in (2, 3):
        sib_copy(j).wait_send()
    for way in range(2):
        hop_copy(way).wait_send()
        for part in range(2):
            ring_copy(way, part).wait_send()
    for kind in range(2):

        @pl.loop(1, TENSOR)
        def _(k):
            part_copy(kind, k).wait_send()
            gath_copy(kind, k).wait_send()

        @pl.loop(0, 3)
        def _(which):
            g_copy(kind, which).wait_send()

    for store in stores:
        store.wait()


def finish(out_ref, gb_ref, ga_ref, out_to, gb_to, ga_to, out_v, gb_v, ga_v, turned_v, sem):
    names = ((ga_ref, ga_v, turned_v, ga_to), (gb_ref, gb_v, gb_v, gb_to), (out_ref, out_v, out_v, out_to))
    loads = [pltpu.make_async_copy(src, held, sem.at[0, n]) for n, (src, held, _, _) in enumerate(names)]
    stores = [pltpu.make_async_copy(held, dst, sem.at[1, n]) for n, (_, _, held, dst) in enumerate(names)]
    for load in loads:
        load.start()
    loads[0].wait()
    turned_v[...] = ga_v[...].T
    stores[0].start()
    for n in (1, 2):
        loads[n].wait()
        stores[n].start()
    for store in stores:
        store.wait()


def on_device(
    tokens,
    destinations,
    counts,
    sequence_job_ids,
    job_owner_slot,
    rank_per_job,
    weight,
    input_factor_table,
    output_factor_table,
    cotangent,
):
    slot_count, seq_len, width = tokens.shape
    max_rank = input_factor_table.shape[2]
    rows = slot_count * seq_len
    anywhere = pl.BlockSpec(memory_space=pl.ANY)
    smem = pl.BlockSpec(memory_space=pltpu.SMEM)
    dma = pltpu.SemaphoreType.DMA
    served = (2, 2, RING, 64, width)
    lanes = (RING, RING, 64, width)
    out, ga, gb = pl.pallas_call(
        kernel,
        out_shape=(
            jax.ShapeDtypeStruct((rows, width), BF),
            jax.ShapeDtypeStruct((max_rank, width), F32),
            jax.ShapeDtypeStruct((max_rank, width), F32),
        ),
        in_specs=[smem] * 5 + [anywhere] * 5,
        out_specs=(anywhere,) * 3,
        scratch_shapes=[
            pltpu.VMEM(tokens.shape, BF),
            pltpu.VMEM((rows, width), BF),
            pltpu.VMEM(input_factor_table.shape, BF),
            pltpu.VMEM(output_factor_table.shape, BF),
            pltpu.VMEM((rows, width), BF),
            pltpu.VMEM((DP, seq_len, width), BF),
            pltpu.VMEM((DP, seq_len, width), BF),
            pltpu.VMEM((DP, 8, 128), jnp.int32),
            pltpu.VMEM((DP, 8, 128), jnp.int32),
            pltpu.VMEM((rows, rows), BF),
            pltpu.VMEM((2 * rows, rows), BF),
            pltpu.VMEM((2 * rows, rows), BF),
            pltpu.VMEM((rows, 2 * rows), BF),
            pltpu.VMEM((rows, width), BF),
            pltpu.VMEM(lanes, BF),
            pltpu.VMEM(served, BF),
            pltpu.VMEM(lanes, BF),
            pltpu.VMEM(served, BF),
            pltpu.VMEM((2, 2, width, max_rank), BF),
            pltpu.VMEM((2, 2, max_rank, width), BF),
            pltpu.VMEM((W_SLOTS, width, width), BF),
            pltpu.VMEM((2, rows, width), BF),
            pltpu.VMEM((4, rows, width), BF),
            pltpu.VMEM((3, rows, width), F32),
            pltpu.VMEM((2, rows // 2, width), BF),
            pltpu.VMEM((2, rows // 2, width), BF),
            pltpu.VMEM((2, 2, rows // 2, width), BF),
            pltpu.VMEM((2, 2, rows // 2, width), BF),
            pltpu.VMEM((2, TENSOR, 128, max_rank), BF),
            pltpu.VMEM((2, TENSOR, 128, max_rank), BF),
            pltpu.VMEM((2, TENSOR, 128, max_rank), BF),
            pltpu.VMEM(served, BF),
            pltpu.VMEM(lanes, BF),
            pltpu.VMEM((2, max_rank, width), F32),
            pltpu.VMEM((2, 4, max_rank, width), BF),
            pltpu.VMEM((2, 3, max_rank, width), BF),
            dma((4,)),
            dma((3,)),
            dma((W_SLOTS,)),
            dma((DP - 1,)),
            dma((DP - 1,)),
            dma((2, DP - 1)),
            dma((2, DP - 1)),
            dma((3, 2)),
            dma((2, 2, 2)),
            dma((8,)),
            dma((8,)),
            dma((2, 8)),
            dma((2, 8)),
            dma((2,)),
            dma((4,)),
            dma((2,)),
            dma((2,)),
            dma((2, 2)),
            dma((2, 2)),
            dma((2, TENSOR - 1)),
            dma((2, TENSOR - 1)),
            dma((2, TENSOR - 1)),
            dma((2, TENSOR - 1)),
            dma((8,)),
            dma((8,)),
            dma((2, 3)),
            dma((2, 3)),
        ],
        compiler_params=pltpu.CompilerParams(
            collective_id=0, has_side_effects=True, vmem_limit_bytes=59 * 2**20
        ),
    )(
        destinations,
        counts,
        sequence_job_ids,
        job_owner_slot,
        rank_per_job,
        tokens,
        cotangent.reshape(rows, width),
        input_factor_table,
        output_factor_table,
        weight,
    )
    out, gb, ga = pl.pallas_call(
        finish,
        out_shape=(
            jax.ShapeDtypeStruct((rows, width), BF),
            jax.ShapeDtypeStruct((max_rank, width), F32),
            jax.ShapeDtypeStruct((width, max_rank), F32),
        ),
        in_specs=[anywhere] * 3,
        out_specs=(anywhere,) * 3,
        scratch_shapes=[
            pltpu.VMEM((rows, width), BF),
            pltpu.VMEM((max_rank, width), F32),
            pltpu.VMEM((max_rank, width), F32),
            pltpu.VMEM((width, max_rank), F32),
            dma((2, 3)),
        ],
    )(out, gb, ga)
    return out.reshape(slot_count, seq_len, width), ga[None], gb[None]


def solution(mesh):
    in_specs = (
        P("dp", None, "tensor"),
        P("dp"),
        P("dp"),
        P("dp"),
        P(),
        P(),
        P("tensor", None),
        P("dp", "tensor", None),
        P("dp", None, "tensor"),
        P("dp", None, "tensor"),
    )
    out_specs = (P("dp", None, "tensor"), P("dp", "tensor", None), P("dp", None, "tensor"))
    return jax.shard_map(
        on_device, mesh=mesh, in_specs=in_specs, out_specs=out_specs, check_vma=False
    )
```

```python
import jax
import jax.numpy as jnp
from jax import lax
from jax.experimental import pallas as pl
from jax.experimental.pallas import tpu as pltpu
from jax.sharding import PartitionSpec as P

BF = jnp.bfloat16
F32 = jnp.float32
RING = 4
DP = RING * RING
TENSOR = 2 * RING
TILE = 256
W_SLOTS = 4
LANES = DP - 2
EARLY = 4


def mm(a, b):
    return jnp.dot(a, b, preferred_element_type=F32)


def kernel(
    dest_ref,
    count_ref,
    job_ref,
    owner_ref,
    rank_ref,
    tok_ref,
    cot_ref,
    a_ref,
    b_ref,
    w_ref,
    out_ref,
    ga_ref,
    gb_ref,
    tok_v,
    cot_v,
    a_v,
    b_v,
    out_v,
    tok_s,
    tok_r,
    facts_s,
    facts_r,
    place_hot,
    x_hot,
    c_hot,
    slot_hot,
    xs,
    x_s,
    x_r,
    c_s,
    c_r,
    fa,
    fb,
    wbuf,
    sib_s,
    sib_r,
    hold,
    hop_s,
    hop_r,
    ring_s,
    ring_r,
    part_s,
    part_r,
    ranks,
    ad_s,
    ad_r,
    g_own,
    g_s,
    g_r,
    in_sem,
    out_sem,
    w_sem,
    facts_ss,
    facts_rs,
    tok_ss,
    tok_rs,
    fac_ss,
    fac_rs,
    c_ss,
    c_rs,
    x_ss,
    x_rs,
    sib_ss,
    sib_rs,
    hop_ss,
    hop_rs,
    ring_ss,
    ring_rs,
    part_ss,
    part_rs,
    gath_ss,
    gath_rs,
    ad_ss,
    ad_rs,
    g_ss,
    g_rs,
):
    seq_len, width = tok_ref.shape[1:]
    rows = DP * seq_len
    half = rows // 2
    me = lax.axis_index("dp")
    t = lax.axis_index("tensor")
    y, z = me // RING, me % RING
    x, c = t // 2, t % 2
    odd = (y + z) % 2
    tiles = width // TILE
    wide_half = width // 2

    def remote(src, dst, send, recv, **where):
        return pltpu.make_async_remote_copy(
            src_ref=src,
            dst_ref=dst,
            send_sem=send,
            recv_sem=recv,
            device_id=where,
            device_id_type=pl.DeviceIdType.MESH,
        )

    def iota(shape, axis):
        return lax.broadcasted_iota(jnp.int32, shape, axis)

    def near(dy, dz):
        return (y + dy + RING) % RING * RING + (z + dz + RING) % RING

    partner = near(1 - odd, odd)
    first = near(-odd, odd - 1)
    local_lane = jnp.where(odd == 1, 3 * RING, 3)

    def owner_of(role):
        return jnp.where(role == 0, me, first)

    def lane_at(k):
        return k + jnp.where(k >= local_lane, 1, 0)

    def lane_server(lane):
        ry, rz = lane // RING, lane % RING
        kind = (y + ry + z + rz) % 2
        dy, dz = (RING - ry) % RING, (RING - rz) % RING
        along, across = jnp.where(kind == 0, dy, dz), jnp.where(kind == 0, dz, dy)
        role = (along + 1) // 2 % 2
        to = near(ry + jnp.where(kind == 0, role, 0), rz + jnp.where(kind == 0, 0, role))
        return to, role, along // 2 * RING + across

    def lane_source(role, slot):
        kind = jnp.where(role == 0, odd, 1 - odd)
        along, across = jnp.where(role == 0, 3 * (slot // RING), 1 + slot // RING), slot % RING
        dy, dz = jnp.where(kind == 0, along, across), jnp.where(kind == 0, across, along)
        fy = jnp.where(role == 0, 0, -odd)
        fz = jnp.where(role == 0, 0, odd - 1)
        return near(fy + dy, fz + dz), (RING - dy) % RING * RING + (RING - dz) % RING

    def rank_at(owner):
        total = jnp.int32(0)
        for j in range(DP):
            total = total + jnp.where(owner_ref[j] == owner, rank_ref[j], 0)
        return total

    def factor_at(owner, columns):
        return 32.0 / jnp.full((1, columns), rank_at(owner).astype(F32), F32)

    def span(start, size):
        return pl.ds(pl.multiple_of(start, size), size)

    loads = [
        pltpu.make_async_copy(src, dst, in_sem.at[n])
        for n, (src, dst) in enumerate(((tok_ref, tok_v), (a_ref, a_v), (b_ref, b_v), (cot_ref, cot_v)))
    ]
    for load in loads:
        load.start()

    barrier = pltpu.get_barrier_semaphore()

    @pl.loop(1, DP)
    def _(k):
        pl.semaphore_signal(
            barrier, inc=1, device_id={"dp": (me + k) % DP}, device_id_type=pl.DeviceIdType.MESH
        )

    @pl.loop(1, TENSOR)
    def _(k):
        pl.semaphore_signal(
            barrier, inc=1, device_id={"tensor": (t + k) % TENSOR}, device_id_type=pl.DeviceIdType.MESH
        )

    def w_copy(i):
        j = i // 2
        block = (x + jnp.where(j == 0, 2, jnp.where(j == 1, 1, jnp.where(j == 2, 3, 0)))) % RING * 2
        block = block + (c + 1 - i % 2) % 2
        return pltpu.make_async_copy(
            w_ref.at[:, span(block * width, width)], wbuf.at[i % W_SLOTS], w_sem.at[i % W_SLOTS]
        )

    for i in range(W_SLOTS):
        w_copy(jnp.int32(i)).start()

    loads[0].wait()

    @pl.loop(0, DP)
    def _(k):
        to = (me + k) % DP
        index = jnp.int32(0)
        for i in range(DP):
            index = jnp.where(lax.shift_right_logical(dest_ref[i], 4) == to, i, index)
        owner = owner_ref[job_ref[index]]
        oy, oz = lax.shift_right_logical(owner, 2), owner & 3
        base = (((oy + RING - to // RING) & 3) * RING + ((oz + RING - to % RING) & 3)) * 2
        row = iota((8, 128), 0)
        facts_s[k] = jnp.where(
            row == 0, dest_ref[index] & 15, jnp.where(row == 1, count_ref[index], base)
        )
        tok_s[k] = tok_v[index]

    tok_r[me] = tok_s[0]
    facts_r[me] = facts_s[0]

    pl.semaphore_wait(barrier, DP - 1 + TENSOR - 1)

    def facts_copy(k):
        return remote(
            facts_s.at[k], facts_r.at[me], facts_ss.at[k - 1], facts_rs.at[k - 1], dp=(me + k) % DP
        )

    def tok_copy(h, k):
        columns = span(h * wide_half, wide_half)
        return remote(
            tok_s.at[k, :, columns],
            tok_r.at[me, :, columns],
            tok_ss.at[h, k - 1],
            tok_rs.at[h, k - 1],
            dp=(me + k) % DP,
        )

    def fac_copy(n):
        table = (fa, fb)[n]
        return remote(table.at[0], table.at[1], fac_ss.at[n], fac_rs.at[n], dp=partner)

    @pl.loop(1, DP)
    def _(k):
        facts_copy(k).start()

    @pl.loop(0, 2)
    def _(h):
        @pl.loop(1, DP)
        def _(k):
            tok_copy(h, k).start()

    my_rank = rank_at(me)
    loads[1].wait()

    @pl.loop(0, width // 128)
    def _(n):
        at = span(n * 128, 128)
        kept = iota((128, a_v.shape[2]), 1) < my_rank
        fa[0, at, :] = jnp.where(kept, a_v[0, at, :].astype(F32), 0.0).astype(BF)

    fac_copy(0).start()
    loads[2].wait()

    @pl.loop(0, width // 128)
    def _(n):
        at = span(n * 128, 128)
        kept = iota((b_v.shape[1], 128), 0) < my_rank
        fb[0, :, at] = jnp.where(kept, b_v[0, :, at].astype(F32), 0.0).astype(BF)

    fac_copy(1).start()

    @pl.loop(1, DP)
    def _(k):
        facts_copy(k).wait_recv()

    slot_c = facts_r[:, 0, :].astype(F32)
    live_c = facts_r[:, 1, :].astype(F32)
    base_c = facts_r[:, 2, :].astype(F32)
    square = (DP, 128)
    diagonal = iota(square, 0) == iota(square, 1)
    slot_l = jnp.sum(jnp.where(diagonal, slot_c, 0.0), 0, keepdims=True)
    base_l = jnp.sum(jnp.where(diagonal, base_c, 0.0), 0, keepdims=True)
    earlier = (base_l == base_c) & (slot_l < slot_c) & (iota(square, 1) < DP)
    turn_c = jnp.sum(jnp.where(earlier, 1.0, 0.0), 1, keepdims=True)
    lane_c = base_c + turn_c
    lane_l = jnp.sum(jnp.where(diagonal, lane_c, 0.0), 0, keepdims=True)
    wide = (DP, rows)
    seq_of = iota(wide, 1) // seq_len
    slot_1, live_1, lane_1 = slot_c[:, :1], live_c[:, :1], lane_c[:, :1]
    in_slot = slot_1 == seq_of.astype(F32)
    in_order = iota(wide, 0) == seq_of
    position = (iota((1, rows), 1) % seq_len).astype(F32)

    def spread(where, value):
        return jnp.sum(jnp.where(where, value, 0.0), 0, keepdims=True)

    live = position < spread(in_order, live_1)
    c_row = spread(in_slot, lane_1) * seq_len + position
    x_row = jnp.where(live, spread(in_order, lane_1) * seq_len + position, -1.0)
    slot_row = jnp.where(live, spread(in_order, slot_1) * seq_len + position, -1.0)

    def build(hot, wanted):
        @pl.loop(0, hot.shape[0] // 64)
        def _(n):
            row = (iota((64, rows), 0) + n * 64).astype(F32)
            hot[span(n * 64, 64), :] = jnp.where(row == wanted, 1.0, 0.0).astype(BF)

    build(c_hot, c_row)

    lane_shape = (DP, 2 * seq_len)

    def x_copy(h, k):
        lane, columns = lane_at(k), span(h * wide_half, wide_half)
        to, role, slot = lane_server(lane)
        return remote(
            x_s.at[lane, :, columns],
            x_r.at[role, slot, :, columns],
            x_ss.at[h, k - 1],
            x_rs.at[h, role, slot],
            dp=to,
        )

    def c_copy(k):
        lane = lane_at(k)
        to, role, slot = lane_server(lane)
        return remote(c_s.at[lane], c_r.at[role, slot], c_ss.at[k - 1], c_rs.at[role, slot], dp=to)

    def x_wait(h, role, slot):
        columns = span(h * wide_half, wide_half)
        remote(
            x_s.at[0, :, columns],
            x_r.at[role, slot, :, columns],
            x_ss.at[h, 0],
            x_rs.at[h, role, slot],
            dp=me,
        ).wait_recv()

    def c_wait(role, slot):
        remote(c_s.at[0], c_r.at[role, slot], c_ss.at[0], c_rs.at[role, slot], dp=me).wait_recv()

    def every_slot(wait):
        @pl.loop(0, 2)
        def _(role):
            @pl.loop(1, 2 * RING)
            def _(slot):
                wait(role, slot)

    loads[3].wait()

    @pl.loop(0, tiles)
    def _(n):
        at = span(n * TILE, TILE)
        c_s[:, :, at] = mm(c_hot[...], cot_v[:, at]).astype(BF).reshape(lane_shape + (TILE,))

    @pl.loop(1, 1 + EARLY)
    def _(k):
        c_copy(k).start()

    build(x_hot, x_row)
    build(place_hot, slot_row)

    @pl.loop(0, rows // 64)
    def _(n):
        row = iota((64, 128), 0) + n * 64
        mine = jnp.where(slot_l == (row // seq_len).astype(F32), lane_l, 0.0)
        place = jnp.sum(mine, 1, keepdims=True) * seq_len + (row % seq_len).astype(F32)[:, :1]
        slot_hot[span(n * 64, 64), :] = jnp.where(
            iota((64, 2 * rows), 1).astype(F32) == place, 1.0, 0.0
        ).astype(BF)

    @pl.loop(0, 2)
    def _(h):
        @pl.loop(1, DP)
        def _(k):
            tok_copy(h, k).wait_recv()

        @pl.loop(0, tiles // 2)
        def _(n):
            at = span(h * wide_half + n * TILE, TILE)
            landed = tok_r[:, :, at].reshape(rows, TILE)
            x_s[:, :, at] = mm(x_hot[...], landed).astype(BF).reshape(lane_shape + (TILE,))

        @pl.loop(1, 1 + LANES)
        def _(k):
            x_copy(h, k).start()

        @pl.loop(0, tiles // 2)
        def _(n):
            at = span(h * wide_half + n * TILE, TILE)
            xs[:, at] = mm(place_hot[...], tok_r[:, :, at].reshape(rows, TILE)).astype(BF)

    @pl.loop(1 + EARLY, 1 + LANES)
    def _(k):
        c_copy(k).start()

    x_r[0, 0], x_r[1, 0] = x_s[0], x_s[local_lane]
    c_r[0, 0], c_r[1, 0] = c_s[0], c_s[local_lane]

    def sib_copy(j):
        return remote(
            sib_s.at[j % 2], sib_r.at[j], sib_ss.at[j % 2], sib_rs.at[j], tensor=x * 2 + (1 - c)
        )

    right, left = ((x + 1) % RING) * 2 + c, ((x + 3) % RING) * 2 + c

    def hop_copy(way):
        return remote(
            hop_s.at[way], hop_r.at[way], hop_ss.at[way], hop_rs.at[way], tensor=(right, left)[way]
        )

    def ring_copy(way, part):
        return remote(
            ring_s.at[way, part],
            ring_r.at[way, part],
            ring_ss.at[way, part],
            ring_rs.at[way, part],
            tensor=(right, left)[way],
        )

    def half_rows(part, put):
        @pl.loop(0, half // 32)
        def _(n):
            put(span(part * half + n * 32, 32), span(n * 32, 32))

    def send_hop(way):
        def put(at, to):
            hop_s[way, to] = (hold[0, at] + sib_r[0, at].astype(F32)).astype(BF)

        half_rows(way, put)
        hop_copy(way).start()

    def send_ring(way, part):
        def put(at, to):
            value = hold[1 - way, at] + sib_r[1 + way, at].astype(F32)
            if way == part:
                value = value + hop_r[way, to].astype(F32)
            ring_s[way, part, to] = value.astype(BF)

        half_rows(part, put)
        ring_copy(way, part).start()

    def part_copy(kind, k):
        to = (t + k) % TENSOR
        return remote(
            part_s.at[kind, to],
            part_r.at[kind, k],
            part_ss.at[kind, k - 1],
            part_rs.at[kind, k - 1],
            tensor=to,
        )

    def gath_copy(kind, k):
        to = (t + k) % TENSOR
        held = ranks.at[kind, t]
        return remote(held, held, gath_ss.at[kind, k - 1], gath_rs.at[kind, k - 1], tensor=to)

    def served(ref, role):
        return ref[role].reshape(rows, width)

    def send_parts(kind, make):
        @pl.loop(0, 2)
        def _(role):
            value = make(role).astype(BF).reshape(4, 128, ranks.shape[3])
            part_s[kind, pl.ds(role * 4, 4)] = value

        @pl.loop(1, TENSOR)
        def _(k):
            part_copy(kind, k).start()

        part_r[kind, 0] = part_s[kind, t]

    def sum_parts(kind, scale):
        @pl.loop(1, TENSOR)
        def _(k):
            part_copy(kind, k).wait_recv()

        total = part_r[kind, 0].astype(F32)
        for k in range(1, TENSOR):
            total = total + part_r[kind, k].astype(F32)
        ranks[kind, t] = (total if scale is None else total * scale).astype(BF)

        @pl.loop(1, TENSOR)
        def _(k):
            gath_copy(kind, k).start()

    def gathered(kind):
        @pl.loop(1, TENSOR)
        def _(k):
            held = ranks.at[kind, (t + TENSOR - k) % TENSOR]
            remote(held, held, gath_ss.at[kind, k - 1], gath_rs.at[kind, k - 1], tensor=t).wait_recv()

    def rank_rows(kind, role):
        return ranks[kind, pl.ds(role * 4, 4)].reshape(rows, ranks.shape[3])

    @pl.loop(0, 4)
    def _(j):
        w_copy(2 * j).wait()

        @pl.when(j >= 2)
        def _():
            sib_copy(j - 2).wait_send()

        @pl.loop(0, tiles)
        def _(n):
            at = span(n * TILE, TILE)
            sib_s[j % 2, :, at] = mm(xs[...], wbuf[(2 * j) % W_SLOTS, :, at]).astype(BF)

        sib_copy(j).start()

        @pl.when(2 * j + W_SLOTS < 8)
        def _():
            w_copy(2 * j + W_SLOTS).start()

        @pl.when(j == 1)
        def _():
            sib_copy(0).wait_recv()
            send_hop(0)
            send_hop(1)

        @pl.when(j == 3)
        def _():
            sib_copy(2).wait_recv()
            send_ring(1, 0)

        w_copy(2 * j + 1).wait()

        @pl.loop(0, tiles)
        def _(n):
            at = span(n * TILE, TILE)
            hold[jnp.where(j == 3, 2, j % 2), :, at] = mm(xs[...], wbuf[(2 * j + 1) % W_SLOTS, :, at])

        @pl.when(2 * j + 1 + W_SLOTS < 8)
        def _():
            w_copy(2 * j + 1 + W_SLOTS).start()

        @pl.when(j == 1)
        def _():
            fac_copy(0).wait_recv()
            every_slot(lambda role, slot: x_wait(0, role, slot))
            every_slot(lambda role, slot: x_wait(1, role, slot))
            send_parts(0, lambda role: mm(served(x_r, role), fa[role]))

        @pl.when(j == 2)
        def _():
            sum_parts(0, None)
            sib_copy(1).wait_recv()
            send_ring(0, 1)

    def ad_copy(role, slot):
        to, lane = lane_source(role, slot)
        return remote(
            ad_s.at[role, slot], ad_r.at[lane], ad_ss.at[role, slot], ad_rs.at[lane], dp=to
        )

    fac_copy(1).wait_recv()
    gathered(0)

    @pl.loop(0, 2)
    def _(role):
        factor = factor_at(owner_of(role), TILE)

        @pl.loop(0, tiles)
        def _(n):
            at = span(n * TILE, TILE)
            value = mm(rank_rows(0, role), fb[role, :, at]) * factor
            ad_s[role, :, :, at] = value.astype(BF).reshape(2 * RING, 64, TILE)

    every_slot(lambda role, slot: ad_copy(role, slot).start())
    ad_r[0], ad_r[local_lane] = ad_s[0, 0], ad_s[1, 0]

    every_slot(c_wait)
    send_parts(
        1,
        lambda role: lax.dot_general(
            served(c_r, role), fb[role], (((1,), (1,)), ((), ())), preferred_element_type=F32
        ),
    )

    def g_copy(n):
        return remote(g_s.at[n], g_r.at[n], g_ss.at[n], g_rs.at[n], dp=first)

    def gradient(n, kind, row_ref):
        for role in (1, 0):
            turned = rank_rows(kind, role).astype(F32).T.astype(BF)
            value = mm(turned, served(row_ref, role)) * (1.0 / seq_len)
            if n == 1:
                value = value * factor_at(owner_of(role), width)
            if role == 1:
                g_s[n] = value.astype(BF)
                g_copy(n).start()
            else:
                g_own[n] = value

    gradient(1, 0, c_r)

    sum_parts(1, factor_at(owner_of(t // 4), ranks.shape[3]))
    for way in range(2):
        hop_copy(way).wait_recv()
        send_ring(way, way)
    gathered(1)
    gradient(0, 1, x_r)

    sib_copy(3).wait_recv()

    @pl.loop(1, 1 + LANES)
    def _(k):
        lane = lane_at(k)
        remote(ad_s.at[0, 0], ad_r.at[lane], ad_ss.at[0, 0], ad_rs.at[lane], dp=me).wait_recv()

    @pl.loop(0, tiles)
    def _(n):
        at = span(n * TILE, TILE)
        back = ad_r[:, :, at].reshape(2 * rows, TILE)
        hold[2, :, at] = hold[2, :, at] + sib_r[3, :, at].astype(F32) + mm(slot_hot[...], back)

    for way in range(2):
        for part in range(2):
            ring_copy(way, part).wait_recv()

    for part in range(2):

        def put(at, to):
            out_v[at] = (
                hold[2, at] + ring_r[0, part, to].astype(F32) + ring_r[1, part, to].astype(F32)
            ).astype(BF)

        half_rows(part, put)
    stores = [pltpu.make_async_copy(out_v, out_ref, out_sem.at[2])]
    stores[0].start()

    for n, g_ref in ((1, gb_ref), (0, ga_ref)):

        g_copy(n).wait_recv()

        @pl.loop(0, g_own.shape[1] // 32)
        def _(k):
            at = span(k * 32, 32)
            g_own[n, at] = g_own[n, at] + g_r[n, at].astype(F32)

        stores.append(pltpu.make_async_copy(g_own.at[n], g_ref, out_sem.at[n]))
        stores[-1].start()

    @pl.loop(1, DP)
    def _(k):
        facts_copy(k).wait_send()
        tok_copy(0, k).wait_send()
        tok_copy(1, k).wait_send()

    @pl.loop(1, 1 + LANES)
    def _(k):
        x_copy(0, k).wait_send()
        x_copy(1, k).wait_send()
        c_copy(k).wait_send()

    every_slot(lambda role, slot: ad_copy(role, slot).wait_send())
    for n in range(2):
        fac_copy(n).wait_send()
        g_copy(n).wait_send()
    for j in (2, 3):
        sib_copy(j).wait_send()
    for way in range(2):
        hop_copy(way).wait_send()
        for part in range(2):
            ring_copy(way, part).wait_send()
    for kind in range(2):

        @pl.loop(1, TENSOR)
        def _(k):
            part_copy(kind, k).wait_send()
            gath_copy(kind, k).wait_send()

    for store in stores:
        store.wait()


def finish(out_ref, gb_ref, ga_ref, out_to, gb_to, ga_to, out_v, gb_v, ga_v, turned_v, sem):
    names = ((ga_ref, ga_v, turned_v, ga_to), (gb_ref, gb_v, gb_v, gb_to), (out_ref, out_v, out_v, out_to))
    loads = [pltpu.make_async_copy(src, held, sem.at[0, n]) for n, (src, held, _, _) in enumerate(names)]
    stores = [pltpu.make_async_copy(held, dst, sem.at[1, n]) for n, (_, _, held, dst) in enumerate(names)]
    for load in loads:
        load.start()
    loads[0].wait()
    turned_v[...] = ga_v[...].T
    stores[0].start()
    for n in (1, 2):
        loads[n].wait()
        stores[n].start()
    for store in stores:
        store.wait()


def on_device(
    tokens,
    destinations,
    counts,
    sequence_job_ids,
    job_owner_slot,
    rank_per_job,
    weight,
    input_factor_table,
    output_factor_table,
    cotangent,
):
    slot_count, seq_len, width = tokens.shape
    max_rank = input_factor_table.shape[2]
    rows = slot_count * seq_len
    anywhere = pl.BlockSpec(memory_space=pl.ANY)
    smem = pl.BlockSpec(memory_space=pltpu.SMEM)
    dma = pltpu.SemaphoreType.DMA
    served = (2, 2 * RING, 2 * seq_len, width)
    lanes = (DP, 2 * seq_len, width)
    out, ga, gb = pl.pallas_call(
        kernel,
        out_shape=(
            jax.ShapeDtypeStruct((rows, width), BF),
            jax.ShapeDtypeStruct((max_rank, width), F32),
            jax.ShapeDtypeStruct((max_rank, width), F32),
        ),
        in_specs=[smem] * 5 + [anywhere] * 5,
        out_specs=(anywhere,) * 3,
        scratch_shapes=[
            pltpu.VMEM(tokens.shape, BF),
            pltpu.VMEM((rows, width), BF),
            pltpu.VMEM(input_factor_table.shape, BF),
            pltpu.VMEM(output_factor_table.shape, BF),
            pltpu.VMEM((rows, width), BF),
            pltpu.VMEM((DP, seq_len, width), BF),
            pltpu.VMEM((DP, seq_len, width), BF),
            pltpu.VMEM((DP, 8, 128), jnp.int32),
            pltpu.VMEM((DP, 8, 128), jnp.int32),
            pltpu.VMEM((rows, rows), BF),
            pltpu.VMEM((2 * rows, rows), BF),
            pltpu.VMEM((2 * rows, rows), BF),
            pltpu.VMEM((rows, 2 * rows), BF),
            pltpu.VMEM((rows, width), BF),
            pltpu.VMEM(lanes, BF),
            pltpu.VMEM(served, BF),
            pltpu.VMEM(lanes, BF),
            pltpu.VMEM(served, BF),
            pltpu.VMEM((2, width, max_rank), BF),
            pltpu.VMEM((2, max_rank, width), BF),
            pltpu.VMEM((W_SLOTS, width, width), BF),
            pltpu.VMEM((2, rows, width), BF),
            pltpu.VMEM((4, rows, width), BF),
            pltpu.VMEM((3, rows, width), F32),
            pltpu.VMEM((2, rows // 2, width), BF),
            pltpu.VMEM((2, rows // 2, width), BF),
            pltpu.VMEM((2, 2, rows // 2, width), BF),
            pltpu.VMEM((2, 2, rows // 2, width), BF),
            pltpu.VMEM((2, TENSOR, 128, max_rank), BF),
            pltpu.VMEM((2, TENSOR, 128, max_rank), BF),
            pltpu.VMEM((2, TENSOR, 128, max_rank), BF),
            pltpu.VMEM(served, BF),
            pltpu.VMEM(lanes, BF),
            pltpu.VMEM((2, max_rank, width), F32),
            pltpu.VMEM((2, max_rank, width), BF),
            pltpu.VMEM((2, max_rank, width), BF),
            dma((4,)),
            dma((3,)),
            dma((W_SLOTS,)),
            dma((DP - 1,)),
            dma((DP - 1,)),
            dma((2, DP - 1)),
            dma((2, DP - 1)),
            dma((2,)),
            dma((2,)),
            dma((LANES,)),
            dma((2, 2 * RING)),
            dma((2, LANES)),
            dma((2, 2, 2 * RING)),
            dma((2,)),
            dma((4,)),
            dma((2,)),
            dma((2,)),
            dma((2, 2)),
            dma((2, 2)),
            dma((2, TENSOR - 1)),
            dma((2, TENSOR - 1)),
            dma((2, TENSOR - 1)),
            dma((2, TENSOR - 1)),
            dma((2, 2 * RING)),
            dma((DP,)),
            dma((2,)),
            dma((2,)),
        ],
        compiler_params=pltpu.CompilerParams(
            collective_id=0, has_side_effects=True, vmem_limit_bytes=58 * 2**20
        ),
    )(
        destinations,
        counts,
        sequence_job_ids,
        job_owner_slot,
        rank_per_job,
        tokens,
        cotangent.reshape(rows, width),
        input_factor_table,
        output_factor_table,
        weight,
    )
    out, gb, ga = pl.pallas_call(
        finish,
        out_shape=(
            jax.ShapeDtypeStruct((rows, width), BF),
            jax.ShapeDtypeStruct((max_rank, width), F32),
            jax.ShapeDtypeStruct((width, max_rank), F32),
        ),
        in_specs=[anywhere] * 3,
        out_specs=(anywhere,) * 3,
        scratch_shapes=[
            pltpu.VMEM((rows, width), BF),
            pltpu.VMEM((max_rank, width), F32),
            pltpu.VMEM((max_rank, width), F32),
            pltpu.VMEM((width, max_rank), F32),
            dma((2, 3)),
        ],
    )(out, gb, ga)
    return out.reshape(slot_count, seq_len, width), ga[None], gb[None]


def solution(mesh):
    in_specs = (
        P("dp", None, "tensor"),
        P("dp"),
        P("dp"),
        P("dp"),
        P(),
        P(),
        P("tensor", None),
        P("dp", "tensor", None),
        P("dp", None, "tensor"),
        P("dp", None, "tensor"),
    )
    out_specs = (P("dp", None, "tensor"), P("dp", "tensor", None), P("dp", None, "tensor"))
    return jax.shard_map(
        on_device, mesh=mesh, in_specs=in_specs, out_specs=out_specs, check_vma=False
    )
```

```python
import jax
import jax.numpy as jnp
from jax import lax
from jax.experimental import pallas as pl
from jax.experimental.pallas import tpu as pltpu
from jax.sharding import PartitionSpec as P

BF = jnp.bfloat16
F32 = jnp.float32
RING = 4
DP = RING * RING
TENSOR = 2 * RING
TILE = 256
W_SLOTS = 4
MOVE, PLACE = (0, 0, -1, 1), (0, 1, 1, 0)
BOTH = slice(0, 2)
MESSAGES = ((2, 2), (2, 3), (3, 2), (3, 3), (2, BOTH), (3, BOTH), (BOTH, 2), (BOTH, 3))


def mm(a, b):
    return jnp.dot(a, b, preferred_element_type=F32)


def kernel(
    dest_ref,
    count_ref,
    job_ref,
    owner_ref,
    rank_ref,
    tok_ref,
    cot_ref,
    a_ref,
    b_ref,
    w_ref,
    out_ref,
    ga_ref,
    gb_ref,
    tok_v,
    cot_v,
    a_v,
    b_v,
    out_v,
    tok_s,
    tok_r,
    facts_s,
    facts_r,
    place_hot,
    x_hot,
    c_hot,
    slot_hot,
    xs,
    x_s,
    x_r,
    c_s,
    c_r,
    fa,
    fb,
    wbuf,
    sib_s,
    sib_r,
    hold,
    hop_s,
    hop_r,
    ring_s,
    ring_r,
    part_s,
    part_r,
    ranks,
    ad_s,
    ad_r,
    g_own,
    g_s,
    g_r,
    in_sem,
    out_sem,
    w_sem,
    facts_ss,
    facts_rs,
    tok_ss,
    tok_rs,
    fac_ss,
    fac_rs,
    c_ss,
    c_rs,
    x_ss,
    x_rs,
    sib_ss,
    sib_rs,
    hop_ss,
    hop_rs,
    ring_ss,
    ring_rs,
    part_ss,
    part_rs,
    gath_ss,
    gath_rs,
    ad_ss,
    ad_rs,
    g_ss,
    g_rs,
):
    seq_len, width = tok_ref.shape[1:]
    rows = DP * seq_len
    half = rows // 2
    me = lax.axis_index("dp")
    t = lax.axis_index("tensor")
    y, z = me // RING, me % RING
    x, c = t // 2, t % 2
    odd = (y + z) % 2
    ahead = 1 - 2 * odd
    others = ((1 - odd, 1 - odd), (odd, 1 - odd), (1 - odd, odd))
    tiles = width // TILE

    def remote(src, dst, send, recv, **where):
        return pltpu.make_async_remote_copy(
            src_ref=src,
            dst_ref=dst,
            send_sem=send,
            recv_sem=recv,
            device_id=where,
            device_id_type=pl.DeviceIdType.MESH,
        )

    def iota(shape, axis):
        return lax.broadcasted_iota(jnp.int32, shape, axis)

    def near(dy, dz):
        return (y + dy + RING) % RING * RING + (z + dz + RING) % RING

    def owner_of(i, j):
        first, second = (y - i + RING) % RING, (z - j + RING) % RING
        shift = (first + second) % 2
        return (first + shift) % RING * RING + (second + shift) % RING

    def rank_at(owner):
        total = jnp.int32(0)
        for j in range(DP):
            total = total + jnp.where(owner_ref[j] == owner, rank_ref[j], 0)
        return total

    def factor_at(owner, columns):
        return 32.0 / jnp.full((1, columns), rank_at(owner).astype(F32), F32)

    def span(start, size):
        return pl.ds(pl.multiple_of(start, size), size)

    loads = [
        pltpu.make_async_copy(src, dst, in_sem.at[n])
        for n, (src, dst) in enumerate(((tok_ref, tok_v), (a_ref, a_v), (b_ref, b_v), (cot_ref, cot_v)))
    ]
    for load in loads:
        load.start()

    barrier = pltpu.get_barrier_semaphore()

    @pl.loop(1, DP)
    def _(k):
        pl.semaphore_signal(
            barrier, inc=1, device_id={"dp": (me + k) % DP}, device_id_type=pl.DeviceIdType.MESH
        )

    @pl.loop(1, TENSOR)
    def _(k):
        pl.semaphore_signal(
            barrier, inc=1, device_id={"tensor": (t + k) % TENSOR}, device_id_type=pl.DeviceIdType.MESH
        )

    def w_copy(i):
        j = i // 2
        block = (x + jnp.where(j == 0, 2, jnp.where(j == 1, 1, jnp.where(j == 2, 3, 0)))) % RING * 2
        block = block + (c + 1 - i % 2) % 2
        return pltpu.make_async_copy(
            w_ref.at[:, span(block * width, width)], wbuf.at[i % W_SLOTS], w_sem.at[i % W_SLOTS]
        )

    for i in range(W_SLOTS):
        w_copy(jnp.int32(i)).start()

    def chosen(to):
        index = jnp.int32(0)
        for i in range(DP):
            index = jnp.where(lax.shift_right_logical(dest_ref[i], 4) == to, i, index)
        return index

    loads[0].wait()

    @pl.loop(0, DP)
    def _(k):
        tok_s[k] = tok_v[chosen((me + k) % DP)]

    tok_r[me] = tok_s[0]

    pl.semaphore_wait(barrier, DP - 1 + TENSOR - 1)

    def facts_copy(k):
        return remote(
            facts_s.at[k], facts_r.at[me], facts_ss.at[k - 1], facts_rs.at[k - 1], dp=(me + k) % DP
        )

    def tok_copy(k):
        return remote(
            tok_s.at[k], tok_r.at[me], tok_ss.at[k - 1], tok_rs.at[k - 1], dp=(me + k) % DP
        )

    def fac_copy(axis, n):
        table = (fa, fb)[n]
        there = ((1 - odd, odd), (odd, 1 - odd))[axis]
        to = (near(ahead, 0), near(0, ahead))[axis]
        return remote(
            table.at[odd, odd], table.at[there], fac_ss.at[axis, n], fac_rs.at[there + (n,)], dp=to
        )

    def fac_wait(n, which):
        for there in which:
            held = (fa, fb)[n].at[there]
            remote(held, held, fac_ss.at[0, n], fac_rs.at[there + (n,)], dp=me).wait_recv()

    def fac_relay(n):
        table = (fa, fb)[n]
        here = ((odd, 1 - odd), (1 - odd, odd))[n]
        to = (near(0, -ahead), near(-ahead, 0))[n]
        return remote(table.at[here], table.at[odd, odd], fac_ss.at[2, n], fac_rs.at[odd, odd, n], dp=to)

    @pl.loop(1, DP)
    def _(k):
        tok_copy(k).start()

    @pl.loop(0, DP)
    def _(k):
        to = (me + k) % DP
        index = chosen(to)
        owner = owner_ref[job_ref[index]]
        oy, oz = lax.shift_right_logical(owner, 2), owner & 3
        shift = (oy + oz) & 1
        dy, dz = (to // RING + RING - oy + shift) & 3, (to % RING + RING - oz + shift) & 3
        base = (dy * RING + dz) * 2
        row = iota((8, 128), 0)
        facts_s[k] = jnp.where(
            row == 0, dest_ref[index] & 15, jnp.where(row == 1, count_ref[index], base)
        )

    facts_r[me] = facts_s[0]

    @pl.loop(1, DP)
    def _(k):
        facts_copy(k).start()

    my_rank = rank_at(me)
    loads[1].wait()

    @pl.loop(0, width // 128)
    def _(n):
        at = span(n * 128, 128)
        kept = iota((128, a_v.shape[2]), 1) < my_rank
        fa[odd, odd, at, :] = jnp.where(kept, a_v[0, at, :].astype(F32), 0.0).astype(BF)

    for axis in range(2):
        fac_copy(axis, 0).start()
    loads[2].wait()

    @pl.loop(0, width // 128)
    def _(n):
        at = span(n * 128, 128)
        kept = iota((b_v.shape[1], 128), 0) < my_rank
        fb[odd, odd, :, at] = jnp.where(kept, b_v[0, :, at].astype(F32), 0.0).astype(BF)

    @pl.loop(1, DP)
    def _(k):
        facts_copy(k).wait_recv()

    slot_c = facts_r[:, 0, :].astype(F32)
    live_c = facts_r[:, 1, :].astype(F32)
    base_c = facts_r[:, 2, :].astype(F32)
    square = (DP, 128)
    diagonal = iota(square, 0) == iota(square, 1)
    slot_l = jnp.sum(jnp.where(diagonal, slot_c, 0.0), 0, keepdims=True)
    base_l = jnp.sum(jnp.where(diagonal, base_c, 0.0), 0, keepdims=True)
    earlier = (base_l == base_c) & (slot_l < slot_c) & (iota(square, 1) < DP)
    turn_c = jnp.sum(jnp.where(earlier, 1.0, 0.0), 1, keepdims=True)
    lane_c = base_c + turn_c
    lane_l = jnp.sum(jnp.where(diagonal, lane_c, 0.0), 0, keepdims=True)
    wide = (DP, rows)
    seq_of = iota(wide, 1) // seq_len
    slot_1, live_1, lane_1 = slot_c[:, :1], live_c[:, :1], lane_c[:, :1]
    in_slot = slot_1 == seq_of.astype(F32)
    in_order = iota(wide, 0) == seq_of
    position = (iota((1, rows), 1) % seq_len).astype(F32)

    def spread(where, value):
        return jnp.sum(jnp.where(where, value, 0.0), 0, keepdims=True)

    live = position < spread(in_order, live_1)
    c_row = spread(in_slot, lane_1) * seq_len + position
    x_row = jnp.where(live, spread(in_order, lane_1) * seq_len + position, -1.0)
    slot_row = jnp.where(live, spread(in_order, slot_1) * seq_len + position, -1.0)

    def build(hot, wanted):
        @pl.loop(0, hot.shape[0] // 64)
        def _(n):
            row = (iota((64, rows), 0) + n * 64).astype(F32)
            hot[span(n * 64, 64), :] = jnp.where(row == wanted, 1.0, 0.0).astype(BF)

    build(c_hot, c_row)

    lane_shape = (RING, RING, 2 * seq_len)

    def lane_place(dy, dz):
        row = PLACE[dy] if dy != BOTH else BOTH
        column = PLACE[dz] if dz != BOTH else BOTH
        return row, column, (dy != BOTH) * 2 + (dz != BOTH)

    def lane_move(dy, dz):
        return (MOVE[dy] if dy != BOTH else 0, MOVE[dz] if dz != BOTH else 0)

    def lane_copy(send, recv, send_sem, recv_sem, m):
        message = MESSAGES[m]
        return remote(
            send.at[message],
            recv.at[lane_place(*message)],
            send_sem.at[m],
            recv_sem.at[m],
            dp=near(*lane_move(*message)),
        )

    def x_copy(m):
        return lane_copy(x_s, x_r, x_ss, x_rs, m)

    def c_copy(m):
        return lane_copy(c_s, c_r, c_ss, c_rs, m)

    loads[3].wait()

    @pl.loop(0, tiles)
    def _(n):
        at = span(n * TILE, TILE)
        c_s[:, :, :, at] = mm(c_hot[...], cot_v[:, at]).astype(BF).reshape(lane_shape + (TILE,))

    for m in range(4):
        c_copy(m).start()
    build(x_hot, x_row)
    build(place_hot, slot_row)

    @pl.loop(0, rows // 64)
    def _(n):
        row = iota((64, 128), 0) + n * 64
        mine = jnp.where(slot_l == (row // seq_len).astype(F32), lane_l, 0.0)
        place = jnp.sum(mine, 1, keepdims=True) * seq_len + (row % seq_len).astype(F32)[:, :1]
        slot_hot[span(n * 64, 64), :] = jnp.where(
            iota((64, 2 * rows), 1).astype(F32) == place, 1.0, 0.0
        ).astype(BF)

    @pl.loop(1, DP)
    def _(k):
        tok_copy(k).wait_recv()

    @pl.loop(0, tiles)
    def _(n):
        at = span(n * TILE, TILE)
        landed = tok_r[:, :, at].reshape(rows, TILE)
        x_s[:, :, :, at] = mm(x_hot[...], landed).astype(BF).reshape(lane_shape + (TILE,))

    for m in range(len(MESSAGES)):
        x_copy(m).start()

    @pl.loop(0, tiles)
    def _(n):
        at = span(n * TILE, TILE)
        xs[:, at] = mm(place_hot[...], tok_r[:, :, at].reshape(rows, TILE)).astype(BF)

    for axis in range(2):
        fac_copy(axis, 1).start()
    for m in range(4, len(MESSAGES)):
        c_copy(m).start()
    x_r[:, :, 0] = x_s[BOTH, BOTH]
    c_r[:, :, 0] = c_s[BOTH, BOTH]

    def sib_copy(j):
        return remote(
            sib_s.at[j % 2], sib_r.at[j], sib_ss.at[j % 2], sib_rs.at[j], tensor=x * 2 + (1 - c)
        )

    right, left = ((x + 1) % RING) * 2 + c, ((x + 3) % RING) * 2 + c

    def hop_copy(way):
        return remote(
            hop_s.at[way], hop_r.at[way], hop_ss.at[way], hop_rs.at[way], tensor=(right, left)[way]
        )

    def ring_copy(way, part):
        return remote(
            ring_s.at[way, part],
            ring_r.at[way, part],
            ring_ss.at[way, part],
            ring_rs.at[way, part],
            tensor=(right, left)[way],
        )

    def half_rows(part, put):
        @pl.loop(0, half // 32)
        def _(n):
            put(span(part * half + n * 32, 32), span(n * 32, 32))

    def send_hop(way):
        def put(at, to):
            hop_s[way, to] = (hold[0, at] + sib_r[0, at].astype(F32)).astype(BF)

        half_rows(way, put)
        hop_copy(way).start()

    def send_ring(way, part):
        def put(at, to):
            value = hold[1 - way, at] + sib_r[1 + way, at].astype(F32)
            if way == part:
                value = value + hop_r[way, to].astype(F32)
            ring_s[way, part, to] = value.astype(BF)

        half_rows(part, put)
        ring_copy(way, part).start()

    def part_copy(kind, k):
        to = (t + k) % TENSOR
        return remote(
            part_s.at[kind, to],
            part_r.at[kind, k],
            part_ss.at[kind, k - 1],
            part_rs.at[kind, k - 1],
            tensor=to,
        )

    def gath_copy(kind, k):
        to = (t + k) % TENSOR
        held = ranks.at[kind, t]
        return remote(held, held, gath_ss.at[kind, k - 1], gath_rs.at[kind, k - 1], tensor=to)

    def served(ref, i, j):
        return ref[i, j].reshape(RING * 64, width)

    def send_parts(kind, make):
        @pl.loop(0, 4)
        def _(q):
            value = make(q // 2, q % 2).astype(BF)
            part_s[kind, 2 * q] = value[:128]
            part_s[kind, 2 * q + 1] = value[128:]

        @pl.loop(1, TENSOR)
        def _(k):
            part_copy(kind, k).start()

        part_r[kind, 0] = part_s[kind, t]

    def sum_parts(kind, scale):
        @pl.loop(1, TENSOR)
        def _(k):
            part_copy(kind, k).wait_recv()

        total = part_r[kind, 0].astype(F32)
        for k in range(1, TENSOR):
            total = total + part_r[kind, k].astype(F32)
        ranks[kind, t] = (total if scale is None else total * scale).astype(BF)

        @pl.loop(1, TENSOR)
        def _(k):
            gath_copy(kind, k).start()

    def gathered(kind):
        @pl.loop(1, TENSOR)
        def _(k):
            held = ranks.at[kind, (t + TENSOR - k) % TENSOR]
            remote(held, held, gath_ss.at[kind, k - 1], gath_rs.at[kind, k - 1], tensor=t).wait_recv()

    def rank_rows(kind, i, j):
        return ranks[kind, pl.ds(i * 4 + j * 2, 2)].reshape(RING * 64, ranks.shape[3])

    @pl.loop(0, 4)
    def _(j):
        w_copy(2 * j).wait()

        @pl.when(j >= 2)
        def _():
            sib_copy(j - 2).wait_send()

        @pl.loop(0, tiles)
        def _(n):
            at = span(n * TILE, TILE)
            sib_s[j % 2, :, at] = mm(xs[...], wbuf[(2 * j) % W_SLOTS, :, at]).astype(BF)

        sib_copy(j).start()

        @pl.when(2 * j + W_SLOTS < 8)
        def _():
            w_copy(2 * j + W_SLOTS).start()

        @pl.when(j == 1)
        def _():
            sib_copy(0).wait_recv()
            send_hop(0)
            send_hop(1)
            fac_wait(0, others[1:])
            fac_relay(0).start()

        @pl.when(j == 3)
        def _():
            sib_copy(2).wait_recv()
            send_ring(1, 0)

        w_copy(2 * j + 1).wait()

        @pl.loop(0, tiles)
        def _(n):
            at = span(n * TILE, TILE)
            hold[jnp.where(j == 3, 2, j % 2), :, at] = mm(xs[...], wbuf[(2 * j + 1) % W_SLOTS, :, at])

        @pl.when(2 * j + 1 + W_SLOTS < 8)
        def _():
            w_copy(2 * j + 1 + W_SLOTS).start()

        @pl.when(j == 1)
        def _():
            fac_wait(0, others[:1])

            for m in range(len(MESSAGES)):
                x_copy(m).wait_recv()
            send_parts(0, lambda i, k: mm(served(x_r, i, k), fa[i, k]))

        @pl.when(j == 2)
        def _():
            fac_wait(1, others[1:])
            fac_relay(1).start()
            sum_parts(0, None)
            sib_copy(1).wait_recv()
            send_ring(0, 1)

    def ad_copy(m):
        message = MESSAGES[m]
        dy, dz = lane_move(*message)
        return remote(
            ad_s.at[lane_place(*message)],
            ad_r.at[message],
            ad_ss.at[m],
            ad_rs.at[m],
            dp=near(-dy, -dz),
        )

    fac_wait(1, others[:1])
    gathered(0)

    @pl.loop(0, 4)
    def _(q):
        i, j = q // 2, q % 2
        value = mm(rank_rows(0, i, j), fb[i, j]) * factor_at(owner_of(i, j), width)
        ad_s[i, j] = value.astype(BF).reshape(RING, 64, width)

    for m in range(len(MESSAGES)):
        ad_copy(m).start()
    ad_r[BOTH, BOTH] = ad_s[:, :, 0]

    for m in range(len(MESSAGES)):
        c_copy(m).wait_recv()
    send_parts(
        1,
        lambda i, j: lax.dot_general(
            served(c_r, i, j), fb[i, j], (((1,), (1,)), ((), ())), preferred_element_type=F32
        ),
    )

    def g_copy(n, which):
        dy = jnp.where(which == 0, -ahead, jnp.where(which == 1, ahead, 0))
        dz = jnp.where(which == 0, -ahead, jnp.where(which == 1, 0, ahead))
        return remote(
            g_s.at[n, which],
            g_r.at[n, which],
            g_ss.at[n, which],
            g_rs.at[n, which],
            dp=near(dy, dz),
        )

    def gradient(n, kind, row_ref):
        @pl.loop(0, 4)
        def _(which):
            i = jnp.where((which == 1) | (which == 3), odd, 1 - odd)
            j = jnp.where(which >= 2, odd, 1 - odd)
            turned = rank_rows(kind, i, j).astype(F32).T.astype(BF)
            value = mm(turned, served(row_ref, i, j)) * (1.0 / seq_len)
            if n == 1:
                value = value * factor_at(owner_of(i, j), width)
            g_own[n] = value
            g_s[n, which] = value.astype(BF)

            @pl.when(which < 3)
            def _():
                g_copy(n, which).start()

    gradient(1, 0, c_r)

    sum_parts(1, factor_at(owner_of(t // 4, (t // 2) % 2), ranks.shape[3]))
    for way in range(2):
        hop_copy(way).wait_recv()
        send_ring(way, way)
    gathered(1)
    gradient(0, 1, x_r)

    sib_copy(3).wait_recv()
    for m in range(len(MESSAGES)):
        ad_copy(m).wait_recv()

    @pl.loop(0, tiles)
    def _(n):
        at = span(n * TILE, TILE)
        back = ad_r[:, :, :, at].reshape(2 * rows, TILE)
        hold[2, :, at] = hold[2, :, at] + sib_r[3, :, at].astype(F32) + mm(slot_hot[...], back)

    for way in range(2):
        for part in range(2):
            ring_copy(way, part).wait_recv()

    for part in range(2):

        def put(at, to):
            out_v[at] = (
                hold[2, at] + ring_r[0, part, to].astype(F32) + ring_r[1, part, to].astype(F32)
            ).astype(BF)

        half_rows(part, put)
    stores = [pltpu.make_async_copy(out_v, out_ref, out_sem.at[2])]
    stores[0].start()

    for n, g_ref in ((1, gb_ref), (0, ga_ref)):

        @pl.loop(0, 3)
        def _(which):
            remote(
                g_s.at[n, which], g_r.at[n, which], g_ss.at[n, which], g_rs.at[n, which], dp=me
            ).wait_recv()

        @pl.loop(0, g_own.shape[1] // 32)
        def _(k):
            at = span(k * 32, 32)
            total = g_own[n, at]
            for which in range(3):
                total = total + g_r[n, which, at].astype(F32)
            g_own[n, at] = total

        stores.append(pltpu.make_async_copy(g_own.at[n], g_ref, out_sem.at[n]))
        stores[-1].start()

    @pl.loop(1, DP)
    def _(k):
        facts_copy(k).wait_send()
        tok_copy(k).wait_send()

    for n in range(2):
        for axis in range(2):
            fac_copy(axis, n).wait_send()
        fac_relay(n).wait_send()
    for m in range(len(MESSAGES)):
        x_copy(m).wait_send()
        c_copy(m).wait_send()
        ad_copy(m).wait_send()
    for j in (2, 3):
        sib_copy(j).wait_send()
    for way in range(2):
        hop_copy(way).wait_send()
        for part in range(2):
            ring_copy(way, part).wait_send()
    for kind in range(2):

        @pl.loop(1, TENSOR)
        def _(k):
            part_copy(kind, k).wait_send()
            gath_copy(kind, k).wait_send()

        @pl.loop(0, 3)
        def _(which):
            g_copy(kind, which).wait_send()

    for store in stores:
        store.wait()


def finish(out_ref, gb_ref, ga_ref, out_to, gb_to, ga_to, out_v, gb_v, ga_v, turned_v, sem):
    names = ((ga_ref, ga_v, turned_v, ga_to), (gb_ref, gb_v, gb_v, gb_to), (out_ref, out_v, out_v, out_to))
    loads = [pltpu.make_async_copy(src, held, sem.at[0, n]) for n, (src, held, _, _) in enumerate(names)]
    stores = [pltpu.make_async_copy(held, dst, sem.at[1, n]) for n, (_, _, held, dst) in enumerate(names)]
    for load in loads:
        load.start()
    loads[0].wait()
    turned_v[...] = ga_v[...].T
    stores[0].start()
    for n in (1, 2):
        loads[n].wait()
        stores[n].start()
    for store in stores:
        store.wait()


def on_device(
    tokens,
    destinations,
    counts,
    sequence_job_ids,
    job_owner_slot,
    rank_per_job,
    weight,
    input_factor_table,
    output_factor_table,
    cotangent,
):
    slot_count, seq_len, width = tokens.shape
    max_rank = input_factor_table.shape[2]
    rows = slot_count * seq_len
    anywhere = pl.BlockSpec(memory_space=pl.ANY)
    smem = pl.BlockSpec(memory_space=pltpu.SMEM)
    dma = pltpu.SemaphoreType.DMA
    served = (2, 2, RING, 64, width)
    lanes = (RING, RING, 64, width)
    out, ga, gb = pl.pallas_call(
        kernel,
        out_shape=(
            jax.ShapeDtypeStruct((rows, width), BF),
            jax.ShapeDtypeStruct((max_rank, width), F32),
            jax.ShapeDtypeStruct((max_rank, width), F32),
        ),
        in_specs=[smem] * 5 + [anywhere] * 5,
        out_specs=(anywhere,) * 3,
        scratch_shapes=[
            pltpu.VMEM(tokens.shape, BF),
            pltpu.VMEM((rows, width), BF),
            pltpu.VMEM(input_factor_table.shape, BF),
            pltpu.VMEM(output_factor_table.shape, BF),
            pltpu.VMEM((rows, width), BF),
            pltpu.VMEM((DP, seq_len, width), BF),
            pltpu.VMEM((DP, seq_len, width), BF),
            pltpu.VMEM((DP, 8, 128), jnp.int32),
            pltpu.VMEM((DP, 8, 128), jnp.int32),
            pltpu.VMEM((rows, rows), BF),
            pltpu.VMEM((2 * rows, rows), BF),
            pltpu.VMEM((2 * rows, rows), BF),
            pltpu.VMEM((rows, 2 * rows), BF),
            pltpu.VMEM((rows, width), BF),
            pltpu.VMEM(lanes, BF),
            pltpu.VMEM(served, BF),
            pltpu.VMEM(lanes, BF),
            pltpu.VMEM(served, BF),
            pltpu.VMEM((2, 2, width, max_rank), BF),
            pltpu.VMEM((2, 2, max_rank, width), BF),
            pltpu.VMEM((W_SLOTS, width, width), BF),
            pltpu.VMEM((2, rows, width), BF),
            pltpu.VMEM((4, rows, width), BF),
            pltpu.VMEM((3, rows, width), F32),
            pltpu.VMEM((2, rows // 2, width), BF),
            pltpu.VMEM((2, rows // 2, width), BF),
            pltpu.VMEM((2, 2, rows // 2, width), BF),
            pltpu.VMEM((2, 2, rows // 2, width), BF),
            pltpu.VMEM((2, TENSOR, 128, max_rank), BF),
            pltpu.VMEM((2, TENSOR, 128, max_rank), BF),
            pltpu.VMEM((2, TENSOR, 128, max_rank), BF),
            pltpu.VMEM(served, BF),
            pltpu.VMEM(lanes, BF),
            pltpu.VMEM((2, max_rank, width), F32),
            pltpu.VMEM((2, 4, max_rank, width), BF),
            pltpu.VMEM((2, 3, max_rank, width), BF),
            dma((4,)),
            dma((3,)),
            dma((W_SLOTS,)),
            dma((DP - 1,)),
            dma((DP - 1,)),
            dma((DP - 1,)),
            dma((DP - 1,)),
            dma((3, 2)),
            dma((2, 2, 2)),
            dma((8,)),
            dma((8,)),
            dma((8,)),
            dma((8,)),
            dma((2,)),
            dma((4,)),
            dma((2,)),
            dma((2,)),
            dma((2, 2)),
            dma((2, 2)),
            dma((2, TENSOR - 1)),
            dma((2, TENSOR - 1)),
            dma((2, TENSOR - 1)),
            dma((2, TENSOR - 1)),
            dma((8,)),
            dma((8,)),
            dma((2, 3)),
            dma((2, 3)),
        ],
        compiler_params=pltpu.CompilerParams(
            collective_id=0, has_side_effects=True, vmem_limit_bytes=59 * 2**20
        ),
    )(
        destinations,
        counts,
        sequence_job_ids,
        job_owner_slot,
        rank_per_job,
        tokens,
        cotangent.reshape(rows, width),
        input_factor_table,
        output_factor_table,
        weight,
    )
    out, gb, ga = pl.pallas_call(
        finish,
        out_shape=(
            jax.ShapeDtypeStruct((rows, width), BF),
            jax.ShapeDtypeStruct((max_rank, width), F32),
            jax.ShapeDtypeStruct((width, max_rank), F32),
        ),
        in_specs=[anywhere] * 3,
        out_specs=(anywhere,) * 3,
        scratch_shapes=[
            pltpu.VMEM((rows, width), BF),
            pltpu.VMEM((max_rank, width), F32),
            pltpu.VMEM((max_rank, width), F32),
            pltpu.VMEM((width, max_rank), F32),
            dma((2, 3)),
        ],
    )(out, gb, ga)
    return out.reshape(slot_count, seq_len, width), ga[None], gb[None]


def solution(mesh):
    in_specs = (
        P("dp", None, "tensor"),
        P("dp"),
        P("dp"),
        P("dp"),
        P(),
        P(),
        P("tensor", None),
        P("dp", "tensor", None),
        P("dp", None, "tensor"),
        P("dp", None, "tensor"),
    )
    out_specs = (P("dp", None, "tensor"), P("dp", "tensor", None), P("dp", None, "tensor"))
    return jax.shard_map(
        on_device, mesh=mesh, in_specs=in_specs, out_specs=out_specs, check_vma=False
    )
```

```python
import jax
import jax.numpy as jnp
from jax import lax
from jax.experimental import pallas as pl
from jax.experimental.pallas import tpu as pltpu
from jax.sharding import PartitionSpec as P

BF = jnp.bfloat16
F32 = jnp.float32
RING = 4
DP = RING * RING
TENSOR = 2 * RING
TILE = 256
W_SLOTS = 3
MOVE, PLACE = (0, 0, -1, 1), (0, 1, 1, 0)
BOTH = slice(0, 2)
MESSAGES = ((2, 2), (2, 3), (3, 2), (3, 3), (2, BOTH), (3, BOTH), (BOTH, 2), (BOTH, 3))


def mm(a, b):
    return jnp.dot(a, b, preferred_element_type=F32)


def kernel(
    dest_ref,
    count_ref,
    job_ref,
    owner_ref,
    rank_ref,
    tok_ref,
    cot_ref,
    a_ref,
    b_ref,
    w_ref,
    out_ref,
    ga_ref,
    gb_ref,
    tok_v,
    cot_v,
    a_v,
    b_v,
    out_v,
    tok_s,
    tok_r,
    facts_s,
    facts_r,
    place_hot,
    x_hot,
    c_hot,
    slot_hot,
    xs,
    x_s,
    x_r,
    c_s,
    c_r,
    fa,
    fb,
    wbuf,
    sib_s,
    sib_r,
    hold,
    hop_s,
    hop_r,
    ring_s,
    ring_r,
    part_s,
    part_r,
    ranks,
    ad_s,
    ad_r,
    g_own,
    g_s,
    g_r,
    in_sem,
    out_sem,
    w_sem,
    facts_ss,
    facts_rs,
    tok_ss,
    tok_rs,
    fac_ss,
    fac_rs,
    c_ss,
    c_rs,
    x_ss,
    x_rs,
    sib_ss,
    sib_rs,
    hop_ss,
    hop_rs,
    ring_ss,
    ring_rs,
    part_ss,
    part_rs,
    gath_ss,
    gath_rs,
    ad_ss,
    ad_rs,
    g_ss,
    g_rs,
):
    seq_len, width = tok_ref.shape[1:]
    rows = DP * seq_len
    half = rows // 2
    me = lax.axis_index("dp")
    t = lax.axis_index("tensor")
    y, z = me // RING, me % RING
    x, c = t // 2, t % 2
    odd = (y + z) % 2
    ahead = 1 - 2 * odd
    others = ((1 - odd, 1 - odd), (odd, 1 - odd), (1 - odd, odd))
    tiles = width // TILE
    wide_half = width // 2

    def remote(src, dst, send, recv, **where):
        return pltpu.make_async_remote_copy(
            src_ref=src,
            dst_ref=dst,
            send_sem=send,
            recv_sem=recv,
            device_id=where,
            device_id_type=pl.DeviceIdType.MESH,
        )

    def iota(shape, axis):
        return lax.broadcasted_iota(jnp.int32, shape, axis)

    def near(dy, dz):
        return (y + dy + RING) % RING * RING + (z + dz + RING) % RING

    def owner_of(i, j):
        first, second = (y - i + RING) % RING, (z - j + RING) % RING
        shift = (first + second) % 2
        return (first + shift) % RING * RING + (second + shift) % RING

    def rank_at(owner):
        total = jnp.int32(0)
        for j in range(DP):
            total = total + jnp.where(owner_ref[j] == owner, rank_ref[j], 0)
        return total

    def factor_at(owner, columns):
        return 32.0 / jnp.full((1, columns), rank_at(owner).astype(F32), F32)

    def span(start, size):
        return pl.ds(pl.multiple_of(start, size), size)

    loads = [
        pltpu.make_async_copy(src, dst, in_sem.at[n])
        for n, (src, dst) in enumerate(((tok_ref, tok_v), (a_ref, a_v), (b_ref, b_v), (cot_ref, cot_v)))
    ]
    for load in loads:
        load.start()

    barrier = pltpu.get_barrier_semaphore()

    @pl.loop(1, DP)
    def _(k):
        pl.semaphore_signal(
            barrier, inc=1, device_id={"dp": (me + k) % DP}, device_id_type=pl.DeviceIdType.MESH
        )

    @pl.loop(1, TENSOR)
    def _(k):
        pl.semaphore_signal(
            barrier, inc=1, device_id={"tensor": (t + k) % TENSOR}, device_id_type=pl.DeviceIdType.MESH
        )

    def w_copy(i):
        j = i // 2
        block = (x + jnp.where(j == 0, 2, jnp.where(j == 1, 1, jnp.where(j == 2, 3, 0)))) % RING * 2
        block = block + (c + 1 - i % 2) % 2
        return pltpu.make_async_copy(
            w_ref.at[:, span(block * width, width)], wbuf.at[i % W_SLOTS], w_sem.at[i % W_SLOTS]
        )

    for i in range(W_SLOTS):
        w_copy(jnp.int32(i)).start()

    loads[0].wait()

    @pl.loop(0, DP)
    def _(k):
        to = (me + k) % DP
        index = jnp.int32(0)
        for i in range(DP):
            index = jnp.where(lax.shift_right_logical(dest_ref[i], 4) == to, i, index)
        owner = owner_ref[job_ref[index]]
        oy, oz = lax.shift_right_logical(owner, 2), owner & 3
        shift = (oy + oz) & 1
        dy, dz = (to // RING + RING - oy + shift) & 3, (to % RING + RING - oz + shift) & 3
        base = (dy * RING + dz) * 2
        row = iota((8, 128), 0)
        facts_s[k] = jnp.where(
            row == 0, dest_ref[index] & 15, jnp.where(row == 1, count_ref[index], base)
        )
        tok_s[k] = tok_v[index]

    tok_r[me] = tok_s[0]
    facts_r[me] = facts_s[0]

    pl.semaphore_wait(barrier, DP - 1 + TENSOR - 1)

    def facts_copy(k):
        return remote(
            facts_s.at[k], facts_r.at[me], facts_ss.at[k - 1], facts_rs.at[k - 1], dp=(me + k) % DP
        )

    def tok_copy(h, k):
        columns = span(h * wide_half, wide_half)
        return remote(
            tok_s.at[k, :, columns],
            tok_r.at[me, :, columns],
            tok_ss.at[h, k - 1],
            tok_rs.at[h, k - 1],
            dp=(me + k) % DP,
        )

    def fac_copy(axis, n):
        table = (fa, fb)[n]
        there = ((1 - odd, odd), (odd, 1 - odd))[axis]
        to = (near(ahead, 0), near(0, ahead))[axis]
        return remote(
            table.at[odd, odd], table.at[there], fac_ss.at[axis, n], fac_rs.at[there + (n,)], dp=to
        )

    def fac_wait(n, which):
        for there in which:
            held = (fa, fb)[n].at[there]
            remote(held, held, fac_ss.at[0, n], fac_rs.at[there + (n,)], dp=me).wait_recv()

    def fac_relay(n):
        table = (fa, fb)[n]
        here = ((odd, 1 - odd), (1 - odd, odd))[n]
        to = (near(0, -ahead), near(-ahead, 0))[n]
        return remote(table.at[here], table.at[odd, odd], fac_ss.at[2, n], fac_rs.at[odd, odd, n], dp=to)

    @pl.loop(1, DP)
    def _(k):
        facts_copy(k).start()

    @pl.loop(0, 2)
    def _(h):
        @pl.loop(1, DP)
        def _(k):
            tok_copy(h, k).start()

    my_rank = rank_at(me)
    loads[1].wait()

    @pl.loop(0, width // 128)
    def _(n):
        at = span(n * 128, 128)
        kept = iota((128, a_v.shape[2]), 1) < my_rank
        fa[odd, odd, at, :] = jnp.where(kept, a_v[0, at, :].astype(F32), 0.0).astype(BF)

    for axis in range(2):
        fac_copy(axis, 0).start()
    @pl.loop(1, DP)
    def _(k):
        facts_copy(k).wait_recv()

    slot_c = facts_r[:, 0, :].astype(F32)
    live_c = facts_r[:, 1, :].astype(F32)
    base_c = facts_r[:, 2, :].astype(F32)
    square = (DP, 128)
    diagonal = iota(square, 0) == iota(square, 1)
    slot_l = jnp.sum(jnp.where(diagonal, slot_c, 0.0), 0, keepdims=True)
    base_l = jnp.sum(jnp.where(diagonal, base_c, 0.0), 0, keepdims=True)
    earlier = (base_l == base_c) & (slot_l < slot_c) & (iota(square, 1) < DP)
    turn_c = jnp.sum(jnp.where(earlier, 1.0, 0.0), 1, keepdims=True)
    lane_c = base_c + turn_c
    lane_l = jnp.sum(jnp.where(diagonal, lane_c, 0.0), 0, keepdims=True)
    wide = (DP, rows)
    seq_of = iota(wide, 1) // seq_len
    slot_1, live_1, lane_1 = slot_c[:, :1], live_c[:, :1], lane_c[:, :1]
    in_slot = slot_1 == seq_of.astype(F32)
    in_order = iota(wide, 0) == seq_of
    position = (iota((1, rows), 1) % seq_len).astype(F32)

    def spread(where, value):
        return jnp.sum(jnp.where(where, value, 0.0), 0, keepdims=True)

    live = position < spread(in_order, live_1)
    c_row = spread(in_slot, lane_1) * seq_len + position
    x_row = jnp.where(live, spread(in_order, lane_1) * seq_len + position, -1.0)
    slot_row = jnp.where(live, spread(in_order, slot_1) * seq_len + position, -1.0)

    def build(hot, wanted):
        @pl.loop(0, hot.shape[0] // 64)
        def _(n):
            row = (iota((64, rows), 0) + n * 64).astype(F32)
            hot[span(n * 64, 64), :] = jnp.where(row == wanted, 1.0, 0.0).astype(BF)

    build(x_hot, x_row)
    build(place_hot, slot_row)

    lane_shape = (RING, RING, 2 * seq_len)

    def lane_place(dy, dz):
        row = PLACE[dy] if dy != BOTH else BOTH
        column = PLACE[dz] if dz != BOTH else BOTH
        return row, column, (dy != BOTH) * 2 + (dz != BOTH)

    def lane_move(dy, dz):
        return (MOVE[dy] if dy != BOTH else 0, MOVE[dz] if dz != BOTH else 0)

    def x_copy(h, m):
        message, columns = MESSAGES[m], span(h * wide_half, wide_half)
        return remote(
            x_s.at[message + (slice(None), columns)],
            x_r.at[lane_place(*message) + (slice(None), columns)],
            x_ss.at[h, m],
            x_rs.at[h, m],
            dp=near(*lane_move(*message)),
        )

    def c_copy(m):
        message = MESSAGES[m]
        return remote(
            c_s.at[message],
            c_r.at[lane_place(*message)],
            c_ss.at[m],
            c_rs.at[m],
            dp=near(*lane_move(*message)),
        )

    @pl.loop(0, 2)
    def _(h):
        @pl.loop(1, DP)
        def _(k):
            tok_copy(h, k).wait_recv()

        @pl.loop(0, tiles // 2)
        def _(n):
            at = span(h * wide_half + n * TILE, TILE)
            landed = tok_r[:, :, at].reshape(rows, TILE)
            x_s[:, :, :, at] = mm(x_hot[...], landed).astype(BF).reshape(lane_shape + (TILE,))

        for m in range(len(MESSAGES)):
            x_copy(h, m).start()

        @pl.loop(0, tiles // 2)
        def _(n):
            at = span(h * wide_half + n * TILE, TILE)
            xs[:, at] = mm(place_hot[...], tok_r[:, :, at].reshape(rows, TILE)).astype(BF)

    loads[2].wait()

    @pl.loop(0, width // 128)
    def _(n):
        at = span(n * 128, 128)
        kept = iota((b_v.shape[1], 128), 0) < my_rank
        fb[odd, odd, :, at] = jnp.where(kept, b_v[0, :, at].astype(F32), 0.0).astype(BF)

    for axis in range(2):
        fac_copy(axis, 1).start()
    build(c_hot, c_row)
    loads[3].wait()

    @pl.loop(0, tiles)
    def _(n):
        at = span(n * TILE, TILE)
        c_s[:, :, :, at] = mm(c_hot[...], cot_v[:, at]).astype(BF).reshape(lane_shape + (TILE,))

    for m in range(len(MESSAGES)):
        c_copy(m).start()
    x_r[:, :, 0] = x_s[BOTH, BOTH]
    c_r[:, :, 0] = c_s[BOTH, BOTH]

    def sib_copy(j):
        return remote(
            sib_s.at[j % 2], sib_r.at[j], sib_ss.at[j % 2], sib_rs.at[j], tensor=x * 2 + (1 - c)
        )

    right, left = ((x + 1) % RING) * 2 + c, ((x + 3) % RING) * 2 + c

    def hop_copy(way):
        return remote(
            hop_s.at[way], hop_r.at[way], hop_ss.at[way], hop_rs.at[way], tensor=(right, left)[way]
        )

    def ring_copy(way, part):
        return remote(
            ring_s.at[way, part],
            ring_r.at[way, part],
            ring_ss.at[way, part],
            ring_rs.at[way, part],
            tensor=(right, left)[way],
        )

    def half_rows(part, put):
        @pl.loop(0, half // 32)
        def _(n):
            put(span(part * half + n * 32, 32), span(n * 32, 32))

    def send_hop(way):
        def put(at, to):
            hop_s[way, to] = (hold[0, at] + sib_r[0, at].astype(F32)).astype(BF)

        half_rows(way, put)
        hop_copy(way).start()

    def send_ring(way, part):
        def put(at, to):
            value = hold[1 - way, at] + sib_r[1 + way, at].astype(F32)
            if way == part:
                value = value + hop_r[way, to].astype(F32)
            ring_s[way, part, to] = value.astype(BF)

        half_rows(part, put)
        ring_copy(way, part).start()

    def part_copy(kind, k):
        to = (t + k) % TENSOR
        return remote(
            part_s.at[kind, to],
            part_r.at[kind, k],
            part_ss.at[kind, k - 1],
            part_rs.at[kind, k - 1],
            tensor=to,
        )

    def gath_copy(kind, k):
        to = (t + k) % TENSOR
        held = ranks.at[kind, t]
        return remote(held, held, gath_ss.at[kind, k - 1], gath_rs.at[kind, k - 1], tensor=to)

    def served(ref, i, j):
        return ref[i, j].reshape(RING * 64, width)

    def send_parts(kind, make):
        @pl.loop(0, 4)
        def _(q):
            value = make(q // 2, q % 2).astype(BF)
            part_s[kind, 2 * q] = value[:128]
            part_s[kind, 2 * q + 1] = value[128:]

        @pl.loop(1, TENSOR)
        def _(k):
            part_copy(kind, k).start()

        part_r[kind, 0] = part_s[kind, t]

    def sum_parts(kind, scale):
        @pl.loop(1, TENSOR)
        def _(k):
            part_copy(kind, k).wait_recv()

        total = part_r[kind, 0].astype(F32)
        for k in range(1, TENSOR):
            total = total + part_r[kind, k].astype(F32)
        ranks[kind, t] = (total if scale is None else total * scale).astype(BF)

        @pl.loop(1, TENSOR)
        def _(k):
            gath_copy(kind, k).start()

    def gathered(kind):
        @pl.loop(1, TENSOR)
        def _(k):
            held = ranks.at[kind, (t + TENSOR - k) % TENSOR]
            remote(held, held, gath_ss.at[kind, k - 1], gath_rs.at[kind, k - 1], tensor=t).wait_recv()

    def rank_rows(kind, i, j):
        return ranks[kind, pl.ds(i * 4 + j * 2, 2)].reshape(RING * 64, ranks.shape[3])

    @pl.loop(0, 4)
    def _(j):
        w_copy(2 * j).wait()

        @pl.when(j >= 2)
        def _():
            sib_copy(j - 2).wait_send()

        @pl.loop(0, tiles)
        def _(n):
            at = span(n * TILE, TILE)
            sib_s[j % 2, :, at] = mm(xs[...], wbuf[(2 * j) % W_SLOTS, :, at]).astype(BF)

        sib_copy(j).start()

        @pl.when(2 * j + W_SLOTS < 8)
        def _():
            w_copy(2 * j + W_SLOTS).start()

        @pl.when(j == 1)
        def _():
            sib_copy(0).wait_recv()
            send_hop(0)
            send_hop(1)
            fac_wait(0, others[1:])
            fac_relay(0).start()

        @pl.when(j == 3)
        def _():
            sib_copy(2).wait_recv()
            send_ring(1, 0)

        w_copy(2 * j + 1).wait()

        @pl.loop(0, tiles)
        def _(n):
            at = span(n * TILE, TILE)
            hold[jnp.where(j == 3, 2, j % 2), :, at] = mm(xs[...], wbuf[(2 * j + 1) % W_SLOTS, :, at])

        @pl.when(2 * j + 1 + W_SLOTS < 8)
        def _():
            w_copy(2 * j + 1 + W_SLOTS).start()

        @pl.when(j == 1)
        def _():
            fac_wait(0, others[:1])

            @pl.loop(0, 2)
            def _(h):
                for m in range(len(MESSAGES)):
                    x_copy(h, m).wait_recv()

            send_parts(0, lambda i, k: mm(served(x_r, i, k), fa[i, k]))

        @pl.when(j == 2)
        def _():
            fac_wait(1, others[1:])
            fac_relay(1).start()
            sum_parts(0, None)
            sib_copy(1).wait_recv()
            send_ring(0, 1)

    def ad_copy(m):
        message = MESSAGES[m]
        dy, dz = lane_move(*message)
        return remote(
            ad_s.at[lane_place(*message)],
            ad_r.at[message],
            ad_ss.at[m],
            ad_rs.at[m],
            dp=near(-dy, -dz),
        )

    fac_wait(1, others[:1])
    gathered(0)

    @pl.loop(0, 4)
    def _(q):
        i, j = q // 2, q % 2
        value = mm(rank_rows(0, i, j), fb[i, j]) * factor_at(owner_of(i, j), width)
        ad_s[i, j] = value.astype(BF).reshape(RING, 64, width)

    for m in range(len(MESSAGES)):
        ad_copy(m).start()
    ad_r[BOTH, BOTH] = ad_s[:, :, 0]

    for m in range(len(MESSAGES)):
        c_copy(m).wait_recv()
    send_parts(
        1,
        lambda i, j: lax.dot_general(
            served(c_r, i, j), fb[i, j], (((1,), (1,)), ((), ())), preferred_element_type=F32
        ),
    )

    def g_copy(n, which):
        dy = jnp.where(which == 0, -ahead, jnp.where(which == 1, ahead, 0))
        dz = jnp.where(which == 0, -ahead, jnp.where(which == 1, 0, ahead))
        return remote(
            g_s.at[n, which],
            g_r.at[n, which],
            g_ss.at[n, which],
            g_rs.at[n, which],
            dp=near(dy, dz),
        )

    def gradient(n, kind, row_ref):
        @pl.loop(0, 4)
        def _(which):
            i = jnp.where((which == 1) | (which == 3), odd, 1 - odd)
            j = jnp.where(which >= 2, odd, 1 - odd)
            turned = rank_rows(kind, i, j).astype(F32).T.astype(BF)
            value = mm(turned, served(row_ref, i, j)) * (1.0 / seq_len)
            if n == 1:
                value = value * factor_at(owner_of(i, j), width)
            g_own[n] = value
            g_s[n, which] = value.astype(BF)

            @pl.when(which < 3)
            def _():
                g_copy(n, which).start()

    gradient(1, 0, c_r)

    @pl.loop(0, rows // 64)
    def _(n):
        row = iota((64, 128), 0) + n * 64
        mine = jnp.where(slot_l == (row // seq_len).astype(F32), lane_l, 0.0)
        place = jnp.sum(mine, 1, keepdims=True) * seq_len + (row % seq_len).astype(F32)[:, :1]
        slot_hot[span(n * 64, 64), :] = jnp.where(
            iota((64, 2 * rows), 1).astype(F32) == place, 1.0, 0.0
        ).astype(BF)

    sum_parts(1, factor_at(owner_of(t // 4, (t // 2) % 2), ranks.shape[3]))
    for way in range(2):
        hop_copy(way).wait_recv()
        send_ring(way, way)
    gathered(1)
    gradient(0, 1, x_r)

    sib_copy(3).wait_recv()
    for m in range(len(MESSAGES)):
        ad_copy(m).wait_recv()

    @pl.loop(0, tiles)
    def _(n):
        at = span(n * TILE, TILE)
        back = ad_r[:, :, :, at].reshape(2 * rows, TILE)
        hold[2, :, at] = hold[2, :, at] + sib_r[3, :, at].astype(F32) + mm(slot_hot[...], back)

    for way in range(2):
        for part in range(2):
            ring_copy(way, part).wait_recv()

    for part in range(2):

        def put(at, to):
            out_v[at] = (
                hold[2, at] + ring_r[0, part, to].astype(F32) + ring_r[1, part, to].astype(F32)
            ).astype(BF)

        half_rows(part, put)
    stores = [pltpu.make_async_copy(out_v, out_ref, out_sem.at[2])]
    stores[0].start()

    for n, g_ref in ((1, gb_ref), (0, ga_ref)):

        @pl.loop(0, 3)
        def _(which):
            remote(
                g_s.at[n, which], g_r.at[n, which], g_ss.at[n, which], g_rs.at[n, which], dp=me
            ).wait_recv()

        @pl.loop(0, g_own.shape[1] // 32)
        def _(k):
            at = span(k * 32, 32)
            total = g_own[n, at]
            for which in range(3):
                total = total + g_r[n, which, at].astype(F32)
            g_own[n, at] = total

        stores.append(pltpu.make_async_copy(g_own.at[n], g_ref, out_sem.at[n]))
        stores[-1].start()

    @pl.loop(1, DP)
    def _(k):
        facts_copy(k).wait_send()
        tok_copy(0, k).wait_send()
        tok_copy(1, k).wait_send()

    for n in range(2):
        for axis in range(2):
            fac_copy(axis, n).wait_send()
        fac_relay(n).wait_send()
    for m in range(len(MESSAGES)):
        for h in range(2):
            x_copy(h, m).wait_send()
        c_copy(m).wait_send()
        ad_copy(m).wait_send()
    for j in (2, 3):
        sib_copy(j).wait_send()
    for way in range(2):
        hop_copy(way).wait_send()
        for part in range(2):
            ring_copy(way, part).wait_send()
    for kind in range(2):

        @pl.loop(1, TENSOR)
        def _(k):
            part_copy(kind, k).wait_send()
            gath_copy(kind, k).wait_send()

        @pl.loop(0, 3)
        def _(which):
            g_copy(kind, which).wait_send()

    for store in stores:
        store.wait()


def finish(out_ref, gb_ref, ga_ref, out_to, gb_to, ga_to, out_v, gb_v, ga_v, turned_v, sem):
    names = ((ga_ref, ga_v, turned_v, ga_to), (gb_ref, gb_v, gb_v, gb_to), (out_ref, out_v, out_v, out_to))
    loads = [pltpu.make_async_copy(src, held, sem.at[0, n]) for n, (src, held, _, _) in enumerate(names)]
    stores = [pltpu.make_async_copy(held, dst, sem.at[1, n]) for n, (_, _, held, dst) in enumerate(names)]
    for load in loads:
        load.start()
    loads[0].wait()
    turned_v[...] = ga_v[...].T
    stores[0].start()
    for n in (1, 2):
        loads[n].wait()
        stores[n].start()
    for store in stores:
        store.wait()


def on_device(
    tokens,
    destinations,
    counts,
    sequence_job_ids,
    job_owner_slot,
    rank_per_job,
    weight,
    input_factor_table,
    output_factor_table,
    cotangent,
):
    slot_count, seq_len, width = tokens.shape
    max_rank = input_factor_table.shape[2]
    rows = slot_count * seq_len
    anywhere = pl.BlockSpec(memory_space=pl.ANY)
    smem = pl.BlockSpec(memory_space=pltpu.SMEM)
    dma = pltpu.SemaphoreType.DMA
    served = (2, 2, RING, 64, width)
    lanes = (RING, RING, 64, width)
    out, ga, gb = pl.pallas_call(
        kernel,
        out_shape=(
            jax.ShapeDtypeStruct((rows, width), BF),
            jax.ShapeDtypeStruct((max_rank, width), F32),
            jax.ShapeDtypeStruct((max_rank, width), F32),
        ),
        in_specs=[smem] * 5 + [anywhere] * 5,
        out_specs=(anywhere,) * 3,
        scratch_shapes=[
            pltpu.VMEM(tokens.shape, BF),
            pltpu.VMEM((rows, width), BF),
            pltpu.VMEM(input_factor_table.shape, BF),
            pltpu.VMEM(output_factor_table.shape, BF),
            pltpu.VMEM((rows, width), BF),
            pltpu.VMEM((DP, seq_len, width), BF),
            pltpu.VMEM((DP, seq_len, width), BF),
            pltpu.VMEM((DP, 8, 128), jnp.int32),
            pltpu.VMEM((DP, 8, 128), jnp.int32),
            pltpu.VMEM((rows, rows), BF),
            pltpu.VMEM((2 * rows, rows), BF),
            pltpu.VMEM((2 * rows, rows), BF),
            pltpu.VMEM((rows, 2 * rows), BF),
            pltpu.VMEM((rows, width), BF),
            pltpu.VMEM(lanes, BF),
            pltpu.VMEM(served, BF),
            pltpu.VMEM(lanes, BF),
            pltpu.VMEM(served, BF),
            pltpu.VMEM((2, 2, width, max_rank), BF),
            pltpu.VMEM((2, 2, max_rank, width), BF),
            pltpu.VMEM((W_SLOTS, width, width), BF),
            pltpu.VMEM((2, rows, width), BF),
            pltpu.VMEM((4, rows, width), BF),
            pltpu.VMEM((3, rows, width), F32),
            pltpu.VMEM((2, rows // 2, width), BF),
            pltpu.VMEM((2, rows // 2, width), BF),
            pltpu.VMEM((2, 2, rows // 2, width), BF),
            pltpu.VMEM((2, 2, rows // 2, width), BF),
            pltpu.VMEM((2, TENSOR, 128, max_rank), BF),
            pltpu.VMEM((2, TENSOR, 128, max_rank), BF),
            pltpu.VMEM((2, TENSOR, 128, max_rank), BF),
            pltpu.VMEM(served, BF),
            pltpu.VMEM(lanes, BF),
            pltpu.VMEM((2, max_rank, width), F32),
            pltpu.VMEM((2, 4, max_rank, width), BF),
            pltpu.VMEM((2, 3, max_rank, width), BF),
            dma((4,)),
            dma((3,)),
            dma((W_SLOTS,)),
            dma((DP - 1,)),
            dma((DP - 1,)),
            dma((2, DP - 1)),
            dma((2, DP - 1)),
            dma((3, 2)),
            dma((2, 2, 2)),
            dma((8,)),
            dma((8,)),
            dma((2, 8)),
            dma((2, 8)),
            dma((2,)),
            dma((4,)),
            dma((2,)),
            dma((2,)),
            dma((2, 2)),
            dma((2, 2)),
            dma((2, TENSOR - 1)),
            dma((2, TENSOR - 1)),
            dma((2, TENSOR - 1)),
            dma((2, TENSOR - 1)),
            dma((8,)),
            dma((8,)),
            dma((2, 3)),
            dma((2, 3)),
        ],
        compiler_params=pltpu.CompilerParams(
            collective_id=0, has_side_effects=True, vmem_limit_bytes=58 * 2**20
        ),
    )(
        destinations,
        counts,
        sequence_job_ids,
        job_owner_slot,
        rank_per_job,
        tokens,
        cotangent.reshape(rows, width),
        input_factor_table,
        output_factor_table,
        weight,
    )
    out, gb, ga = pl.pallas_call(
        finish,
        out_shape=(
            jax.ShapeDtypeStruct((rows, width), BF),
            jax.ShapeDtypeStruct((max_rank, width), F32),
            jax.ShapeDtypeStruct((width, max_rank), F32),
        ),
        in_specs=[anywhere] * 3,
        out_specs=(anywhere,) * 3,
        scratch_shapes=[
            pltpu.VMEM((rows, width), BF),
            pltpu.VMEM((max_rank, width), F32),
            pltpu.VMEM((max_rank, width), F32),
            pltpu.VMEM((width, max_rank), F32),
            dma((2, 3)),
        ],
    )(out, gb, ga)
    return out.reshape(slot_count, seq_len, width), ga[None], gb[None]


def solution(mesh):
    in_specs = (
        P("dp", None, "tensor"),
        P("dp"),
        P("dp"),
        P("dp"),
        P(),
        P(),
        P("tensor", None),
        P("dp", "tensor", None),
        P("dp", None, "tensor"),
        P("dp", None, "tensor"),
    )
    out_specs = (P("dp", None, "tensor"), P("dp", "tensor", None), P("dp", None, "tensor"))
    return jax.shard_map(
        on_device, mesh=mesh, in_specs=in_specs, out_specs=out_specs, check_vma=False
    )
```

```python
import jax
import jax.numpy as jnp
from jax import lax
from jax.experimental import pallas as pl
from jax.experimental.pallas import tpu as pltpu
from jax.sharding import PartitionSpec as P

BF = jnp.bfloat16
F32 = jnp.float32
RING = 4
DP = RING * RING
TENSOR = 2 * RING
TILE = 256
W_SLOTS = 3
MOVE, PLACE = (0, 0, -1, 1), (0, 1, 1, 0)
BOTH = slice(0, 2)
MESSAGES = ((2, 2), (2, 3), (3, 2), (3, 3), (2, BOTH), (3, BOTH), (BOTH, 2), (BOTH, 3))


def mm(a, b):
    return jnp.dot(a, b, preferred_element_type=F32)


def kernel(
    dest_ref,
    count_ref,
    job_ref,
    owner_ref,
    rank_ref,
    tok_ref,
    cot_ref,
    a_ref,
    b_ref,
    w_ref,
    out_ref,
    ga_ref,
    gb_ref,
    tok_v,
    cot_v,
    a_v,
    b_v,
    out_v,
    tok_s,
    tok_r,
    facts_s,
    facts_r,
    place_hot,
    x_hot,
    c_hot,
    slot_hot,
    xs,
    x_s,
    x_r,
    c_s,
    c_r,
    fa,
    fb,
    wbuf,
    sib_s,
    sib_r,
    hold,
    hop_s,
    hop_r,
    ring_s,
    ring_r,
    part_s,
    part_r,
    ranks,
    ad_s,
    ad_r,
    g_own,
    g_s,
    g_r,
    in_sem,
    out_sem,
    w_sem,
    facts_ss,
    facts_rs,
    tok_ss,
    tok_rs,
    fac_ss,
    fac_rs,
    c_ss,
    c_rs,
    x_ss,
    x_rs,
    sib_ss,
    sib_rs,
    tile_ss,
    tile_rs,
    hop_ss,
    hop_rs,
    ring_ss,
    ring_rs,
    part_ss,
    part_rs,
    gath_ss,
    gath_rs,
    ad_ss,
    ad_rs,
    g_ss,
    g_rs,
):
    seq_len, width = tok_ref.shape[1:]
    rows = DP * seq_len
    half = rows // 2
    me = lax.axis_index("dp")
    t = lax.axis_index("tensor")
    y, z = me // RING, me % RING
    x, c = t // 2, t % 2
    odd = (y + z) % 2
    ahead = 1 - 2 * odd
    others = ((1 - odd, 1 - odd), (odd, 1 - odd), (1 - odd, odd))
    tiles = width // TILE
    wide_half = width // 2

    def remote(src, dst, send, recv, **where):
        return pltpu.make_async_remote_copy(
            src_ref=src,
            dst_ref=dst,
            send_sem=send,
            recv_sem=recv,
            device_id=where,
            device_id_type=pl.DeviceIdType.MESH,
        )

    def iota(shape, axis):
        return lax.broadcasted_iota(jnp.int32, shape, axis)

    def near(dy, dz):
        return (y + dy + RING) % RING * RING + (z + dz + RING) % RING

    def owner_of(i, j):
        first, second = (y - i + RING) % RING, (z - j + RING) % RING
        shift = (first + second) % 2
        return (first + shift) % RING * RING + (second + shift) % RING

    def rank_at(owner):
        total = jnp.int32(0)
        for j in range(DP):
            total = total + jnp.where(owner_ref[j] == owner, rank_ref[j], 0)
        return total

    def factor_at(owner, columns):
        return 32.0 / jnp.full((1, columns), rank_at(owner).astype(F32), F32)

    def span(start, size):
        return pl.ds(pl.multiple_of(start, size), size)

    loads = [
        pltpu.make_async_copy(src, dst, in_sem.at[n])
        for n, (src, dst) in enumerate(((tok_ref, tok_v), (a_ref, a_v), (b_ref, b_v), (cot_ref, cot_v)))
    ]
    for load in loads:
        load.start()

    barrier = pltpu.get_barrier_semaphore()

    @pl.loop(1, DP)
    def _(k):
        pl.semaphore_signal(
            barrier, inc=1, device_id={"dp": (me + k) % DP}, device_id_type=pl.DeviceIdType.MESH
        )

    @pl.loop(1, TENSOR)
    def _(k):
        pl.semaphore_signal(
            barrier, inc=1, device_id={"tensor": (t + k) % TENSOR}, device_id_type=pl.DeviceIdType.MESH
        )

    def w_copy(i):
        j = i // 2
        block = (x + jnp.where(j == 0, 2, jnp.where(j == 1, 1, jnp.where(j == 2, 3, 0)))) % RING * 2
        block = block + (c + 1 - i % 2) % 2
        return pltpu.make_async_copy(
            w_ref.at[:, span(block * width, width)], wbuf.at[i % W_SLOTS], w_sem.at[i % W_SLOTS]
        )

    for i in range(W_SLOTS):
        w_copy(jnp.int32(i)).start()

    loads[0].wait()

    @pl.loop(0, DP)
    def _(k):
        to = (me + k) % DP
        index = jnp.int32(0)
        for i in range(DP):
            index = jnp.where(lax.shift_right_logical(dest_ref[i], 4) == to, i, index)
        owner = owner_ref[job_ref[index]]
        oy, oz = lax.shift_right_logical(owner, 2), owner & 3
        shift = (oy + oz) & 1
        dy, dz = (to // RING + RING - oy + shift) & 3, (to % RING + RING - oz + shift) & 3
        base = (dy * RING + dz) * 2
        row = iota((8, 128), 0)
        facts_s[k] = jnp.where(
            row == 0, dest_ref[index] & 15, jnp.where(row == 1, count_ref[index], base)
        )
        tok_s[k] = tok_v[index]

    tok_r[me] = tok_s[0]
    facts_r[me] = facts_s[0]

    pl.semaphore_wait(barrier, DP - 1 + TENSOR - 1)

    def facts_copy(k):
        return remote(
            facts_s.at[k], facts_r.at[me], facts_ss.at[k - 1], facts_rs.at[k - 1], dp=(me + k) % DP
        )

    def tok_copy(h, k):
        columns = span(h * wide_half, wide_half)
        return remote(
            tok_s.at[k, :, columns],
            tok_r.at[me, :, columns],
            tok_ss.at[h, k - 1],
            tok_rs.at[h, k - 1],
            dp=(me + k) % DP,
        )

    def fac_copy(axis, n):
        table = (fa, fb)[n]
        there = ((1 - odd, odd), (odd, 1 - odd))[axis]
        to = (near(ahead, 0), near(0, ahead))[axis]
        return remote(
            table.at[odd, odd], table.at[there], fac_ss.at[axis, n], fac_rs.at[there + (n,)], dp=to
        )

    def fac_wait(n, which):
        for there in which:
            held = (fa, fb)[n].at[there]
            remote(held, held, fac_ss.at[0, n], fac_rs.at[there + (n,)], dp=me).wait_recv()

    def fac_relay(n):
        table = (fa, fb)[n]
        here = ((odd, 1 - odd), (1 - odd, odd))[n]
        to = (near(0, -ahead), near(-ahead, 0))[n]
        return remote(table.at[here], table.at[odd, odd], fac_ss.at[2, n], fac_rs.at[odd, odd, n], dp=to)

    @pl.loop(1, DP)
    def _(k):
        facts_copy(k).start()

    @pl.loop(0, 2)
    def _(h):
        @pl.loop(1, DP)
        def _(k):
            tok_copy(h, k).start()

    my_rank = rank_at(me)
    loads[1].wait()

    @pl.loop(0, width // 128)
    def _(n):
        at = span(n * 128, 128)
        kept = iota((128, a_v.shape[2]), 1) < my_rank
        fa[odd, odd, at, :] = jnp.where(kept, a_v[0, at, :].astype(F32), 0.0).astype(BF)

    for axis in range(2):
        fac_copy(axis, 0).start()
    @pl.loop(1, DP)
    def _(k):
        facts_copy(k).wait_recv()

    slot_c = facts_r[:, 0, :].astype(F32)
    live_c = facts_r[:, 1, :].astype(F32)
    base_c = facts_r[:, 2, :].astype(F32)
    square = (DP, 128)
    diagonal = iota(square, 0) == iota(square, 1)
    slot_l = jnp.sum(jnp.where(diagonal, slot_c, 0.0), 0, keepdims=True)
    base_l = jnp.sum(jnp.where(diagonal, base_c, 0.0), 0, keepdims=True)
    earlier = (base_l == base_c) & (slot_l < slot_c) & (iota(square, 1) < DP)
    turn_c = jnp.sum(jnp.where(earlier, 1.0, 0.0), 1, keepdims=True)
    lane_c = base_c + turn_c
    lane_l = jnp.sum(jnp.where(diagonal, lane_c, 0.0), 0, keepdims=True)
    wide = (DP, rows)
    seq_of = iota(wide, 1) // seq_len
    slot_1, live_1, lane_1 = slot_c[:, :1], live_c[:, :1], lane_c[:, :1]
    in_slot = slot_1 == seq_of.astype(F32)
    in_order = iota(wide, 0) == seq_of
    position = (iota((1, rows), 1) % seq_len).astype(F32)

    def spread(where, value):
        return jnp.sum(jnp.where(where, value, 0.0), 0, keepdims=True)

    live = position < spread(in_order, live_1)
    c_row = spread(in_slot, lane_1) * seq_len + position
    x_row = jnp.where(live, spread(in_order, lane_1) * seq_len + position, -1.0)
    slot_row = jnp.where(live, spread(in_order, slot_1) * seq_len + position, -1.0)

    def build(hot, wanted):
        @pl.loop(0, hot.shape[0] // 64)
        def _(n):
            row = (iota((64, rows), 0) + n * 64).astype(F32)
            hot[span(n * 64, 64), :] = jnp.where(row == wanted, 1.0, 0.0).astype(BF)

    build(x_hot, x_row)
    build(place_hot, slot_row)

    lane_shape = (RING, RING, 2 * seq_len)

    def lane_place(dy, dz):
        row = PLACE[dy] if dy != BOTH else BOTH
        column = PLACE[dz] if dz != BOTH else BOTH
        return row, column, (dy != BOTH) * 2 + (dz != BOTH)

    def lane_move(dy, dz):
        return (MOVE[dy] if dy != BOTH else 0, MOVE[dz] if dz != BOTH else 0)

    def x_copy(h, m):
        message, columns = MESSAGES[m], span(h * wide_half, wide_half)
        return remote(
            x_s.at[message + (slice(None), columns)],
            x_r.at[lane_place(*message) + (slice(None), columns)],
            x_ss.at[h, m],
            x_rs.at[h, m],
            dp=near(*lane_move(*message)),
        )

    def c_copy(m):
        message = MESSAGES[m]
        return remote(
            c_s.at[message],
            c_r.at[lane_place(*message)],
            c_ss.at[m],
            c_rs.at[m],
            dp=near(*lane_move(*message)),
        )

    @pl.loop(0, 2)
    def _(h):
        @pl.loop(1, DP)
        def _(k):
            tok_copy(h, k).wait_recv()

        @pl.loop(0, tiles // 2)
        def _(n):
            at = span(h * wide_half + n * TILE, TILE)
            landed = tok_r[:, :, at].reshape(rows, TILE)
            x_s[:, :, :, at] = mm(x_hot[...], landed).astype(BF).reshape(lane_shape + (TILE,))

        for m in range(len(MESSAGES)):
            x_copy(h, m).start()

        @pl.loop(0, tiles // 2)
        def _(n):
            at = span(h * wide_half + n * TILE, TILE)
            xs[:, at] = mm(place_hot[...], tok_r[:, :, at].reshape(rows, TILE)).astype(BF)

    loads[2].wait()

    @pl.loop(0, width // 128)
    def _(n):
        at = span(n * 128, 128)
        kept = iota((b_v.shape[1], 128), 0) < my_rank
        fb[odd, odd, :, at] = jnp.where(kept, b_v[0, :, at].astype(F32), 0.0).astype(BF)

    for axis in range(2):
        fac_copy(axis, 1).start()
    build(c_hot, c_row)
    loads[3].wait()

    @pl.loop(0, tiles)
    def _(n):
        at = span(n * TILE, TILE)
        c_s[:, :, :, at] = mm(c_hot[...], cot_v[:, at]).astype(BF).reshape(lane_shape + (TILE,))

    for m in range(len(MESSAGES)):
        c_copy(m).start()
    x_r[:, :, 0] = x_s[BOTH, BOTH]
    c_r[:, :, 0] = c_s[BOTH, BOTH]

    def sib_copy(j):
        return remote(
            sib_s.at[j % 2], sib_r.at[j], sib_ss.at[j % 2], sib_rs.at[j], tensor=x * 2 + (1 - c)
        )

    right, left = ((x + 1) % RING) * 2 + c, ((x + 3) % RING) * 2 + c

    def hop_copy(way, n):
        at = span(n * TILE, TILE)
        return remote(
            hop_s.at[way, :, at],
            hop_r.at[way, :, at],
            hop_ss.at[way, n],
            hop_rs.at[way, n],
            tensor=(right, left)[way],
        )

    def sib_tile(n):
        at = span(n * TILE, TILE)
        return remote(
            sib_s.at[0, :, at], sib_r.at[0, :, at], tile_ss.at[n], tile_rs.at[n], tensor=x * 2 + (1 - c)
        )

    def ring_copy(way, part):
        return remote(
            ring_s.at[way, part],
            ring_r.at[way, part],
            ring_ss.at[way, part],
            ring_rs.at[way, part],
            tensor=(right, left)[way],
        )

    def half_rows(part, put):
        @pl.loop(0, half // 32)
        def _(n):
            put(span(part * half + n * 32, 32), span(n * 32, 32))

    def send_hop(n):
        at = span(n * TILE, TILE)
        sib_tile(n).wait_recv()
        for way in range(2):
            part = slice(way * half, (way + 1) * half)
            hop_s[way, :, at] = (hold[0, part, at] + sib_r[0, part, at].astype(F32)).astype(BF)
            hop_copy(way, n).start()

    def send_ring(way, part):
        def put(at, to):
            value = hold[1 - way, at] + sib_r[1 + way, at].astype(F32)
            if way == part:
                value = value + hop_r[way, to].astype(F32)
            ring_s[way, part, to] = value.astype(BF)

        half_rows(part, put)
        ring_copy(way, part).start()

    def part_copy(kind, k):
        to = (t + k) % TENSOR
        return remote(
            part_s.at[kind, to],
            part_r.at[kind, k],
            part_ss.at[kind, k - 1],
            part_rs.at[kind, k - 1],
            tensor=to,
        )

    def gath_copy(kind, k):
        to = (t + k) % TENSOR
        held = ranks.at[kind, t]
        return remote(held, held, gath_ss.at[kind, k - 1], gath_rs.at[kind, k - 1], tensor=to)

    def served(ref, i, j):
        return ref[i, j].reshape(RING * 64, width)

    def send_parts(kind, make):
        @pl.loop(0, 4)
        def _(q):
            value = make(q // 2, q % 2).astype(BF)
            part_s[kind, 2 * q] = value[:128]
            part_s[kind, 2 * q + 1] = value[128:]

        @pl.loop(1, TENSOR)
        def _(k):
            part_copy(kind, k).start()

        part_r[kind, 0] = part_s[kind, t]

    def sum_parts(kind, scale):
        @pl.loop(1, TENSOR)
        def _(k):
            part_copy(kind, k).wait_recv()

        total = part_r[kind, 0].astype(F32)
        for k in range(1, TENSOR):
            total = total + part_r[kind, k].astype(F32)
        ranks[kind, t] = (total if scale is None else total * scale).astype(BF)

        @pl.loop(1, TENSOR)
        def _(k):
            gath_copy(kind, k).start()

    def gathered(kind):
        @pl.loop(1, TENSOR)
        def _(k):
            held = ranks.at[kind, (t + TENSOR - k) % TENSOR]
            remote(held, held, gath_ss.at[kind, k - 1], gath_rs.at[kind, k - 1], tensor=t).wait_recv()

    def rank_rows(kind, i, j):
        return ranks[kind, pl.ds(i * 4 + j * 2, 2)].reshape(RING * 64, ranks.shape[3])

    for i in range(2):
        w_copy(jnp.int32(i)).wait()

    @pl.loop(0, tiles)
    def _(n):
        at = span(n * TILE, TILE)
        sib_s[0, :, at] = mm(xs[...], wbuf[0, :, at]).astype(BF)
        sib_tile(n).start()
        hold[0, :, at] = mm(xs[...], wbuf[1, :, at])

        @pl.when(n > 0)
        def _():
            send_hop(n - 1)

    for i in range(2):
        w_copy(jnp.int32(i + W_SLOTS)).start()
    send_hop(jnp.int32(tiles - 1))

    @pl.loop(1, 4)
    def _(j):
        w_copy(2 * j).wait()

        @pl.when(j == 2)
        def _():
            for n in range(tiles):
                sib_tile(n).wait_send()

        @pl.when(j == 3)
        def _():
            sib_copy(1).wait_send()

        @pl.loop(0, tiles)
        def _(n):
            at = span(n * TILE, TILE)
            sib_s[j % 2, :, at] = mm(xs[...], wbuf[(2 * j) % W_SLOTS, :, at]).astype(BF)

        sib_copy(j).start()

        @pl.when(2 * j + W_SLOTS < 8)
        def _():
            w_copy(2 * j + W_SLOTS).start()

        @pl.when(j == 1)
        def _():
            fac_wait(0, others[1:])
            fac_relay(0).start()

        @pl.when(j == 3)
        def _():
            sib_copy(2).wait_recv()
            send_ring(1, 0)

        w_copy(2 * j + 1).wait()

        @pl.loop(0, tiles)
        def _(n):
            at = span(n * TILE, TILE)
            hold[jnp.where(j == 3, 2, j % 2), :, at] = mm(xs[...], wbuf[(2 * j + 1) % W_SLOTS, :, at])

        @pl.when(2 * j + 1 + W_SLOTS < 8)
        def _():
            w_copy(2 * j + 1 + W_SLOTS).start()

        @pl.when(j == 1)
        def _():
            fac_wait(0, others[:1])

            @pl.loop(0, 2)
            def _(h):
                for m in range(len(MESSAGES)):
                    x_copy(h, m).wait_recv()

            send_parts(0, lambda i, k: mm(served(x_r, i, k), fa[i, k]))

        @pl.when(j == 2)
        def _():
            fac_wait(1, others[1:])
            fac_relay(1).start()
            sum_parts(0, None)
            sib_copy(1).wait_recv()
            send_ring(0, 1)

    def ad_copy(m):
        message = MESSAGES[m]
        dy, dz = lane_move(*message)
        return remote(
            ad_s.at[lane_place(*message)],
            ad_r.at[message],
            ad_ss.at[m],
            ad_rs.at[m],
            dp=near(-dy, -dz),
        )

    fac_wait(1, others[:1])
    gathered(0)

    @pl.loop(0, 4)
    def _(q):
        i, j = q // 2, q % 2
        value = mm(rank_rows(0, i, j), fb[i, j]) * factor_at(owner_of(i, j), width)
        ad_s[i, j] = value.astype(BF).reshape(RING, 64, width)

    for m in range(len(MESSAGES)):
        ad_copy(m).start()
    ad_r[BOTH, BOTH] = ad_s[:, :, 0]

    for m in range(len(MESSAGES)):
        c_copy(m).wait_recv()
    send_parts(
        1,
        lambda i, j: lax.dot_general(
            served(c_r, i, j), fb[i, j], (((1,), (1,)), ((), ())), preferred_element_type=F32
        ),
    )

    def g_copy(n, which):
        dy = jnp.where(which == 0, -ahead, jnp.where(which == 1, ahead, 0))
        dz = jnp.where(which == 0, -ahead, jnp.where(which == 1, 0, ahead))
        return remote(
            g_s.at[n, which],
            g_r.at[n, which],
            g_ss.at[n, which],
            g_rs.at[n, which],
            dp=near(dy, dz),
        )

    def gradient(n, kind, row_ref):
        @pl.loop(0, 4)
        def _(which):
            i = jnp.where((which == 1) | (which == 3), odd, 1 - odd)
            j = jnp.where(which >= 2, odd, 1 - odd)
            turned = rank_rows(kind, i, j).astype(F32).T.astype(BF)
            value = mm(turned, served(row_ref, i, j)) * (1.0 / seq_len)
            if n == 1:
                value = value * factor_at(owner_of(i, j), width)
            g_own[n] = value
            g_s[n, which] = value.astype(BF)

            @pl.when(which < 3)
            def _():
                g_copy(n, which).start()

    gradient(1, 0, c_r)

    @pl.loop(0, rows // 64)
    def _(n):
        row = iota((64, 128), 0) + n * 64
        mine = jnp.where(slot_l == (row // seq_len).astype(F32), lane_l, 0.0)
        place = jnp.sum(mine, 1, keepdims=True) * seq_len + (row % seq_len).astype(F32)[:, :1]
        slot_hot[span(n * 64, 64), :] = jnp.where(
            iota((64, 2 * rows), 1).astype(F32) == place, 1.0, 0.0
        ).astype(BF)

    sum_parts(1, factor_at(owner_of(t // 4, (t // 2) % 2), ranks.shape[3]))
    for way in range(2):
        for n in range(tiles):
            hop_copy(way, n).wait_recv()
        send_ring(way, way)
    gathered(1)
    gradient(0, 1, x_r)

    sib_copy(3).wait_recv()
    for m in range(len(MESSAGES)):
        ad_copy(m).wait_recv()

    @pl.loop(0, tiles)
    def _(n):
        at = span(n * TILE, TILE)
        back = ad_r[:, :, :, at].reshape(2 * rows, TILE)
        hold[2, :, at] = hold[2, :, at] + sib_r[3, :, at].astype(F32) + mm(slot_hot[...], back)

    for way in range(2):
        for part in range(2):
            ring_copy(way, part).wait_recv()

    for part in range(2):

        def put(at, to):
            out_v[at] = (
                hold[2, at] + ring_r[0, part, to].astype(F32) + ring_r[1, part, to].astype(F32)
            ).astype(BF)

        half_rows(part, put)
    stores = [pltpu.make_async_copy(out_v, out_ref, out_sem.at[2])]
    stores[0].start()

    for n, g_ref in ((1, gb_ref), (0, ga_ref)):

        @pl.loop(0, 3)
        def _(which):
            remote(
                g_s.at[n, which], g_r.at[n, which], g_ss.at[n, which], g_rs.at[n, which], dp=me
            ).wait_recv()

        @pl.loop(0, g_own.shape[1] // 32)
        def _(k):
            at = span(k * 32, 32)
            total = g_own[n, at]
            for which in range(3):
                total = total + g_r[n, which, at].astype(F32)
            g_own[n, at] = total

        stores.append(pltpu.make_async_copy(g_own.at[n], g_ref, out_sem.at[n]))
        stores[-1].start()

    @pl.loop(1, DP)
    def _(k):
        facts_copy(k).wait_send()
        tok_copy(0, k).wait_send()
        tok_copy(1, k).wait_send()

    for n in range(2):
        for axis in range(2):
            fac_copy(axis, n).wait_send()
        fac_relay(n).wait_send()
    for m in range(len(MESSAGES)):
        for h in range(2):
            x_copy(h, m).wait_send()
        c_copy(m).wait_send()
        ad_copy(m).wait_send()
    for j in (2, 3):
        sib_copy(j).wait_send()
    for way in range(2):
        for n in range(tiles):
            hop_copy(way, n).wait_send()
        for part in range(2):
            ring_copy(way, part).wait_send()
    for kind in range(2):

        @pl.loop(1, TENSOR)
        def _(k):
            part_copy(kind, k).wait_send()
            gath_copy(kind, k).wait_send()

        @pl.loop(0, 3)
        def _(which):
            g_copy(kind, which).wait_send()

    for store in stores:
        store.wait()


def finish(out_ref, gb_ref, ga_ref, out_to, gb_to, ga_to, out_v, gb_v, ga_v, turned_v, sem):
    names = ((ga_ref, ga_v, turned_v, ga_to), (gb_ref, gb_v, gb_v, gb_to), (out_ref, out_v, out_v, out_to))
    loads = [pltpu.make_async_copy(src, held, sem.at[0, n]) for n, (src, held, _, _) in enumerate(names)]
    stores = [pltpu.make_async_copy(held, dst, sem.at[1, n]) for n, (_, _, held, dst) in enumerate(names)]
    for load in loads:
        load.start()
    loads[0].wait()
    turned_v[...] = ga_v[...].T
    stores[0].start()
    for n in (1, 2):
        loads[n].wait()
        stores[n].start()
    for store in stores:
        store.wait()


def on_device(
    tokens,
    destinations,
    counts,
    sequence_job_ids,
    job_owner_slot,
    rank_per_job,
    weight,
    input_factor_table,
    output_factor_table,
    cotangent,
):
    slot_count, seq_len, width = tokens.shape
    max_rank = input_factor_table.shape[2]
    rows = slot_count * seq_len
    anywhere = pl.BlockSpec(memory_space=pl.ANY)
    smem = pl.BlockSpec(memory_space=pltpu.SMEM)
    dma = pltpu.SemaphoreType.DMA
    served = (2, 2, RING, 64, width)
    lanes = (RING, RING, 64, width)
    out, ga, gb = pl.pallas_call(
        kernel,
        out_shape=(
            jax.ShapeDtypeStruct((rows, width), BF),
            jax.ShapeDtypeStruct((max_rank, width), F32),
            jax.ShapeDtypeStruct((max_rank, width), F32),
        ),
        in_specs=[smem] * 5 + [anywhere] * 5,
        out_specs=(anywhere,) * 3,
        scratch_shapes=[
            pltpu.VMEM(tokens.shape, BF),
            pltpu.VMEM((rows, width), BF),
            pltpu.VMEM(input_factor_table.shape, BF),
            pltpu.VMEM(output_factor_table.shape, BF),
            pltpu.VMEM((rows, width), BF),
            pltpu.VMEM((DP, seq_len, width), BF),
            pltpu.VMEM((DP, seq_len, width), BF),
            pltpu.VMEM((DP, 8, 128), jnp.int32),
            pltpu.VMEM((DP, 8, 128), jnp.int32),
            pltpu.VMEM((rows, rows), BF),
            pltpu.VMEM((2 * rows, rows), BF),
            pltpu.VMEM((2 * rows, rows), BF),
            pltpu.VMEM((rows, 2 * rows), BF),
            pltpu.VMEM((rows, width), BF),
            pltpu.VMEM(lanes, BF),
            pltpu.VMEM(served, BF),
            pltpu.VMEM(lanes, BF),
            pltpu.VMEM(served, BF),
            pltpu.VMEM((2, 2, width, max_rank), BF),
            pltpu.VMEM((2, 2, max_rank, width), BF),
            pltpu.VMEM((W_SLOTS, width, width), BF),
            pltpu.VMEM((2, rows, width), BF),
            pltpu.VMEM((4, rows, width), BF),
            pltpu.VMEM((3, rows, width), F32),
            pltpu.VMEM((2, rows // 2, width), BF),
            pltpu.VMEM((2, rows // 2, width), BF),
            pltpu.VMEM((2, 2, rows // 2, width), BF),
            pltpu.VMEM((2, 2, rows // 2, width), BF),
            pltpu.VMEM((2, TENSOR, 128, max_rank), BF),
            pltpu.VMEM((2, TENSOR, 128, max_rank), BF),
            pltpu.VMEM((2, TENSOR, 128, max_rank), BF),
            pltpu.VMEM(served, BF),
            pltpu.VMEM(lanes, BF),
            pltpu.VMEM((2, max_rank, width), F32),
            pltpu.VMEM((2, 4, max_rank, width), BF),
            pltpu.VMEM((2, 3, max_rank, width), BF),
            dma((4,)),
            dma((3,)),
            dma((W_SLOTS,)),
            dma((DP - 1,)),
            dma((DP - 1,)),
            dma((2, DP - 1)),
            dma((2, DP - 1)),
            dma((3, 2)),
            dma((2, 2, 2)),
            dma((8,)),
            dma((8,)),
            dma((2, 8)),
            dma((2, 8)),
            dma((2,)),
            dma((4,)),
            dma((4,)),
            dma((4,)),
            dma((2, 4)),
            dma((2, 4)),
            dma((2, 2)),
            dma((2, 2)),
            dma((2, TENSOR - 1)),
            dma((2, TENSOR - 1)),
            dma((2, TENSOR - 1)),
            dma((2, TENSOR - 1)),
            dma((8,)),
            dma((8,)),
            dma((2, 3)),
            dma((2, 3)),
        ],
        compiler_params=pltpu.CompilerParams(
            collective_id=0, has_side_effects=True, vmem_limit_bytes=58 * 2**20
        ),
    )(
        destinations,
        counts,
        sequence_job_ids,
        job_owner_slot,
        rank_per_job,
        tokens,
        cotangent.reshape(rows, width),
        input_factor_table,
        output_factor_table,
        weight,
    )
    out, gb, ga = pl.pallas_call(
        finish,
        out_shape=(
            jax.ShapeDtypeStruct((rows, width), BF),
            jax.ShapeDtypeStruct((max_rank, width), F32),
            jax.ShapeDtypeStruct((width, max_rank), F32),
        ),
        in_specs=[anywhere] * 3,
        out_specs=(anywhere,) * 3,
        scratch_shapes=[
            pltpu.VMEM((rows, width), BF),
            pltpu.VMEM((max_rank, width), F32),
            pltpu.VMEM((max_rank, width), F32),
            pltpu.VMEM((width, max_rank), F32),
            dma((2, 3)),
        ],
    )(out, gb, ga)
    return out.reshape(slot_count, seq_len, width), ga[None], gb[None]


def solution(mesh):
    in_specs = (
        P("dp", None, "tensor"),
        P("dp"),
        P("dp"),
        P("dp"),
        P(),
        P(),
        P("tensor", None),
        P("dp", "tensor", None),
        P("dp", None, "tensor"),
        P("dp", None, "tensor"),
    )
    out_specs = (P("dp", None, "tensor"), P("dp", "tensor", None), P("dp", None, "tensor"))
    return jax.shard_map(
        on_device, mesh=mesh, in_specs=in_specs, out_specs=out_specs, check_vma=False
    )
```

```python
import jax
import jax.numpy as jnp
from jax import lax
from jax.experimental import pallas as pl
from jax.experimental.pallas import tpu as pltpu
from jax.sharding import PartitionSpec as P

BF = jnp.bfloat16
F32 = jnp.float32
RING = 4
DP = RING * RING
TENSOR = 2 * RING
TILE = 256
W_SLOTS = 3
MOVE, PLACE = (0, 0, -1, 1), (0, 1, 1, 0)
BOTH = slice(0, 2)
MESSAGES = ((2, BOTH), (BOTH, 2), (3, BOTH), (BOTH, 3), (2, 2), (3, 3), (2, 3), (3, 2))
NEIGHBOURS = ((0, 1), (1, 0), (0, 3), (3, 0), (1, 1), (3, 3), (1, 3), (3, 1))
OTHERS = NEIGHBOURS + ((0, 2), (2, 0), (2, 1), (1, 2), (2, 3), (3, 2), (2, 2))


def mm(a, b):
    return jnp.dot(a, b, preferred_element_type=F32)


def kernel(
    dest_ref,
    count_ref,
    job_ref,
    owner_ref,
    rank_ref,
    tok_ref,
    cot_ref,
    a_ref,
    b_ref,
    w_ref,
    out_ref,
    ga_ref,
    gb_ref,
    tok_v,
    cot_v,
    a_v,
    b_v,
    out_v,
    tok_s,
    tok_r,
    facts_s,
    facts_r,
    place_hot,
    x_hot,
    c_hot,
    slot_hot,
    xs,
    x_s,
    x_r,
    c_s,
    c_r,
    fa,
    fb,
    wbuf,
    sib_s,
    sib_r,
    hold,
    hop_s,
    hop_r,
    ring_s,
    ring_r,
    part_s,
    part_r,
    ranks,
    ad_s,
    ad_r,
    g_own,
    g_s,
    g_r,
    in_sem,
    out_sem,
    w_sem,
    facts_ss,
    facts_rs,
    tok_ss,
    tok_rs,
    fac_ss,
    fac_rs,
    c_ss,
    c_rs,
    x_ss,
    x_rs,
    sib_ss,
    sib_rs,
    hop_ss,
    hop_rs,
    ring_ss,
    ring_rs,
    part_ss,
    part_rs,
    gath_ss,
    gath_rs,
    ad_ss,
    ad_rs,
    g_ss,
    g_rs,
):
    seq_len, width = tok_ref.shape[1:]
    rows = DP * seq_len
    half = rows // 2
    me = lax.axis_index("dp")
    t = lax.axis_index("tensor")
    y, z = me // RING, me % RING
    x, c = t // 2, t % 2
    odd = (y + z) % 2
    ahead = 1 - 2 * odd
    others = ((1 - odd, 1 - odd), (odd, 1 - odd), (1 - odd, odd))
    tiles = width // TILE
    wide_half = width // 2

    def remote(src, dst, send, recv, **where):
        return pltpu.make_async_remote_copy(
            src_ref=src,
            dst_ref=dst,
            send_sem=send,
            recv_sem=recv,
            device_id=where,
            device_id_type=pl.DeviceIdType.MESH,
        )

    def iota(shape, axis):
        return lax.broadcasted_iota(jnp.int32, shape, axis)

    def near(dy, dz):
        return (y + dy + RING) % RING * RING + (z + dz + RING) % RING

    def owner_of(i, j):
        first, second = (y - i + RING) % RING, (z - j + RING) % RING
        shift = (first + second) % 2
        return (first + shift) % RING * RING + (second + shift) % RING

    def rank_at(owner):
        total = jnp.int32(0)
        for j in range(DP):
            total = total + jnp.where(owner_ref[j] == owner, rank_ref[j], 0)
        return total

    def factor_at(owner, columns):
        return 32.0 / jnp.full((1, columns), rank_at(owner).astype(F32), F32)

    def span(start, size):
        return pl.ds(pl.multiple_of(start, size), size)

    loads = [
        pltpu.make_async_copy(src, dst, in_sem.at[n])
        for n, (src, dst) in enumerate(((tok_ref, tok_v), (a_ref, a_v), (b_ref, b_v), (cot_ref, cot_v)))
    ]
    for load in loads:
        load.start()

    barrier = pltpu.get_barrier_semaphore()

    @pl.loop(1, DP)
    def _(k):
        pl.semaphore_signal(
            barrier, inc=1, device_id={"dp": (me + k) % DP}, device_id_type=pl.DeviceIdType.MESH
        )

    @pl.loop(1, TENSOR)
    def _(k):
        pl.semaphore_signal(
            barrier, inc=1, device_id={"tensor": (t + k) % TENSOR}, device_id_type=pl.DeviceIdType.MESH
        )

    def w_copy(i):
        j = i // 2
        block = (x + jnp.where(j == 0, 2, jnp.where(j == 1, 1, jnp.where(j == 2, 3, 0)))) % RING * 2
        block = block + (c + 1 - i % 2) % 2
        return pltpu.make_async_copy(
            w_ref.at[:, span(block * width, width)], wbuf.at[i % W_SLOTS], w_sem.at[i % W_SLOTS]
        )

    for i in range(W_SLOTS):
        w_copy(jnp.int32(i)).start()

    def chosen(to):
        index = jnp.int32(0)
        for i in range(DP):
            index = jnp.where(lax.shift_right_logical(dest_ref[i], 4) == to, i, index)
        return index

    @pl.loop(0, DP)
    def _(to):
        index = chosen(to)
        owner = owner_ref[job_ref[index]]
        oy, oz = lax.shift_right_logical(owner, 2), owner & 3
        shift = (oy + oz) & 1
        dy, dz = (to // RING + RING - oy + shift) & 3, (to % RING + RING - oz + shift) & 3
        base = (dy * RING + dz) * 2
        row = iota((8, 128), 0)
        facts_s[to] = jnp.where(
            row == 0, dest_ref[index] & 15, jnp.where(row == 1, count_ref[index], base)
        )

    facts_r[me] = facts_s[me]
    loads[0].wait()

    @pl.loop(0, DP)
    def _(to):
        tok_s[to] = tok_v[chosen(to)]

    tok_r[me] = tok_s[me]

    pl.semaphore_wait(barrier, DP - 1 + TENSOR - 1)

    def facts_copy(k):
        to = near(*OTHERS[k])
        return remote(facts_s.at[to], facts_r.at[me], facts_ss.at[k], facts_rs.at[k], dp=to)

    def tok_copy(h, k):
        to, columns = near(*OTHERS[k]), span(h * wide_half, wide_half)
        return remote(
            tok_s.at[to, :, columns],
            tok_r.at[me, :, columns],
            tok_ss.at[h, k],
            tok_rs.at[h, k],
            dp=to,
        )

    def fac_copy(which, n):
        table = (fa, fb)[n]
        there = ((1 - odd, odd), (odd, 1 - odd), (1 - odd, 1 - odd))[which]
        to = (near(ahead, 0), near(0, ahead), near(ahead, ahead))[which]
        return remote(
            table.at[odd, odd], table.at[there], fac_ss.at[which, n], fac_rs.at[there + (n,)], dp=to
        )

    def fac_wait(n):
        for there in others:
            held = (fa, fb)[n].at[there]
            remote(held, held, fac_ss.at[0, n], fac_rs.at[there + (n,)], dp=me).wait_recv()

    for k in range(DP - 1):
        facts_copy(k).start()

    @pl.loop(0, 2)
    def _(h):
        for k in range(DP - 1):
            tok_copy(h, k).start()

    my_rank = rank_at(me)
    loads[1].wait()

    @pl.loop(0, width // 128)
    def _(n):
        at = span(n * 128, 128)
        kept = iota((128, a_v.shape[2]), 1) < my_rank
        fa[odd, odd, at, :] = jnp.where(kept, a_v[0, at, :].astype(F32), 0.0).astype(BF)

    for which in range(3):
        fac_copy(which, 0).start()
    for k in range(DP - 1):
        facts_copy(k).wait_recv()

    slot_c = facts_r[:, 0, :].astype(F32)
    live_c = facts_r[:, 1, :].astype(F32)
    base_c = facts_r[:, 2, :].astype(F32)
    square = (DP, 128)
    diagonal = iota(square, 0) == iota(square, 1)
    slot_l = jnp.sum(jnp.where(diagonal, slot_c, 0.0), 0, keepdims=True)
    base_l = jnp.sum(jnp.where(diagonal, base_c, 0.0), 0, keepdims=True)
    earlier = (base_l == base_c) & (slot_l < slot_c) & (iota(square, 1) < DP)
    turn_c = jnp.sum(jnp.where(earlier, 1.0, 0.0), 1, keepdims=True)
    lane_c = base_c + turn_c
    lane_l = jnp.sum(jnp.where(diagonal, lane_c, 0.0), 0, keepdims=True)
    wide = (DP, rows)
    seq_of = iota(wide, 1) // seq_len
    slot_1, live_1, lane_1 = slot_c[:, :1], live_c[:, :1], lane_c[:, :1]
    in_slot = slot_1 == seq_of.astype(F32)
    in_order = iota(wide, 0) == seq_of
    position = (iota((1, rows), 1) % seq_len).astype(F32)

    def spread(where, value):
        return jnp.sum(jnp.where(where, value, 0.0), 0, keepdims=True)

    live = position < spread(in_order, live_1)
    c_row = spread(in_slot, lane_1) * seq_len + position
    x_row = jnp.where(live, spread(in_order, lane_1) * seq_len + position, -1.0)
    slot_row = jnp.where(live, spread(in_order, slot_1) * seq_len + position, -1.0)

    def build(hot, wanted):
        @pl.loop(0, hot.shape[0] // 64)
        def _(n):
            row = (iota((64, rows), 0) + n * 64).astype(F32)
            hot[span(n * 64, 64), :] = jnp.where(row == wanted, 1.0, 0.0).astype(BF)

    build(x_hot, x_row)
    build(place_hot, slot_row)

    lane_shape = (RING, RING, 2 * seq_len)

    def lane_place(dy, dz):
        row = PLACE[dy] if dy != BOTH else BOTH
        column = PLACE[dz] if dz != BOTH else BOTH
        return row, column, (dy != BOTH) * 2 + (dz != BOTH)

    def lane_move(dy, dz):
        return (MOVE[dy] if dy != BOTH else 0, MOVE[dz] if dz != BOTH else 0)

    def x_copy(h, m):
        message, columns = MESSAGES[m], span(h * wide_half, wide_half)
        return remote(
            x_s.at[message + (slice(None), columns)],
            x_r.at[lane_place(*message) + (slice(None), columns)],
            x_ss.at[h, m],
            x_rs.at[h, m],
            dp=near(*lane_move(*message)),
        )

    def c_copy(m):
        message = MESSAGES[m]
        return remote(
            c_s.at[message],
            c_r.at[lane_place(*message)],
            c_ss.at[m],
            c_rs.at[m],
            dp=near(*lane_move(*message)),
        )

    @pl.loop(0, 2)
    def _(h):
        for k in range(DP - 1):
            tok_copy(h, k).wait_recv()

        @pl.loop(0, tiles // 2)
        def _(n):
            at = span(h * wide_half + n * TILE, TILE)
            landed = tok_r[:, :, at].reshape(rows, TILE)
            x_s[:, :, :, at] = mm(x_hot[...], landed).astype(BF).reshape(lane_shape + (TILE,))

        for m in range(len(MESSAGES)):
            x_copy(h, m).start()

        @pl.loop(0, tiles // 2)
        def _(n):
            at = span(h * wide_half + n * TILE, TILE)
            xs[:, at] = mm(place_hot[...], tok_r[:, :, at].reshape(rows, TILE)).astype(BF)

    loads[2].wait()

    @pl.loop(0, width // 128)
    def _(n):
        at = span(n * 128, 128)
        kept = iota((b_v.shape[1], 128), 0) < my_rank
        fb[odd, odd, :, at] = jnp.where(kept, b_v[0, :, at].astype(F32), 0.0).astype(BF)

    for which in range(3):
        fac_copy(which, 1).start()
    build(c_hot, c_row)
    loads[3].wait()

    @pl.loop(0, tiles)
    def _(n):
        at = span(n * TILE, TILE)
        c_s[:, :, :, at] = mm(c_hot[...], cot_v[:, at]).astype(BF).reshape(lane_shape + (TILE,))

    for m in range(len(MESSAGES)):
        c_copy(m).start()
    x_r[:, :, 0] = x_s[BOTH, BOTH]
    c_r[:, :, 0] = c_s[BOTH, BOTH]

    def sib_copy(j):
        return remote(
            sib_s.at[j % 2], sib_r.at[j], sib_ss.at[j % 2], sib_rs.at[j], tensor=x * 2 + (1 - c)
        )

    right, left = ((x + 1) % RING) * 2 + c, ((x + 3) % RING) * 2 + c

    def hop_copy(way):
        return remote(
            hop_s.at[way], hop_r.at[way], hop_ss.at[way], hop_rs.at[way], tensor=(right, left)[way]
        )

    def ring_copy(way, part):
        return remote(
            ring_s.at[way, part],
            ring_r.at[way, part],
            ring_ss.at[way, part],
            ring_rs.at[way, part],
            tensor=(right, left)[way],
        )

    def half_rows(part, put):
        @pl.loop(0, half // 32)
        def _(n):
            put(span(part * half + n * 32, 32), span(n * 32, 32))

    def send_hop(way):
        def put(at, to):
            hop_s[way, to] = (hold[0, at] + sib_r[0, at].astype(F32)).astype(BF)

        half_rows(way, put)
        hop_copy(way).start()

    def send_ring(way, part):
        def put(at, to):
            value = hold[1 - way, at] + sib_r[1 + way, at].astype(F32)
            if way == part:
                value = value + hop_r[way, to].astype(F32)
            ring_s[way, part, to] = value.astype(BF)

        half_rows(part, put)
        ring_copy(way, part).start()

    def part_copy(kind, k):
        to = (t + k) % TENSOR
        return remote(
            part_s.at[kind, to],
            part_r.at[kind, k],
            part_ss.at[kind, k - 1],
            part_rs.at[kind, k - 1],
            tensor=to,
        )

    def gath_copy(kind, k):
        to = (t + k) % TENSOR
        held = ranks.at[kind, t]
        return remote(held, held, gath_ss.at[kind, k - 1], gath_rs.at[kind, k - 1], tensor=to)

    def served(ref, i, j):
        return ref[i, j].reshape(RING * 64, width)

    def send_parts(kind, make):
        @pl.loop(0, 4)
        def _(q):
            value = make(q // 2, q % 2).astype(BF)
            part_s[kind, 2 * q] = value[:128]
            part_s[kind, 2 * q + 1] = value[128:]

        @pl.loop(1, TENSOR)
        def _(k):
            part_copy(kind, k).start()

        part_r[kind, 0] = part_s[kind, t]

    def sum_parts(kind, scale):
        @pl.loop(1, TENSOR)
        def _(k):
            part_copy(kind, k).wait_recv()

        total = part_r[kind, 0].astype(F32)
        for k in range(1, TENSOR):
            total = total + part_r[kind, k].astype(F32)
        ranks[kind, t] = (total if scale is None else total * scale).astype(BF)

        @pl.loop(1, TENSOR)
        def _(k):
            gath_copy(kind, k).start()

    def gathered(kind):
        @pl.loop(1, TENSOR)
        def _(k):
            held = ranks.at[kind, (t + TENSOR - k) % TENSOR]
            remote(held, held, gath_ss.at[kind, k - 1], gath_rs.at[kind, k - 1], tensor=t).wait_recv()

    def rank_rows(kind, i, j):
        return ranks[kind, pl.ds(i * 4 + j * 2, 2)].reshape(RING * 64, ranks.shape[3])

    @pl.loop(0, 4)
    def _(j):
        w_copy(2 * j).wait()

        @pl.when(j >= 2)
        def _():
            sib_copy(j - 2).wait_send()

        @pl.loop(0, tiles)
        def _(n):
            at = span(n * TILE, TILE)
            sib_s[j % 2, :, at] = mm(xs[...], wbuf[(2 * j) % W_SLOTS, :, at]).astype(BF)

        sib_copy(j).start()

        @pl.when(2 * j + W_SLOTS < 8)
        def _():
            w_copy(2 * j + W_SLOTS).start()

        @pl.when(j == 1)
        def _():
            sib_copy(0).wait_recv()
            send_hop(0)
            send_hop(1)

        @pl.when(j == 3)
        def _():
            sib_copy(2).wait_recv()
            send_ring(1, 0)

        w_copy(2 * j + 1).wait()

        @pl.loop(0, tiles)
        def _(n):
            at = span(n * TILE, TILE)
            hold[jnp.where(j == 3, 2, j % 2), :, at] = mm(xs[...], wbuf[(2 * j + 1) % W_SLOTS, :, at])

        @pl.when(2 * j + 1 + W_SLOTS < 8)
        def _():
            w_copy(2 * j + 1 + W_SLOTS).start()

        @pl.when(j == 1)
        def _():
            fac_wait(0)

            @pl.loop(0, 2)
            def _(h):
                for m in range(len(MESSAGES)):
                    x_copy(h, m).wait_recv()

            send_parts(0, lambda i, k: mm(served(x_r, i, k), fa[i, k]))

        @pl.when(j == 2)
        def _():
            sum_parts(0, None)
            sib_copy(1).wait_recv()
            send_ring(0, 1)

    def ad_copy(m):
        message = MESSAGES[m]
        dy, dz = lane_move(*message)
        return remote(
            ad_s.at[lane_place(*message)],
            ad_r.at[message],
            ad_ss.at[m],
            ad_rs.at[m],
            dp=near(-dy, -dz),
        )

    fac_wait(1)
    gathered(0)

    @pl.loop(0, 4)
    def _(q):
        i, j = q // 2, q % 2
        value = mm(rank_rows(0, i, j), fb[i, j]) * factor_at(owner_of(i, j), width)
        ad_s[i, j] = value.astype(BF).reshape(RING, 64, width)

    for m in range(len(MESSAGES)):
        ad_copy(m).start()
    ad_r[BOTH, BOTH] = ad_s[:, :, 0]

    for m in range(len(MESSAGES)):
        c_copy(m).wait_recv()
    send_parts(
        1,
        lambda i, j: lax.dot_general(
            served(c_r, i, j), fb[i, j], (((1,), (1,)), ((), ())), preferred_element_type=F32
        ),
    )

    def g_copy(n, which):
        dy = jnp.where(which == 0, -ahead, jnp.where(which == 1, ahead, 0))
        dz = jnp.where(which == 0, -ahead, jnp.where(which == 1, 0, ahead))
        return remote(
            g_s.at[n, which],
            g_r.at[n, which],
            g_ss.at[n, which],
            g_rs.at[n, which],
            dp=near(dy, dz),
        )

    def gradient(n, kind, row_ref):
        @pl.loop(0, 4)
        def _(which):
            i = jnp.where((which == 1) | (which == 3), odd, 1 - odd)
            j = jnp.where(which >= 2, odd, 1 - odd)
            turned = rank_rows(kind, i, j).astype(F32).T.astype(BF)
            value = mm(turned, served(row_ref, i, j)) * (1.0 / seq_len)
            if n == 1:
                value = value * factor_at(owner_of(i, j), width)
            g_own[n] = value
            g_s[n, which] = value.astype(BF)

            @pl.when(which < 3)
            def _():
                g_copy(n, which).start()

    gradient(1, 0, c_r)

    @pl.loop(0, rows // 64)
    def _(n):
        row = iota((64, 128), 0) + n * 64
        mine = jnp.where(slot_l == (row // seq_len).astype(F32), lane_l, 0.0)
        place = jnp.sum(mine, 1, keepdims=True) * seq_len + (row % seq_len).astype(F32)[:, :1]
        slot_hot[span(n * 64, 64), :] = jnp.where(
            iota((64, 2 * rows), 1).astype(F32) == place, 1.0, 0.0
        ).astype(BF)

    sum_parts(1, factor_at(owner_of(t // 4, (t // 2) % 2), ranks.shape[3]))
    for way in range(2):
        hop_copy(way).wait_recv()
        send_ring(way, way)
    gathered(1)
    gradient(0, 1, x_r)

    sib_copy(3).wait_recv()
    for m in range(len(MESSAGES)):
        ad_copy(m).wait_recv()

    @pl.loop(0, tiles)
    def _(n):
        at = span(n * TILE, TILE)
        back = ad_r[:, :, :, at].reshape(2 * rows, TILE)
        hold[2, :, at] = hold[2, :, at] + sib_r[3, :, at].astype(F32) + mm(slot_hot[...], back)

    for way in range(2):
        for part in range(2):
            ring_copy(way, part).wait_recv()

    for part in range(2):

        def put(at, to):
            out_v[at] = (
                hold[2, at] + ring_r[0, part, to].astype(F32) + ring_r[1, part, to].astype(F32)
            ).astype(BF)

        half_rows(part, put)
    stores = [pltpu.make_async_copy(out_v, out_ref, out_sem.at[2])]
    stores[0].start()

    for n, g_ref in ((1, gb_ref), (0, ga_ref)):

        @pl.loop(0, 3)
        def _(which):
            remote(
                g_s.at[n, which], g_r.at[n, which], g_ss.at[n, which], g_rs.at[n, which], dp=me
            ).wait_recv()

        @pl.loop(0, g_own.shape[1] // 32)
        def _(k):
            at = span(k * 32, 32)
            total = g_own[n, at]
            for which in range(3):
                total = total + g_r[n, which, at].astype(F32)
            g_own[n, at] = total

        stores.append(pltpu.make_async_copy(g_own.at[n], g_ref, out_sem.at[n]))
        stores[-1].start()

    for k in range(DP - 1):
        facts_copy(k).wait_send()
        tok_copy(0, k).wait_send()
        tok_copy(1, k).wait_send()

    for n in range(2):
        for which in range(3):
            fac_copy(which, n).wait_send()
    for m in range(len(MESSAGES)):
        for h in range(2):
            x_copy(h, m).wait_send()
        c_copy(m).wait_send()
        ad_copy(m).wait_send()
    for j in (2, 3):
        sib_copy(j).wait_send()
    for way in range(2):
        hop_copy(way).wait_send()
        for part in range(2):
            ring_copy(way, part).wait_send()
    for kind in range(2):

        @pl.loop(1, TENSOR)
        def _(k):
            part_copy(kind, k).wait_send()
            gath_copy(kind, k).wait_send()

        @pl.loop(0, 3)
        def _(which):
            g_copy(kind, which).wait_send()

    for store in stores:
        store.wait()


def finish(out_ref, gb_ref, ga_ref, out_to, gb_to, ga_to, out_v, gb_v, ga_v, turned_v, sem):
    names = ((ga_ref, ga_v, turned_v, ga_to), (gb_ref, gb_v, gb_v, gb_to), (out_ref, out_v, out_v, out_to))
    loads = [pltpu.make_async_copy(src, held, sem.at[0, n]) for n, (src, held, _, _) in enumerate(names)]
    stores = [pltpu.make_async_copy(held, dst, sem.at[1, n]) for n, (_, _, held, dst) in enumerate(names)]
    for load in loads:
        load.start()
    loads[0].wait()
    turned_v[...] = ga_v[...].T
    stores[0].start()
    for n in (1, 2):
        loads[n].wait()
        stores[n].start()
    for store in stores:
        store.wait()


def on_device(
    tokens,
    destinations,
    counts,
    sequence_job_ids,
    job_owner_slot,
    rank_per_job,
    weight,
    input_factor_table,
    output_factor_table,
    cotangent,
):
    slot_count, seq_len, width = tokens.shape
    max_rank = input_factor_table.shape[2]
    rows = slot_count * seq_len
    anywhere = pl.BlockSpec(memory_space=pl.ANY)
    smem = pl.BlockSpec(memory_space=pltpu.SMEM)
    dma = pltpu.SemaphoreType.DMA
    served = (2, 2, RING, 64, width)
    lanes = (RING, RING, 64, width)
    out, ga, gb = pl.pallas_call(
        kernel,
        out_shape=(
            jax.ShapeDtypeStruct((rows, width), BF),
            jax.ShapeDtypeStruct((max_rank, width), F32),
            jax.ShapeDtypeStruct((max_rank, width), F32),
        ),
        in_specs=[smem] * 5 + [anywhere] * 5,
        out_specs=(anywhere,) * 3,
        scratch_shapes=[
            pltpu.VMEM(tokens.shape, BF),
            pltpu.VMEM((rows, width), BF),
            pltpu.VMEM(input_factor_table.shape, BF),
            pltpu.VMEM(output_factor_table.shape, BF),
            pltpu.VMEM((rows, width), BF),
            pltpu.VMEM((DP, seq_len, width), BF),
            pltpu.VMEM((DP, seq_len, width), BF),
            pltpu.VMEM((DP, 8, 128), jnp.int32),
            pltpu.VMEM((DP, 8, 128), jnp.int32),
            pltpu.VMEM((rows, rows), BF),
            pltpu.VMEM((2 * rows, rows), BF),
            pltpu.VMEM((2 * rows, rows), BF),
            pltpu.VMEM((rows, 2 * rows), BF),
            pltpu.VMEM((rows, width), BF),
            pltpu.VMEM(lanes, BF),
            pltpu.VMEM(served, BF),
            pltpu.VMEM(lanes, BF),
            pltpu.VMEM(served, BF),
            pltpu.VMEM((2, 2, width, max_rank), BF),
            pltpu.VMEM((2, 2, max_rank, width), BF),
            pltpu.VMEM((W_SLOTS, width, width), BF),
            pltpu.VMEM((2, rows, width), BF),
            pltpu.VMEM((4, rows, width), BF),
            pltpu.VMEM((3, rows, width), F32),
            pltpu.VMEM((2, rows // 2, width), BF),
            pltpu.VMEM((2, rows // 2, width), BF),
            pltpu.VMEM((2, 2, rows // 2, width), BF),
            pltpu.VMEM((2, 2, rows // 2, width), BF),
            pltpu.VMEM((2, TENSOR, 128, max_rank), BF),
            pltpu.VMEM((2, TENSOR, 128, max_rank), BF),
            pltpu.VMEM((2, TENSOR, 128, max_rank), BF),
            pltpu.VMEM(served, BF),
            pltpu.VMEM(lanes, BF),
            pltpu.VMEM((2, max_rank, width), F32),
            pltpu.VMEM((2, 4, max_rank, width), BF),
            pltpu.VMEM((2, 3, max_rank, width), BF),
            dma((4,)),
            dma((3,)),
            dma((W_SLOTS,)),
            dma((DP - 1,)),
            dma((DP - 1,)),
            dma((2, DP - 1)),
            dma((2, DP - 1)),
            dma((3, 2)),
            dma((2, 2, 2)),
            dma((8,)),
            dma((8,)),
            dma((2, 8)),
            dma((2, 8)),
            dma((2,)),
            dma((4,)),
            dma((2,)),
            dma((2,)),
            dma((2, 2)),
            dma((2, 2)),
            dma((2, TENSOR - 1)),
            dma((2, TENSOR - 1)),
            dma((2, TENSOR - 1)),
            dma((2, TENSOR - 1)),
            dma((8,)),
            dma((8,)),
            dma((2, 3)),
            dma((2, 3)),
        ],
        compiler_params=pltpu.CompilerParams(
            collective_id=0, has_side_effects=True, vmem_limit_bytes=58 * 2**20
        ),
    )(
        destinations,
        counts,
        sequence_job_ids,
        job_owner_slot,
        rank_per_job,
        tokens,
        cotangent.reshape(rows, width),
        input_factor_table,
        output_factor_table,
        weight,
    )
    out, gb, ga = pl.pallas_call(
        finish,
        out_shape=(
            jax.ShapeDtypeStruct((rows, width), BF),
            jax.ShapeDtypeStruct((max_rank, width), F32),
            jax.ShapeDtypeStruct((width, max_rank), F32),
        ),
        in_specs=[anywhere] * 3,
        out_specs=(anywhere,) * 3,
        scratch_shapes=[
            pltpu.VMEM((rows, width), BF),
            pltpu.VMEM((max_rank, width), F32),
            pltpu.VMEM((max_rank, width), F32),
            pltpu.VMEM((width, max_rank), F32),
            dma((2, 3)),
        ],
    )(out, gb, ga)
    return out.reshape(slot_count, seq_len, width), ga[None], gb[None]


def solution(mesh):
    in_specs = (
        P("dp", None, "tensor"),
        P("dp"),
        P("dp"),
        P("dp"),
        P(),
        P(),
        P("tensor", None),
        P("dp", "tensor", None),
        P("dp", None, "tensor"),
        P("dp", None, "tensor"),
    )
    out_specs = (P("dp", None, "tensor"), P("dp", "tensor", None), P("dp", None, "tensor"))
    return jax.shard_map(
        on_device, mesh=mesh, in_specs=in_specs, out_specs=out_specs, check_vma=False
    )
```

```python
import jax
import jax.numpy as jnp
from jax import lax
from jax.experimental import pallas as pl
from jax.experimental.pallas import tpu as pltpu
from jax.sharding import PartitionSpec as P

BF = jnp.bfloat16
F32 = jnp.float32
RING = 4
DP = RING * RING
TENSOR = 2 * RING
TILE = 256
W_SLOTS = 3
MOVE, PLACE = (0, 0, -1, 1), (0, 1, 1, 0)
BOTH = slice(0, 2)
MESSAGES = ((2, BOTH), (BOTH, 2), (3, BOTH), (BOTH, 3), (2, 2), (3, 3), (2, 3), (3, 2))
NEIGHBOURS = ((0, 1), (1, 0), (0, 3), (3, 0), (1, 1), (3, 3), (1, 3), (3, 1))
OTHERS = NEIGHBOURS + ((0, 2), (2, 0), (2, 1), (1, 2), (2, 3), (3, 2), (2, 2))


def mm(a, b):
    return jnp.dot(a, b, preferred_element_type=F32)


def kernel(
    dest_ref,
    count_ref,
    job_ref,
    owner_ref,
    rank_ref,
    tok_ref,
    cot_ref,
    a_ref,
    b_ref,
    w_ref,
    out_ref,
    ga_ref,
    gb_ref,
    tok_v,
    cot_v,
    a_v,
    b_v,
    out_v,
    tok_s,
    tok_r,
    facts_s,
    facts_r,
    place_hot,
    x_hot,
    c_hot,
    slot_hot,
    xs,
    x_s,
    x_r,
    c_s,
    c_r,
    fa,
    fb,
    wbuf,
    sib_s,
    sib_r,
    hold,
    hop_s,
    hop_r,
    ring_s,
    ring_r,
    part_s,
    part_r,
    ranks,
    ad_s,
    ad_r,
    g_own,
    g_s,
    g_r,
    in_sem,
    out_sem,
    w_sem,
    facts_ss,
    facts_rs,
    tok_ss,
    tok_rs,
    fac_ss,
    fac_rs,
    c_ss,
    c_rs,
    x_ss,
    x_rs,
    sib_ss,
    sib_rs,
    tile_ss,
    tile_rs,
    hop_ss,
    hop_rs,
    ring_ss,
    ring_rs,
    part_ss,
    part_rs,
    gath_ss,
    gath_rs,
    ad_ss,
    ad_rs,
    g_ss,
    g_rs,
):
    seq_len, width = tok_ref.shape[1:]
    rows = DP * seq_len
    half = rows // 2
    me = lax.axis_index("dp")
    t = lax.axis_index("tensor")
    y, z = me // RING, me % RING
    x, c = t // 2, t % 2
    odd = (y + z) % 2
    ahead = 1 - 2 * odd
    others = ((1 - odd, 1 - odd), (odd, 1 - odd), (1 - odd, odd))
    tiles = width // TILE
    wide_half = width // 2

    def remote(src, dst, send, recv, **where):
        return pltpu.make_async_remote_copy(
            src_ref=src,
            dst_ref=dst,
            send_sem=send,
            recv_sem=recv,
            device_id=where,
            device_id_type=pl.DeviceIdType.MESH,
        )

    def iota(shape, axis):
        return lax.broadcasted_iota(jnp.int32, shape, axis)

    def near(dy, dz):
        return (y + dy + RING) % RING * RING + (z + dz + RING) % RING

    def owner_of(i, j):
        first, second = (y - i + RING) % RING, (z - j + RING) % RING
        shift = (first + second) % 2
        return (first + shift) % RING * RING + (second + shift) % RING

    def rank_at(owner):
        total = jnp.int32(0)
        for j in range(DP):
            total = total + jnp.where(owner_ref[j] == owner, rank_ref[j], 0)
        return total

    def factor_at(owner, columns):
        return 32.0 / jnp.full((1, columns), rank_at(owner).astype(F32), F32)

    def span(start, size):
        return pl.ds(pl.multiple_of(start, size), size)

    loads = [
        pltpu.make_async_copy(src, dst, in_sem.at[n])
        for n, (src, dst) in enumerate(((tok_ref, tok_v), (a_ref, a_v), (b_ref, b_v), (cot_ref, cot_v)))
    ]
    for load in loads:
        load.start()

    barrier = pltpu.get_barrier_semaphore()

    @pl.loop(1, DP)
    def _(k):
        pl.semaphore_signal(
            barrier, inc=1, device_id={"dp": (me + k) % DP}, device_id_type=pl.DeviceIdType.MESH
        )

    @pl.loop(1, TENSOR)
    def _(k):
        pl.semaphore_signal(
            barrier, inc=1, device_id={"tensor": (t + k) % TENSOR}, device_id_type=pl.DeviceIdType.MESH
        )

    def w_copy(i):
        j = i // 2
        block = (x + jnp.where(j == 0, 2, jnp.where(j == 1, 1, jnp.where(j == 2, 3, 0)))) % RING * 2
        block = block + (c + 1 - i % 2) % 2
        return pltpu.make_async_copy(
            w_ref.at[:, span(block * width, width)], wbuf.at[i % W_SLOTS], w_sem.at[i % W_SLOTS]
        )

    for i in range(W_SLOTS):
        w_copy(jnp.int32(i)).start()

    def chosen(to):
        index = jnp.int32(0)
        for i in range(DP):
            index = jnp.where(lax.shift_right_logical(dest_ref[i], 4) == to, i, index)
        return index

    @pl.loop(0, DP)
    def _(to):
        index = chosen(to)
        owner = owner_ref[job_ref[index]]
        oy, oz = lax.shift_right_logical(owner, 2), owner & 3
        shift = (oy + oz) & 1
        dy, dz = (to // RING + RING - oy + shift) & 3, (to % RING + RING - oz + shift) & 3
        base = (dy * RING + dz) * 2
        row = iota((8, 128), 0)
        facts_s[to] = jnp.where(
            row == 0, dest_ref[index] & 15, jnp.where(row == 1, count_ref[index], base)
        )

    facts_r[me] = facts_s[me]
    loads[0].wait()

    @pl.loop(0, DP)
    def _(to):
        tok_s[to] = tok_v[chosen(to)]

    tok_r[me] = tok_s[me]

    pl.semaphore_wait(barrier, DP - 1 + TENSOR - 1)

    def facts_copy(k):
        to = near(*OTHERS[k])
        return remote(facts_s.at[to], facts_r.at[me], facts_ss.at[k], facts_rs.at[k], dp=to)

    def tok_copy(h, k):
        to, columns = near(*OTHERS[k]), span(h * wide_half, wide_half)
        return remote(
            tok_s.at[to, :, columns],
            tok_r.at[me, :, columns],
            tok_ss.at[h, k],
            tok_rs.at[h, k],
            dp=to,
        )

    def fac_copy(which, n):
        table = (fa, fb)[n]
        there = ((1 - odd, odd), (odd, 1 - odd), (1 - odd, 1 - odd))[which]
        to = (near(ahead, 0), near(0, ahead), near(ahead, ahead))[which]
        return remote(
            table.at[odd, odd], table.at[there], fac_ss.at[which, n], fac_rs.at[there + (n,)], dp=to
        )

    def fac_wait(n):
        for there in others:
            held = (fa, fb)[n].at[there]
            remote(held, held, fac_ss.at[0, n], fac_rs.at[there + (n,)], dp=me).wait_recv()

    for k in range(DP - 1):
        facts_copy(k).start()

    @pl.loop(0, 2)
    def _(h):
        for k in range(DP - 1):
            tok_copy(h, k).start()

    my_rank = rank_at(me)
    loads[1].wait()

    @pl.loop(0, width // 128)
    def _(n):
        at = span(n * 128, 128)
        kept = iota((128, a_v.shape[2]), 1) < my_rank
        fa[odd, odd, at, :] = jnp.where(kept, a_v[0, at, :].astype(F32), 0.0).astype(BF)

    for which in range(3):
        fac_copy(which, 0).start()
    for k in range(DP - 1):
        facts_copy(k).wait_recv()

    slot_c = facts_r[:, 0, :].astype(F32)
    live_c = facts_r[:, 1, :].astype(F32)
    base_c = facts_r[:, 2, :].astype(F32)
    square = (DP, 128)
    diagonal = iota(square, 0) == iota(square, 1)
    slot_l = jnp.sum(jnp.where(diagonal, slot_c, 0.0), 0, keepdims=True)
    base_l = jnp.sum(jnp.where(diagonal, base_c, 0.0), 0, keepdims=True)
    earlier = (base_l == base_c) & (slot_l < slot_c) & (iota(square, 1) < DP)
    turn_c = jnp.sum(jnp.where(earlier, 1.0, 0.0), 1, keepdims=True)
    lane_c = base_c + turn_c
    lane_l = jnp.sum(jnp.where(diagonal, lane_c, 0.0), 0, keepdims=True)
    wide = (DP, rows)
    seq_of = iota(wide, 1) // seq_len
    slot_1, live_1, lane_1 = slot_c[:, :1], live_c[:, :1], lane_c[:, :1]
    in_slot = slot_1 == seq_of.astype(F32)
    in_order = iota(wide, 0) == seq_of
    position = (iota((1, rows), 1) % seq_len).astype(F32)

    def spread(where, value):
        return jnp.sum(jnp.where(where, value, 0.0), 0, keepdims=True)

    live = position < spread(in_order, live_1)
    c_row = spread(in_slot, lane_1) * seq_len + position
    x_row = jnp.where(live, spread(in_order, lane_1) * seq_len + position, -1.0)
    slot_row = jnp.where(live, spread(in_order, slot_1) * seq_len + position, -1.0)

    def build(hot, wanted):
        @pl.loop(0, hot.shape[0] // 64)
        def _(n):
            row = (iota((64, rows), 0) + n * 64).astype(F32)
            hot[span(n * 64, 64), :] = jnp.where(row == wanted, 1.0, 0.0).astype(BF)

    build(x_hot, x_row)
    build(place_hot, slot_row)

    lane_shape = (RING, RING, 2 * seq_len)

    def lane_place(dy, dz):
        row = PLACE[dy] if dy != BOTH else BOTH
        column = PLACE[dz] if dz != BOTH else BOTH
        return row, column, (dy != BOTH) * 2 + (dz != BOTH)

    def lane_move(dy, dz):
        return (MOVE[dy] if dy != BOTH else 0, MOVE[dz] if dz != BOTH else 0)

    def x_copy(h, m):
        message, columns = MESSAGES[m], span(h * wide_half, wide_half)
        return remote(
            x_s.at[message + (slice(None), columns)],
            x_r.at[lane_place(*message) + (slice(None), columns)],
            x_ss.at[h, m],
            x_rs.at[h, m],
            dp=near(*lane_move(*message)),
        )

    def c_copy(m):
        message = MESSAGES[m]
        return remote(
            c_s.at[message],
            c_r.at[lane_place(*message)],
            c_ss.at[m],
            c_rs.at[m],
            dp=near(*lane_move(*message)),
        )

    @pl.loop(0, 2)
    def _(h):
        for k in range(DP - 1):
            tok_copy(h, k).wait_recv()

        @pl.loop(0, tiles // 2)
        def _(n):
            at = span(h * wide_half + n * TILE, TILE)
            landed = tok_r[:, :, at].reshape(rows, TILE)
            x_s[:, :, :, at] = mm(x_hot[...], landed).astype(BF).reshape(lane_shape + (TILE,))

        for m in range(len(MESSAGES)):
            x_copy(h, m).start()

        @pl.loop(0, tiles // 2)
        def _(n):
            at = span(h * wide_half + n * TILE, TILE)
            xs[:, at] = mm(place_hot[...], tok_r[:, :, at].reshape(rows, TILE)).astype(BF)

    loads[2].wait()

    @pl.loop(0, width // 128)
    def _(n):
        at = span(n * 128, 128)
        kept = iota((b_v.shape[1], 128), 0) < my_rank
        fb[odd, odd, :, at] = jnp.where(kept, b_v[0, :, at].astype(F32), 0.0).astype(BF)

    for which in range(3):
        fac_copy(which, 1).start()
    build(c_hot, c_row)
    loads[3].wait()

    @pl.loop(0, tiles)
    def _(n):
        at = span(n * TILE, TILE)
        c_s[:, :, :, at] = mm(c_hot[...], cot_v[:, at]).astype(BF).reshape(lane_shape + (TILE,))

    for m in range(len(MESSAGES)):
        c_copy(m).start()
    x_r[:, :, 0] = x_s[BOTH, BOTH]
    c_r[:, :, 0] = c_s[BOTH, BOTH]

    def sib_copy(j):
        return remote(
            sib_s.at[j % 2], sib_r.at[j], sib_ss.at[j % 2], sib_rs.at[j], tensor=x * 2 + (1 - c)
        )

    right, left = ((x + 1) % RING) * 2 + c, ((x + 3) % RING) * 2 + c

    def hop_copy(way, n):
        at = span(n * TILE, TILE)
        return remote(
            hop_s.at[way, :, at],
            hop_r.at[way, :, at],
            hop_ss.at[way, n],
            hop_rs.at[way, n],
            tensor=(right, left)[way],
        )

    def sib_tile(n):
        at = span(n * TILE, TILE)
        return remote(
            sib_s.at[0, :, at], sib_r.at[0, :, at], tile_ss.at[n], tile_rs.at[n], tensor=x * 2 + (1 - c)
        )

    def ring_copy(way, part):
        return remote(
            ring_s.at[way, part],
            ring_r.at[way, part],
            ring_ss.at[way, part],
            ring_rs.at[way, part],
            tensor=(right, left)[way],
        )

    def half_rows(part, put):
        @pl.loop(0, half // 32)
        def _(n):
            put(span(part * half + n * 32, 32), span(n * 32, 32))

    def send_hop(n):
        at = span(n * TILE, TILE)
        sib_tile(n).wait_recv()
        for way in range(2):
            part = slice(way * half, (way + 1) * half)
            hop_s[way, :, at] = (hold[0, part, at] + sib_r[0, part, at].astype(F32)).astype(BF)
            hop_copy(way, n).start()

    def send_ring(way, part):
        def put(at, to):
            value = hold[1 - way, at] + sib_r[1 + way, at].astype(F32)
            if way == part:
                value = value + hop_r[way, to].astype(F32)
            ring_s[way, part, to] = value.astype(BF)

        half_rows(part, put)
        ring_copy(way, part).start()

    def part_copy(kind, k):
        to = (t + k) % TENSOR
        return remote(
            part_s.at[kind, to],
            part_r.at[kind, k],
            part_ss.at[kind, k - 1],
            part_rs.at[kind, k - 1],
            tensor=to,
        )

    def gath_copy(kind, k):
        to = (t + k) % TENSOR
        held = ranks.at[kind, t]
        return remote(held, held, gath_ss.at[kind, k - 1], gath_rs.at[kind, k - 1], tensor=to)

    def served(ref, i, j):
        return ref[i, j].reshape(RING * 64, width)

    def send_parts(kind, make):
        @pl.loop(0, 4)
        def _(q):
            value = make(q // 2, q % 2).astype(BF)
            part_s[kind, 2 * q] = value[:128]
            part_s[kind, 2 * q + 1] = value[128:]

        @pl.loop(1, TENSOR)
        def _(k):
            part_copy(kind, k).start()

        part_r[kind, 0] = part_s[kind, t]

    def sum_parts(kind, scale):
        @pl.loop(1, TENSOR)
        def _(k):
            part_copy(kind, k).wait_recv()

        total = part_r[kind, 0].astype(F32)
        for k in range(1, TENSOR):
            total = total + part_r[kind, k].astype(F32)
        ranks[kind, t] = (total if scale is None else total * scale).astype(BF)

        @pl.loop(1, TENSOR)
        def _(k):
            gath_copy(kind, k).start()

    def gathered(kind):
        @pl.loop(1, TENSOR)
        def _(k):
            held = ranks.at[kind, (t + TENSOR - k) % TENSOR]
            remote(held, held, gath_ss.at[kind, k - 1], gath_rs.at[kind, k - 1], tensor=t).wait_recv()

    def rank_rows(kind, i, j):
        return ranks[kind, pl.ds(i * 4 + j * 2, 2)].reshape(RING * 64, ranks.shape[3])

    for i in range(2):
        w_copy(jnp.int32(i)).wait()

    @pl.loop(0, tiles)
    def _(n):
        at = span(n * TILE, TILE)
        sib_s[0, :, at] = mm(xs[...], wbuf[0, :, at]).astype(BF)
        sib_tile(n).start()
        hold[0, :, at] = mm(xs[...], wbuf[1, :, at])

        @pl.when(n > 0)
        def _():
            send_hop(n - 1)

    for i in range(2):
        w_copy(jnp.int32(i + W_SLOTS)).start()
    send_hop(jnp.int32(tiles - 1))

    @pl.loop(1, 4)
    def _(j):
        w_copy(2 * j).wait()

        @pl.when(j == 2)
        def _():
            for n in range(tiles):
                sib_tile(n).wait_send()

        @pl.when(j == 3)
        def _():
            sib_copy(1).wait_send()

        @pl.loop(0, tiles)
        def _(n):
            at = span(n * TILE, TILE)
            sib_s[j % 2, :, at] = mm(xs[...], wbuf[(2 * j) % W_SLOTS, :, at]).astype(BF)

        sib_copy(j).start()

        @pl.when(2 * j + W_SLOTS < 8)
        def _():
            w_copy(2 * j + W_SLOTS).start()

        @pl.when(j == 2)
        def _():
            sib_copy(1).wait_recv()
            send_ring(0, 1)

        @pl.when(j == 3)
        def _():
            sib_copy(2).wait_recv()
            send_ring(1, 0)

        w_copy(2 * j + 1).wait()

        @pl.loop(0, tiles)
        def _(n):
            at = span(n * TILE, TILE)
            hold[jnp.where(j == 3, 2, j % 2), :, at] = mm(xs[...], wbuf[(2 * j + 1) % W_SLOTS, :, at])

        @pl.when(2 * j + 1 + W_SLOTS < 8)
        def _():
            w_copy(2 * j + 1 + W_SLOTS).start()

        @pl.when(j == 2)
        def _():
            fac_wait(0)

            @pl.loop(0, 2)
            def _(h):
                for m in range(len(MESSAGES)):
                    x_copy(h, m).wait_recv()

            send_parts(0, lambda i, k: mm(served(x_r, i, k), fa[i, k]))

    sum_parts(0, None)

    def ad_copy(m):
        message = MESSAGES[m]
        dy, dz = lane_move(*message)
        return remote(
            ad_s.at[lane_place(*message)],
            ad_r.at[message],
            ad_ss.at[m],
            ad_rs.at[m],
            dp=near(-dy, -dz),
        )

    fac_wait(1)
    gathered(0)

    @pl.loop(0, 4)
    def _(q):
        i, j = q // 2, q % 2
        value = mm(rank_rows(0, i, j), fb[i, j]) * factor_at(owner_of(i, j), width)
        ad_s[i, j] = value.astype(BF).reshape(RING, 64, width)

    for m in range(len(MESSAGES)):
        ad_copy(m).start()
    ad_r[BOTH, BOTH] = ad_s[:, :, 0]

    for m in range(len(MESSAGES)):
        c_copy(m).wait_recv()
    send_parts(
        1,
        lambda i, j: lax.dot_general(
            served(c_r, i, j), fb[i, j], (((1,), (1,)), ((), ())), preferred_element_type=F32
        ),
    )

    def g_copy(n, which):
        dy = jnp.where(which == 0, -ahead, jnp.where(which == 1, ahead, 0))
        dz = jnp.where(which == 0, -ahead, jnp.where(which == 1, 0, ahead))
        return remote(
            g_s.at[n, which],
            g_r.at[n, which],
            g_ss.at[n, which],
            g_rs.at[n, which],
            dp=near(dy, dz),
        )

    def gradient(n, kind, row_ref):
        @pl.loop(0, 4)
        def _(which):
            i = jnp.where((which == 1) | (which == 3), odd, 1 - odd)
            j = jnp.where(which >= 2, odd, 1 - odd)
            turned = rank_rows(kind, i, j).astype(F32).T.astype(BF)
            value = mm(turned, served(row_ref, i, j)) * (1.0 / seq_len)
            if n == 1:
                value = value * factor_at(owner_of(i, j), width)
            g_own[n] = value
            g_s[n, which] = value.astype(BF)

            @pl.when(which < 3)
            def _():
                g_copy(n, which).start()

    gradient(1, 0, c_r)

    @pl.loop(0, rows // 64)
    def _(n):
        row = iota((64, 128), 0) + n * 64
        mine = jnp.where(slot_l == (row // seq_len).astype(F32), lane_l, 0.0)
        place = jnp.sum(mine, 1, keepdims=True) * seq_len + (row % seq_len).astype(F32)[:, :1]
        slot_hot[span(n * 64, 64), :] = jnp.where(
            iota((64, 2 * rows), 1).astype(F32) == place, 1.0, 0.0
        ).astype(BF)

    sum_parts(1, factor_at(owner_of(t // 4, (t // 2) % 2), ranks.shape[3]))
    for way in range(2):
        for n in range(tiles):
            hop_copy(way, n).wait_recv()
        send_ring(way, way)
    gathered(1)
    gradient(0, 1, x_r)

    sib_copy(3).wait_recv()
    for m in range(len(MESSAGES)):
        ad_copy(m).wait_recv()

    @pl.loop(0, tiles)
    def _(n):
        at = span(n * TILE, TILE)
        back = ad_r[:, :, :, at].reshape(2 * rows, TILE)
        hold[2, :, at] = hold[2, :, at] + sib_r[3, :, at].astype(F32) + mm(slot_hot[...], back)

    for way in range(2):
        for part in range(2):
            ring_copy(way, part).wait_recv()

    for part in range(2):

        def put(at, to):
            out_v[at] = (
                hold[2, at] + ring_r[0, part, to].astype(F32) + ring_r[1, part, to].astype(F32)
            ).astype(BF)

        half_rows(part, put)
    stores = [pltpu.make_async_copy(out_v, out_ref, out_sem.at[2])]
    stores[0].start()

    for n, g_ref in ((1, gb_ref), (0, ga_ref)):

        @pl.loop(0, 3)
        def _(which):
            remote(
                g_s.at[n, which], g_r.at[n, which], g_ss.at[n, which], g_rs.at[n, which], dp=me
            ).wait_recv()

        @pl.loop(0, g_own.shape[1] // 32)
        def _(k):
            at = span(k * 32, 32)
            total = g_own[n, at]
            for which in range(3):
                total = total + g_r[n, which, at].astype(F32)
            g_own[n, at] = total

        stores.append(pltpu.make_async_copy(g_own.at[n], g_ref, out_sem.at[n]))
        stores[-1].start()

    for k in range(DP - 1):
        facts_copy(k).wait_send()
        tok_copy(0, k).wait_send()
        tok_copy(1, k).wait_send()

    for n in range(2):
        for which in range(3):
            fac_copy(which, n).wait_send()
    for m in range(len(MESSAGES)):
        for h in range(2):
            x_copy(h, m).wait_send()
        c_copy(m).wait_send()
        ad_copy(m).wait_send()
    for j in (2, 3):
        sib_copy(j).wait_send()
    for way in range(2):
        for n in range(tiles):
            hop_copy(way, n).wait_send()
        for part in range(2):
            ring_copy(way, part).wait_send()
    for kind in range(2):

        @pl.loop(1, TENSOR)
        def _(k):
            part_copy(kind, k).wait_send()
            gath_copy(kind, k).wait_send()

        @pl.loop(0, 3)
        def _(which):
            g_copy(kind, which).wait_send()

    for store in stores:
        store.wait()


def finish(out_ref, gb_ref, ga_ref, out_to, gb_to, ga_to, out_v, gb_v, ga_v, turned_v, sem):
    names = ((ga_ref, ga_v, turned_v, ga_to), (gb_ref, gb_v, gb_v, gb_to), (out_ref, out_v, out_v, out_to))
    loads = [pltpu.make_async_copy(src, held, sem.at[0, n]) for n, (src, held, _, _) in enumerate(names)]
    stores = [pltpu.make_async_copy(held, dst, sem.at[1, n]) for n, (_, _, held, dst) in enumerate(names)]
    for load in loads:
        load.start()
    loads[0].wait()
    turned_v[...] = ga_v[...].T
    stores[0].start()
    for n in (1, 2):
        loads[n].wait()
        stores[n].start()
    for store in stores:
        store.wait()


def on_device(
    tokens,
    destinations,
    counts,
    sequence_job_ids,
    job_owner_slot,
    rank_per_job,
    weight,
    input_factor_table,
    output_factor_table,
    cotangent,
):
    slot_count, seq_len, width = tokens.shape
    max_rank = input_factor_table.shape[2]
    rows = slot_count * seq_len
    anywhere = pl.BlockSpec(memory_space=pl.ANY)
    smem = pl.BlockSpec(memory_space=pltpu.SMEM)
    dma = pltpu.SemaphoreType.DMA
    served = (2, 2, RING, 64, width)
    lanes = (RING, RING, 64, width)
    out, ga, gb = pl.pallas_call(
        kernel,
        out_shape=(
            jax.ShapeDtypeStruct((rows, width), BF),
            jax.ShapeDtypeStruct((max_rank, width), F32),
            jax.ShapeDtypeStruct((max_rank, width), F32),
        ),
        in_specs=[smem] * 5 + [anywhere] * 5,
        out_specs=(anywhere,) * 3,
        scratch_shapes=[
            pltpu.VMEM(tokens.shape, BF),
            pltpu.VMEM((rows, width), BF),
            pltpu.VMEM(input_factor_table.shape, BF),
            pltpu.VMEM(output_factor_table.shape, BF),
            pltpu.VMEM((rows, width), BF),
            pltpu.VMEM((DP, seq_len, width), BF),
            pltpu.VMEM((DP, seq_len, width), BF),
            pltpu.VMEM((DP, 8, 128), jnp.int32),
            pltpu.VMEM((DP, 8, 128), jnp.int32),
            pltpu.VMEM((rows, rows), BF),
            pltpu.VMEM((2 * rows, rows), BF),
            pltpu.VMEM((2 * rows, rows), BF),
            pltpu.VMEM((rows, 2 * rows), BF),
            pltpu.VMEM((rows, width), BF),
            pltpu.VMEM(lanes, BF),
            pltpu.VMEM(served, BF),
            pltpu.VMEM(lanes, BF),
            pltpu.VMEM(served, BF),
            pltpu.VMEM((2, 2, width, max_rank), BF),
            pltpu.VMEM((2, 2, max_rank, width), BF),
            pltpu.VMEM((W_SLOTS, width, width), BF),
            pltpu.VMEM((2, rows, width), BF),
            pltpu.VMEM((4, rows, width), BF),
            pltpu.VMEM((3, rows, width), F32),
            pltpu.VMEM((2, rows // 2, width), BF),
            pltpu.VMEM((2, rows // 2, width), BF),
            pltpu.VMEM((2, 2, rows // 2, width), BF),
            pltpu.VMEM((2, 2, rows // 2, width), BF),
            pltpu.VMEM((2, TENSOR, 128, max_rank), BF),
            pltpu.VMEM((2, TENSOR, 128, max_rank), BF),
            pltpu.VMEM((2, TENSOR, 128, max_rank), BF),
            pltpu.VMEM(served, BF),
            pltpu.VMEM(lanes, BF),
            pltpu.VMEM((2, max_rank, width), F32),
            pltpu.VMEM((2, 4, max_rank, width), BF),
            pltpu.VMEM((2, 3, max_rank, width), BF),
            dma((4,)),
            dma((3,)),
            dma((W_SLOTS,)),
            dma((DP - 1,)),
            dma((DP - 1,)),
            dma((2, DP - 1)),
            dma((2, DP - 1)),
            dma((3, 2)),
            dma((2, 2, 2)),
            dma((8,)),
            dma((8,)),
            dma((2, 8)),
            dma((2, 8)),
            dma((2,)),
            dma((4,)),
            dma((4,)),
            dma((4,)),
            dma((2, 4)),
            dma((2, 4)),
            dma((2, 2)),
            dma((2, 2)),
            dma((2, TENSOR - 1)),
            dma((2, TENSOR - 1)),
            dma((2, TENSOR - 1)),
            dma((2, TENSOR - 1)),
            dma((8,)),
            dma((8,)),
            dma((2, 3)),
            dma((2, 3)),
        ],
        compiler_params=pltpu.CompilerParams(
            collective_id=0, has_side_effects=True, vmem_limit_bytes=58 * 2**20
        ),
    )(
        destinations,
        counts,
        sequence_job_ids,
        job_owner_slot,
        rank_per_job,
        tokens,
        cotangent.reshape(rows, width),
        input_factor_table,
        output_factor_table,
        weight,
    )
    out, gb, ga = pl.pallas_call(
        finish,
        out_shape=(
            jax.ShapeDtypeStruct((rows, width), BF),
            jax.ShapeDtypeStruct((max_rank, width), F32),
            jax.ShapeDtypeStruct((width, max_rank), F32),
        ),
        in_specs=[anywhere] * 3,
        out_specs=(anywhere,) * 3,
        scratch_shapes=[
            pltpu.VMEM((rows, width), BF),
            pltpu.VMEM((max_rank, width), F32),
            pltpu.VMEM((max_rank, width), F32),
            pltpu.VMEM((width, max_rank), F32),
            dma((2, 3)),
        ],
    )(out, gb, ga)
    return out.reshape(slot_count, seq_len, width), ga[None], gb[None]


def solution(mesh):
    in_specs = (
        P("dp", None, "tensor"),
        P("dp"),
        P("dp"),
        P("dp"),
        P(),
        P(),
        P("tensor", None),
        P("dp", "tensor", None),
        P("dp", None, "tensor"),
        P("dp", None, "tensor"),
    )
    out_specs = (P("dp", None, "tensor"), P("dp", "tensor", None), P("dp", None, "tensor"))
    return jax.shard_map(
        on_device, mesh=mesh, in_specs=in_specs, out_specs=out_specs, check_vma=False
    )
```

```python
import jax
import jax.numpy as jnp
from jax import lax
from jax.experimental import pallas as pl
from jax.experimental.pallas import tpu as pltpu
from jax.sharding import PartitionSpec as P

BF = jnp.bfloat16
F32 = jnp.float32
RING = 4
DP = RING * RING
TENSOR = 2 * RING
TILE = 256
W_SLOTS = 3
MOVE, PLACE = (0, 0, -1, 1), (0, 1, 1, 0)
BOTH = slice(0, 2)
MESSAGES = ((2, BOTH), (BOTH, 2), (3, BOTH), (BOTH, 3), (2, 2), (3, 3), (2, 3), (3, 2))
NEIGHBOURS = ((0, 1), (1, 0), (0, 3), (3, 0), (1, 1), (3, 3), (1, 3), (3, 1))
OTHERS = NEIGHBOURS + ((0, 2), (2, 0), (2, 1), (1, 2), (2, 3), (3, 2), (2, 2))


def mm(a, b):
    return jnp.dot(a, b, preferred_element_type=F32)


def kernel(
    dest_ref,
    count_ref,
    job_ref,
    owner_ref,
    rank_ref,
    tok_ref,
    cot_ref,
    a_ref,
    b_ref,
    w_ref,
    out_ref,
    ga_ref,
    gb_ref,
    tok_v,
    cot_v,
    a_v,
    b_v,
    out_v,
    tok_s,
    tok_r,
    facts_s,
    facts_r,
    place_hot,
    x_hot,
    c_hot,
    slot_hot,
    xs,
    x_s,
    x_r,
    c_s,
    c_r,
    fa,
    fb,
    wbuf,
    sib_s,
    sib_r,
    hold,
    hop_s,
    hop_r,
    ring_s,
    ring_r,
    part_s,
    part_r,
    ranks,
    ad_s,
    ad_r,
    g_own,
    g_s,
    g_r,
    in_sem,
    out_sem,
    w_sem,
    facts_ss,
    facts_rs,
    tok_ss,
    tok_rs,
    fac_ss,
    fac_rs,
    c_ss,
    c_rs,
    x_ss,
    x_rs,
    sib_ss,
    sib_rs,
    hop_ss,
    hop_rs,
    ring_ss,
    ring_rs,
    part_ss,
    part_rs,
    gath_ss,
    gath_rs,
    ad_ss,
    ad_rs,
    g_ss,
    g_rs,
):
    seq_len, width = tok_ref.shape[1:]
    rows = DP * seq_len
    half = rows // 2
    me = lax.axis_index("dp")
    t = lax.axis_index("tensor")
    y, z = me // RING, me % RING
    x, c = t // 2, t % 2
    odd = (y + z) % 2
    ahead = 1 - 2 * odd
    others = ((1 - odd, 1 - odd), (odd, 1 - odd), (1 - odd, odd))
    tiles = width // TILE
    wide_half = width // 2

    def remote(src, dst, send, recv, **where):
        return pltpu.make_async_remote_copy(
            src_ref=src,
            dst_ref=dst,
            send_sem=send,
            recv_sem=recv,
            device_id=where,
            device_id_type=pl.DeviceIdType.MESH,
        )

    def iota(shape, axis):
        return lax.broadcasted_iota(jnp.int32, shape, axis)

    def near(dy, dz):
        return (y + dy + RING) % RING * RING + (z + dz + RING) % RING

    def owner_of(i, j):
        first, second = (y - i + RING) % RING, (z - j + RING) % RING
        shift = (first + second) % 2
        return (first + shift) % RING * RING + (second + shift) % RING

    def rank_at(owner):
        total = jnp.int32(0)
        for j in range(DP):
            total = total + jnp.where(owner_ref[j] == owner, rank_ref[j], 0)
        return total

    def factor_at(owner, columns):
        return 32.0 / jnp.full((1, columns), rank_at(owner).astype(F32), F32)

    def span(start, size):
        return pl.ds(pl.multiple_of(start, size), size)

    loads = [
        pltpu.make_async_copy(src, dst, in_sem.at[n])
        for n, (src, dst) in enumerate(((tok_ref, tok_v), (a_ref, a_v), (b_ref, b_v), (cot_ref, cot_v)))
    ]
    for load in loads:
        load.start()

    barrier = pltpu.get_barrier_semaphore()

    @pl.loop(1, DP)
    def _(k):
        pl.semaphore_signal(
            barrier, inc=1, device_id={"dp": (me + k) % DP}, device_id_type=pl.DeviceIdType.MESH
        )

    @pl.loop(1, TENSOR)
    def _(k):
        pl.semaphore_signal(
            barrier, inc=1, device_id={"tensor": (t + k) % TENSOR}, device_id_type=pl.DeviceIdType.MESH
        )

    def w_copy(i):
        j = i // 2
        block = (x + jnp.where(j == 0, 2, jnp.where(j == 1, 1, jnp.where(j == 2, 3, 0)))) % RING * 2
        block = block + (c + 1 - i % 2) % 2
        return pltpu.make_async_copy(
            w_ref.at[:, span(block * width, width)], wbuf.at[i % W_SLOTS], w_sem.at[i % W_SLOTS]
        )

    for i in range(W_SLOTS):
        w_copy(jnp.int32(i)).start()

    def chosen(to):
        index = jnp.int32(0)
        for i in range(DP):
            index = jnp.where(lax.shift_right_logical(dest_ref[i], 4) == to, i, index)
        return index

    @pl.loop(0, DP)
    def _(to):
        index = chosen(to)
        owner = owner_ref[job_ref[index]]
        oy, oz = lax.shift_right_logical(owner, 2), owner & 3
        shift = (oy + oz) & 1
        dy, dz = (to // RING + RING - oy + shift) & 3, (to % RING + RING - oz + shift) & 3
        base = (dy * RING + dz) * 2
        row = iota((8, 128), 0)
        facts_s[to] = jnp.where(
            row == 0, dest_ref[index] & 15, jnp.where(row == 1, count_ref[index], base)
        )

    facts_r[me] = facts_s[me]
    loads[0].wait()

    @pl.loop(0, DP)
    def _(to):
        tok_s[to] = tok_v[chosen(to)]

    tok_r[me] = tok_s[me]

    pl.semaphore_wait(barrier, DP - 1 + TENSOR - 1)

    def facts_copy(k):
        to = near(*OTHERS[k])
        return remote(facts_s.at[to], facts_r.at[me], facts_ss.at[k], facts_rs.at[k], dp=to)

    def tok_copy(h, k):
        to, columns = near(*OTHERS[k]), span(h * wide_half, wide_half)
        return remote(
            tok_s.at[to, :, columns],
            tok_r.at[me, :, columns],
            tok_ss.at[h, k],
            tok_rs.at[h, k],
            dp=to,
        )

    def fac_copy(axis, n):
        table = (fa, fb)[n]
        there = ((1 - odd, odd), (odd, 1 - odd))[axis]
        to = (near(ahead, 0), near(0, ahead))[axis]
        return remote(
            table.at[odd, odd], table.at[there], fac_ss.at[axis, n], fac_rs.at[there + (n,)], dp=to
        )

    def fac_wait(n, which):
        for there in which:
            held = (fa, fb)[n].at[there]
            remote(held, held, fac_ss.at[0, n], fac_rs.at[there + (n,)], dp=me).wait_recv()

    def fac_relay(n):
        table = (fa, fb)[n]
        here = ((odd, 1 - odd), (1 - odd, odd))[n]
        to = (near(0, -ahead), near(-ahead, 0))[n]
        return remote(table.at[here], table.at[odd, odd], fac_ss.at[2, n], fac_rs.at[odd, odd, n], dp=to)

    for k in range(DP - 1):
        facts_copy(k).start()

    @pl.loop(0, 2)
    def _(h):
        for k in range(DP - 1):
            tok_copy(h, k).start()

    my_rank = rank_at(me)
    loads[1].wait()

    @pl.loop(0, width // 128)
    def _(n):
        at = span(n * 128, 128)
        kept = iota((128, a_v.shape[2]), 1) < my_rank
        fa[odd, odd, at, :] = jnp.where(kept, a_v[0, at, :].astype(F32), 0.0).astype(BF)

    for axis in range(2):
        fac_copy(axis, 0).start()
    loads[2].wait()

    @pl.loop(0, width // 128)
    def _(n):
        at = span(n * 128, 128)
        kept = iota((b_v.shape[1], 128), 0) < my_rank
        fb[odd, odd, :, at] = jnp.where(kept, b_v[0, :, at].astype(F32), 0.0).astype(BF)

    for axis in range(2):
        fac_copy(axis, 1).start()
    for k in range(DP - 1):
        facts_copy(k).wait_recv()

    slot_c = facts_r[:, 0, :].astype(F32)
    live_c = facts_r[:, 1, :].astype(F32)
    base_c = facts_r[:, 2, :].astype(F32)
    square = (DP, 128)
    diagonal = iota(square, 0) == iota(square, 1)
    slot_l = jnp.sum(jnp.where(diagonal, slot_c, 0.0), 0, keepdims=True)
    base_l = jnp.sum(jnp.where(diagonal, base_c, 0.0), 0, keepdims=True)
    earlier = (base_l == base_c) & (slot_l < slot_c) & (iota(square, 1) < DP)
    turn_c = jnp.sum(jnp.where(earlier, 1.0, 0.0), 1, keepdims=True)
    lane_c = base_c + turn_c
    lane_l = jnp.sum(jnp.where(diagonal, lane_c, 0.0), 0, keepdims=True)
    wide = (DP, rows)
    seq_of = iota(wide, 1) // seq_len
    slot_1, live_1, lane_1 = slot_c[:, :1], live_c[:, :1], lane_c[:, :1]
    in_slot = slot_1 == seq_of.astype(F32)
    in_order = iota(wide, 0) == seq_of
    position = (iota((1, rows), 1) % seq_len).astype(F32)

    def spread(where, value):
        return jnp.sum(jnp.where(where, value, 0.0), 0, keepdims=True)

    live = position < spread(in_order, live_1)
    c_row = spread(in_slot, lane_1) * seq_len + position
    x_row = jnp.where(live, spread(in_order, lane_1) * seq_len + position, -1.0)
    slot_row = jnp.where(live, spread(in_order, slot_1) * seq_len + position, -1.0)

    def build(hot, wanted):
        @pl.loop(0, hot.shape[0] // 64)
        def _(n):
            row = (iota((64, rows), 0) + n * 64).astype(F32)
            hot[span(n * 64, 64), :] = jnp.where(row == wanted, 1.0, 0.0).astype(BF)

    build(x_hot, x_row)
    build(place_hot, slot_row)

    lane_shape = (RING, RING, 2 * seq_len)

    def lane_place(dy, dz):
        row = PLACE[dy] if dy != BOTH else BOTH
        column = PLACE[dz] if dz != BOTH else BOTH
        return row, column, (dy != BOTH) * 2 + (dz != BOTH)

    def lane_move(dy, dz):
        return (MOVE[dy] if dy != BOTH else 0, MOVE[dz] if dz != BOTH else 0)

    def x_copy(h, m):
        message, columns = MESSAGES[m], span(h * wide_half, wide_half)
        return remote(
            x_s.at[message + (slice(None), columns)],
            x_r.at[lane_place(*message) + (slice(None), columns)],
            x_ss.at[h, m],
            x_rs.at[h, m],
            dp=near(*lane_move(*message)),
        )

    def c_copy(m):
        message = MESSAGES[m]
        return remote(
            c_s.at[message],
            c_r.at[lane_place(*message)],
            c_ss.at[m],
            c_rs.at[m],
            dp=near(*lane_move(*message)),
        )

    @pl.loop(0, 2)
    def _(h):
        for k in range(DP - 1):
            tok_copy(h, k).wait_recv()

        @pl.loop(0, tiles // 2)
        def _(n):
            at = span(h * wide_half + n * TILE, TILE)
            landed = tok_r[:, :, at].reshape(rows, TILE)
            x_s[:, :, :, at] = mm(x_hot[...], landed).astype(BF).reshape(lane_shape + (TILE,))

        for m in range(len(MESSAGES)):
            x_copy(h, m).start()

        @pl.loop(0, tiles // 2)
        def _(n):
            at = span(h * wide_half + n * TILE, TILE)
            xs[:, at] = mm(place_hot[...], tok_r[:, :, at].reshape(rows, TILE)).astype(BF)

    build(c_hot, c_row)
    loads[3].wait()

    @pl.loop(0, tiles)
    def _(n):
        at = span(n * TILE, TILE)
        c_s[:, :, :, at] = mm(c_hot[...], cot_v[:, at]).astype(BF).reshape(lane_shape + (TILE,))

    fac_wait(0, others[1:])
    fac_relay(0).start()
    x_r[:, :, 0] = x_s[BOTH, BOTH]
    c_r[:, :, 0] = c_s[BOTH, BOTH]

    def sib_copy(j):
        return remote(
            sib_s.at[j % 2], sib_r.at[j], sib_ss.at[j % 2], sib_rs.at[j], tensor=x * 2 + (1 - c)
        )

    right, left = ((x + 1) % RING) * 2 + c, ((x + 3) % RING) * 2 + c

    def hop_copy(way):
        return remote(
            hop_s.at[way], hop_r.at[way], hop_ss.at[way], hop_rs.at[way], tensor=(right, left)[way]
        )

    def ring_copy(way, part):
        return remote(
            ring_s.at[way, part],
            ring_r.at[way, part],
            ring_ss.at[way, part],
            ring_rs.at[way, part],
            tensor=(right, left)[way],
        )

    def half_rows(part, put):
        @pl.loop(0, half // 32)
        def _(n):
            put(span(part * half + n * 32, 32), span(n * 32, 32))

    def send_hop(way):
        def put(at, to):
            hop_s[way, to] = (hold[0, at] + sib_r[0, at].astype(F32)).astype(BF)

        half_rows(way, put)
        hop_copy(way).start()

    def send_ring(way, part):
        def put(at, to):
            value = hold[1 - way, at] + sib_r[1 + way, at].astype(F32)
            if way == part:
                value = value + hop_r[way, to].astype(F32)
            ring_s[way, part, to] = value.astype(BF)

        half_rows(part, put)
        ring_copy(way, part).start()

    def part_copy(kind, k):
        to = (t + k) % TENSOR
        return remote(
            part_s.at[kind, to],
            part_r.at[kind, k],
            part_ss.at[kind, k - 1],
            part_rs.at[kind, k - 1],
            tensor=to,
        )

    def gath_copy(kind, k):
        to = (t + k) % TENSOR
        held = ranks.at[kind, t]
        return remote(held, held, gath_ss.at[kind, k - 1], gath_rs.at[kind, k - 1], tensor=to)

    def served(ref, i, j):
        return ref[i, j].reshape(RING * 64, width)

    def send_parts(kind, make):
        @pl.loop(0, 4)
        def _(q):
            value = make(q // 2, q % 2).astype(BF)
            part_s[kind, 2 * q] = value[:128]
            part_s[kind, 2 * q + 1] = value[128:]

        @pl.loop(1, TENSOR)
        def _(k):
            part_copy(kind, k).start()

        part_r[kind, 0] = part_s[kind, t]

    def sum_parts(kind, scale):
        @pl.loop(1, TENSOR)
        def _(k):
            part_copy(kind, k).wait_recv()

        total = part_r[kind, 0].astype(F32)
        for k in range(1, TENSOR):
            total = total + part_r[kind, k].astype(F32)
        ranks[kind, t] = (total if scale is None else total * scale).astype(BF)

        @pl.loop(1, TENSOR)
        def _(k):
            gath_copy(kind, k).start()

    def gathered(kind):
        @pl.loop(1, TENSOR)
        def _(k):
            held = ranks.at[kind, (t + TENSOR - k) % TENSOR]
            remote(held, held, gath_ss.at[kind, k - 1], gath_rs.at[kind, k - 1], tensor=t).wait_recv()

    def rank_rows(kind, i, j):
        return ranks[kind, pl.ds(i * 4 + j * 2, 2)].reshape(RING * 64, ranks.shape[3])

    @pl.loop(0, 4)
    def _(j):
        w_copy(2 * j).wait()

        @pl.when(j >= 2)
        def _():
            sib_copy(j - 2).wait_send()

        @pl.loop(0, tiles)
        def _(n):
            at = span(n * TILE, TILE)
            sib_s[j % 2, :, at] = mm(xs[...], wbuf[(2 * j) % W_SLOTS, :, at]).astype(BF)

        sib_copy(j).start()

        @pl.when(2 * j + W_SLOTS < 8)
        def _():
            w_copy(2 * j + W_SLOTS).start()

        @pl.when(j == 1)
        def _():
            sib_copy(0).wait_recv()
            send_hop(0)
            send_hop(1)

        @pl.when(j == 3)
        def _():
            sib_copy(2).wait_recv()
            send_ring(1, 0)

        w_copy(2 * j + 1).wait()

        @pl.loop(0, tiles)
        def _(n):
            at = span(n * TILE, TILE)
            hold[jnp.where(j == 3, 2, j % 2), :, at] = mm(xs[...], wbuf[(2 * j + 1) % W_SLOTS, :, at])

        @pl.when(2 * j + 1 + W_SLOTS < 8)
        def _():
            w_copy(2 * j + 1 + W_SLOTS).start()

        @pl.when(j == 0)
        def _():
            fac_wait(1, others[1:])
            fac_relay(1).start()
            for m in range(len(MESSAGES)):
                c_copy(m).start()

        @pl.when(j == 1)
        def _():
            fac_wait(0, others[:1])

            @pl.loop(0, 2)
            def _(h):
                for m in range(len(MESSAGES)):
                    x_copy(h, m).wait_recv()

            send_parts(0, lambda i, k: mm(served(x_r, i, k), fa[i, k]))

        @pl.when(j == 2)
        def _():
            sum_parts(0, None)
            sib_copy(1).wait_recv()
            send_ring(0, 1)

    def ad_copy(m):
        message = MESSAGES[m]
        dy, dz = lane_move(*message)
        return remote(
            ad_s.at[lane_place(*message)],
            ad_r.at[message],
            ad_ss.at[m],
            ad_rs.at[m],
            dp=near(-dy, -dz),
        )

    fac_wait(1, others[:1])
    gathered(0)

    @pl.loop(0, 4)
    def _(q):
        i, j = q // 2, q % 2
        value = mm(rank_rows(0, i, j), fb[i, j]) * factor_at(owner_of(i, j), width)
        ad_s[i, j] = value.astype(BF).reshape(RING, 64, width)

    for m in range(len(MESSAGES)):
        ad_copy(m).start()
    ad_r[BOTH, BOTH] = ad_s[:, :, 0]

    for m in range(len(MESSAGES)):
        c_copy(m).wait_recv()
    send_parts(
        1,
        lambda i, j: lax.dot_general(
            served(c_r, i, j), fb[i, j], (((1,), (1,)), ((), ())), preferred_element_type=F32
        ),
    )

    def g_copy(n, which):
        dy = jnp.where(which == 0, -ahead, jnp.where(which == 1, ahead, 0))
        dz = jnp.where(which == 0, -ahead, jnp.where(which == 1, 0, ahead))
        return remote(
            g_s.at[n, which],
            g_r.at[n, which],
            g_ss.at[n, which],
            g_rs.at[n, which],
            dp=near(dy, dz),
        )

    def gradient(n, kind, row_ref):
        @pl.loop(0, 4)
        def _(which):
            i = jnp.where((which == 1) | (which == 3), odd, 1 - odd)
            j = jnp.where(which >= 2, odd, 1 - odd)
            turned = rank_rows(kind, i, j).astype(F32).T.astype(BF)
            value = mm(turned, served(row_ref, i, j)) * (1.0 / seq_len)
            if n == 1:
                value = value * factor_at(owner_of(i, j), width)
            g_own[n] = value
            g_s[n, which] = value.astype(BF)

            @pl.when(which < 3)
            def _():
                g_copy(n, which).start()

    gradient(1, 0, c_r)

    @pl.loop(0, rows // 64)
    def _(n):
        row = iota((64, 128), 0) + n * 64
        mine = jnp.where(slot_l == (row // seq_len).astype(F32), lane_l, 0.0)
        place = jnp.sum(mine, 1, keepdims=True) * seq_len + (row % seq_len).astype(F32)[:, :1]
        slot_hot[span(n * 64, 64), :] = jnp.where(
            iota((64, 2 * rows), 1).astype(F32) == place, 1.0, 0.0
        ).astype(BF)

    sum_parts(1, factor_at(owner_of(t // 4, (t // 2) % 2), ranks.shape[3]))
    for way in range(2):
        hop_copy(way).wait_recv()
        send_ring(way, way)
    gathered(1)
    gradient(0, 1, x_r)

    sib_copy(3).wait_recv()
    for m in range(len(MESSAGES)):
        ad_copy(m).wait_recv()

    @pl.loop(0, tiles)
    def _(n):
        at = span(n * TILE, TILE)
        back = ad_r[:, :, :, at].reshape(2 * rows, TILE)
        hold[2, :, at] = hold[2, :, at] + sib_r[3, :, at].astype(F32) + mm(slot_hot[...], back)

    for way in range(2):
        for part in range(2):
            ring_copy(way, part).wait_recv()

    for part in range(2):

        def put(at, to):
            out_v[at] = (
                hold[2, at] + ring_r[0, part, to].astype(F32) + ring_r[1, part, to].astype(F32)
            ).astype(BF)

        half_rows(part, put)
    stores = [pltpu.make_async_copy(out_v, out_ref, out_sem.at[2])]
    stores[0].start()

    for n, g_ref in ((1, gb_ref), (0, ga_ref)):

        @pl.loop(0, 3)
        def _(which):
            remote(
                g_s.at[n, which], g_r.at[n, which], g_ss.at[n, which], g_rs.at[n, which], dp=me
            ).wait_recv()

        @pl.loop(0, g_own.shape[1] // 32)
        def _(k):
            at = span(k * 32, 32)
            total = g_own[n, at]
            for which in range(3):
                total = total + g_r[n, which, at].astype(F32)
            g_own[n, at] = total

        stores.append(pltpu.make_async_copy(g_own.at[n], g_ref, out_sem.at[n]))
        stores[-1].start()

    for k in range(DP - 1):
        facts_copy(k).wait_send()
        tok_copy(0, k).wait_send()
        tok_copy(1, k).wait_send()

    for n in range(2):
        for axis in range(2):
            fac_copy(axis, n).wait_send()
        fac_relay(n).wait_send()
    for m in range(len(MESSAGES)):
        for h in range(2):
            x_copy(h, m).wait_send()
        c_copy(m).wait_send()
        ad_copy(m).wait_send()
    for j in (2, 3):
        sib_copy(j).wait_send()
    for way in range(2):
        hop_copy(way).wait_send()
        for part in range(2):
            ring_copy(way, part).wait_send()
    for kind in range(2):

        @pl.loop(1, TENSOR)
        def _(k):
            part_copy(kind, k).wait_send()
            gath_copy(kind, k).wait_send()

        @pl.loop(0, 3)
        def _(which):
            g_copy(kind, which).wait_send()

    for store in stores:
        store.wait()


def finish(out_ref, gb_ref, ga_ref, out_to, gb_to, ga_to, out_v, gb_v, ga_v, turned_v, sem):
    names = ((ga_ref, ga_v, turned_v, ga_to), (gb_ref, gb_v, gb_v, gb_to), (out_ref, out_v, out_v, out_to))
    loads = [pltpu.make_async_copy(src, held, sem.at[0, n]) for n, (src, held, _, _) in enumerate(names)]
    stores = [pltpu.make_async_copy(held, dst, sem.at[1, n]) for n, (_, _, held, dst) in enumerate(names)]
    for load in loads:
        load.start()
    loads[0].wait()
    turned_v[...] = ga_v[...].T
    stores[0].start()
    for n in (1, 2):
        loads[n].wait()
        stores[n].start()
    for store in stores:
        store.wait()


def on_device(
    tokens,
    destinations,
    counts,
    sequence_job_ids,
    job_owner_slot,
    rank_per_job,
    weight,
    input_factor_table,
    output_factor_table,
    cotangent,
):
    slot_count, seq_len, width = tokens.shape
    max_rank = input_factor_table.shape[2]
    rows = slot_count * seq_len
    anywhere = pl.BlockSpec(memory_space=pl.ANY)
    smem = pl.BlockSpec(memory_space=pltpu.SMEM)
    dma = pltpu.SemaphoreType.DMA
    served = (2, 2, RING, 64, width)
    lanes = (RING, RING, 64, width)
    out, ga, gb = pl.pallas_call(
        kernel,
        out_shape=(
            jax.ShapeDtypeStruct((rows, width), BF),
            jax.ShapeDtypeStruct((max_rank, width), F32),
            jax.ShapeDtypeStruct((max_rank, width), F32),
        ),
        in_specs=[smem] * 5 + [anywhere] * 5,
        out_specs=(anywhere,) * 3,
        scratch_shapes=[
            pltpu.VMEM(tokens.shape, BF),
            pltpu.VMEM((rows, width), BF),
            pltpu.VMEM(input_factor_table.shape, BF),
            pltpu.VMEM(output_factor_table.shape, BF),
            pltpu.VMEM((rows, width), BF),
            pltpu.VMEM((DP, seq_len, width), BF),
            pltpu.VMEM((DP, seq_len, width), BF),
            pltpu.VMEM((DP, 8, 128), jnp.int32),
            pltpu.VMEM((DP, 8, 128), jnp.int32),
            pltpu.VMEM((rows, rows), BF),
            pltpu.VMEM((2 * rows, rows), BF),
            pltpu.VMEM((2 * rows, rows), BF),
            pltpu.VMEM((rows, 2 * rows), BF),
            pltpu.VMEM((rows, width), BF),
            pltpu.VMEM(lanes, BF),
            pltpu.VMEM(served, BF),
            pltpu.VMEM(lanes, BF),
            pltpu.VMEM(served, BF),
            pltpu.VMEM((2, 2, width, max_rank), BF),
            pltpu.VMEM((2, 2, max_rank, width), BF),
            pltpu.VMEM((W_SLOTS, width, width), BF),
            pltpu.VMEM((2, rows, width), BF),
            pltpu.VMEM((4, rows, width), BF),
            pltpu.VMEM((3, rows, width), F32),
            pltpu.VMEM((2, rows // 2, width), BF),
            pltpu.VMEM((2, rows // 2, width), BF),
            pltpu.VMEM((2, 2, rows // 2, width), BF),
            pltpu.VMEM((2, 2, rows // 2, width), BF),
            pltpu.VMEM((2, TENSOR, 128, max_rank), BF),
            pltpu.VMEM((2, TENSOR, 128, max_rank), BF),
            pltpu.VMEM((2, TENSOR, 128, max_rank), BF),
            pltpu.VMEM(served, BF),
            pltpu.VMEM(lanes, BF),
            pltpu.VMEM((2, max_rank, width), F32),
            pltpu.VMEM((2, 4, max_rank, width), BF),
            pltpu.VMEM((2, 3, max_rank, width), BF),
            dma((4,)),
            dma((3,)),
            dma((W_SLOTS,)),
            dma((DP - 1,)),
            dma((DP - 1,)),
            dma((2, DP - 1)),
            dma((2, DP - 1)),
            dma((3, 2)),
            dma((2, 2, 2)),
            dma((8,)),
            dma((8,)),
            dma((2, 8)),
            dma((2, 8)),
            dma((2,)),
            dma((4,)),
            dma((2,)),
            dma((2,)),
            dma((2, 2)),
            dma((2, 2)),
            dma((2, TENSOR - 1)),
            dma((2, TENSOR - 1)),
            dma((2, TENSOR - 1)),
            dma((2, TENSOR - 1)),
            dma((8,)),
            dma((8,)),
            dma((2, 3)),
            dma((2, 3)),
        ],
        compiler_params=pltpu.CompilerParams(
            collective_id=0, has_side_effects=True, vmem_limit_bytes=58 * 2**20
        ),
    )(
        destinations,
        counts,
        sequence_job_ids,
        job_owner_slot,
        rank_per_job,
        tokens,
        cotangent.reshape(rows, width),
        input_factor_table,
        output_factor_table,
        weight,
    )
    out, gb, ga = pl.pallas_call(
        finish,
        out_shape=(
            jax.ShapeDtypeStruct((rows, width), BF),
            jax.ShapeDtypeStruct((max_rank, width), F32),
            jax.ShapeDtypeStruct((width, max_rank), F32),
        ),
        in_specs=[anywhere] * 3,
        out_specs=(anywhere,) * 3,
        scratch_shapes=[
            pltpu.VMEM((rows, width), BF),
            pltpu.VMEM((max_rank, width), F32),
            pltpu.VMEM((max_rank, width), F32),
            pltpu.VMEM((width, max_rank), F32),
            dma((2, 3)),
        ],
    )(out, gb, ga)
    return out.reshape(slot_count, seq_len, width), ga[None], gb[None]


def solution(mesh):
    in_specs = (
        P("dp", None, "tensor"),
        P("dp"),
        P("dp"),
        P("dp"),
        P(),
        P(),
        P("tensor", None),
        P("dp", "tensor", None),
        P("dp", None, "tensor"),
        P("dp", None, "tensor"),
    )
    out_specs = (P("dp", None, "tensor"), P("dp", "tensor", None), P("dp", None, "tensor"))
    return jax.shard_map(
        on_device, mesh=mesh, in_specs=in_specs, out_specs=out_specs, check_vma=False
    )
```

```python
import jax
import jax.numpy as jnp
from jax import lax
from jax.experimental import pallas as pl
from jax.experimental.pallas import tpu as pltpu
from jax.sharding import PartitionSpec as P

BF = jnp.bfloat16
F32 = jnp.float32
RING = 4
DP = RING * RING
TENSOR = 2 * RING
TILE = 256
W_SLOTS = 3
MOVE, PLACE = (0, 0, -1, 1), (0, 1, 1, 0)
BOTH = slice(0, 2)
MESSAGES = ((2, BOTH), (BOTH, 2), (3, BOTH), (BOTH, 3), (2, 2), (3, 3), (2, 3), (3, 2))
NEIGHBOURS = ((0, 1), (1, 0), (0, 3), (3, 0), (1, 1), (3, 3), (1, 3), (3, 1))
OTHERS = NEIGHBOURS + ((0, 2), (2, 0), (2, 1), (1, 2), (2, 3), (3, 2), (2, 2))


def mm(a, b):
    return jnp.dot(a, b, preferred_element_type=F32)


def kernel(
    dest_ref,
    count_ref,
    job_ref,
    owner_ref,
    rank_ref,
    tok_ref,
    cot_ref,
    a_ref,
    b_ref,
    w_ref,
    out_ref,
    ga_ref,
    gb_ref,
    tok_v,
    cot_v,
    a_v,
    b_v,
    out_v,
    tok_s,
    tok_r,
    facts_s,
    facts_r,
    place_hot,
    x_hot,
    c_hot,
    slot_hot,
    xs,
    x_s,
    x_r,
    c_s,
    c_r,
    fa,
    fb,
    wbuf,
    sib_s,
    sib_r,
    hold,
    hop_s,
    hop_r,
    ring_s,
    ring_r,
    part_s,
    part_r,
    ranks,
    ad_s,
    ad_r,
    g_own,
    g_mid,
    g_s,
    g_r,
    in_sem,
    out_sem,
    w_sem,
    facts_ss,
    facts_rs,
    tok_ss,
    tok_rs,
    fac_ss,
    fac_rs,
    c_ss,
    c_rs,
    x_ss,
    x_rs,
    sib_ss,
    sib_rs,
    hop_ss,
    hop_rs,
    ring_ss,
    ring_rs,
    part_ss,
    part_rs,
    gath_ss,
    gath_rs,
    ad_ss,
    ad_rs,
    g_ss,
    g_rs,
):
    seq_len, width = tok_ref.shape[1:]
    rows = DP * seq_len
    half = rows // 2
    me = lax.axis_index("dp")
    t = lax.axis_index("tensor")
    y, z = me // RING, me % RING
    x, c = t // 2, t % 2
    odd = (y + z) % 2
    ahead = 1 - 2 * odd
    others = ((1 - odd, 1 - odd), (odd, 1 - odd), (1 - odd, odd))
    tiles = width // TILE
    wide_half = width // 2

    def remote(src, dst, send, recv, **where):
        return pltpu.make_async_remote_copy(
            src_ref=src,
            dst_ref=dst,
            send_sem=send,
            recv_sem=recv,
            device_id=where,
            device_id_type=pl.DeviceIdType.MESH,
        )

    def iota(shape, axis):
        return lax.broadcasted_iota(jnp.int32, shape, axis)

    def near(dy, dz):
        return (y + dy + RING) % RING * RING + (z + dz + RING) % RING

    def owner_of(i, j):
        first, second = (y - i + RING) % RING, (z - j + RING) % RING
        shift = (first + second) % 2
        return (first + shift) % RING * RING + (second + shift) % RING

    def rank_at(owner):
        total = jnp.int32(0)
        for j in range(DP):
            total = total + jnp.where(owner_ref[j] == owner, rank_ref[j], 0)
        return total

    def factor_at(owner, columns):
        return 32.0 / jnp.full((1, columns), rank_at(owner).astype(F32), F32)

    def span(start, size):
        return pl.ds(pl.multiple_of(start, size), size)

    loads = [
        pltpu.make_async_copy(src, dst, in_sem.at[n])
        for n, (src, dst) in enumerate(((tok_ref, tok_v), (a_ref, a_v), (b_ref, b_v), (cot_ref, cot_v)))
    ]
    for load in loads:
        load.start()

    barrier = pltpu.get_barrier_semaphore()

    @pl.loop(1, DP)
    def _(k):
        pl.semaphore_signal(
            barrier, inc=1, device_id={"dp": (me + k) % DP}, device_id_type=pl.DeviceIdType.MESH
        )

    @pl.loop(1, TENSOR)
    def _(k):
        pl.semaphore_signal(
            barrier, inc=1, device_id={"tensor": (t + k) % TENSOR}, device_id_type=pl.DeviceIdType.MESH
        )

    def w_copy(i):
        j = i // 2
        block = (x + jnp.where(j == 0, 2, jnp.where(j == 1, 1, jnp.where(j == 2, 3, 0)))) % RING * 2
        block = block + (c + 1 - i % 2) % 2
        return pltpu.make_async_copy(
            w_ref.at[:, span(block * width, width)], wbuf.at[i % W_SLOTS], w_sem.at[i % W_SLOTS]
        )

    for i in range(W_SLOTS):
        w_copy(jnp.int32(i)).start()

    def chosen(to):
        index = jnp.int32(0)
        for i in range(DP):
            index = jnp.where(lax.shift_right_logical(dest_ref[i], 4) == to, i, index)
        return index

    @pl.loop(0, DP)
    def _(to):
        index = chosen(to)
        owner = owner_ref[job_ref[index]]
        oy, oz = lax.shift_right_logical(owner, 2), owner & 3
        shift = (oy + oz) & 1
        dy, dz = (to // RING + RING - oy + shift) & 3, (to % RING + RING - oz + shift) & 3
        base = (dy * RING + dz) * 2
        row = iota((8, 128), 0)
        facts_s[to] = jnp.where(
            row == 0, dest_ref[index] & 15, jnp.where(row == 1, count_ref[index], base)
        )

    facts_r[me] = facts_s[me]
    loads[0].wait()

    @pl.loop(0, DP)
    def _(to):
        tok_s[to] = tok_v[chosen(to)]

    tok_r[me] = tok_s[me]

    pl.semaphore_wait(barrier, DP - 1 + TENSOR - 1)

    def facts_copy(k):
        to = near(*OTHERS[k])
        return remote(facts_s.at[to], facts_r.at[me], facts_ss.at[k], facts_rs.at[k], dp=to)

    def tok_copy(h, k):
        to, columns = near(*OTHERS[k]), span(h * wide_half, wide_half)
        return remote(
            tok_s.at[to, :, columns],
            tok_r.at[me, :, columns],
            tok_ss.at[h, k],
            tok_rs.at[h, k],
            dp=to,
        )

    def fac_copy(axis, n):
        table = (fa, fb)[n]
        there = ((1 - odd, odd), (odd, 1 - odd))[axis]
        to = (near(ahead, 0), near(0, ahead))[axis]
        return remote(
            table.at[odd, odd], table.at[there], fac_ss.at[axis, n], fac_rs.at[there + (n,)], dp=to
        )

    def fac_wait(n, which):
        for there in which:
            held = (fa, fb)[n].at[there]
            remote(held, held, fac_ss.at[0, n], fac_rs.at[there + (n,)], dp=me).wait_recv()

    def fac_relay(n):
        table = (fa, fb)[n]
        here = ((odd, 1 - odd), (1 - odd, odd))[n]
        to = (near(0, -ahead), near(-ahead, 0))[n]
        return remote(table.at[here], table.at[odd, odd], fac_ss.at[2, n], fac_rs.at[odd, odd, n], dp=to)

    for k in range(DP - 1):
        facts_copy(k).start()

    @pl.loop(0, 2)
    def _(h):
        for k in range(DP - 1):
            tok_copy(h, k).start()

    my_rank = rank_at(me)
    loads[1].wait()

    @pl.loop(0, width // 128)
    def _(n):
        at = span(n * 128, 128)
        kept = iota((128, a_v.shape[2]), 1) < my_rank
        fa[odd, odd, at, :] = jnp.where(kept, a_v[0, at, :].astype(F32), 0.0).astype(BF)

    for axis in range(2):
        fac_copy(axis, 0).start()
    loads[2].wait()

    @pl.loop(0, width // 128)
    def _(n):
        at = span(n * 128, 128)
        kept = iota((b_v.shape[1], 128), 0) < my_rank
        fb[odd, odd, :, at] = jnp.where(kept, b_v[0, :, at].astype(F32), 0.0).astype(BF)

    for k in range(DP - 1):
        facts_copy(k).wait_recv()

    slot_c = facts_r[:, 0, :].astype(F32)
    live_c = facts_r[:, 1, :].astype(F32)
    base_c = facts_r[:, 2, :].astype(F32)
    square = (DP, 128)
    diagonal = iota(square, 0) == iota(square, 1)
    slot_l = jnp.sum(jnp.where(diagonal, slot_c, 0.0), 0, keepdims=True)
    base_l = jnp.sum(jnp.where(diagonal, base_c, 0.0), 0, keepdims=True)
    earlier = (base_l == base_c) & (slot_l < slot_c) & (iota(square, 1) < DP)
    turn_c = jnp.sum(jnp.where(earlier, 1.0, 0.0), 1, keepdims=True)
    lane_c = base_c + turn_c
    lane_l = jnp.sum(jnp.where(diagonal, lane_c, 0.0), 0, keepdims=True)
    wide = (DP, rows)
    seq_of = iota(wide, 1) // seq_len
    slot_1, live_1, lane_1 = slot_c[:, :1], live_c[:, :1], lane_c[:, :1]
    in_slot = slot_1 == seq_of.astype(F32)
    in_order = iota(wide, 0) == seq_of
    position = (iota((1, rows), 1) % seq_len).astype(F32)

    def spread(where, value):
        return jnp.sum(jnp.where(where, value, 0.0), 0, keepdims=True)

    live = position < spread(in_order, live_1)
    c_row = spread(in_slot, lane_1) * seq_len + position
    x_row = jnp.where(live, spread(in_order, lane_1) * seq_len + position, -1.0)
    slot_row = jnp.where(live, spread(in_order, slot_1) * seq_len + position, -1.0)

    def build(hot, wanted):
        @pl.loop(0, hot.shape[0] // 64)
        def _(n):
            row = (iota((64, rows), 0) + n * 64).astype(F32)
            hot[span(n * 64, 64), :] = jnp.where(row == wanted, 1.0, 0.0).astype(BF)

    build(x_hot, x_row)
    build(place_hot, slot_row)

    lane_shape = (RING, RING, 2 * seq_len)

    def lane_place(dy, dz):
        row = PLACE[dy] if dy != BOTH else BOTH
        column = PLACE[dz] if dz != BOTH else BOTH
        return row, column, (dy != BOTH) * 2 + (dz != BOTH)

    def lane_move(dy, dz):
        return (MOVE[dy] if dy != BOTH else 0, MOVE[dz] if dz != BOTH else 0)

    def x_copy(h, m):
        message, columns = MESSAGES[m], span(h * wide_half, wide_half)
        return remote(
            x_s.at[message + (slice(None), columns)],
            x_r.at[lane_place(*message) + (slice(None), columns)],
            x_ss.at[h, m],
            x_rs.at[h, m],
            dp=near(*lane_move(*message)),
        )

    def c_copy(m):
        message = MESSAGES[m]
        return remote(
            c_s.at[message],
            c_r.at[lane_place(*message)],
            c_ss.at[m],
            c_rs.at[m],
            dp=near(*lane_move(*message)),
        )

    @pl.loop(0, 2)
    def _(h):
        for k in range(DP - 1):
            tok_copy(h, k).wait_recv()

        @pl.loop(0, tiles // 2)
        def _(n):
            at = span(h * wide_half + n * TILE, TILE)
            landed = tok_r[:, :, at].reshape(rows, TILE)
            x_s[:, :, :, at] = mm(x_hot[...], landed).astype(BF).reshape(lane_shape + (TILE,))

        for m in range(len(MESSAGES)):
            x_copy(h, m).start()

        @pl.loop(0, tiles // 2)
        def _(n):
            at = span(h * wide_half + n * TILE, TILE)
            xs[:, at] = mm(place_hot[...], tok_r[:, :, at].reshape(rows, TILE)).astype(BF)

    for axis in range(2):
        fac_copy(axis, 1).start()
    build(c_hot, c_row)
    loads[3].wait()

    @pl.loop(0, tiles)
    def _(n):
        at = span(n * TILE, TILE)
        c_s[:, :, :, at] = mm(c_hot[...], cot_v[:, at]).astype(BF).reshape(lane_shape + (TILE,))

    fac_wait(0, others[1:])
    fac_relay(0).start()
    x_r[:, :, 0] = x_s[BOTH, BOTH]
    c_r[:, :, 0] = c_s[BOTH, BOTH]

    def sib_copy(j):
        return remote(
            sib_s.at[j % 2], sib_r.at[j], sib_ss.at[j % 2], sib_rs.at[j], tensor=x * 2 + (1 - c)
        )

    right, left = ((x + 1) % RING) * 2 + c, ((x + 3) % RING) * 2 + c

    def hop_copy(way):
        return remote(
            hop_s.at[way], hop_r.at[way], hop_ss.at[way], hop_rs.at[way], tensor=(right, left)[way]
        )

    def ring_copy(way, part):
        return remote(
            ring_s.at[way, part],
            ring_r.at[way, part],
            ring_ss.at[way, part],
            ring_rs.at[way, part],
            tensor=(right, left)[way],
        )

    def half_rows(part, put):
        @pl.loop(0, half // 32)
        def _(n):
            put(span(part * half + n * 32, 32), span(n * 32, 32))

    def send_hop(way):
        def put(at, to):
            hop_s[way, to] = (hold[0, at] + sib_r[0, at].astype(F32)).astype(BF)

        half_rows(way, put)
        hop_copy(way).start()

    def send_ring(way, part):
        def put(at, to):
            value = hold[1 - way, at] + sib_r[1 + way, at].astype(F32)
            if way == part:
                value = value + hop_r[way, to].astype(F32)
            ring_s[way, part, to] = value.astype(BF)

        half_rows(part, put)
        ring_copy(way, part).start()

    def part_copy(kind, k):
        to = (t + k) % TENSOR
        return remote(
            part_s.at[kind, to],
            part_r.at[kind, k],
            part_ss.at[kind, k - 1],
            part_rs.at[kind, k - 1],
            tensor=to,
        )

    def gath_copy(kind, k):
        to = (t + k) % TENSOR
        held = ranks.at[kind, t]
        return remote(held, held, gath_ss.at[kind, k - 1], gath_rs.at[kind, k - 1], tensor=to)

    def served(ref, i, j):
        return ref[i, j].reshape(RING * 64, width)

    def send_parts(kind, make):
        @pl.loop(0, 4)
        def _(q):
            value = make(q // 2, q % 2).astype(BF)
            part_s[kind, 2 * q] = value[:128]
            part_s[kind, 2 * q + 1] = value[128:]

        @pl.loop(1, TENSOR)
        def _(k):
            part_copy(kind, k).start()

        part_r[kind, 0] = part_s[kind, t]

    def sum_parts(kind, scale):
        @pl.loop(1, TENSOR)
        def _(k):
            part_copy(kind, k).wait_recv()

        total = part_r[kind, 0].astype(F32)
        for k in range(1, TENSOR):
            total = total + part_r[kind, k].astype(F32)
        ranks[kind, t] = (total if scale is None else total * scale).astype(BF)

        @pl.loop(1, TENSOR)
        def _(k):
            gath_copy(kind, k).start()

    def gathered(kind):
        @pl.loop(1, TENSOR)
        def _(k):
            held = ranks.at[kind, (t + TENSOR - k) % TENSOR]
            remote(held, held, gath_ss.at[kind, k - 1], gath_rs.at[kind, k - 1], tensor=t).wait_recv()

    def rank_rows(kind, i, j):
        return ranks[kind, pl.ds(i * 4 + j * 2, 2)].reshape(RING * 64, ranks.shape[3])

    @pl.loop(0, 4)
    def _(j):
        w_copy(2 * j).wait()

        @pl.when(j >= 2)
        def _():
            sib_copy(j - 2).wait_send()

        @pl.loop(0, tiles)
        def _(n):
            at = span(n * TILE, TILE)
            sib_s[j % 2, :, at] = mm(xs[...], wbuf[(2 * j) % W_SLOTS, :, at]).astype(BF)

        sib_copy(j).start()

        @pl.when(2 * j + W_SLOTS < 8)
        def _():
            w_copy(2 * j + W_SLOTS).start()

        @pl.when(j == 1)
        def _():
            sib_copy(0).wait_recv()
            send_hop(0)
            send_hop(1)

        @pl.when(j == 3)
        def _():
            sib_copy(2).wait_recv()
            send_ring(1, 0)

        w_copy(2 * j + 1).wait()

        @pl.loop(0, tiles)
        def _(n):
            at = span(n * TILE, TILE)
            hold[jnp.where(j == 3, 2, j % 2), :, at] = mm(xs[...], wbuf[(2 * j + 1) % W_SLOTS, :, at])

        @pl.when(2 * j + 1 + W_SLOTS < 8)
        def _():
            w_copy(2 * j + 1 + W_SLOTS).start()

        @pl.when(j == 1)
        def _():
            fac_wait(0, others[:1])

            @pl.loop(0, 2)
            def _(h):
                for m in range(len(MESSAGES)):
                    x_copy(h, m).wait_recv()

            send_parts(0, lambda i, k: mm(served(x_r, i, k), fa[i, k]))
            fac_wait(1, others[1:])
            fac_relay(1).start()
            for m in range(len(MESSAGES)):
                c_copy(m).start()

        @pl.when(j == 2)
        def _():
            sum_parts(0, None)
            sib_copy(1).wait_recv()
            send_ring(0, 1)

    def ad_copy(m):
        message = MESSAGES[m]
        dy, dz = lane_move(*message)
        return remote(
            ad_s.at[lane_place(*message)],
            ad_r.at[message],
            ad_ss.at[m],
            ad_rs.at[m],
            dp=near(-dy, -dz),
        )

    fac_wait(1, others[:1])
    gathered(0)

    @pl.loop(0, 4)
    def _(q):
        i, j = q // 2, q % 2
        value = mm(rank_rows(0, i, j), fb[i, j]) * factor_at(owner_of(i, j), width)
        ad_s[i, j] = value.astype(BF).reshape(RING, 64, width)

    for m in range(len(MESSAGES)):
        ad_copy(m).start()
    ad_r[BOTH, BOTH] = ad_s[:, :, 0]

    for m in range(len(MESSAGES)):
        c_copy(m).wait_recv()
    send_parts(
        1,
        lambda i, j: lax.dot_general(
            served(c_r, i, j), fb[i, j], (((1,), (1,)), ((), ())), preferred_element_type=F32
        ),
    )

    def g_copy(n, which):
        dy = jnp.where(which == 0, -ahead * (1 - n), jnp.where(which == 1, ahead, 0))
        dz = jnp.where(which == 0, -ahead, jnp.where(which == 1, 0, ahead))
        return remote(
            g_s.at[n, which],
            g_r.at[n, which],
            g_ss.at[n, which],
            g_rs.at[n, which],
            dp=near(dy, dz),
        )

    def gradient(n, kind, row_ref):
        @pl.loop(0, 4)
        def _(which):
            i = jnp.where((which == 1) | (which == 3), odd, 1 - odd)
            j = jnp.where(which >= 2, odd, 1 - odd)
            turned = rank_rows(kind, i, j).astype(F32).T.astype(BF)
            value = mm(turned, served(row_ref, i, j)) * (1.0 / seq_len)
            if n == 1:
                value = value * factor_at(owner_of(i, j), width)
            g_own[n] = value
            g_s[n, which] = value.astype(BF)
            if n == 1:

                @pl.when(which == 1)
                def _():
                    g_mid[...] = value

            @pl.when((which == 0) | (which == 2) | ((which == 1) & (n == 0)))
            def _():
                g_copy(n, which).start()

    def pass_gradient():
        g_copy(1, 0).wait_recv()

        @pl.loop(0, g_mid.shape[0] // 32)
        def _(k):
            at = span(k * 32, 32)
            g_s[1, 1, at] = (g_mid[at] + g_r[1, 0, at].astype(F32)).astype(BF)

        g_copy(1, 1).start()

    gradient(1, 0, c_r)

    @pl.loop(0, rows // 64)
    def _(n):
        row = iota((64, 128), 0) + n * 64
        mine = jnp.where(slot_l == (row // seq_len).astype(F32), lane_l, 0.0)
        place = jnp.sum(mine, 1, keepdims=True) * seq_len + (row % seq_len).astype(F32)[:, :1]
        slot_hot[span(n * 64, 64), :] = jnp.where(
            iota((64, 2 * rows), 1).astype(F32) == place, 1.0, 0.0
        ).astype(BF)

    sum_parts(1, factor_at(owner_of(t // 4, (t // 2) % 2), ranks.shape[3]))
    for way in range(2):
        hop_copy(way).wait_recv()
        send_ring(way, way)
    pass_gradient()
    gathered(1)
    gradient(0, 1, x_r)

    sib_copy(3).wait_recv()
    for m in range(len(MESSAGES)):
        ad_copy(m).wait_recv()

    @pl.loop(0, tiles)
    def _(n):
        at = span(n * TILE, TILE)
        back = ad_r[:, :, :, at].reshape(2 * rows, TILE)
        hold[2, :, at] = hold[2, :, at] + sib_r[3, :, at].astype(F32) + mm(slot_hot[...], back)

    for way in range(2):
        for part in range(2):
            ring_copy(way, part).wait_recv()

    for part in range(2):

        def put(at, to):
            out_v[at] = (
                hold[2, at] + ring_r[0, part, to].astype(F32) + ring_r[1, part, to].astype(F32)
            ).astype(BF)

        half_rows(part, put)
    stores = [pltpu.make_async_copy(out_v, out_ref, out_sem.at[2])]
    stores[0].start()

    for n, g_ref in ((1, gb_ref), (0, ga_ref)):

        @pl.loop(n, 3)
        def _(which):
            g_copy(n, which).wait_recv()

        @pl.loop(0, g_own.shape[1] // 32)
        def _(k):
            at = span(k * 32, 32)
            total = g_own[n, at]
            for which in range(n, 3):
                total = total + g_r[n, which, at].astype(F32)
            g_own[n, at] = total

        stores.append(pltpu.make_async_copy(g_own.at[n], g_ref, out_sem.at[n]))
        stores[-1].start()

    for k in range(DP - 1):
        facts_copy(k).wait_send()
        tok_copy(0, k).wait_send()
        tok_copy(1, k).wait_send()

    for n in range(2):
        for axis in range(2):
            fac_copy(axis, n).wait_send()
        fac_relay(n).wait_send()
    for m in range(len(MESSAGES)):
        for h in range(2):
            x_copy(h, m).wait_send()
        c_copy(m).wait_send()
        ad_copy(m).wait_send()
    for j in (2, 3):
        sib_copy(j).wait_send()
    for way in range(2):
        hop_copy(way).wait_send()
        for part in range(2):
            ring_copy(way, part).wait_send()
    for kind in range(2):

        @pl.loop(1, TENSOR)
        def _(k):
            part_copy(kind, k).wait_send()
            gath_copy(kind, k).wait_send()

        @pl.loop(0, 3)
        def _(which):
            g_copy(kind, which).wait_send()

    for store in stores:
        store.wait()


def finish(out_ref, gb_ref, ga_ref, out_to, gb_to, ga_to, out_v, gb_v, ga_v, turned_v, sem):
    names = ((ga_ref, ga_v, turned_v, ga_to), (gb_ref, gb_v, gb_v, gb_to), (out_ref, out_v, out_v, out_to))
    loads = [pltpu.make_async_copy(src, held, sem.at[0, n]) for n, (src, held, _, _) in enumerate(names)]
    stores = [pltpu.make_async_copy(held, dst, sem.at[1, n]) for n, (_, _, held, dst) in enumerate(names)]
    for load in loads:
        load.start()
    loads[0].wait()
    turned_v[...] = ga_v[...].T
    stores[0].start()
    for n in (1, 2):
        loads[n].wait()
        stores[n].start()
    for store in stores:
        store.wait()


def on_device(
    tokens,
    destinations,
    counts,
    sequence_job_ids,
    job_owner_slot,
    rank_per_job,
    weight,
    input_factor_table,
    output_factor_table,
    cotangent,
):
    slot_count, seq_len, width = tokens.shape
    max_rank = input_factor_table.shape[2]
    rows = slot_count * seq_len
    anywhere = pl.BlockSpec(memory_space=pl.ANY)
    smem = pl.BlockSpec(memory_space=pltpu.SMEM)
    dma = pltpu.SemaphoreType.DMA
    served = (2, 2, RING, 64, width)
    lanes = (RING, RING, 64, width)
    out, ga, gb = pl.pallas_call(
        kernel,
        out_shape=(
            jax.ShapeDtypeStruct((rows, width), BF),
            jax.ShapeDtypeStruct((max_rank, width), F32),
            jax.ShapeDtypeStruct((max_rank, width), F32),
        ),
        in_specs=[smem] * 5 + [anywhere] * 5,
        out_specs=(anywhere,) * 3,
        scratch_shapes=[
            pltpu.VMEM(tokens.shape, BF),
            pltpu.VMEM((rows, width), BF),
            pltpu.VMEM(input_factor_table.shape, BF),
            pltpu.VMEM(output_factor_table.shape, BF),
            pltpu.VMEM((rows, width), BF),
            pltpu.VMEM((DP, seq_len, width), BF),
            pltpu.VMEM((DP, seq_len, width), BF),
            pltpu.VMEM((DP, 8, 128), jnp.int32),
            pltpu.VMEM((DP, 8, 128), jnp.int32),
            pltpu.VMEM((rows, rows), BF),
            pltpu.VMEM((2 * rows, rows), BF),
            pltpu.VMEM((2 * rows, rows), BF),
            pltpu.VMEM((rows, 2 * rows), BF),
            pltpu.VMEM((rows, width), BF),
            pltpu.VMEM(lanes, BF),
            pltpu.VMEM(served, BF),
            pltpu.VMEM(lanes, BF),
            pltpu.VMEM(served, BF),
            pltpu.VMEM((2, 2, width, max_rank), BF),
            pltpu.VMEM((2, 2, max_rank, width), BF),
            pltpu.VMEM((W_SLOTS, width, width), BF),
            pltpu.VMEM((2, rows, width), BF),
            pltpu.VMEM((4, rows, width), BF),
            pltpu.VMEM((3, rows, width), F32),
            pltpu.VMEM((2, rows // 2, width), BF),
            pltpu.VMEM((2, rows // 2, width), BF),
            pltpu.VMEM((2, 2, rows // 2, width), BF),
            pltpu.VMEM((2, 2, rows // 2, width), BF),
            pltpu.VMEM((2, TENSOR, 128, max_rank), BF),
            pltpu.VMEM((2, TENSOR, 128, max_rank), BF),
            pltpu.VMEM((2, TENSOR, 128, max_rank), BF),
            pltpu.VMEM(served, BF),
            pltpu.VMEM(lanes, BF),
            pltpu.VMEM((2, max_rank, width), F32),
            pltpu.VMEM((max_rank, width), F32),
            pltpu.VMEM((2, 4, max_rank, width), BF),
            pltpu.VMEM((2, 3, max_rank, width), BF),
            dma((4,)),
            dma((3,)),
            dma((W_SLOTS,)),
            dma((DP - 1,)),
            dma((DP - 1,)),
            dma((2, DP - 1)),
            dma((2, DP - 1)),
            dma((3, 2)),
            dma((2, 2, 2)),
            dma((8,)),
            dma((8,)),
            dma((2, 8)),
            dma((2, 8)),
            dma((2,)),
            dma((4,)),
            dma((2,)),
            dma((2,)),
            dma((2, 2)),
            dma((2, 2)),
            dma((2, TENSOR - 1)),
            dma((2, TENSOR - 1)),
            dma((2, TENSOR - 1)),
            dma((2, TENSOR - 1)),
            dma((8,)),
            dma((8,)),
            dma((2, 3)),
            dma((2, 3)),
        ],
        compiler_params=pltpu.CompilerParams(
            collective_id=0, has_side_effects=True, vmem_limit_bytes=58 * 2**20
        ),
    )(
        destinations,
        counts,
        sequence_job_ids,
        job_owner_slot,
        rank_per_job,
        tokens,
        cotangent.reshape(rows, width),
        input_factor_table,
        output_factor_table,
        weight,
    )
    out, gb, ga = pl.pallas_call(
        finish,
        out_shape=(
            jax.ShapeDtypeStruct((rows, width), BF),
            jax.ShapeDtypeStruct((max_rank, width), F32),
            jax.ShapeDtypeStruct((width, max_rank), F32),
        ),
        in_specs=[anywhere] * 3,
        out_specs=(anywhere,) * 3,
        scratch_shapes=[
            pltpu.VMEM((rows, width), BF),
            pltpu.VMEM((max_rank, width), F32),
            pltpu.VMEM((max_rank, width), F32),
            pltpu.VMEM((width, max_rank), F32),
            dma((2, 3)),
        ],
    )(out, gb, ga)
    return out.reshape(slot_count, seq_len, width), ga[None], gb[None]


def solution(mesh):
    in_specs = (
        P("dp", None, "tensor"),
        P("dp"),
        P("dp"),
        P("dp"),
        P(),
        P(),
        P("tensor", None),
        P("dp", "tensor", None),
        P("dp", None, "tensor"),
        P("dp", None, "tensor"),
    )
    out_specs = (P("dp", None, "tensor"), P("dp", "tensor", None), P("dp", None, "tensor"))
    return jax.shard_map(
        on_device, mesh=mesh, in_specs=in_specs, out_specs=out_specs, check_vma=False
    )
```

```python
import jax
import jax.numpy as jnp
from jax import lax
from jax.experimental import pallas as pl
from jax.experimental.pallas import tpu as pltpu
from jax.sharding import PartitionSpec as P

BF = jnp.bfloat16
F32 = jnp.float32
RING = 4
DP = RING * RING
TENSOR = 2 * RING
TILE = 256
W_SLOTS = 3
MOVE, PLACE = (0, 0, -1, 1), (0, 1, 1, 0)
BOTH = slice(0, 2)
MESSAGES = ((2, BOTH), (BOTH, 2), (3, BOTH), (BOTH, 3), (2, 2), (3, 3), (2, 3), (3, 2))
NEIGHBOURS = ((0, 1), (1, 0), (0, 3), (3, 0), (1, 1), (3, 3), (1, 3), (3, 1))
OTHERS = NEIGHBOURS + ((0, 2), (2, 0), (2, 1), (1, 2), (2, 3), (3, 2), (2, 2))


def mm(a, b):
    return jnp.dot(a, b, preferred_element_type=F32)


def kernel(
    dest_ref,
    count_ref,
    job_ref,
    owner_ref,
    rank_ref,
    tok_ref,
    cot_ref,
    a_ref,
    b_ref,
    w_ref,
    out_ref,
    ga_ref,
    gb_ref,
    tok_v,
    cot_v,
    a_v,
    b_v,
    out_v,
    tok_s,
    tok_r,
    facts_s,
    facts_r,
    place_hot,
    x_hot,
    c_hot,
    slot_hot,
    xs,
    x_s,
    x_r,
    c_s,
    c_r,
    fa,
    fb,
    wbuf,
    sib_s,
    sib_r,
    hold,
    hop_s,
    hop_r,
    ring_s,
    ring_r,
    part_s,
    part_r,
    ranks,
    ad_s,
    ad_r,
    g_own,
    g_mid,
    g_s,
    g_r,
    in_sem,
    out_sem,
    w_sem,
    facts_ss,
    facts_rs,
    tok_ss,
    tok_rs,
    fac_ss,
    fac_rs,
    c_ss,
    c_rs,
    x_ss,
    x_rs,
    sib_ss,
    sib_rs,
    tile_ss,
    tile_rs,
    hop_ss,
    hop_rs,
    ring_ss,
    ring_rs,
    part_ss,
    part_rs,
    gath_ss,
    gath_rs,
    ad_ss,
    ad_rs,
    g_ss,
    g_rs,
):
    seq_len, width = tok_ref.shape[1:]
    rows = DP * seq_len
    half = rows // 2
    me = lax.axis_index("dp")
    t = lax.axis_index("tensor")
    y, z = me // RING, me % RING
    x, c = t // 2, t % 2
    odd = (y + z) % 2
    ahead = 1 - 2 * odd
    others = ((1 - odd, 1 - odd), (odd, 1 - odd), (1 - odd, odd))
    tiles = width // TILE
    wide_half = width // 2

    def remote(src, dst, send, recv, **where):
        return pltpu.make_async_remote_copy(
            src_ref=src,
            dst_ref=dst,
            send_sem=send,
            recv_sem=recv,
            device_id=where,
            device_id_type=pl.DeviceIdType.MESH,
        )

    def iota(shape, axis):
        return lax.broadcasted_iota(jnp.int32, shape, axis)

    def near(dy, dz):
        return (y + dy + RING) % RING * RING + (z + dz + RING) % RING

    def owner_of(i, j):
        first, second = (y - i + RING) % RING, (z - j + RING) % RING
        shift = (first + second) % 2
        return (first + shift) % RING * RING + (second + shift) % RING

    def rank_at(owner):
        total = jnp.int32(0)
        for j in range(DP):
            total = total + jnp.where(owner_ref[j] == owner, rank_ref[j], 0)
        return total

    def factor_at(owner, columns):
        return 32.0 / jnp.full((1, columns), rank_at(owner).astype(F32), F32)

    def span(start, size):
        return pl.ds(pl.multiple_of(start, size), size)

    loads = [
        pltpu.make_async_copy(src, dst, in_sem.at[n])
        for n, (src, dst) in enumerate(((tok_ref, tok_v), (a_ref, a_v), (b_ref, b_v), (cot_ref, cot_v)))
    ]
    for load in loads:
        load.start()

    barrier = pltpu.get_barrier_semaphore()

    @pl.loop(1, DP)
    def _(k):
        pl.semaphore_signal(
            barrier, inc=1, device_id={"dp": (me + k) % DP}, device_id_type=pl.DeviceIdType.MESH
        )

    @pl.loop(1, TENSOR)
    def _(k):
        pl.semaphore_signal(
            barrier, inc=1, device_id={"tensor": (t + k) % TENSOR}, device_id_type=pl.DeviceIdType.MESH
        )

    def w_copy(i):
        j = i // 2
        block = (x + jnp.where(j == 0, 2, jnp.where(j == 1, 1, jnp.where(j == 2, 3, 0)))) % RING * 2
        block = block + (c + 1 - i % 2) % 2
        return pltpu.make_async_copy(
            w_ref.at[:, span(block * width, width)], wbuf.at[i % W_SLOTS], w_sem.at[i % W_SLOTS]
        )

    for i in range(W_SLOTS):
        w_copy(jnp.int32(i)).start()

    def chosen(to):
        index = jnp.int32(0)
        for i in range(DP):
            index = jnp.where(lax.shift_right_logical(dest_ref[i], 4) == to, i, index)
        return index

    @pl.loop(0, DP)
    def _(to):
        index = chosen(to)
        owner = owner_ref[job_ref[index]]
        oy, oz = lax.shift_right_logical(owner, 2), owner & 3
        shift = (oy + oz) & 1
        dy, dz = (to // RING + RING - oy + shift) & 3, (to % RING + RING - oz + shift) & 3
        base = (dy * RING + dz) * 2
        row = iota((8, 128), 0)
        facts_s[to] = jnp.where(
            row == 0, dest_ref[index] & 15, jnp.where(row == 1, count_ref[index], base)
        )

    facts_r[me] = facts_s[me]
    loads[0].wait()

    @pl.loop(0, DP)
    def _(to):
        tok_s[to] = tok_v[chosen(to)]

    tok_r[me] = tok_s[me]

    pl.semaphore_wait(barrier, DP - 1 + TENSOR - 1)

    def facts_copy(k):
        to = near(*OTHERS[k])
        return remote(facts_s.at[to], facts_r.at[me], facts_ss.at[k], facts_rs.at[k], dp=to)

    def tok_copy(h, k):
        to, columns = near(*OTHERS[k]), span(h * wide_half, wide_half)
        return remote(
            tok_s.at[to, :, columns],
            tok_r.at[me, :, columns],
            tok_ss.at[h, k],
            tok_rs.at[h, k],
            dp=to,
        )

    def fac_copy(axis, n):
        table = (fa, fb)[n]
        there = ((1 - odd, odd), (odd, 1 - odd))[axis]
        to = (near(ahead, 0), near(0, ahead))[axis]
        return remote(
            table.at[odd, odd], table.at[there], fac_ss.at[axis, n], fac_rs.at[there + (n,)], dp=to
        )

    def fac_wait(n, which):
        for there in which:
            held = (fa, fb)[n].at[there]
            remote(held, held, fac_ss.at[0, n], fac_rs.at[there + (n,)], dp=me).wait_recv()

    def fac_relay(n):
        table = (fa, fb)[n]
        here = ((odd, 1 - odd), (1 - odd, odd))[n]
        to = (near(0, -ahead), near(-ahead, 0))[n]
        return remote(table.at[here], table.at[odd, odd], fac_ss.at[2, n], fac_rs.at[odd, odd, n], dp=to)

    for k in range(DP - 1):
        facts_copy(k).start()

    @pl.loop(0, 2)
    def _(h):
        for k in range(DP - 1):
            tok_copy(h, k).start()

    my_rank = rank_at(me)
    loads[1].wait()

    @pl.loop(0, width // 128)
    def _(n):
        at = span(n * 128, 128)
        kept = iota((128, a_v.shape[2]), 1) < my_rank
        fa[odd, odd, at, :] = jnp.where(kept, a_v[0, at, :].astype(F32), 0.0).astype(BF)

    for axis in range(2):
        fac_copy(axis, 0).start()
    loads[2].wait()

    @pl.loop(0, width // 128)
    def _(n):
        at = span(n * 128, 128)
        kept = iota((b_v.shape[1], 128), 0) < my_rank
        fb[odd, odd, :, at] = jnp.where(kept, b_v[0, :, at].astype(F32), 0.0).astype(BF)

    for k in range(DP - 1):
        facts_copy(k).wait_recv()

    slot_c = facts_r[:, 0, :].astype(F32)
    live_c = facts_r[:, 1, :].astype(F32)
    base_c = facts_r[:, 2, :].astype(F32)
    square = (DP, 128)
    diagonal = iota(square, 0) == iota(square, 1)
    slot_l = jnp.sum(jnp.where(diagonal, slot_c, 0.0), 0, keepdims=True)
    base_l = jnp.sum(jnp.where(diagonal, base_c, 0.0), 0, keepdims=True)
    earlier = (base_l == base_c) & (slot_l < slot_c) & (iota(square, 1) < DP)
    turn_c = jnp.sum(jnp.where(earlier, 1.0, 0.0), 1, keepdims=True)
    lane_c = base_c + turn_c
    lane_l = jnp.sum(jnp.where(diagonal, lane_c, 0.0), 0, keepdims=True)
    wide = (DP, rows)
    seq_of = iota(wide, 1) // seq_len
    slot_1, live_1, lane_1 = slot_c[:, :1], live_c[:, :1], lane_c[:, :1]
    in_slot = slot_1 == seq_of.astype(F32)
    in_order = iota(wide, 0) == seq_of
    position = (iota((1, rows), 1) % seq_len).astype(F32)

    def spread(where, value):
        return jnp.sum(jnp.where(where, value, 0.0), 0, keepdims=True)

    live = position < spread(in_order, live_1)
    c_row = spread(in_slot, lane_1) * seq_len + position
    x_row = jnp.where(live, spread(in_order, lane_1) * seq_len + position, -1.0)
    slot_row = jnp.where(live, spread(in_order, slot_1) * seq_len + position, -1.0)

    def build(hot, wanted):
        @pl.loop(0, hot.shape[0] // 64)
        def _(n):
            row = (iota((64, rows), 0) + n * 64).astype(F32)
            hot[span(n * 64, 64), :] = jnp.where(row == wanted, 1.0, 0.0).astype(BF)

    build(x_hot, x_row)
    build(place_hot, slot_row)

    lane_shape = (RING, RING, 2 * seq_len)

    def lane_place(dy, dz):
        row = PLACE[dy] if dy != BOTH else BOTH
        column = PLACE[dz] if dz != BOTH else BOTH
        return row, column, (dy != BOTH) * 2 + (dz != BOTH)

    def lane_move(dy, dz):
        return (MOVE[dy] if dy != BOTH else 0, MOVE[dz] if dz != BOTH else 0)

    def x_copy(h, m):
        message, columns = MESSAGES[m], span(h * wide_half, wide_half)
        return remote(
            x_s.at[message + (slice(None), columns)],
            x_r.at[lane_place(*message) + (slice(None), columns)],
            x_ss.at[h, m],
            x_rs.at[h, m],
            dp=near(*lane_move(*message)),
        )

    def c_copy(m):
        message = MESSAGES[m]
        return remote(
            c_s.at[message],
            c_r.at[lane_place(*message)],
            c_ss.at[m],
            c_rs.at[m],
            dp=near(*lane_move(*message)),
        )

    @pl.loop(0, 2)
    def _(h):
        for k in range(DP - 1):
            tok_copy(h, k).wait_recv()

        @pl.loop(0, tiles // 2)
        def _(n):
            at = span(h * wide_half + n * TILE, TILE)
            landed = tok_r[:, :, at].reshape(rows, TILE)
            x_s[:, :, :, at] = mm(x_hot[...], landed).astype(BF).reshape(lane_shape + (TILE,))

        for m in range(len(MESSAGES)):
            x_copy(h, m).start()

        @pl.loop(0, tiles // 2)
        def _(n):
            at = span(h * wide_half + n * TILE, TILE)
            xs[:, at] = mm(place_hot[...], tok_r[:, :, at].reshape(rows, TILE)).astype(BF)

    for axis in range(2):
        fac_copy(axis, 1).start()
    build(c_hot, c_row)
    loads[3].wait()

    @pl.loop(0, tiles)
    def _(n):
        at = span(n * TILE, TILE)
        c_s[:, :, :, at] = mm(c_hot[...], cot_v[:, at]).astype(BF).reshape(lane_shape + (TILE,))

    fac_wait(0, others[1:])
    fac_relay(0).start()
    x_r[:, :, 0] = x_s[BOTH, BOTH]
    c_r[:, :, 0] = c_s[BOTH, BOTH]

    def sib_copy(j):
        return remote(
            sib_s.at[j % 2], sib_r.at[j], sib_ss.at[j % 2], sib_rs.at[j], tensor=x * 2 + (1 - c)
        )

    right, left = ((x + 1) % RING) * 2 + c, ((x + 3) % RING) * 2 + c

    def hop_copy(way, n):
        at = span(n * TILE, TILE)
        return remote(
            hop_s.at[way, :, at],
            hop_r.at[way, :, at],
            hop_ss.at[way, n],
            hop_rs.at[way, n],
            tensor=(right, left)[way],
        )

    def sib_tile(n):
        at = span(n * TILE, TILE)
        return remote(
            sib_s.at[0, :, at], sib_r.at[0, :, at], tile_ss.at[n], tile_rs.at[n], tensor=x * 2 + (1 - c)
        )

    def ring_copy(way, part):
        return remote(
            ring_s.at[way, part],
            ring_r.at[way, part],
            ring_ss.at[way, part],
            ring_rs.at[way, part],
            tensor=(right, left)[way],
        )

    def half_rows(part, put):
        @pl.loop(0, half // 32)
        def _(n):
            put(span(part * half + n * 32, 32), span(n * 32, 32))

    def send_hop(n):
        at = span(n * TILE, TILE)
        sib_tile(n).wait_recv()
        for way in range(2):
            part = slice(way * half, (way + 1) * half)
            hop_s[way, :, at] = (hold[0, part, at] + sib_r[0, part, at].astype(F32)).astype(BF)
            hop_copy(way, n).start()

    def send_ring(way, part):
        def put(at, to):
            value = hold[1 - way, at] + sib_r[1 + way, at].astype(F32)
            if way == part:
                value = value + hop_r[way, to].astype(F32)
            ring_s[way, part, to] = value.astype(BF)

        half_rows(part, put)
        ring_copy(way, part).start()

    def part_copy(kind, k):
        to = (t + k) % TENSOR
        return remote(
            part_s.at[kind, to],
            part_r.at[kind, k],
            part_ss.at[kind, k - 1],
            part_rs.at[kind, k - 1],
            tensor=to,
        )

    def gath_copy(kind, k):
        to = (t + k) % TENSOR
        held = ranks.at[kind, t]
        return remote(held, held, gath_ss.at[kind, k - 1], gath_rs.at[kind, k - 1], tensor=to)

    def served(ref, i, j):
        return ref[i, j].reshape(RING * 64, width)

    def send_parts(kind, make):
        @pl.loop(0, 4)
        def _(q):
            value = make(q // 2, q % 2).astype(BF)
            part_s[kind, 2 * q] = value[:128]
            part_s[kind, 2 * q + 1] = value[128:]

        @pl.loop(1, TENSOR)
        def _(k):
            part_copy(kind, k).start()

        part_r[kind, 0] = part_s[kind, t]

    def sum_parts(kind, scale):
        @pl.loop(1, TENSOR)
        def _(k):
            part_copy(kind, k).wait_recv()

        total = part_r[kind, 0].astype(F32)
        for k in range(1, TENSOR):
            total = total + part_r[kind, k].astype(F32)
        ranks[kind, t] = (total if scale is None else total * scale).astype(BF)

        @pl.loop(1, TENSOR)
        def _(k):
            gath_copy(kind, k).start()

    def gathered(kind):
        @pl.loop(1, TENSOR)
        def _(k):
            held = ranks.at[kind, (t + TENSOR - k) % TENSOR]
            remote(held, held, gath_ss.at[kind, k - 1], gath_rs.at[kind, k - 1], tensor=t).wait_recv()

    def rank_rows(kind, i, j):
        return ranks[kind, pl.ds(i * 4 + j * 2, 2)].reshape(RING * 64, ranks.shape[3])

    for i in range(2):
        w_copy(jnp.int32(i)).wait()

    @pl.loop(0, tiles)
    def _(n):
        at = span(n * TILE, TILE)
        sib_s[0, :, at] = mm(xs[...], wbuf[0, :, at]).astype(BF)
        sib_tile(n).start()
        hold[0, :, at] = mm(xs[...], wbuf[1, :, at])

        @pl.when(n > 0)
        def _():
            send_hop(n - 1)

    for i in range(2):
        w_copy(jnp.int32(i + W_SLOTS)).start()
    send_hop(jnp.int32(tiles - 1))

    @pl.loop(1, 4)
    def _(j):
        w_copy(2 * j).wait()

        @pl.when(j == 2)
        def _():
            for n in range(tiles):
                sib_tile(n).wait_send()

        @pl.when(j == 3)
        def _():
            sib_copy(1).wait_send()

        @pl.loop(0, tiles)
        def _(n):
            at = span(n * TILE, TILE)
            sib_s[j % 2, :, at] = mm(xs[...], wbuf[(2 * j) % W_SLOTS, :, at]).astype(BF)

        sib_copy(j).start()

        @pl.when(2 * j + W_SLOTS < 8)
        def _():
            w_copy(2 * j + W_SLOTS).start()

        @pl.when(j == 3)
        def _():
            sib_copy(2).wait_recv()
            send_ring(1, 0)

        w_copy(2 * j + 1).wait()

        @pl.loop(0, tiles)
        def _(n):
            at = span(n * TILE, TILE)
            hold[jnp.where(j == 3, 2, j % 2), :, at] = mm(xs[...], wbuf[(2 * j + 1) % W_SLOTS, :, at])

        @pl.when(2 * j + 1 + W_SLOTS < 8)
        def _():
            w_copy(2 * j + 1 + W_SLOTS).start()

        @pl.when(j == 1)
        def _():
            fac_wait(0, others[:1])

            @pl.loop(0, 2)
            def _(h):
                for m in range(len(MESSAGES)):
                    x_copy(h, m).wait_recv()

            send_parts(0, lambda i, k: mm(served(x_r, i, k), fa[i, k]))
            for m in range(4):
                c_copy(m).start()
            fac_wait(1, others[1:])
            fac_relay(1).start()
            for m in range(4, len(MESSAGES)):
                c_copy(m).start()

        @pl.when(j == 2)
        def _():
            sum_parts(0, None)
            sib_copy(1).wait_recv()
            send_ring(0, 1)

    def ad_copy(m):
        message = MESSAGES[m]
        dy, dz = lane_move(*message)
        return remote(
            ad_s.at[lane_place(*message)],
            ad_r.at[message],
            ad_ss.at[m],
            ad_rs.at[m],
            dp=near(-dy, -dz),
        )

    fac_wait(1, others[:1])
    gathered(0)

    @pl.loop(0, 4)
    def _(q):
        i, j = q // 2, q % 2
        value = mm(rank_rows(0, i, j), fb[i, j]) * factor_at(owner_of(i, j), width)
        ad_s[i, j] = value.astype(BF).reshape(RING, 64, width)

    for m in range(len(MESSAGES)):
        ad_copy(m).start()
    ad_r[BOTH, BOTH] = ad_s[:, :, 0]

    for m in range(len(MESSAGES)):
        c_copy(m).wait_recv()
    send_parts(
        1,
        lambda i, j: lax.dot_general(
            served(c_r, i, j), fb[i, j], (((1,), (1,)), ((), ())), preferred_element_type=F32
        ),
    )

    def g_copy(n, which):
        dy = jnp.where(which == 0, -ahead * (1 - n), jnp.where(which == 1, ahead, 0))
        dz = jnp.where(which == 0, -ahead, jnp.where(which == 1, 0, ahead))
        return remote(
            g_s.at[n, which],
            g_r.at[n, which],
            g_ss.at[n, which],
            g_rs.at[n, which],
            dp=near(dy, dz),
        )

    def gradient(n, kind, row_ref):
        @pl.loop(0, 4)
        def _(which):
            i = jnp.where((which == 1) | (which == 3), odd, 1 - odd)
            j = jnp.where(which >= 2, odd, 1 - odd)
            turned = rank_rows(kind, i, j).astype(F32).T.astype(BF)
            value = mm(turned, served(row_ref, i, j)) * (1.0 / seq_len)
            if n == 1:
                value = value * factor_at(owner_of(i, j), width)
            g_own[n] = value
            g_s[n, which] = value.astype(BF)
            if n == 1:

                @pl.when(which == 1)
                def _():
                    g_mid[...] = value

            @pl.when((which == 0) | (which == 2) | ((which == 1) & (n == 0)))
            def _():
                g_copy(n, which).start()

    def pass_gradient():
        g_copy(1, 0).wait_recv()

        @pl.loop(0, g_mid.shape[0] // 32)
        def _(k):
            at = span(k * 32, 32)
            g_s[1, 1, at] = (g_mid[at] + g_r[1, 0, at].astype(F32)).astype(BF)

        g_copy(1, 1).start()

    gradient(1, 0, c_r)

    @pl.loop(0, rows // 64)
    def _(n):
        row = iota((64, 128), 0) + n * 64
        mine = jnp.where(slot_l == (row // seq_len).astype(F32), lane_l, 0.0)
        place = jnp.sum(mine, 1, keepdims=True) * seq_len + (row % seq_len).astype(F32)[:, :1]
        slot_hot[span(n * 64, 64), :] = jnp.where(
            iota((64, 2 * rows), 1).astype(F32) == place, 1.0, 0.0
        ).astype(BF)

    sum_parts(1, factor_at(owner_of(t // 4, (t // 2) % 2), ranks.shape[3]))
    for way in range(2):
        for n in range(tiles):
            hop_copy(way, n).wait_recv()
        send_ring(way, way)
    pass_gradient()
    gathered(1)
    gradient(0, 1, x_r)

    sib_copy(3).wait_recv()
    for m in range(len(MESSAGES)):
        ad_copy(m).wait_recv()

    @pl.loop(0, tiles)
    def _(n):
        at = span(n * TILE, TILE)
        back = ad_r[:, :, :, at].reshape(2 * rows, TILE)
        hold[2, :, at] = hold[2, :, at] + sib_r[3, :, at].astype(F32) + mm(slot_hot[...], back)

    for way in range(2):
        for part in range(2):
            ring_copy(way, part).wait_recv()

    for part in range(2):

        def put(at, to):
            out_v[at] = (
                hold[2, at] + ring_r[0, part, to].astype(F32) + ring_r[1, part, to].astype(F32)
            ).astype(BF)

        half_rows(part, put)
    stores = [pltpu.make_async_copy(out_v, out_ref, out_sem.at[2])]
    stores[0].start()

    for n, g_ref in ((1, gb_ref), (0, ga_ref)):

        @pl.loop(n, 3)
        def _(which):
            g_copy(n, which).wait_recv()

        @pl.loop(0, g_own.shape[1] // 32)
        def _(k):
            at = span(k * 32, 32)
            total = g_own[n, at]
            for which in range(n, 3):
                total = total + g_r[n, which, at].astype(F32)
            g_own[n, at] = total

        stores.append(pltpu.make_async_copy(g_own.at[n], g_ref, out_sem.at[n]))
        stores[-1].start()

    for k in range(DP - 1):
        facts_copy(k).wait_send()
        tok_copy(0, k).wait_send()
        tok_copy(1, k).wait_send()

    for n in range(2):
        for axis in range(2):
            fac_copy(axis, n).wait_send()
        fac_relay(n).wait_send()
    for m in range(len(MESSAGES)):
        for h in range(2):
            x_copy(h, m).wait_send()
        c_copy(m).wait_send()
        ad_copy(m).wait_send()
    for j in (2, 3):
        sib_copy(j).wait_send()
    for way in range(2):
        for n in range(tiles):
            hop_copy(way, n).wait_send()
        for part in range(2):
            ring_copy(way, part).wait_send()
    for kind in range(2):

        @pl.loop(1, TENSOR)
        def _(k):
            part_copy(kind, k).wait_send()
            gath_copy(kind, k).wait_send()

        @pl.loop(0, 3)
        def _(which):
            g_copy(kind, which).wait_send()

    for store in stores:
        store.wait()


def finish(out_ref, gb_ref, ga_ref, out_to, gb_to, ga_to, out_v, gb_v, ga_v, turned_v, sem):
    names = ((ga_ref, ga_v, turned_v, ga_to), (gb_ref, gb_v, gb_v, gb_to), (out_ref, out_v, out_v, out_to))
    loads = [pltpu.make_async_copy(src, held, sem.at[0, n]) for n, (src, held, _, _) in enumerate(names)]
    stores = [pltpu.make_async_copy(held, dst, sem.at[1, n]) for n, (_, _, held, dst) in enumerate(names)]
    for load in loads:
        load.start()
    loads[0].wait()
    turned_v[...] = ga_v[...].T
    stores[0].start()
    for n in (1, 2):
        loads[n].wait()
        stores[n].start()
    for store in stores:
        store.wait()


def on_device(
    tokens,
    destinations,
    counts,
    sequence_job_ids,
    job_owner_slot,
    rank_per_job,
    weight,
    input_factor_table,
    output_factor_table,
    cotangent,
):
    slot_count, seq_len, width = tokens.shape
    max_rank = input_factor_table.shape[2]
    rows = slot_count * seq_len
    anywhere = pl.BlockSpec(memory_space=pl.ANY)
    smem = pl.BlockSpec(memory_space=pltpu.SMEM)
    dma = pltpu.SemaphoreType.DMA
    served = (2, 2, RING, 64, width)
    lanes = (RING, RING, 64, width)
    out, ga, gb = pl.pallas_call(
        kernel,
        out_shape=(
            jax.ShapeDtypeStruct((rows, width), BF),
            jax.ShapeDtypeStruct((max_rank, width), F32),
            jax.ShapeDtypeStruct((max_rank, width), F32),
        ),
        in_specs=[smem] * 5 + [anywhere] * 5,
        out_specs=(anywhere,) * 3,
        scratch_shapes=[
            pltpu.VMEM(tokens.shape, BF),
            pltpu.VMEM((rows, width), BF),
            pltpu.VMEM(input_factor_table.shape, BF),
            pltpu.VMEM(output_factor_table.shape, BF),
            pltpu.VMEM((rows, width), BF),
            pltpu.VMEM((DP, seq_len, width), BF),
            pltpu.VMEM((DP, seq_len, width), BF),
            pltpu.VMEM((DP, 8, 128), jnp.int32),
            pltpu.VMEM((DP, 8, 128), jnp.int32),
            pltpu.VMEM((rows, rows), BF),
            pltpu.VMEM((2 * rows, rows), BF),
            pltpu.VMEM((2 * rows, rows), BF),
            pltpu.VMEM((rows, 2 * rows), BF),
            pltpu.VMEM((rows, width), BF),
            pltpu.VMEM(lanes, BF),
            pltpu.VMEM(served, BF),
            pltpu.VMEM(lanes, BF),
            pltpu.VMEM(served, BF),
            pltpu.VMEM((2, 2, width, max_rank), BF),
            pltpu.VMEM((2, 2, max_rank, width), BF),
            pltpu.VMEM((W_SLOTS, width, width), BF),
            pltpu.VMEM((2, rows, width), BF),
            pltpu.VMEM((4, rows, width), BF),
            pltpu.VMEM((3, rows, width), F32),
            pltpu.VMEM((2, rows // 2, width), BF),
            pltpu.VMEM((2, rows // 2, width), BF),
            pltpu.VMEM((2, 2, rows // 2, width), BF),
            pltpu.VMEM((2, 2, rows // 2, width), BF),
            pltpu.VMEM((2, TENSOR, 128, max_rank), BF),
            pltpu.VMEM((2, TENSOR, 128, max_rank), BF),
            pltpu.VMEM((2, TENSOR, 128, max_rank), BF),
            pltpu.VMEM(served, BF),
            pltpu.VMEM(lanes, BF),
            pltpu.VMEM((2, max_rank, width), F32),
            pltpu.VMEM((max_rank, width), F32),
            pltpu.VMEM((2, 4, max_rank, width), BF),
            pltpu.VMEM((2, 3, max_rank, width), BF),
            dma((4,)),
            dma((3,)),
            dma((W_SLOTS,)),
            dma((DP - 1,)),
            dma((DP - 1,)),
            dma((2, DP - 1)),
            dma((2, DP - 1)),
            dma((3, 2)),
            dma((2, 2, 2)),
            dma((8,)),
            dma((8,)),
            dma((2, 8)),
            dma((2, 8)),
            dma((2,)),
            dma((4,)),
            dma((4,)),
            dma((4,)),
            dma((2, 4)),
            dma((2, 4)),
            dma((2, 2)),
            dma((2, 2)),
            dma((2, TENSOR - 1)),
            dma((2, TENSOR - 1)),
            dma((2, TENSOR - 1)),
            dma((2, TENSOR - 1)),
            dma((8,)),
            dma((8,)),
            dma((2, 3)),
            dma((2, 3)),
        ],
        compiler_params=pltpu.CompilerParams(
            collective_id=0, has_side_effects=True, vmem_limit_bytes=58 * 2**20
        ),
    )(
        destinations,
        counts,
        sequence_job_ids,
        job_owner_slot,
        rank_per_job,
        tokens,
        cotangent.reshape(rows, width),
        input_factor_table,
        output_factor_table,
        weight,
    )
    out, gb, ga = pl.pallas_call(
        finish,
        out_shape=(
            jax.ShapeDtypeStruct((rows, width), BF),
            jax.ShapeDtypeStruct((max_rank, width), F32),
            jax.ShapeDtypeStruct((width, max_rank), F32),
        ),
        in_specs=[anywhere] * 3,
        out_specs=(anywhere,) * 3,
        scratch_shapes=[
            pltpu.VMEM((rows, width), BF),
            pltpu.VMEM((max_rank, width), F32),
            pltpu.VMEM((max_rank, width), F32),
            pltpu.VMEM((width, max_rank), F32),
            dma((2, 3)),
        ],
    )(out, gb, ga)
    return out.reshape(slot_count, seq_len, width), ga[None], gb[None]


def solution(mesh):
    in_specs = (
        P("dp", None, "tensor"),
        P("dp"),
        P("dp"),
        P("dp"),
        P(),
        P(),
        P("tensor", None),
        P("dp", "tensor", None),
        P("dp", None, "tensor"),
        P("dp", None, "tensor"),
    )
    out_specs = (P("dp", None, "tensor"), P("dp", "tensor", None), P("dp", None, "tensor"))
    return jax.shard_map(
        on_device, mesh=mesh, in_specs=in_specs, out_specs=out_specs, check_vma=False
    )
```

```python
import jax
import jax.numpy as jnp
from jax import lax
from jax.experimental import pallas as pl
from jax.experimental.pallas import tpu as pltpu
from jax.sharding import PartitionSpec as P

BF = jnp.bfloat16
F32 = jnp.float32
RING = 4
DP = RING * RING
TENSOR = 2 * RING
TILE = 256
W_SLOTS = 3
MOVE, PLACE = (0, 0, -1, 1), (0, 1, 1, 0)
BOTH = slice(0, 2)
MESSAGES = ((2, BOTH), (BOTH, 2), (3, BOTH), (BOTH, 3), (2, 2), (3, 3), (2, 3), (3, 2))
NEIGHBOURS = ((0, 1), (1, 0), (0, 3), (3, 0), (1, 1), (3, 3), (1, 3), (3, 1))
OTHERS = NEIGHBOURS + ((0, 2), (2, 0), (2, 1), (1, 2), (2, 3), (3, 2), (2, 2))


def mm(a, b):
    return jnp.dot(a, b, preferred_element_type=F32)


def kernel(
    dest_ref,
    count_ref,
    job_ref,
    owner_ref,
    rank_ref,
    tok_ref,
    cot_ref,
    a_ref,
    b_ref,
    w_ref,
    out_ref,
    ga_ref,
    gb_ref,
    tok_v,
    cot_v,
    a_v,
    b_v,
    out_v,
    tok_s,
    tok_r,
    source,
    facts_s,
    facts_r,
    place_hot,
    x_hot,
    c_hot,
    slot_hot,
    xs,
    x_s,
    x_r,
    c_s,
    c_r,
    fa,
    fb,
    wbuf,
    sib_s,
    sib_r,
    hold,
    hop_s,
    hop_r,
    ring_s,
    ring_r,
    part_s,
    part_r,
    ranks,
    ad_s,
    ad_r,
    g_own,
    g_mid,
    g_s,
    g_r,
    in_sem,
    out_sem,
    w_sem,
    facts_ss,
    facts_rs,
    tok_ss,
    tok_rs,
    fac_ss,
    fac_rs,
    c_ss,
    c_rs,
    x_ss,
    x_rs,
    sib_ss,
    sib_rs,
    tile_ss,
    tile_rs,
    hop_ss,
    hop_rs,
    ring_ss,
    ring_rs,
    part_ss,
    part_rs,
    gath_ss,
    gath_rs,
    ad_ss,
    ad_rs,
    g_ss,
    g_rs,
):
    seq_len, width = tok_ref.shape[1:]
    rows = DP * seq_len
    half = rows // 2
    me = lax.axis_index("dp")
    t = lax.axis_index("tensor")
    y, z = me // RING, me % RING
    x, c = t // 2, t % 2
    odd = (y + z) % 2
    ahead = 1 - 2 * odd
    others = ((1 - odd, 1 - odd), (odd, 1 - odd), (1 - odd, odd))
    tiles = width // TILE
    wide_half = width // 2

    def remote(src, dst, send, recv, **where):
        return pltpu.make_async_remote_copy(
            src_ref=src,
            dst_ref=dst,
            send_sem=send,
            recv_sem=recv,
            device_id=where,
            device_id_type=pl.DeviceIdType.MESH,
        )

    def iota(shape, axis):
        return lax.broadcasted_iota(jnp.int32, shape, axis)

    def near(dy, dz):
        return (y + dy + RING) % RING * RING + (z + dz + RING) % RING

    def owner_of(i, j):
        first, second = (y - i + RING) % RING, (z - j + RING) % RING
        shift = (first + second) % 2
        return (first + shift) % RING * RING + (second + shift) % RING

    def rank_at(owner):
        total = jnp.int32(0)
        for j in range(DP):
            total = total + jnp.where(owner_ref[j] == owner, rank_ref[j], 0)
        return total

    def factor_at(owner, columns):
        return 32.0 / jnp.full((1, columns), rank_at(owner).astype(F32), F32)

    def span(start, size):
        return pl.ds(pl.multiple_of(start, size), size)

    loads = [
        pltpu.make_async_copy(src, dst, in_sem.at[n])
        for n, (src, dst) in enumerate(((tok_ref, tok_v), (a_ref, a_v), (b_ref, b_v), (cot_ref, cot_v)))
    ]
    for load in loads:
        load.start()

    barrier = pltpu.get_barrier_semaphore()

    @pl.loop(1, DP)
    def _(k):
        pl.semaphore_signal(
            barrier, inc=1, device_id={"dp": (me + k) % DP}, device_id_type=pl.DeviceIdType.MESH
        )

    @pl.loop(1, TENSOR)
    def _(k):
        pl.semaphore_signal(
            barrier, inc=1, device_id={"tensor": (t + k) % TENSOR}, device_id_type=pl.DeviceIdType.MESH
        )

    def w_copy(i):
        j = i // 2
        block = (x + jnp.where(j == 0, 2, jnp.where(j == 1, 1, jnp.where(j == 2, 3, 0)))) % RING * 2
        block = block + (c + 1 - i % 2) % 2
        return pltpu.make_async_copy(
            w_ref.at[:, span(block * width, width)], wbuf.at[i % W_SLOTS], w_sem.at[i % W_SLOTS]
        )

    for i in range(W_SLOTS):
        w_copy(jnp.int32(i)).start()

    def chosen(to):
        index = jnp.int32(0)
        for i in range(DP):
            index = jnp.where(lax.shift_right_logical(dest_ref[i], 4) == to, i, index)
        return index

    @pl.loop(0, DP)
    def _(to):
        index = chosen(to)
        source[to] = index
        owner = owner_ref[job_ref[index]]
        oy, oz = lax.shift_right_logical(owner, 2), owner & 3
        shift = (oy + oz) & 1
        dy, dz = (to // RING + RING - oy + shift) & 3, (to % RING + RING - oz + shift) & 3
        base = (dy * RING + dz) * 2
        row = iota((8, 128), 0)
        facts_s[to] = jnp.where(
            row == 0, dest_ref[index] & 15, jnp.where(row == 1, count_ref[index], base)
        )

    facts_r[me] = facts_s[me]
    loads[0].wait()

    @pl.loop(0, DP)
    def _(to):
        tok_s[to] = tok_v[source[to]]

    tok_r[me] = tok_s[me]

    pl.semaphore_wait(barrier, DP - 1 + TENSOR - 1)

    def facts_copy(k):
        to = near(*OTHERS[k])
        return remote(facts_s.at[to], facts_r.at[me], facts_ss.at[k], facts_rs.at[k], dp=to)

    def tok_copy(h, k):
        to, columns = near(*OTHERS[k]), span(h * wide_half, wide_half)
        return remote(
            tok_s.at[to, :, columns],
            tok_r.at[me, :, columns],
            tok_ss.at[h, k],
            tok_rs.at[h, k],
            dp=to,
        )

    def fac_copy(axis, n):
        table = (fa, fb)[n]
        there = ((1 - odd, odd), (odd, 1 - odd))[axis]
        to = (near(ahead, 0), near(0, ahead))[axis]
        return remote(
            table.at[odd, odd], table.at[there], fac_ss.at[axis, n], fac_rs.at[there + (n,)], dp=to
        )

    def fac_wait(n, which):
        for there in which:
            held = (fa, fb)[n].at[there]
            remote(held, held, fac_ss.at[0, n], fac_rs.at[there + (n,)], dp=me).wait_recv()

    def fac_relay(n):
        table = (fa, fb)[n]
        here = ((odd, 1 - odd), (1 - odd, odd))[n]
        to = (near(0, -ahead), near(-ahead, 0))[n]
        return remote(table.at[here], table.at[odd, odd], fac_ss.at[2, n], fac_rs.at[odd, odd, n], dp=to)

    for k in range(DP - 1):
        facts_copy(k).start()

    @pl.loop(0, 2)
    def _(h):
        for k in range(DP - 1):
            tok_copy(h, k).start()

    my_rank = rank_at(me)
    loads[1].wait()

    @pl.loop(0, width // 128)
    def _(n):
        at = span(n * 128, 128)
        kept = iota((128, a_v.shape[2]), 1) < my_rank
        fa[odd, odd, at, :] = jnp.where(kept, a_v[0, at, :].astype(F32), 0.0).astype(BF)

    for axis in range(2):
        fac_copy(axis, 0).start()
    loads[2].wait()

    @pl.loop(0, width // 128)
    def _(n):
        at = span(n * 128, 128)
        kept = iota((b_v.shape[1], 128), 0) < my_rank
        fb[odd, odd, :, at] = jnp.where(kept, b_v[0, :, at].astype(F32), 0.0).astype(BF)

    for k in range(DP - 1):
        facts_copy(k).wait_recv()

    slot_c = facts_r[:, 0, :].astype(F32)
    live_c = facts_r[:, 1, :].astype(F32)
    base_c = facts_r[:, 2, :].astype(F32)
    square = (DP, 128)
    diagonal = iota(square, 0) == iota(square, 1)
    slot_l = jnp.sum(jnp.where(diagonal, slot_c, 0.0), 0, keepdims=True)
    base_l = jnp.sum(jnp.where(diagonal, base_c, 0.0), 0, keepdims=True)
    earlier = (base_l == base_c) & (slot_l < slot_c) & (iota(square, 1) < DP)
    turn_c = jnp.sum(jnp.where(earlier, 1.0, 0.0), 1, keepdims=True)
    lane_c = base_c + turn_c
    lane_l = jnp.sum(jnp.where(diagonal, lane_c, 0.0), 0, keepdims=True)
    wide = (DP, rows)
    seq_of = iota(wide, 1) // seq_len
    slot_1, live_1, lane_1 = slot_c[:, :1], live_c[:, :1], lane_c[:, :1]
    in_slot = slot_1 == seq_of.astype(F32)
    in_order = iota(wide, 0) == seq_of
    position = (iota((1, rows), 1) % seq_len).astype(F32)

    def spread(where, value):
        return jnp.sum(jnp.where(where, value, 0.0), 0, keepdims=True)

    live = position < spread(in_order, live_1)
    c_row = spread(in_slot, lane_1) * seq_len + position
    x_row = jnp.where(live, spread(in_order, lane_1) * seq_len + position, -1.0)
    slot_row = jnp.where(live, spread(in_order, slot_1) * seq_len + position, -1.0)

    def build(hot, wanted):
        @pl.loop(0, hot.shape[0] // 64)
        def _(n):
            row = (iota((64, rows), 0) + n * 64).astype(F32)
            hot[span(n * 64, 64), :] = jnp.where(row == wanted, 1.0, 0.0).astype(BF)

    build(x_hot, x_row)
    build(place_hot, slot_row)

    lane_shape = (RING, RING, 2 * seq_len)

    def lane_place(dy, dz):
        row = PLACE[dy] if dy != BOTH else BOTH
        column = PLACE[dz] if dz != BOTH else BOTH
        return row, column, (dy != BOTH) * 2 + (dz != BOTH)

    def lane_move(dy, dz):
        return (MOVE[dy] if dy != BOTH else 0, MOVE[dz] if dz != BOTH else 0)

    def x_copy(h, m):
        message, columns = MESSAGES[m], span(h * wide_half, wide_half)
        return remote(
            x_s.at[message + (slice(None), columns)],
            x_r.at[lane_place(*message) + (slice(None), columns)],
            x_ss.at[h, m],
            x_rs.at[h, m],
            dp=near(*lane_move(*message)),
        )

    def c_copy(m):
        message = MESSAGES[m]
        return remote(
            c_s.at[message],
            c_r.at[lane_place(*message)],
            c_ss.at[m],
            c_rs.at[m],
            dp=near(*lane_move(*message)),
        )

    @pl.loop(0, 2)
    def _(h):
        for k in range(DP - 1):
            tok_copy(h, k).wait_recv()

        @pl.loop(0, tiles // 2)
        def _(n):
            at = span(h * wide_half + n * TILE, TILE)
            landed = tok_r[:, :, at].reshape(rows, TILE)
            x_s[:, :, :, at] = mm(x_hot[...], landed).astype(BF).reshape(lane_shape + (TILE,))

        for m in range(len(MESSAGES)):
            x_copy(h, m).start()

        @pl.loop(0, tiles // 2)
        def _(n):
            at = span(h * wide_half + n * TILE, TILE)
            xs[:, at] = mm(place_hot[...], tok_r[:, :, at].reshape(rows, TILE)).astype(BF)

    for axis in range(2):
        fac_copy(axis, 1).start()
    build(c_hot, c_row)
    loads[3].wait()

    @pl.loop(0, tiles)
    def _(n):
        at = span(n * TILE, TILE)
        c_s[:, :, :, at] = mm(c_hot[...], cot_v[:, at]).astype(BF).reshape(lane_shape + (TILE,))

    fac_wait(0, others[1:])
    fac_relay(0).start()
    x_r[:, :, 0] = x_s[BOTH, BOTH]
    c_r[:, :, 0] = c_s[BOTH, BOTH]

    def sib_copy(j):
        return remote(
            sib_s.at[j % 2], sib_r.at[j], sib_ss.at[j % 2], sib_rs.at[j], tensor=x * 2 + (1 - c)
        )

    right, left = ((x + 1) % RING) * 2 + c, ((x + 3) % RING) * 2 + c

    def hop_copy(way, n):
        at = span(n * TILE, TILE)
        return remote(
            hop_s.at[way, :, at],
            hop_r.at[way, :, at],
            hop_ss.at[way, n],
            hop_rs.at[way, n],
            tensor=(right, left)[way],
        )

    def sib_tile(n):
        at = span(n * TILE, TILE)
        return remote(
            sib_s.at[0, :, at], sib_r.at[0, :, at], tile_ss.at[n], tile_rs.at[n], tensor=x * 2 + (1 - c)
        )

    def ring_copy(way, part):
        return remote(
            ring_s.at[way, part],
            ring_r.at[way, part],
            ring_ss.at[way, part],
            ring_rs.at[way, part],
            tensor=(right, left)[way],
        )

    def half_rows(part, put):
        @pl.loop(0, half // 32)
        def _(n):
            put(span(part * half + n * 32, 32), span(n * 32, 32))

    def send_hop(n):
        at = span(n * TILE, TILE)
        sib_tile(n).wait_recv()
        for way in range(2):
            part = slice(way * half, (way + 1) * half)
            hop_s[way, :, at] = (hold[0, part, at] + sib_r[0, part, at].astype(F32)).astype(BF)
            hop_copy(way, n).start()

    def sum_ring(way, part):
        def put(at, to):
            value = hold[1 - way, at] + sib_r[1 + way, at].astype(F32)
            if way == part:
                value = value + hop_r[way, to].astype(F32)
            ring_s[way, part, to] = value.astype(BF)

        half_rows(part, put)

    def part_copy(kind, k):
        to = (t + k) % TENSOR
        return remote(
            part_s.at[kind, to],
            part_r.at[kind, k],
            part_ss.at[kind, k - 1],
            part_rs.at[kind, k - 1],
            tensor=to,
        )

    def gath_copy(kind, k):
        to = (t + k) % TENSOR
        held = ranks.at[kind, t]
        return remote(held, held, gath_ss.at[kind, k - 1], gath_rs.at[kind, k - 1], tensor=to)

    def served(ref, i, j):
        return ref[i, j].reshape(RING * 64, width)

    def send_parts(kind, make):
        @pl.loop(0, 4)
        def _(q):
            value = make(q // 2, q % 2).astype(BF)
            for piece in range(2):
                block = 2 * q + piece
                part_s[kind, block] = value[piece * 128 : (piece + 1) * 128]
                k = (block - t + TENSOR) % TENSOR

                @pl.when(k > 0)
                def _():
                    part_copy(kind, k).start()

        part_r[kind, 0] = part_s[kind, t]

    def sum_parts(kind, scale):
        @pl.loop(1, TENSOR)
        def _(k):
            part_copy(kind, k).wait_recv()

        total = part_r[kind, 0].astype(F32)
        for k in range(1, TENSOR):
            total = total + part_r[kind, k].astype(F32)
        ranks[kind, t] = (total if scale is None else total * scale).astype(BF)

        @pl.loop(1, TENSOR)
        def _(k):
            gath_copy(kind, k).start()

    def gathered(kind):
        @pl.loop(1, TENSOR)
        def _(k):
            held = ranks.at[kind, (t + TENSOR - k) % TENSOR]
            remote(held, held, gath_ss.at[kind, k - 1], gath_rs.at[kind, k - 1], tensor=t).wait_recv()

    def rank_rows(kind, i, j):
        return ranks[kind, pl.ds(i * 4 + j * 2, 2)].reshape(RING * 64, ranks.shape[3])

    for i in range(2):
        w_copy(jnp.int32(i)).wait()

    @pl.loop(0, tiles)
    def _(n):
        at = span(n * TILE, TILE)
        sib_s[0, :, at] = mm(xs[...], wbuf[0, :, at]).astype(BF)
        sib_tile(n).start()
        hold[0, :, at] = mm(xs[...], wbuf[1, :, at])

        @pl.when(n > 0)
        def _():
            send_hop(n - 1)

    for i in range(2):
        w_copy(jnp.int32(i + W_SLOTS)).start()
    send_hop(jnp.int32(tiles - 1))

    @pl.loop(1, 4)
    def _(j):
        w_copy(2 * j).wait()

        @pl.when(j == 2)
        def _():
            for n in range(tiles):
                sib_tile(n).wait_send()

        @pl.when(j == 3)
        def _():
            sib_copy(1).wait_send()

        @pl.loop(0, tiles)
        def _(n):
            at = span(n * TILE, TILE)
            sib_s[j % 2, :, at] = mm(xs[...], wbuf[(2 * j) % W_SLOTS, :, at]).astype(BF)

        sib_copy(j).start()

        @pl.when(2 * j + W_SLOTS < 8)
        def _():
            w_copy(2 * j + W_SLOTS).start()

        w_copy(2 * j + 1).wait()

        @pl.loop(0, tiles)
        def _(n):
            at = span(n * TILE, TILE)
            hold[jnp.where(j == 3, 2, j % 2), :, at] = mm(xs[...], wbuf[(2 * j + 1) % W_SLOTS, :, at])

        @pl.when(2 * j + 1 + W_SLOTS < 8)
        def _():
            w_copy(2 * j + 1 + W_SLOTS).start()

        @pl.when(j == 1)
        def _():
            fac_wait(0, others[:1])

            @pl.loop(0, 2)
            def _(h):
                for m in range(len(MESSAGES)):
                    x_copy(h, m).wait_recv()

            send_parts(0, lambda i, k: mm(served(x_r, i, k), fa[i, k]))
            for m in range(4):
                c_copy(m).start()
            fac_wait(1, others[1:])
            fac_relay(1).start()
            for m in range(4, len(MESSAGES)):
                c_copy(m).start()

        @pl.when(j == 2)
        def _():
            sum_parts(0, None)
            for way in range(2):
                sib_copy(1 + way).wait_recv()
                sum_ring(way, 1 - way)
                ring_copy(way, 1 - way).start()

    def ad_copy(m):
        message = MESSAGES[m]
        dy, dz = lane_move(*message)
        return remote(
            ad_s.at[lane_place(*message)],
            ad_r.at[message],
            ad_ss.at[m],
            ad_rs.at[m],
            dp=near(-dy, -dz),
        )

    fac_wait(1, others[:1])
    gathered(0)

    @pl.loop(0, 4)
    def _(q):
        i, j = q // 2, q % 2
        value = mm(rank_rows(0, i, j), fb[i, j]) * factor_at(owner_of(i, j), width)
        ad_s[i, j] = value.astype(BF).reshape(RING, 64, width)

    for m in range(len(MESSAGES)):
        ad_copy(m).start()
    ad_r[BOTH, BOTH] = ad_s[:, :, 0]

    for m in range(len(MESSAGES)):
        c_copy(m).wait_recv()
    send_parts(
        1,
        lambda i, j: lax.dot_general(
            served(c_r, i, j), fb[i, j], (((1,), (1,)), ((), ())), preferred_element_type=F32
        ),
    )

    def g_copy(n, which):
        dy = jnp.where(which == 0, -ahead * (1 - n), jnp.where(which == 1, ahead, 0))
        dz = jnp.where(which == 0, -ahead, jnp.where(which == 1, 0, ahead))
        return remote(
            g_s.at[n, which],
            g_r.at[n, which],
            g_ss.at[n, which],
            g_rs.at[n, which],
            dp=near(dy, dz),
        )

    def gradient(n, kind, row_ref):
        @pl.loop(0, 4)
        def _(which):
            i = jnp.where((which == 1) | (which == 3), odd, 1 - odd)
            j = jnp.where(which >= 2, odd, 1 - odd)
            turned = rank_rows(kind, i, j).astype(F32).T.astype(BF)
            value = mm(turned, served(row_ref, i, j)) * (1.0 / seq_len)
            if n == 1:
                value = value * factor_at(owner_of(i, j), width)
            g_own[n] = value
            g_s[n, which] = value.astype(BF)
            if n == 1:

                @pl.when(which == 1)
                def _():
                    g_mid[...] = value

            @pl.when((which == 0) | (which == 2) | ((which == 1) & (n == 0)))
            def _():
                g_copy(n, which).start()

    def pass_gradient():
        g_copy(1, 0).wait_recv()

        @pl.loop(0, g_mid.shape[0] // 32)
        def _(k):
            at = span(k * 32, 32)
            g_s[1, 1, at] = (g_mid[at] + g_r[1, 0, at].astype(F32)).astype(BF)

        g_copy(1, 1).start()

    gradient(1, 0, c_r)

    @pl.loop(0, rows // 64)
    def _(n):
        row = iota((64, 128), 0) + n * 64
        mine = jnp.where(slot_l == (row // seq_len).astype(F32), lane_l, 0.0)
        place = jnp.sum(mine, 1, keepdims=True) * seq_len + (row % seq_len).astype(F32)[:, :1]
        slot_hot[span(n * 64, 64), :] = jnp.where(
            iota((64, 2 * rows), 1).astype(F32) == place, 1.0, 0.0
        ).astype(BF)

    for way in range(2):
        for n in range(tiles):
            hop_copy(way, n).wait_recv()
        sum_ring(way, way)
    sum_parts(1, factor_at(owner_of(t // 4, (t // 2) % 2), ranks.shape[3]))
    for way in range(2):
        ring_copy(way, way).start()
    pass_gradient()
    gathered(1)
    gradient(0, 1, x_r)

    sib_copy(3).wait_recv()
    for m in range(len(MESSAGES)):
        ad_copy(m).wait_recv()

    @pl.loop(0, tiles)
    def _(n):
        at = span(n * TILE, TILE)
        back = ad_r[:, :, :, at].reshape(2 * rows, TILE)
        hold[2, :, at] = hold[2, :, at] + sib_r[3, :, at].astype(F32) + mm(slot_hot[...], back)

    for way in range(2):
        for part in range(2):
            ring_copy(way, part).wait_recv()

    for part in range(2):

        def put(at, to):
            out_v[at] = (
                hold[2, at] + ring_r[0, part, to].astype(F32) + ring_r[1, part, to].astype(F32)
            ).astype(BF)

        half_rows(part, put)
    stores = [pltpu.make_async_copy(out_v, out_ref, out_sem.at[2])]
    stores[0].start()

    for n, g_ref in ((1, gb_ref), (0, ga_ref)):

        @pl.loop(n, 3)
        def _(which):
            g_copy(n, which).wait_recv()

        @pl.loop(0, g_own.shape[1] // 32)
        def _(k):
            at = span(k * 32, 32)
            total = g_own[n, at]
            for which in range(n, 3):
                total = total + g_r[n, which, at].astype(F32)
            g_own[n, at] = total

        stores.append(pltpu.make_async_copy(g_own.at[n], g_ref, out_sem.at[n]))
        stores[-1].start()

    for k in range(DP - 1):
        facts_copy(k).wait_send()
        tok_copy(0, k).wait_send()
        tok_copy(1, k).wait_send()

    for n in range(2):
        for axis in range(2):
            fac_copy(axis, n).wait_send()
        fac_relay(n).wait_send()
    for m in range(len(MESSAGES)):
        for h in range(2):
            x_copy(h, m).wait_send()
        c_copy(m).wait_send()
        ad_copy(m).wait_send()
    for j in (2, 3):
        sib_copy(j).wait_send()
    for way in range(2):
        for n in range(tiles):
            hop_copy(way, n).wait_send()
        for part in range(2):
            ring_copy(way, part).wait_send()
    for kind in range(2):

        @pl.loop(1, TENSOR)
        def _(k):
            part_copy(kind, k).wait_send()
            gath_copy(kind, k).wait_send()

        @pl.loop(0, 3)
        def _(which):
            g_copy(kind, which).wait_send()

    for store in stores:
        store.wait()


def finish(out_ref, gb_ref, ga_ref, out_to, gb_to, ga_to, out_v, gb_v, ga_v, turned_v, sem):
    names = ((ga_ref, ga_v, turned_v, ga_to), (gb_ref, gb_v, gb_v, gb_to), (out_ref, out_v, out_v, out_to))
    loads = [pltpu.make_async_copy(src, held, sem.at[0, n]) for n, (src, held, _, _) in enumerate(names)]
    stores = [pltpu.make_async_copy(held, dst, sem.at[1, n]) for n, (_, _, held, dst) in enumerate(names)]
    for load in loads:
        load.start()
    loads[0].wait()
    turned_v[...] = ga_v[...].T
    stores[0].start()
    for n in (1, 2):
        loads[n].wait()
        stores[n].start()
    for store in stores:
        store.wait()


def on_device(
    tokens,
    destinations,
    counts,
    sequence_job_ids,
    job_owner_slot,
    rank_per_job,
    weight,
    input_factor_table,
    output_factor_table,
    cotangent,
):
    slot_count, seq_len, width = tokens.shape
    max_rank = input_factor_table.shape[2]
    rows = slot_count * seq_len
    anywhere = pl.BlockSpec(memory_space=pl.ANY)
    smem = pl.BlockSpec(memory_space=pltpu.SMEM)
    dma = pltpu.SemaphoreType.DMA
    served = (2, 2, RING, 64, width)
    lanes = (RING, RING, 64, width)
    out, ga, gb = pl.pallas_call(
        kernel,
        out_shape=(
            jax.ShapeDtypeStruct((rows, width), BF),
            jax.ShapeDtypeStruct((max_rank, width), F32),
            jax.ShapeDtypeStruct((max_rank, width), F32),
        ),
        in_specs=[smem] * 5 + [anywhere] * 5,
        out_specs=(anywhere,) * 3,
        scratch_shapes=[
            pltpu.VMEM(tokens.shape, BF),
            pltpu.VMEM((rows, width), BF),
            pltpu.VMEM(input_factor_table.shape, BF),
            pltpu.VMEM(output_factor_table.shape, BF),
            pltpu.VMEM((rows, width), BF),
            pltpu.VMEM((DP, seq_len, width), BF),
            pltpu.VMEM((DP, seq_len, width), BF),
            pltpu.SMEM((DP,), jnp.int32),
            pltpu.VMEM((DP, 8, 128), jnp.int32),
            pltpu.VMEM((DP, 8, 128), jnp.int32),
            pltpu.VMEM((rows, rows), BF),
            pltpu.VMEM((2 * rows, rows), BF),
            pltpu.VMEM((2 * rows, rows), BF),
            pltpu.VMEM((rows, 2 * rows), BF),
            pltpu.VMEM((rows, width), BF),
            pltpu.VMEM(lanes, BF),
            pltpu.VMEM(served, BF),
            pltpu.VMEM(lanes, BF),
            pltpu.VMEM(served, BF),
            pltpu.VMEM((2, 2, width, max_rank), BF),
            pltpu.VMEM((2, 2, max_rank, width), BF),
            pltpu.VMEM((W_SLOTS, width, width), BF),
            pltpu.VMEM((2, rows, width), BF),
            pltpu.VMEM((4, rows, width), BF),
            pltpu.VMEM((3, rows, width), F32),
            pltpu.VMEM((2, rows // 2, width), BF),
            pltpu.VMEM((2, rows // 2, width), BF),
            pltpu.VMEM((2, 2, rows // 2, width), BF),
            pltpu.VMEM((2, 2, rows // 2, width), BF),
            pltpu.VMEM((2, TENSOR, 128, max_rank), BF),
            pltpu.VMEM((2, TENSOR, 128, max_rank), BF),
            pltpu.VMEM((2, TENSOR, 128, max_rank), BF),
            pltpu.VMEM(served, BF),
            pltpu.VMEM(lanes, BF),
            pltpu.VMEM((2, max_rank, width), F32),
            pltpu.VMEM((max_rank, width), F32),
            pltpu.VMEM((2, 4, max_rank, width), BF),
            pltpu.VMEM((2, 3, max_rank, width), BF),
            dma((4,)),
            dma((3,)),
            dma((W_SLOTS,)),
            dma((DP - 1,)),
            dma((DP - 1,)),
            dma((2, DP - 1)),
            dma((2, DP - 1)),
            dma((3, 2)),
            dma((2, 2, 2)),
            dma((8,)),
            dma((8,)),
            dma((2, 8)),
            dma((2, 8)),
            dma((2,)),
            dma((4,)),
            dma((4,)),
            dma((4,)),
            dma((2, 4)),
            dma((2, 4)),
            dma((2, 2)),
            dma((2, 2)),
            dma((2, TENSOR - 1)),
            dma((2, TENSOR - 1)),
            dma((2, TENSOR - 1)),
            dma((2, TENSOR - 1)),
            dma((8,)),
            dma((8,)),
            dma((2, 3)),
            dma((2, 3)),
        ],
        compiler_params=pltpu.CompilerParams(
            collective_id=0, has_side_effects=True, vmem_limit_bytes=58 * 2**20
        ),
    )(
        destinations,
        counts,
        sequence_job_ids,
        job_owner_slot,
        rank_per_job,
        tokens,
        cotangent.reshape(rows, width),
        input_factor_table,
        output_factor_table,
        weight,
    )
    out, gb, ga = pl.pallas_call(
        finish,
        out_shape=(
            jax.ShapeDtypeStruct((rows, width), BF),
            jax.ShapeDtypeStruct((max_rank, width), F32),
            jax.ShapeDtypeStruct((width, max_rank), F32),
        ),
        in_specs=[anywhere] * 3,
        out_specs=(anywhere,) * 3,
        scratch_shapes=[
            pltpu.VMEM((rows, width), BF),
            pltpu.VMEM((max_rank, width), F32),
            pltpu.VMEM((max_rank, width), F32),
            pltpu.VMEM((width, max_rank), F32),
            dma((2, 3)),
        ],
    )(out, gb, ga)
    return out.reshape(slot_count, seq_len, width), ga[None], gb[None]


def solution(mesh):
    in_specs = (
        P("dp", None, "tensor"),
        P("dp"),
        P("dp"),
        P("dp"),
        P(),
        P(),
        P("tensor", None),
        P("dp", "tensor", None),
        P("dp", None, "tensor"),
        P("dp", None, "tensor"),
    )
    out_specs = (P("dp", None, "tensor"), P("dp", "tensor", None), P("dp", None, "tensor"))
    return jax.shard_map(
        on_device, mesh=mesh, in_specs=in_specs, out_specs=out_specs, check_vma=False
    )
```

```python
import jax
import jax.numpy as jnp
from jax import lax
from jax.experimental import pallas as pl
from jax.experimental.pallas import tpu as pltpu
from jax.sharding import PartitionSpec as P

BF = jnp.bfloat16
F32 = jnp.float32
RING = 4
DP = RING * RING
TENSOR = 2 * RING
TILE = 256
W_SLOTS = 3
MOVE, PLACE = (0, 0, -1, 1), (0, 1, 1, 0)
BOTH = slice(0, 2)
MESSAGES = ((2, BOTH), (BOTH, 2), (3, BOTH), (BOTH, 3), (2, 2), (3, 3), (2, 3), (3, 2))
NEIGHBOURS = ((0, 1), (1, 0), (0, 3), (3, 0), (1, 1), (3, 3), (1, 3), (3, 1))
OTHERS = NEIGHBOURS + ((0, 2), (2, 0), (2, 1), (1, 2), (2, 3), (3, 2), (2, 2))


def mm(a, b):
    return jnp.dot(a, b, preferred_element_type=F32)


def kernel(
    dest_ref,
    count_ref,
    job_ref,
    owner_ref,
    rank_ref,
    tok_ref,
    cot_ref,
    a_ref,
    b_ref,
    w_ref,
    out_ref,
    ga_ref,
    gb_ref,
    tok_v,
    cot_v,
    a_v,
    b_v,
    out_v,
    tok_s,
    tok_r,
    source,
    facts_s,
    facts_r,
    place_hot,
    x_hot,
    c_hot,
    slot_hot,
    xs,
    x_s,
    x_r,
    c_s,
    c_r,
    fa,
    fb,
    wbuf,
    sib_s,
    sib_r,
    hold,
    hop_s,
    hop_r,
    ring_s,
    ring_r,
    part_s,
    part_r,
    ranks,
    ad_s,
    ad_r,
    g_own,
    g_mid,
    g_s,
    g_r,
    in_sem,
    out_sem,
    w_sem,
    facts_ss,
    facts_rs,
    tok_ss,
    tok_rs,
    fac_ss,
    fac_rs,
    c_ss,
    c_rs,
    x_ss,
    x_rs,
    sib_ss,
    sib_rs,
    tile_ss,
    tile_rs,
    hop_ss,
    hop_rs,
    ring_ss,
    ring_rs,
    part_ss,
    part_rs,
    gath_ss,
    gath_rs,
    ad_ss,
    ad_rs,
    g_ss,
    g_rs,
):
    seq_len, width = tok_ref.shape[1:]
    rows = DP * seq_len
    half = rows // 2
    me = lax.axis_index("dp")
    t = lax.axis_index("tensor")
    y, z = me // RING, me % RING
    x, c = t // 2, t % 2
    odd = (y + z) % 2
    ahead = 1 - 2 * odd
    others = ((1 - odd, 1 - odd), (odd, 1 - odd), (1 - odd, odd))
    tiles = width // TILE
    wide_half = width // 2

    def remote(src, dst, send, recv, **where):
        return pltpu.make_async_remote_copy(
            src_ref=src,
            dst_ref=dst,
            send_sem=send,
            recv_sem=recv,
            device_id=where,
            device_id_type=pl.DeviceIdType.MESH,
        )

    def iota(shape, axis):
        return lax.broadcasted_iota(jnp.int32, shape, axis)

    def near(dy, dz):
        return (y + dy + RING) % RING * RING + (z + dz + RING) % RING

    def owner_of(i, j):
        first, second = (y - i + RING) % RING, (z - j + RING) % RING
        shift = (first + second) % 2
        return (first + shift) % RING * RING + (second + shift) % RING

    def rank_at(owner):
        total = jnp.int32(0)
        for j in range(DP):
            total = total + jnp.where(owner_ref[j] == owner, rank_ref[j], 0)
        return total

    def factor_at(owner, columns):
        return 32.0 / jnp.full((1, columns), rank_at(owner).astype(F32), F32)

    def span(start, size):
        return pl.ds(pl.multiple_of(start, size), size)

    loads = [
        pltpu.make_async_copy(src, dst, in_sem.at[n])
        for n, (src, dst) in enumerate(((tok_ref, tok_v), (a_ref, a_v), (b_ref, b_v), (cot_ref, cot_v)))
    ]
    for load in loads:
        load.start()

    barrier = pltpu.get_barrier_semaphore()

    @pl.loop(1, DP)
    def _(k):
        pl.semaphore_signal(
            barrier, inc=1, device_id={"dp": (me + k) % DP}, device_id_type=pl.DeviceIdType.MESH
        )

    @pl.loop(1, TENSOR)
    def _(k):
        pl.semaphore_signal(
            barrier, inc=1, device_id={"tensor": (t + k) % TENSOR}, device_id_type=pl.DeviceIdType.MESH
        )

    def w_copy(i):
        j = i // 2
        block = (x + jnp.where(j == 0, 2, jnp.where(j == 1, 1, jnp.where(j == 2, 3, 0)))) % RING * 2
        block = block + (c + 1 - i % 2) % 2
        return pltpu.make_async_copy(
            w_ref.at[:, span(block * width, width)], wbuf.at[i % W_SLOTS], w_sem.at[i % W_SLOTS]
        )

    for i in range(W_SLOTS):
        w_copy(jnp.int32(i)).start()

    def chosen(to):
        index = jnp.int32(0)
        for i in range(DP):
            index = jnp.where(lax.shift_right_logical(dest_ref[i], 4) == to, i, index)
        return index

    @pl.loop(0, DP)
    def _(to):
        index = chosen(to)
        source[to] = index
        owner = owner_ref[job_ref[index]]
        oy, oz = lax.shift_right_logical(owner, 2), owner & 3
        shift = (oy + oz) & 1
        dy, dz = (to // RING + RING - oy + shift) & 3, (to % RING + RING - oz + shift) & 3
        base = (dy * RING + dz) * 2
        row = iota((8, 128), 0)
        facts_s[to] = jnp.where(
            row == 0, dest_ref[index] & 15, jnp.where(row == 1, count_ref[index], base)
        )

    facts_r[me] = facts_s[me]
    loads[0].wait()

    @pl.loop(0, DP)
    def _(to):
        tok_s[to] = tok_v[source[to]]

    tok_r[me] = tok_s[me]

    pl.semaphore_wait(barrier, DP - 1 + TENSOR - 1)

    def facts_copy(k):
        to = near(*OTHERS[k])
        return remote(facts_s.at[to], facts_r.at[me], facts_ss.at[k], facts_rs.at[k], dp=to)

    def tok_copy(h, k):
        to, columns = near(*OTHERS[k]), span(h * wide_half, wide_half)
        return remote(
            tok_s.at[to, :, columns],
            tok_r.at[me, :, columns],
            tok_ss.at[h, k],
            tok_rs.at[h, k],
            dp=to,
        )

    def fac_copy(axis, n):
        table = (fa, fb)[n]
        there = ((1 - odd, odd), (odd, 1 - odd))[axis]
        to = (near(ahead, 0), near(0, ahead))[axis]
        return remote(
            table.at[odd, odd], table.at[there], fac_ss.at[axis, n], fac_rs.at[there + (n,)], dp=to
        )

    def fac_wait(n, which):
        for there in which:
            held = (fa, fb)[n].at[there]
            remote(held, held, fac_ss.at[0, n], fac_rs.at[there + (n,)], dp=me).wait_recv()

    def fac_relay(n):
        table = (fa, fb)[n]
        here = ((odd, 1 - odd), (1 - odd, odd))[n]
        to = (near(0, -ahead), near(-ahead, 0))[n]
        return remote(table.at[here], table.at[odd, odd], fac_ss.at[2, n], fac_rs.at[odd, odd, n], dp=to)

    for k in range(DP - 1):
        facts_copy(k).start()

    @pl.loop(0, 2)
    def _(h):
        for k in range(DP - 1):
            tok_copy(h, k).start()

    my_rank = rank_at(me)
    loads[1].wait()

    @pl.loop(0, width // 128)
    def _(n):
        at = span(n * 128, 128)
        kept = iota((128, a_v.shape[2]), 1) < my_rank
        fa[odd, odd, at, :] = jnp.where(kept, a_v[0, at, :].astype(F32), 0.0).astype(BF)

    for axis in range(2):
        fac_copy(axis, 0).start()
    loads[2].wait()

    @pl.loop(0, width // 128)
    def _(n):
        at = span(n * 128, 128)
        kept = iota((b_v.shape[1], 128), 0) < my_rank
        fb[odd, odd, :, at] = jnp.where(kept, b_v[0, :, at].astype(F32), 0.0).astype(BF)

    for k in range(DP - 1):
        facts_copy(k).wait_recv()

    slot_c = facts_r[:, 0, :].astype(F32)
    live_c = facts_r[:, 1, :].astype(F32)
    base_c = facts_r[:, 2, :].astype(F32)
    square = (DP, 128)
    diagonal = iota(square, 0) == iota(square, 1)
    slot_l = jnp.sum(jnp.where(diagonal, slot_c, 0.0), 0, keepdims=True)
    base_l = jnp.sum(jnp.where(diagonal, base_c, 0.0), 0, keepdims=True)
    earlier = (base_l == base_c) & (slot_l < slot_c) & (iota(square, 1) < DP)
    turn_c = jnp.sum(jnp.where(earlier, 1.0, 0.0), 1, keepdims=True)
    lane_c = base_c + turn_c
    lane_l = jnp.sum(jnp.where(diagonal, lane_c, 0.0), 0, keepdims=True)
    wide = (DP, rows)
    seq_of = iota(wide, 1) // seq_len
    slot_1, live_1, lane_1 = slot_c[:, :1], live_c[:, :1], lane_c[:, :1]
    in_slot = slot_1 == seq_of.astype(F32)
    in_order = iota(wide, 0) == seq_of
    position = (iota((1, rows), 1) % seq_len).astype(F32)

    def spread(where, value):
        return jnp.sum(jnp.where(where, value, 0.0), 0, keepdims=True)

    live = position < spread(in_order, live_1)
    c_row = spread(in_slot, lane_1) * seq_len + position
    x_row = jnp.where(live, spread(in_order, lane_1) * seq_len + position, -1.0)
    slot_row = jnp.where(live, spread(in_order, slot_1) * seq_len + position, -1.0)

    def build(hot, wanted):
        @pl.loop(0, hot.shape[0] // 64)
        def _(n):
            row = (iota((64, rows), 0) + n * 64).astype(F32)
            hot[span(n * 64, 64), :] = jnp.where(row == wanted, 1.0, 0.0).astype(BF)

    build(x_hot, x_row)
    build(place_hot, slot_row)

    lane_shape = (RING, RING, 2 * seq_len)

    def lane_place(dy, dz):
        row = PLACE[dy] if dy != BOTH else BOTH
        column = PLACE[dz] if dz != BOTH else BOTH
        return row, column, (dy != BOTH) * 2 + (dz != BOTH)

    def lane_move(dy, dz):
        return (MOVE[dy] if dy != BOTH else 0, MOVE[dz] if dz != BOTH else 0)

    def x_copy(h, m):
        message, columns = MESSAGES[m], span(h * wide_half, wide_half)
        return remote(
            x_s.at[message + (slice(None), columns)],
            x_r.at[lane_place(*message) + (slice(None), columns)],
            x_ss.at[h, m],
            x_rs.at[h, m],
            dp=near(*lane_move(*message)),
        )

    def c_copy(m):
        message = MESSAGES[m]
        return remote(
            c_s.at[message],
            c_r.at[lane_place(*message)],
            c_ss.at[m],
            c_rs.at[m],
            dp=near(*lane_move(*message)),
        )

    @pl.loop(0, 2)
    def _(h):
        for k in range(DP - 1):
            tok_copy(h, k).wait_recv()

        @pl.loop(0, tiles // 2)
        def _(n):
            at = span(h * wide_half + n * TILE, TILE)
            landed = tok_r[:, :, at].reshape(rows, TILE)
            x_s[:, :, :, at] = mm(x_hot[...], landed).astype(BF).reshape(lane_shape + (TILE,))

        for m in range(len(MESSAGES)):
            x_copy(h, m).start()

        @pl.loop(0, tiles // 2)
        def _(n):
            at = span(h * wide_half + n * TILE, TILE)
            xs[:, at] = mm(place_hot[...], tok_r[:, :, at].reshape(rows, TILE)).astype(BF)

    for axis in range(2):
        fac_copy(axis, 1).start()
    build(c_hot, c_row)
    loads[3].wait()

    @pl.loop(0, tiles)
    def _(n):
        at = span(n * TILE, TILE)
        c_s[:, :, :, at] = mm(c_hot[...], cot_v[:, at]).astype(BF).reshape(lane_shape + (TILE,))

    fac_wait(0, others[1:])
    fac_relay(0).start()
    for m in range(4):
        c_copy(m).start()
    x_r[:, :, 0] = x_s[BOTH, BOTH]
    c_r[:, :, 0] = c_s[BOTH, BOTH]

    def sib_copy(j):
        return remote(
            sib_s.at[j % 2], sib_r.at[j], sib_ss.at[j % 2], sib_rs.at[j], tensor=x * 2 + (1 - c)
        )

    right, left = ((x + 1) % RING) * 2 + c, ((x + 3) % RING) * 2 + c

    def hop_copy(way, n):
        at = span(n * TILE, TILE)
        return remote(
            hop_s.at[way, :, at],
            hop_r.at[way, :, at],
            hop_ss.at[way, n],
            hop_rs.at[way, n],
            tensor=(right, left)[way],
        )

    def sib_tile(n):
        at = span(n * TILE, TILE)
        return remote(
            sib_s.at[0, :, at], sib_r.at[0, :, at], tile_ss.at[n], tile_rs.at[n], tensor=x * 2 + (1 - c)
        )

    def ring_copy(way, part):
        return remote(
            ring_s.at[way, part],
            ring_r.at[way, part],
            ring_ss.at[way, part],
            ring_rs.at[way, part],
            tensor=(right, left)[way],
        )

    def half_rows(part, put):
        @pl.loop(0, half // 32)
        def _(n):
            put(span(part * half + n * 32, 32), span(n * 32, 32))

    def send_hop(n):
        at = span(n * TILE, TILE)
        sib_tile(n).wait_recv()
        for way in range(2):
            part = slice(way * half, (way + 1) * half)
            hop_s[way, :, at] = (hold[0, part, at] + sib_r[0, part, at].astype(F32)).astype(BF)
            hop_copy(way, n).start()

    def sum_ring(way, part):
        def put(at, to):
            value = hold[1 - way, at] + sib_r[1 + way, at].astype(F32)
            if way == part:
                value = value + hop_r[way, to].astype(F32)
            ring_s[way, part, to] = value.astype(BF)

        half_rows(part, put)

    def part_copy(kind, k):
        to = (t + k) % TENSOR
        return remote(
            part_s.at[kind, to],
            part_r.at[kind, k],
            part_ss.at[kind, k - 1],
            part_rs.at[kind, k - 1],
            tensor=to,
        )

    def gath_copy(kind, k):
        to = (t + k) % TENSOR
        held = ranks.at[kind, t]
        return remote(held, held, gath_ss.at[kind, k - 1], gath_rs.at[kind, k - 1], tensor=to)

    def served(ref, i, j):
        return ref[i, j].reshape(RING * 64, width)

    def send_parts(kind, make):
        @pl.loop(0, 4)
        def _(q):
            value = make(q // 2, q % 2).astype(BF)
            for piece in range(2):
                block = 2 * q + piece
                part_s[kind, block] = value[piece * 128 : (piece + 1) * 128]
                k = (block - t + TENSOR) % TENSOR

                @pl.when(k > 0)
                def _():
                    part_copy(kind, k).start()

        part_r[kind, 0] = part_s[kind, t]

    def sum_parts(kind, scale):
        @pl.loop(1, TENSOR)
        def _(k):
            part_copy(kind, k).wait_recv()

        total = part_r[kind, 0].astype(F32)
        for k in range(1, TENSOR):
            total = total + part_r[kind, k].astype(F32)
        ranks[kind, t] = (total if scale is None else total * scale).astype(BF)

        @pl.loop(1, TENSOR)
        def _(k):
            gath_copy(kind, k).start()

    def gathered(kind):
        @pl.loop(1, TENSOR)
        def _(k):
            held = ranks.at[kind, (t + TENSOR - k) % TENSOR]
            remote(held, held, gath_ss.at[kind, k - 1], gath_rs.at[kind, k - 1], tensor=t).wait_recv()

    def rank_rows(kind, i, j):
        return ranks[kind, pl.ds(i * 4 + j * 2, 2)].reshape(RING * 64, ranks.shape[3])

    for i in range(2):
        w_copy(jnp.int32(i)).wait()

    @pl.loop(0, tiles)
    def _(n):
        at = span(n * TILE, TILE)
        sib_s[0, :, at] = mm(xs[...], wbuf[0, :, at]).astype(BF)
        sib_tile(n).start()
        hold[0, :, at] = mm(xs[...], wbuf[1, :, at])

        @pl.when(n > 0)
        def _():
            send_hop(n - 1)

    for i in range(2):
        w_copy(jnp.int32(i + W_SLOTS)).start()
    send_hop(jnp.int32(tiles - 1))

    @pl.loop(1, 4)
    def _(j):
        w_copy(2 * j).wait()

        @pl.when(j == 2)
        def _():
            for n in range(tiles):
                sib_tile(n).wait_send()

        @pl.when(j == 3)
        def _():
            sib_copy(1).wait_send()

        @pl.loop(0, tiles)
        def _(n):
            at = span(n * TILE, TILE)
            sib_s[j % 2, :, at] = mm(xs[...], wbuf[(2 * j) % W_SLOTS, :, at]).astype(BF)

        sib_copy(j).start()

        @pl.when(2 * j + W_SLOTS < 8)
        def _():
            w_copy(2 * j + W_SLOTS).start()

        w_copy(2 * j + 1).wait()

        @pl.loop(0, tiles)
        def _(n):
            at = span(n * TILE, TILE)
            hold[jnp.where(j == 3, 2, j % 2), :, at] = mm(xs[...], wbuf[(2 * j + 1) % W_SLOTS, :, at])

        @pl.when(2 * j + 1 + W_SLOTS < 8)
        def _():
            w_copy(2 * j + 1 + W_SLOTS).start()

        @pl.when(j == 1)
        def _():
            fac_wait(0, others[:1])

            @pl.loop(0, 2)
            def _(h):
                for m in range(len(MESSAGES)):
                    x_copy(h, m).wait_recv()

            send_parts(0, lambda i, k: mm(served(x_r, i, k), fa[i, k]))
            fac_wait(1, others[1:])
            fac_relay(1).start()
            for m in range(4, len(MESSAGES)):
                c_copy(m).start()

        @pl.when(j == 2)
        def _():
            sum_parts(0, None)
            for way in range(2):
                sib_copy(1 + way).wait_recv()
                sum_ring(way, 1 - way)
                ring_copy(way, 1 - way).start()

    def ad_copy(m):
        message = MESSAGES[m]
        dy, dz = lane_move(*message)
        return remote(
            ad_s.at[lane_place(*message)],
            ad_r.at[message],
            ad_ss.at[m],
            ad_rs.at[m],
            dp=near(-dy, -dz),
        )

    fac_wait(1, others[:1])
    gathered(0)

    @pl.loop(0, 4)
    def _(q):
        i, j = q // 2, q % 2
        value = mm(rank_rows(0, i, j), fb[i, j]) * factor_at(owner_of(i, j), width)
        ad_s[i, j] = value.astype(BF).reshape(RING, 64, width)

    for m in range(len(MESSAGES)):
        ad_copy(m).start()
    ad_r[BOTH, BOTH] = ad_s[:, :, 0]

    for m in range(len(MESSAGES)):
        c_copy(m).wait_recv()
    send_parts(
        1,
        lambda i, j: lax.dot_general(
            served(c_r, i, j), fb[i, j], (((1,), (1,)), ((), ())), preferred_element_type=F32
        ),
    )

    def g_copy(n, which):
        dy = jnp.where(which == 0, -ahead * (1 - n), jnp.where(which == 1, ahead, 0))
        dz = jnp.where(which == 0, -ahead, jnp.where(which == 1, 0, ahead))
        return remote(
            g_s.at[n, which],
            g_r.at[n, which],
            g_ss.at[n, which],
            g_rs.at[n, which],
            dp=near(dy, dz),
        )

    def gradient(n, kind, row_ref):
        @pl.loop(0, 4)
        def _(which):
            i = jnp.where((which == 1) | (which == 3), odd, 1 - odd)
            j = jnp.where(which >= 2, odd, 1 - odd)
            turned = rank_rows(kind, i, j).astype(F32).T.astype(BF)
            value = mm(turned, served(row_ref, i, j)) * (1.0 / seq_len)
            if n == 1:
                value = value * factor_at(owner_of(i, j), width)
            g_own[n] = value
            g_s[n, which] = value.astype(BF)
            if n == 1:

                @pl.when(which == 1)
                def _():
                    g_mid[...] = value

            @pl.when((which == 0) | (which == 2) | ((which == 1) & (n == 0)))
            def _():
                g_copy(n, which).start()

    def pass_gradient():
        g_copy(1, 0).wait_recv()

        @pl.loop(0, g_mid.shape[0] // 32)
        def _(k):
            at = span(k * 32, 32)
            g_s[1, 1, at] = (g_mid[at] + g_r[1, 0, at].astype(F32)).astype(BF)

        g_copy(1, 1).start()

    gradient(1, 0, c_r)

    @pl.loop(0, rows // 64)
    def _(n):
        row = iota((64, 128), 0) + n * 64
        mine = jnp.where(slot_l == (row // seq_len).astype(F32), lane_l, 0.0)
        place = jnp.sum(mine, 1, keepdims=True) * seq_len + (row % seq_len).astype(F32)[:, :1]
        slot_hot[span(n * 64, 64), :] = jnp.where(
            iota((64, 2 * rows), 1).astype(F32) == place, 1.0, 0.0
        ).astype(BF)

    for way in range(2):
        for n in range(tiles):
            hop_copy(way, n).wait_recv()
        sum_ring(way, way)
    sum_parts(1, factor_at(owner_of(t // 4, (t // 2) % 2), ranks.shape[3]))
    for way in range(2):
        ring_copy(way, way).start()
    pass_gradient()
    gathered(1)
    gradient(0, 1, x_r)

    sib_copy(3).wait_recv()
    for m in range(len(MESSAGES)):
        ad_copy(m).wait_recv()

    @pl.loop(0, tiles)
    def _(n):
        at = span(n * TILE, TILE)
        back = ad_r[:, :, :, at].reshape(2 * rows, TILE)
        hold[2, :, at] = hold[2, :, at] + sib_r[3, :, at].astype(F32) + mm(slot_hot[...], back)

    for way in range(2):
        for part in range(2):
            ring_copy(way, part).wait_recv()

    for part in range(2):

        def put(at, to):
            out_v[at] = (
                hold[2, at] + ring_r[0, part, to].astype(F32) + ring_r[1, part, to].astype(F32)
            ).astype(BF)

        half_rows(part, put)
    stores = [pltpu.make_async_copy(out_v, out_ref, out_sem.at[2])]
    stores[0].start()

    for n, g_ref in ((1, gb_ref), (0, ga_ref)):

        @pl.loop(n, 3)
        def _(which):
            g_copy(n, which).wait_recv()

        @pl.loop(0, g_own.shape[1] // 32)
        def _(k):
            at = span(k * 32, 32)
            total = g_own[n, at]
            for which in range(n, 3):
                total = total + g_r[n, which, at].astype(F32)
            g_own[n, at] = total

        stores.append(pltpu.make_async_copy(g_own.at[n], g_ref, out_sem.at[n]))
        stores[-1].start()

    for k in range(DP - 1):
        facts_copy(k).wait_send()
        tok_copy(0, k).wait_send()
        tok_copy(1, k).wait_send()

    for n in range(2):
        for axis in range(2):
            fac_copy(axis, n).wait_send()
        fac_relay(n).wait_send()
    for m in range(len(MESSAGES)):
        for h in range(2):
            x_copy(h, m).wait_send()
        c_copy(m).wait_send()
        ad_copy(m).wait_send()
    for j in (2, 3):
        sib_copy(j).wait_send()
    for way in range(2):
        for n in range(tiles):
            hop_copy(way, n).wait_send()
        for part in range(2):
            ring_copy(way, part).wait_send()
    for kind in range(2):

        @pl.loop(1, TENSOR)
        def _(k):
            part_copy(kind, k).wait_send()
            gath_copy(kind, k).wait_send()

        @pl.loop(0, 3)
        def _(which):
            g_copy(kind, which).wait_send()

    for store in stores:
        store.wait()


def finish(out_ref, gb_ref, ga_ref, out_to, gb_to, ga_to, out_v, gb_v, ga_v, turned_v, sem):
    names = ((ga_ref, ga_v, turned_v, ga_to), (gb_ref, gb_v, gb_v, gb_to), (out_ref, out_v, out_v, out_to))
    loads = [pltpu.make_async_copy(src, held, sem.at[0, n]) for n, (src, held, _, _) in enumerate(names)]
    stores = [pltpu.make_async_copy(held, dst, sem.at[1, n]) for n, (_, _, held, dst) in enumerate(names)]
    for load in loads:
        load.start()
    loads[0].wait()
    turned_v[...] = ga_v[...].T
    stores[0].start()
    for n in (1, 2):
        loads[n].wait()
        stores[n].start()
    for store in stores:
        store.wait()


def on_device(
    tokens,
    destinations,
    counts,
    sequence_job_ids,
    job_owner_slot,
    rank_per_job,
    weight,
    input_factor_table,
    output_factor_table,
    cotangent,
):
    slot_count, seq_len, width = tokens.shape
    max_rank = input_factor_table.shape[2]
    rows = slot_count * seq_len
    anywhere = pl.BlockSpec(memory_space=pl.ANY)
    smem = pl.BlockSpec(memory_space=pltpu.SMEM)
    dma = pltpu.SemaphoreType.DMA
    served = (2, 2, RING, 64, width)
    lanes = (RING, RING, 64, width)
    out, ga, gb = pl.pallas_call(
        kernel,
        out_shape=(
            jax.ShapeDtypeStruct((rows, width), BF),
            jax.ShapeDtypeStruct((max_rank, width), F32),
            jax.ShapeDtypeStruct((max_rank, width), F32),
        ),
        in_specs=[smem] * 5 + [anywhere] * 5,
        out_specs=(anywhere,) * 3,
        scratch_shapes=[
            pltpu.VMEM(tokens.shape, BF),
            pltpu.VMEM((rows, width), BF),
            pltpu.VMEM(input_factor_table.shape, BF),
            pltpu.VMEM(output_factor_table.shape, BF),
            pltpu.VMEM((rows, width), BF),
            pltpu.VMEM((DP, seq_len, width), BF),
            pltpu.VMEM((DP, seq_len, width), BF),
            pltpu.SMEM((DP,), jnp.int32),
            pltpu.VMEM((DP, 8, 128), jnp.int32),
            pltpu.VMEM((DP, 8, 128), jnp.int32),
            pltpu.VMEM((rows, rows), BF),
            pltpu.VMEM((2 * rows, rows), BF),
            pltpu.VMEM((2 * rows, rows), BF),
            pltpu.VMEM((rows, 2 * rows), BF),
            pltpu.VMEM((rows, width), BF),
            pltpu.VMEM(lanes, BF),
            pltpu.VMEM(served, BF),
            pltpu.VMEM(lanes, BF),
            pltpu.VMEM(served, BF),
            pltpu.VMEM((2, 2, width, max_rank), BF),
            pltpu.VMEM((2, 2, max_rank, width), BF),
            pltpu.VMEM((W_SLOTS, width, width), BF),
            pltpu.VMEM((2, rows, width), BF),
            pltpu.VMEM((4, rows, width), BF),
            pltpu.VMEM((3, rows, width), F32),
            pltpu.VMEM((2, rows // 2, width), BF),
            pltpu.VMEM((2, rows // 2, width), BF),
            pltpu.VMEM((2, 2, rows // 2, width), BF),
            pltpu.VMEM((2, 2, rows // 2, width), BF),
            pltpu.VMEM((2, TENSOR, 128, max_rank), BF),
            pltpu.VMEM((2, TENSOR, 128, max_rank), BF),
            pltpu.VMEM((2, TENSOR, 128, max_rank), BF),
            pltpu.VMEM(served, BF),
            pltpu.VMEM(lanes, BF),
            pltpu.VMEM((2, max_rank, width), F32),
            pltpu.VMEM((max_rank, width), F32),
            pltpu.VMEM((2, 4, max_rank, width), BF),
            pltpu.VMEM((2, 3, max_rank, width), BF),
            dma((4,)),
            dma((3,)),
            dma((W_SLOTS,)),
            dma((DP - 1,)),
            dma((DP - 1,)),
            dma((2, DP - 1)),
            dma((2, DP - 1)),
            dma((3, 2)),
            dma((2, 2, 2)),
            dma((8,)),
            dma((8,)),
            dma((2, 8)),
            dma((2, 8)),
            dma((2,)),
            dma((4,)),
            dma((4,)),
            dma((4,)),
            dma((2, 4)),
            dma((2, 4)),
            dma((2, 2)),
            dma((2, 2)),
            dma((2, TENSOR - 1)),
            dma((2, TENSOR - 1)),
            dma((2, TENSOR - 1)),
            dma((2, TENSOR - 1)),
            dma((8,)),
            dma((8,)),
            dma((2, 3)),
            dma((2, 3)),
        ],
        compiler_params=pltpu.CompilerParams(
            collective_id=0, has_side_effects=True, vmem_limit_bytes=58 * 2**20
        ),
    )(
        destinations,
        counts,
        sequence_job_ids,
        job_owner_slot,
        rank_per_job,
        tokens,
        cotangent.reshape(rows, width),
        input_factor_table,
        output_factor_table,
        weight,
    )
    out, gb, ga = pl.pallas_call(
        finish,
        out_shape=(
            jax.ShapeDtypeStruct((rows, width), BF),
            jax.ShapeDtypeStruct((max_rank, width), F32),
            jax.ShapeDtypeStruct((width, max_rank), F32),
        ),
        in_specs=[anywhere] * 3,
        out_specs=(anywhere,) * 3,
        scratch_shapes=[
            pltpu.VMEM((rows, width), BF),
            pltpu.VMEM((max_rank, width), F32),
            pltpu.VMEM((max_rank, width), F32),
            pltpu.VMEM((width, max_rank), F32),
            dma((2, 3)),
        ],
    )(out, gb, ga)
    return out.reshape(slot_count, seq_len, width), ga[None], gb[None]


def solution(mesh):
    in_specs = (
        P("dp", None, "tensor"),
        P("dp"),
        P("dp"),
        P("dp"),
        P(),
        P(),
        P("tensor", None),
        P("dp", "tensor", None),
        P("dp", None, "tensor"),
        P("dp", None, "tensor"),
    )
    out_specs = (P("dp", None, "tensor"), P("dp", "tensor", None), P("dp", None, "tensor"))
    return jax.shard_map(
        on_device, mesh=mesh, in_specs=in_specs, out_specs=out_specs, check_vma=False
    )
```

```python
import jax
import jax.numpy as jnp
from jax import lax
from jax.experimental import pallas as pl
from jax.experimental.pallas import tpu as pltpu
from jax.sharding import PartitionSpec as P

BF = jnp.bfloat16
F32 = jnp.float32
RING = 4
DP = RING * RING
TENSOR = 2 * RING
TILE = 256
W_SLOTS = 3
MOVE, PLACE = (0, 0, -1, 1), (0, 1, 1, 0)
BOTH = slice(0, 2)
MESSAGES = ((2, BOTH), (BOTH, 2), (3, BOTH), (BOTH, 3), (2, 2), (3, 3), (2, 3), (3, 2))
NEIGHBOURS = ((0, 1), (1, 0), (0, 3), (3, 0), (1, 1), (3, 3), (1, 3), (3, 1))
OTHERS = NEIGHBOURS + ((0, 2), (2, 0), (2, 1), (1, 2), (2, 3), (3, 2), (2, 2))


def mm(a, b):
    return jnp.dot(a, b, preferred_element_type=F32)


def kernel(
    dest_ref,
    count_ref,
    job_ref,
    owner_ref,
    rank_ref,
    tok_ref,
    cot_ref,
    a_ref,
    b_ref,
    w_ref,
    out_ref,
    ga_ref,
    gb_ref,
    tok_v,
    cot_v,
    a_v,
    b_v,
    out_v,
    tok_s,
    tok_r,
    source,
    facts_s,
    facts_r,
    place_hot,
    x_hot,
    c_hot,
    slot_hot,
    xs,
    x_s,
    x_r,
    c_s,
    c_r,
    fa,
    fb,
    wbuf,
    sib_s,
    sib_r,
    hold,
    hop_s,
    hop_r,
    ring_s,
    ring_r,
    part_s,
    part_r,
    ranks,
    ad_s,
    ad_r,
    g_own,
    g_mid,
    g_s,
    g_r,
    in_sem,
    out_sem,
    w_sem,
    facts_ss,
    facts_rs,
    tok_ss,
    tok_rs,
    fac_ss,
    fac_rs,
    c_ss,
    c_rs,
    x_ss,
    x_rs,
    sib_ss,
    sib_rs,
    tile_ss,
    tile_rs,
    hop_ss,
    hop_rs,
    ring_ss,
    ring_rs,
    part_ss,
    part_rs,
    gath_ss,
    gath_rs,
    ad_ss,
    ad_rs,
    g_ss,
    g_rs,
):
    seq_len, width = tok_ref.shape[1:]
    rows = DP * seq_len
    half = rows // 2
    me = lax.axis_index("dp")
    t = lax.axis_index("tensor")
    y, z = me // RING, me % RING
    x, c = t // 2, t % 2
    odd = (y + z) % 2
    ahead = 1 - 2 * odd
    others = ((1 - odd, 1 - odd), (odd, 1 - odd), (1 - odd, odd))
    tiles = width // TILE
    wide_half = width // 2

    def remote(src, dst, send, recv, **where):
        return pltpu.make_async_remote_copy(
            src_ref=src,
            dst_ref=dst,
            send_sem=send,
            recv_sem=recv,
            device_id=where,
            device_id_type=pl.DeviceIdType.MESH,
        )

    def iota(shape, axis):
        return lax.broadcasted_iota(jnp.int32, shape, axis)

    def near(dy, dz):
        return (y + dy + RING) % RING * RING + (z + dz + RING) % RING

    def owner_of(i, j):
        first, second = (y - i + RING) % RING, (z - j + RING) % RING
        shift = (first + second) % 2
        return (first + shift) % RING * RING + (second + shift) % RING

    def rank_at(owner):
        total = jnp.int32(0)
        for j in range(DP):
            total = total + jnp.where(owner_ref[j] == owner, rank_ref[j], 0)
        return total

    def factor_at(owner, columns):
        return 32.0 / jnp.full((1, columns), rank_at(owner).astype(F32), F32)

    def span(start, size):
        return pl.ds(pl.multiple_of(start, size), size)

    loads = [
        pltpu.make_async_copy(src, dst, in_sem.at[n])
        for n, (src, dst) in enumerate(((tok_ref, tok_v), (a_ref, a_v), (b_ref, b_v), (cot_ref, cot_v)))
    ]
    for load in loads:
        load.start()

    barrier = pltpu.get_barrier_semaphore()

    @pl.loop(1, DP)
    def _(k):
        pl.semaphore_signal(
            barrier, inc=1, device_id={"dp": (me + k) % DP}, device_id_type=pl.DeviceIdType.MESH
        )

    @pl.loop(1, TENSOR)
    def _(k):
        pl.semaphore_signal(
            barrier, inc=1, device_id={"tensor": (t + k) % TENSOR}, device_id_type=pl.DeviceIdType.MESH
        )

    def w_copy(i):
        j = i // 2
        block = (x + jnp.where(j == 0, 2, jnp.where(j == 1, 1, jnp.where(j == 2, 3, 0)))) % RING * 2
        block = block + (c + 1 - i % 2) % 2
        return pltpu.make_async_copy(
            w_ref.at[:, span(block * width, width)], wbuf.at[i % W_SLOTS], w_sem.at[i % W_SLOTS]
        )

    for i in range(W_SLOTS):
        w_copy(jnp.int32(i)).start()

    def chosen(to):
        index = jnp.int32(0)
        for i in range(DP):
            index = jnp.where(lax.shift_right_logical(dest_ref[i], 4) == to, i, index)
        return index

    @pl.loop(0, DP)
    def _(to):
        index = chosen(to)
        source[to] = index
        owner = owner_ref[job_ref[index]]
        oy, oz = lax.shift_right_logical(owner, 2), owner & 3
        shift = (oy + oz) & 1
        dy, dz = (to // RING + RING - oy + shift) & 3, (to % RING + RING - oz + shift) & 3
        base = (dy * RING + dz) * 2
        row = iota((8, 128), 0)
        facts_s[to] = jnp.where(
            row == 0, dest_ref[index] & 15, jnp.where(row == 1, count_ref[index], base)
        )

    facts_r[me] = facts_s[me]
    loads[0].wait()

    @pl.loop(0, DP)
    def _(to):
        tok_s[to] = tok_v[source[to]]

    tok_r[me] = tok_s[me]

    pl.semaphore_wait(barrier, DP - 1 + TENSOR - 1)

    def facts_copy(k):
        to = near(*OTHERS[k])
        return remote(facts_s.at[to], facts_r.at[me], facts_ss.at[k], facts_rs.at[k], dp=to)

    def tok_copy(h, k):
        to, columns = near(*OTHERS[k]), span(h * wide_half, wide_half)
        return remote(
            tok_s.at[to, :, columns],
            tok_r.at[me, :, columns],
            tok_ss.at[h, k],
            tok_rs.at[h, k],
            dp=to,
        )

    def fac_copy(axis, n):
        table = (fa, fb)[n]
        there = ((1 - odd, odd), (odd, 1 - odd))[axis]
        to = (near(ahead, 0), near(0, ahead))[axis]
        return remote(
            table.at[odd, odd], table.at[there], fac_ss.at[axis, n], fac_rs.at[there + (n,)], dp=to
        )

    def fac_wait(n, which):
        for there in which:
            held = (fa, fb)[n].at[there]
            remote(held, held, fac_ss.at[0, n], fac_rs.at[there + (n,)], dp=me).wait_recv()

    def fac_relay(n):
        table = (fa, fb)[n]
        here = ((odd, 1 - odd), (1 - odd, odd))[n]
        to = (near(0, -ahead), near(-ahead, 0))[n]
        return remote(table.at[here], table.at[odd, odd], fac_ss.at[2, n], fac_rs.at[odd, odd, n], dp=to)

    for k in range(DP - 1):
        facts_copy(k).start()

    @pl.loop(0, 2)
    def _(h):
        for k in range(DP - 1):
            tok_copy(h, k).start()

    my_rank = rank_at(me)
    loads[1].wait()

    @pl.loop(0, width // 128)
    def _(n):
        at = span(n * 128, 128)
        kept = iota((128, a_v.shape[2]), 1) < my_rank
        fa[odd, odd, at, :] = jnp.where(kept, a_v[0, at, :].astype(F32), 0.0).astype(BF)

    for axis in range(2):
        fac_copy(axis, 0).start()
    loads[2].wait()

    @pl.loop(0, width // 128)
    def _(n):
        at = span(n * 128, 128)
        kept = iota((b_v.shape[1], 128), 0) < my_rank
        fb[odd, odd, :, at] = jnp.where(kept, b_v[0, :, at].astype(F32), 0.0).astype(BF)

    for k in range(DP - 1):
        facts_copy(k).wait_recv()

    slot_c = facts_r[:, 0, :].astype(F32)
    live_c = facts_r[:, 1, :].astype(F32)
    base_c = facts_r[:, 2, :].astype(F32)
    square = (DP, 128)
    diagonal = iota(square, 0) == iota(square, 1)
    slot_l = jnp.sum(jnp.where(diagonal, slot_c, 0.0), 0, keepdims=True)
    base_l = jnp.sum(jnp.where(diagonal, base_c, 0.0), 0, keepdims=True)
    earlier = (base_l == base_c) & (slot_l < slot_c) & (iota(square, 1) < DP)
    turn_c = jnp.sum(jnp.where(earlier, 1.0, 0.0), 1, keepdims=True)
    lane_c = base_c + turn_c
    lane_l = jnp.sum(jnp.where(diagonal, lane_c, 0.0), 0, keepdims=True)
    wide = (DP, rows)
    seq_of = iota(wide, 1) // seq_len
    slot_1, live_1, lane_1 = slot_c[:, :1], live_c[:, :1], lane_c[:, :1]
    in_slot = slot_1 == seq_of.astype(F32)
    in_order = iota(wide, 0) == seq_of
    position = (iota((1, rows), 1) % seq_len).astype(F32)

    def spread(where, value):
        return jnp.sum(jnp.where(where, value, 0.0), 0, keepdims=True)

    live = position < spread(in_order, live_1)
    c_row = spread(in_slot, lane_1) * seq_len + position
    x_row = jnp.where(live, spread(in_order, lane_1) * seq_len + position, -1.0)
    slot_row = jnp.where(live, spread(in_order, slot_1) * seq_len + position, -1.0)

    def build(hot, wanted):
        @pl.loop(0, hot.shape[0] // 64)
        def _(n):
            row = (iota((64, rows), 0) + n * 64).astype(F32)
            hot[span(n * 64, 64), :] = jnp.where(row == wanted, 1.0, 0.0).astype(BF)

    build(x_hot, x_row)
    build(place_hot, slot_row)

    lane_shape = (RING, RING, 2 * seq_len)

    def lane_place(dy, dz):
        row = PLACE[dy] if dy != BOTH else BOTH
        column = PLACE[dz] if dz != BOTH else BOTH
        return row, column, (dy != BOTH) * 2 + (dz != BOTH)

    def lane_move(dy, dz):
        return (MOVE[dy] if dy != BOTH else 0, MOVE[dz] if dz != BOTH else 0)

    def x_copy(h, m):
        message, columns = MESSAGES[m], span(h * wide_half, wide_half)
        return remote(
            x_s.at[message + (slice(None), columns)],
            x_r.at[lane_place(*message) + (slice(None), columns)],
            x_ss.at[h, m],
            x_rs.at[h, m],
            dp=near(*lane_move(*message)),
        )

    def c_copy(m):
        message = MESSAGES[m]
        return remote(
            c_s.at[message],
            c_r.at[lane_place(*message)],
            c_ss.at[m],
            c_rs.at[m],
            dp=near(*lane_move(*message)),
        )

    @pl.loop(0, 2)
    def _(h):
        for k in range(DP - 1):
            tok_copy(h, k).wait_recv()

        @pl.loop(0, tiles // 2)
        def _(n):
            at = span(h * wide_half + n * TILE, TILE)
            landed = tok_r[:, :, at].reshape(rows, TILE)
            x_s[:, :, :, at] = mm(x_hot[...], landed).astype(BF).reshape(lane_shape + (TILE,))

        for m in range(len(MESSAGES)):
            x_copy(h, m).start()

        @pl.loop(0, tiles // 2)
        def _(n):
            at = span(h * wide_half + n * TILE, TILE)
            xs[:, at] = mm(place_hot[...], tok_r[:, :, at].reshape(rows, TILE)).astype(BF)

    for axis in range(2):
        fac_copy(axis, 1).start()
    build(c_hot, c_row)
    loads[3].wait()

    @pl.loop(0, tiles)
    def _(n):
        at = span(n * TILE, TILE)
        c_s[:, :, :, at] = mm(c_hot[...], cot_v[:, at]).astype(BF).reshape(lane_shape + (TILE,))

    fac_wait(0, others[1:])
    fac_relay(0).start()
    for m in range(4):
        c_copy(m).start()
    x_r[:, :, 0] = x_s[BOTH, BOTH]
    c_r[:, :, 0] = c_s[BOTH, BOTH]

    def sib_copy(j):
        return remote(
            sib_s.at[j % 2], sib_r.at[j], sib_ss.at[j % 2], sib_rs.at[j], tensor=x * 2 + (1 - c)
        )

    right, left = ((x + 1) % RING) * 2 + c, ((x + 3) % RING) * 2 + c

    def hop_copy(way, n):
        at = span(n * TILE, TILE)
        return remote(
            hop_s.at[way, :, at],
            hop_r.at[way, :, at],
            hop_ss.at[way, n],
            hop_rs.at[way, n],
            tensor=(right, left)[way],
        )

    def sib_tile(n):
        at = span(n * TILE, TILE)
        return remote(
            sib_s.at[0, :, at], sib_r.at[0, :, at], tile_ss.at[n], tile_rs.at[n], tensor=x * 2 + (1 - c)
        )

    def ring_copy(way, part):
        return remote(
            ring_s.at[way, part],
            ring_r.at[way, part],
            ring_ss.at[way, part],
            ring_rs.at[way, part],
            tensor=(right, left)[way],
        )

    def half_rows(part, put):
        @pl.loop(0, half // 32)
        def _(n):
            put(span(part * half + n * 32, 32), span(n * 32, 32))

    def send_hop(n):
        at = span(n * TILE, TILE)
        sib_tile(n).wait_recv()
        for way in range(2):
            part = slice(way * half, (way + 1) * half)
            hop_s[way, :, at] = (hold[0, part, at] + sib_r[0, part, at].astype(F32)).astype(BF)
            hop_copy(way, n).start()

    def sum_ring(way, part):
        def put(at, to):
            value = hold[1 - way, at] + sib_r[1 + way, at].astype(F32)
            if way == part:
                value = value + hop_r[way, to].astype(F32)
            ring_s[way, part, to] = value.astype(BF)

        half_rows(part, put)

    def part_copy(kind, k):
        to = (t + k) % TENSOR
        return remote(
            part_s.at[kind, to],
            part_r.at[kind, k],
            part_ss.at[kind, k - 1],
            part_rs.at[kind, k - 1],
            tensor=to,
        )

    def gath_copy(kind, k):
        to = (t + k) % TENSOR
        held = ranks.at[kind, t]
        return remote(held, held, gath_ss.at[kind, k - 1], gath_rs.at[kind, k - 1], tensor=to)

    def served(ref, i, j):
        return ref[i, j].reshape(RING * 64, width)

    def send_parts(kind, make):
        @pl.loop(0, 4)
        def _(q):
            value = make(q // 2, q % 2).astype(BF)
            for piece in range(2):
                block = 2 * q + piece
                part_s[kind, block] = value[piece * 128 : (piece + 1) * 128]
                k = (block - t + TENSOR) % TENSOR

                @pl.when(k > 0)
                def _():
                    part_copy(kind, k).start()

        part_r[kind, 0] = part_s[kind, t]

    def sum_parts(kind, scale):
        @pl.loop(1, TENSOR)
        def _(k):
            part_copy(kind, k).wait_recv()

        total = part_r[kind, 0].astype(F32)
        for k in range(1, TENSOR):
            total = total + part_r[kind, k].astype(F32)
        ranks[kind, t] = (total if scale is None else total * scale).astype(BF)

        @pl.loop(1, TENSOR)
        def _(k):
            gath_copy(kind, k).start()

    def gathered(kind):
        @pl.loop(1, TENSOR)
        def _(k):
            held = ranks.at[kind, (t + TENSOR - k) % TENSOR]
            remote(held, held, gath_ss.at[kind, k - 1], gath_rs.at[kind, k - 1], tensor=t).wait_recv()

    def rank_rows(kind, i, j):
        return ranks[kind, pl.ds(i * 4 + j * 2, 2)].reshape(RING * 64, ranks.shape[3])

    for i in range(2):
        w_copy(jnp.int32(i)).wait()

    @pl.loop(0, tiles)
    def _(n):
        at = span(n * TILE, TILE)
        sib_s[0, :, at] = mm(xs[...], wbuf[0, :, at]).astype(BF)
        sib_tile(n).start()
        hold[0, :, at] = mm(xs[...], wbuf[1, :, at])

        @pl.when(n > 0)
        def _():
            send_hop(n - 1)

    for i in range(2):
        w_copy(jnp.int32(i + W_SLOTS)).start()
    send_hop(jnp.int32(tiles - 1))

    @pl.loop(1, 4)
    def _(j):
        w_copy(2 * j).wait()

        @pl.when(j == 2)
        def _():
            for n in range(tiles):
                sib_tile(n).wait_send()

        @pl.when(j == 3)
        def _():
            sib_copy(1).wait_send()

        @pl.loop(0, tiles)
        def _(n):
            at = span(n * TILE, TILE)
            sib_s[j % 2, :, at] = mm(xs[...], wbuf[(2 * j) % W_SLOTS, :, at]).astype(BF)

        sib_copy(j).start()

        @pl.when(2 * j + W_SLOTS < 8)
        def _():
            w_copy(2 * j + W_SLOTS).start()

        w_copy(2 * j + 1).wait()

        @pl.loop(0, tiles)
        def _(n):
            at = span(n * TILE, TILE)
            hold[jnp.where(j == 3, 2, j % 2), :, at] = mm(xs[...], wbuf[(2 * j + 1) % W_SLOTS, :, at])

        @pl.when(2 * j + 1 + W_SLOTS < 8)
        def _():
            w_copy(2 * j + 1 + W_SLOTS).start()

        @pl.when(j == 1)
        def _():
            fac_wait(0, others[:1])

            @pl.loop(0, 2)
            def _(h):
                for m in range(len(MESSAGES)):
                    x_copy(h, m).wait_recv()

            send_parts(0, lambda i, k: mm(served(x_r, i, k), fa[i, k]))
            fac_wait(1, others[1:])
            fac_relay(1).start()
            for m in range(4, len(MESSAGES)):
                c_copy(m).start()

        @pl.when(j == 2)
        def _():
            sum_parts(0, None)
            for way in range(2):
                sib_copy(1 + way).wait_recv()
                sum_ring(way, 1 - way)
                ring_copy(way, 1 - way).start()

    def ad_copy(m):
        message = MESSAGES[m]
        dy, dz = lane_move(*message)
        return remote(
            ad_s.at[lane_place(*message)],
            ad_r.at[message],
            ad_ss.at[m],
            ad_rs.at[m],
            dp=near(-dy, -dz),
        )

    fac_wait(1, others[:1])
    gathered(0)

    @pl.loop(0, 4)
    def _(q):
        i, j = q // 2, q % 2
        value = mm(rank_rows(0, i, j), fb[i, j]) * factor_at(owner_of(i, j), width)
        ad_s[i, j] = value.astype(BF).reshape(RING, 64, width)

    for m in range(len(MESSAGES)):
        ad_copy(m).start()
    ad_r[BOTH, BOTH] = ad_s[:, :, 0]

    for m in range(len(MESSAGES)):
        c_copy(m).wait_recv()
    send_parts(
        1,
        lambda i, j: lax.dot_general(
            served(c_r, i, j), fb[i, j], (((1,), (1,)), ((), ())), preferred_element_type=F32
        ),
    )

    def g_copy(n, which):
        dy = jnp.where(which == 0, -ahead * (1 - n), jnp.where(which == 1, ahead, 0))
        dz = jnp.where(which == 0, -ahead, jnp.where(which == 1, 0, ahead))
        return remote(
            g_s.at[n, which],
            g_r.at[n, which],
            g_ss.at[n, which],
            g_rs.at[n, which],
            dp=near(dy, dz),
        )

    def gradient(n, kind, row_ref):
        @pl.loop(0, 4)
        def _(which):
            i = jnp.where((which == 1) | (which == 3), odd, 1 - odd)
            j = jnp.where(which >= 2, odd, 1 - odd)
            turned = rank_rows(kind, i, j).astype(F32).T.astype(BF)
            value = mm(turned, served(row_ref, i, j)) * (1.0 / seq_len)
            if n == 1:
                value = value * factor_at(owner_of(i, j), width)
            g_own[n] = value
            g_s[n, which] = value.astype(BF)
            if n == 1:

                @pl.when(which == 1)
                def _():
                    g_mid[...] = value

            @pl.when((which == 0) | (which == 2) | ((which == 1) & (n == 0)))
            def _():
                g_copy(n, which).start()

    def pass_gradient():
        g_copy(1, 0).wait_recv()

        @pl.loop(0, g_mid.shape[0] // 32)
        def _(k):
            at = span(k * 32, 32)
            g_s[1, 1, at] = (g_mid[at] + g_r[1, 0, at].astype(F32)).astype(BF)

        g_copy(1, 1).start()

    gradient(1, 0, c_r)

    @pl.loop(0, rows // 64)
    def _(n):
        row = iota((64, 128), 0) + n * 64
        mine = jnp.where(slot_l == (row // seq_len).astype(F32), lane_l, 0.0)
        place = jnp.sum(mine, 1, keepdims=True) * seq_len + (row % seq_len).astype(F32)[:, :1]
        slot_hot[span(n * 64, 64), :] = jnp.where(
            iota((64, 2 * rows), 1).astype(F32) == place, 1.0, 0.0
        ).astype(BF)

    for way in range(2):
        for n in range(tiles):
            hop_copy(way, n).wait_recv()
        sum_ring(way, way)
    sum_parts(1, factor_at(owner_of(t // 4, (t // 2) % 2), ranks.shape[3]))
    for way in range(2):
        ring_copy(way, way).start()
    gathered(1)
    gradient(0, 1, x_r)
    pass_gradient()

    sib_copy(3).wait_recv()
    for m in range(len(MESSAGES)):
        ad_copy(m).wait_recv()

    @pl.loop(0, tiles)
    def _(n):
        at = span(n * TILE, TILE)
        back = ad_r[:, :, :, at].reshape(2 * rows, TILE)
        hold[2, :, at] = hold[2, :, at] + sib_r[3, :, at].astype(F32) + mm(slot_hot[...], back)

    for way in range(2):
        for part in range(2):
            ring_copy(way, part).wait_recv()

    for part in range(2):

        def put(at, to):
            out_v[at] = (
                hold[2, at] + ring_r[0, part, to].astype(F32) + ring_r[1, part, to].astype(F32)
            ).astype(BF)

        half_rows(part, put)
    stores = [pltpu.make_async_copy(out_v, out_ref, out_sem.at[2])]
    stores[0].start()

    for n, g_ref in ((1, gb_ref), (0, ga_ref)):

        @pl.loop(n, 3)
        def _(which):
            g_copy(n, which).wait_recv()

        @pl.loop(0, g_own.shape[1] // 32)
        def _(k):
            at = span(k * 32, 32)
            total = g_own[n, at]
            for which in range(n, 3):
                total = total + g_r[n, which, at].astype(F32)
            g_own[n, at] = total

        stores.append(pltpu.make_async_copy(g_own.at[n], g_ref, out_sem.at[n]))
        stores[-1].start()

    for k in range(DP - 1):
        facts_copy(k).wait_send()
        tok_copy(0, k).wait_send()
        tok_copy(1, k).wait_send()

    for n in range(2):
        for axis in range(2):
            fac_copy(axis, n).wait_send()
        fac_relay(n).wait_send()
    for m in range(len(MESSAGES)):
        for h in range(2):
            x_copy(h, m).wait_send()
        c_copy(m).wait_send()
        ad_copy(m).wait_send()
    for j in (2, 3):
        sib_copy(j).wait_send()
    for way in range(2):
        for n in range(tiles):
            hop_copy(way, n).wait_send()
        for part in range(2):
            ring_copy(way, part).wait_send()
    for kind in range(2):

        @pl.loop(1, TENSOR)
        def _(k):
            part_copy(kind, k).wait_send()
            gath_copy(kind, k).wait_send()

        @pl.loop(0, 3)
        def _(which):
            g_copy(kind, which).wait_send()

    for store in stores:
        store.wait()


def finish(out_ref, gb_ref, ga_ref, out_to, gb_to, ga_to, out_v, gb_v, ga_v, turned_v, sem):
    names = ((ga_ref, ga_v, turned_v, ga_to), (gb_ref, gb_v, gb_v, gb_to), (out_ref, out_v, out_v, out_to))
    loads = [pltpu.make_async_copy(src, held, sem.at[0, n]) for n, (src, held, _, _) in enumerate(names)]
    stores = [pltpu.make_async_copy(held, dst, sem.at[1, n]) for n, (_, _, held, dst) in enumerate(names)]
    for load in loads:
        load.start()
    loads[0].wait()
    turned_v[...] = ga_v[...].T
    stores[0].start()
    for n in (1, 2):
        loads[n].wait()
        stores[n].start()
    for store in stores:
        store.wait()


def on_device(
    tokens,
    destinations,
    counts,
    sequence_job_ids,
    job_owner_slot,
    rank_per_job,
    weight,
    input_factor_table,
    output_factor_table,
    cotangent,
):
    slot_count, seq_len, width = tokens.shape
    max_rank = input_factor_table.shape[2]
    rows = slot_count * seq_len
    anywhere = pl.BlockSpec(memory_space=pl.ANY)
    smem = pl.BlockSpec(memory_space=pltpu.SMEM)
    dma = pltpu.SemaphoreType.DMA
    served = (2, 2, RING, 64, width)
    lanes = (RING, RING, 64, width)
    out, ga, gb = pl.pallas_call(
        kernel,
        out_shape=(
            jax.ShapeDtypeStruct((rows, width), BF),
            jax.ShapeDtypeStruct((max_rank, width), F32),
            jax.ShapeDtypeStruct((max_rank, width), F32),
        ),
        in_specs=[smem] * 5 + [anywhere] * 5,
        out_specs=(anywhere,) * 3,
        scratch_shapes=[
            pltpu.VMEM(tokens.shape, BF),
            pltpu.VMEM((rows, width), BF),
            pltpu.VMEM(input_factor_table.shape, BF),
            pltpu.VMEM(output_factor_table.shape, BF),
            pltpu.VMEM((rows, width), BF),
            pltpu.VMEM((DP, seq_len, width), BF),
            pltpu.VMEM((DP, seq_len, width), BF),
            pltpu.SMEM((DP,), jnp.int32),
            pltpu.VMEM((DP, 8, 128), jnp.int32),
            pltpu.VMEM((DP, 8, 128), jnp.int32),
            pltpu.VMEM((rows, rows), BF),
            pltpu.VMEM((2 * rows, rows), BF),
            pltpu.VMEM((2 * rows, rows), BF),
            pltpu.VMEM((rows, 2 * rows), BF),
            pltpu.VMEM((rows, width), BF),
            pltpu.VMEM(lanes, BF),
            pltpu.VMEM(served, BF),
            pltpu.VMEM(lanes, BF),
            pltpu.VMEM(served, BF),
            pltpu.VMEM((2, 2, width, max_rank), BF),
            pltpu.VMEM((2, 2, max_rank, width), BF),
            pltpu.VMEM((W_SLOTS, width, width), BF),
            pltpu.VMEM((2, rows, width), BF),
            pltpu.VMEM((4, rows, width), BF),
            pltpu.VMEM((3, rows, width), F32),
            pltpu.VMEM((2, rows // 2, width), BF),
            pltpu.VMEM((2, rows // 2, width), BF),
            pltpu.VMEM((2, 2, rows // 2, width), BF),
            pltpu.VMEM((2, 2, rows // 2, width), BF),
            pltpu.VMEM((2, TENSOR, 128, max_rank), BF),
            pltpu.VMEM((2, TENSOR, 128, max_rank), BF),
            pltpu.VMEM((2, TENSOR, 128, max_rank), BF),
            pltpu.VMEM(served, BF),
            pltpu.VMEM(lanes, BF),
            pltpu.VMEM((2, max_rank, width), F32),
            pltpu.VMEM((max_rank, width), F32),
            pltpu.VMEM((2, 4, max_rank, width), BF),
            pltpu.VMEM((2, 3, max_rank, width), BF),
            dma((4,)),
            dma((3,)),
            dma((W_SLOTS,)),
            dma((DP - 1,)),
            dma((DP - 1,)),
            dma((2, DP - 1)),
            dma((2, DP - 1)),
            dma((3, 2)),
            dma((2, 2, 2)),
            dma((8,)),
            dma((8,)),
            dma((2, 8)),
            dma((2, 8)),
            dma((2,)),
            dma((4,)),
            dma((4,)),
            dma((4,)),
            dma((2, 4)),
            dma((2, 4)),
            dma((2, 2)),
            dma((2, 2)),
            dma((2, TENSOR - 1)),
            dma((2, TENSOR - 1)),
            dma((2, TENSOR - 1)),
            dma((2, TENSOR - 1)),
            dma((8,)),
            dma((8,)),
            dma((2, 3)),
            dma((2, 3)),
        ],
        compiler_params=pltpu.CompilerParams(
            collective_id=0, has_side_effects=True, vmem_limit_bytes=58 * 2**20
        ),
    )(
        destinations,
        counts,
        sequence_job_ids,
        job_owner_slot,
        rank_per_job,
        tokens,
        cotangent.reshape(rows, width),
        input_factor_table,
        output_factor_table,
        weight,
    )
    out, gb, ga = pl.pallas_call(
        finish,
        out_shape=(
            jax.ShapeDtypeStruct((rows, width), BF),
            jax.ShapeDtypeStruct((max_rank, width), F32),
            jax.ShapeDtypeStruct((width, max_rank), F32),
        ),
        in_specs=[anywhere] * 3,
        out_specs=(anywhere,) * 3,
        scratch_shapes=[
            pltpu.VMEM((rows, width), BF),
            pltpu.VMEM((max_rank, width), F32),
            pltpu.VMEM((max_rank, width), F32),
            pltpu.VMEM((width, max_rank), F32),
            dma((2, 3)),
        ],
    )(out, gb, ga)
    return out.reshape(slot_count, seq_len, width), ga[None], gb[None]


def solution(mesh):
    in_specs = (
        P("dp", None, "tensor"),
        P("dp"),
        P("dp"),
        P("dp"),
        P(),
        P(),
        P("tensor", None),
        P("dp", "tensor", None),
        P("dp", None, "tensor"),
        P("dp", None, "tensor"),
    )
    out_specs = (P("dp", None, "tensor"), P("dp", "tensor", None), P("dp", None, "tensor"))
    return jax.shard_map(
        on_device, mesh=mesh, in_specs=in_specs, out_specs=out_specs, check_vma=False
    )
```

```python
import jax
import jax.numpy as jnp
from jax import lax
from jax.experimental import pallas as pl
from jax.experimental.pallas import tpu as pltpu
from jax.sharding import PartitionSpec as P

BF = jnp.bfloat16
F32 = jnp.float32
RING = 4
DP = RING * RING
TENSOR = 2 * RING
TILE = 256
W_SLOTS = 3
MOVE, PLACE = (0, 0, -1, 1), (0, 1, 1, 0)
BOTH = slice(0, 2)
MESSAGES = ((2, BOTH), (BOTH, 2), (3, BOTH), (BOTH, 3), (2, 2), (3, 3), (2, 3), (3, 2))
NEIGHBOURS = ((0, 1), (1, 0), (0, 3), (3, 0), (1, 1), (3, 3), (1, 3), (3, 1))
OTHERS = NEIGHBOURS + ((0, 2), (2, 0), (2, 1), (1, 2), (2, 3), (3, 2), (2, 2))


def mm(a, b):
    return jnp.dot(a, b, preferred_element_type=F32)


def kernel(
    dest_ref,
    count_ref,
    job_ref,
    owner_ref,
    rank_ref,
    tok_ref,
    cot_ref,
    a_ref,
    b_ref,
    w_ref,
    out_ref,
    ga_ref,
    gb_ref,
    tok_v,
    cot_v,
    a_v,
    b_v,
    out_v,
    tok_s,
    tok_r,
    source,
    facts_s,
    facts_r,
    place_hot,
    x_hot,
    c_hot,
    slot_hot,
    xs,
    x_s,
    x_r,
    c_s,
    c_r,
    fa,
    fb,
    wbuf,
    sib_s,
    sib_r,
    hold,
    hop_s,
    hop_r,
    ring_s,
    ring_r,
    part_s,
    part_r,
    ranks,
    ad_s,
    ad_r,
    g_own,
    g_mid,
    g_s,
    g_r,
    in_sem,
    out_sem,
    w_sem,
    facts_ss,
    facts_rs,
    tok_ss,
    tok_rs,
    fac_ss,
    fac_rs,
    c_ss,
    c_rs,
    x_ss,
    x_rs,
    sib_ss,
    sib_rs,
    tile_ss,
    tile_rs,
    hop_ss,
    hop_rs,
    ring_ss,
    ring_rs,
    part_ss,
    part_rs,
    gath_ss,
    gath_rs,
    ad_ss,
    ad_rs,
    g_ss,
    g_rs,
):
    seq_len, width = tok_ref.shape[1:]
    rows = DP * seq_len
    half = rows // 2
    me = lax.axis_index("dp")
    t = lax.axis_index("tensor")
    y, z = me // RING, me % RING
    x, c = t // 2, t % 2
    odd = (y + z) % 2
    ahead = 1 - 2 * odd
    others = ((1 - odd, 1 - odd), (odd, 1 - odd), (1 - odd, odd))
    tiles = width // TILE
    wide_half = width // 2

    def remote(src, dst, send, recv, **where):
        return pltpu.make_async_remote_copy(
            src_ref=src,
            dst_ref=dst,
            send_sem=send,
            recv_sem=recv,
            device_id=where,
            device_id_type=pl.DeviceIdType.MESH,
        )

    def iota(shape, axis):
        return lax.broadcasted_iota(jnp.int32, shape, axis)

    def near(dy, dz):
        return (y + dy + RING) % RING * RING + (z + dz + RING) % RING

    def owner_of(i, j):
        first, second = (y - i + RING) % RING, (z - j + RING) % RING
        shift = (first + second) % 2
        return (first + shift) % RING * RING + (second + shift) % RING

    def rank_at(owner):
        total = jnp.int32(0)
        for j in range(DP):
            total = total + jnp.where(owner_ref[j] == owner, rank_ref[j], 0)
        return total

    def factor_at(owner, columns):
        return 32.0 / jnp.full((1, columns), rank_at(owner).astype(F32), F32)

    def span(start, size):
        return pl.ds(pl.multiple_of(start, size), size)

    loads = [
        pltpu.make_async_copy(src, dst, in_sem.at[n])
        for n, (src, dst) in enumerate(((tok_ref, tok_v), (a_ref, a_v), (b_ref, b_v), (cot_ref, cot_v)))
    ]
    for load in loads:
        load.start()

    barrier = pltpu.get_barrier_semaphore()

    @pl.loop(1, DP)
    def _(k):
        pl.semaphore_signal(
            barrier, inc=1, device_id={"dp": (me + k) % DP}, device_id_type=pl.DeviceIdType.MESH
        )

    @pl.loop(1, TENSOR)
    def _(k):
        pl.semaphore_signal(
            barrier, inc=1, device_id={"tensor": (t + k) % TENSOR}, device_id_type=pl.DeviceIdType.MESH
        )

    def w_copy(i):
        j = i // 2
        block = (x + jnp.where(j == 0, 2, jnp.where(j == 1, 1, jnp.where(j == 2, 3, 0)))) % RING * 2
        block = block + (c + 1 - i % 2) % 2
        return pltpu.make_async_copy(
            w_ref.at[:, span(block * width, width)], wbuf.at[i % W_SLOTS], w_sem.at[i % W_SLOTS]
        )

    for i in range(W_SLOTS):
        w_copy(jnp.int32(i)).start()

    def chosen(to):
        index = jnp.int32(0)
        for i in range(DP):
            index = jnp.where(lax.shift_right_logical(dest_ref[i], 4) == to, i, index)
        return index

    @pl.loop(0, DP)
    def _(to):
        index = chosen(to)
        source[to] = index
        owner = owner_ref[job_ref[index]]
        oy, oz = lax.shift_right_logical(owner, 2), owner & 3
        shift = (oy + oz) & 1
        dy, dz = (to // RING + RING - oy + shift) & 3, (to % RING + RING - oz + shift) & 3
        base = (dy * RING + dz) * 2
        row = iota((8, 128), 0)
        facts_s[to] = jnp.where(
            row == 0, dest_ref[index] & 15, jnp.where(row == 1, count_ref[index], base)
        )

    facts_r[me] = facts_s[me]
    loads[0].wait()

    @pl.loop(0, DP)
    def _(to):
        tok_s[to] = tok_v[source[to]]

    tok_r[me] = tok_s[me]

    pl.semaphore_wait(barrier, DP - 1 + TENSOR - 1)

    def facts_copy(k):
        to = near(*OTHERS[k])
        return remote(facts_s.at[to], facts_r.at[me], facts_ss.at[k], facts_rs.at[k], dp=to)

    def tok_copy(h, k):
        to, columns = near(*OTHERS[k]), span(h * wide_half, wide_half)
        return remote(
            tok_s.at[to, :, columns],
            tok_r.at[me, :, columns],
            tok_ss.at[h, k],
            tok_rs.at[h, k],
            dp=to,
        )

    def fac_copy(axis, n):
        table = (fa, fb)[n]
        there = ((1 - odd, odd), (odd, 1 - odd))[axis]
        to = (near(ahead, 0), near(0, ahead))[axis]
        return remote(
            table.at[odd, odd], table.at[there], fac_ss.at[axis, n], fac_rs.at[there + (n,)], dp=to
        )

    def fac_wait(n, which):
        for there in which:
            held = (fa, fb)[n].at[there]
            remote(held, held, fac_ss.at[0, n], fac_rs.at[there + (n,)], dp=me).wait_recv()

    def fac_relay(n):
        table = (fa, fb)[n]
        here = ((odd, 1 - odd), (1 - odd, odd))[n]
        to = (near(0, -ahead), near(-ahead, 0))[n]
        return remote(table.at[here], table.at[odd, odd], fac_ss.at[2, n], fac_rs.at[odd, odd, n], dp=to)

    for k in range(DP - 1):
        facts_copy(k).start()

    @pl.loop(0, 2)
    def _(h):
        for k in range(DP - 1):
            tok_copy(h, k).start()

    my_rank = rank_at(me)
    loads[1].wait()

    @pl.loop(0, width // 128)
    def _(n):
        at = span(n * 128, 128)
        kept = iota((128, a_v.shape[2]), 1) < my_rank
        fa[odd, odd, at, :] = jnp.where(kept, a_v[0, at, :].astype(F32), 0.0).astype(BF)

    for axis in range(2):
        fac_copy(axis, 0).start()
    loads[2].wait()

    @pl.loop(0, width // 128)
    def _(n):
        at = span(n * 128, 128)
        kept = iota((b_v.shape[1], 128), 0) < my_rank
        fb[odd, odd, :, at] = jnp.where(kept, b_v[0, :, at].astype(F32), 0.0).astype(BF)

    for k in range(DP - 1):
        facts_copy(k).wait_recv()

    slot_c = facts_r[:, 0, :].astype(F32)
    live_c = facts_r[:, 1, :].astype(F32)
    base_c = facts_r[:, 2, :].astype(F32)
    square = (DP, 128)
    diagonal = iota(square, 0) == iota(square, 1)
    slot_l = jnp.sum(jnp.where(diagonal, slot_c, 0.0), 0, keepdims=True)
    base_l = jnp.sum(jnp.where(diagonal, base_c, 0.0), 0, keepdims=True)
    earlier = (base_l == base_c) & (slot_l < slot_c) & (iota(square, 1) < DP)
    turn_c = jnp.sum(jnp.where(earlier, 1.0, 0.0), 1, keepdims=True)
    lane_c = base_c + turn_c
    lane_l = jnp.sum(jnp.where(diagonal, lane_c, 0.0), 0, keepdims=True)
    wide = (DP, rows)
    seq_of = iota(wide, 1) // seq_len
    slot_1, live_1, lane_1 = slot_c[:, :1], live_c[:, :1], lane_c[:, :1]
    in_slot = slot_1 == seq_of.astype(F32)
    in_order = iota(wide, 0) == seq_of
    position = (iota((1, rows), 1) % seq_len).astype(F32)

    def spread(where, value):
        return jnp.sum(jnp.where(where, value, 0.0), 0, keepdims=True)

    live = position < spread(in_order, live_1)
    c_row = spread(in_slot, lane_1) * seq_len + position
    x_row = jnp.where(live, spread(in_order, lane_1) * seq_len + position, -1.0)
    slot_row = jnp.where(live, spread(in_order, slot_1) * seq_len + position, -1.0)

    def build(hot, wanted):
        @pl.loop(0, hot.shape[0] // 64)
        def _(n):
            row = (iota((64, rows), 0) + n * 64).astype(F32)
            hot[span(n * 64, 64), :] = jnp.where(row == wanted, 1.0, 0.0).astype(BF)

    build(x_hot, x_row)
    build(place_hot, slot_row)

    lane_shape = (RING, RING, 2 * seq_len)

    def lane_place(dy, dz):
        row = PLACE[dy] if dy != BOTH else BOTH
        column = PLACE[dz] if dz != BOTH else BOTH
        return row, column, (dy != BOTH) * 2 + (dz != BOTH)

    def lane_move(dy, dz):
        return (MOVE[dy] if dy != BOTH else 0, MOVE[dz] if dz != BOTH else 0)

    def x_copy(h, m):
        message, columns = MESSAGES[m], span(h * wide_half, wide_half)
        return remote(
            x_s.at[message + (slice(None), columns)],
            x_r.at[lane_place(*message) + (slice(None), columns)],
            x_ss.at[h, m],
            x_rs.at[h, m],
            dp=near(*lane_move(*message)),
        )

    def c_copy(m):
        message = MESSAGES[m]
        return remote(
            c_s.at[message],
            c_r.at[lane_place(*message)],
            c_ss.at[m],
            c_rs.at[m],
            dp=near(*lane_move(*message)),
        )

    @pl.loop(0, 2)
    def _(h):
        for k in range(DP - 1):
            tok_copy(h, k).wait_recv()

        @pl.loop(0, tiles // 2)
        def _(n):
            at = span(h * wide_half + n * TILE, TILE)
            landed = tok_r[:, :, at].reshape(rows, TILE)
            x_s[:, :, :, at] = mm(x_hot[...], landed).astype(BF).reshape(lane_shape + (TILE,))

        for m in range(len(MESSAGES)):
            x_copy(h, m).start()

        @pl.loop(0, tiles // 2)
        def _(n):
            at = span(h * wide_half + n * TILE, TILE)
            xs[:, at] = mm(place_hot[...], tok_r[:, :, at].reshape(rows, TILE)).astype(BF)

    for axis in range(2):
        fac_copy(axis, 1).start()
    build(c_hot, c_row)
    loads[3].wait()

    @pl.loop(0, tiles)
    def _(n):
        at = span(n * TILE, TILE)
        c_s[:, :, :, at] = mm(c_hot[...], cot_v[:, at]).astype(BF).reshape(lane_shape + (TILE,))

    fac_wait(0, others[1:])
    fac_relay(0).start()
    for m in range(4):
        c_copy(m).start()
    x_r[:, :, 0] = x_s[BOTH, BOTH]
    c_r[:, :, 0] = c_s[BOTH, BOTH]

    def sib_copy(j):
        return remote(
            sib_s.at[j % 2], sib_r.at[j], sib_ss.at[j % 2], sib_rs.at[j], tensor=x * 2 + (1 - c)
        )

    right, left = ((x + 1) % RING) * 2 + c, ((x + 3) % RING) * 2 + c

    def hop_copy(way, n):
        at = span(n * TILE, TILE)
        return remote(
            hop_s.at[way, :, at],
            hop_r.at[way, :, at],
            hop_ss.at[way, n],
            hop_rs.at[way, n],
            tensor=(right, left)[way],
        )

    def sib_tile(n):
        at = span(n * TILE, TILE)
        return remote(
            sib_s.at[0, :, at], sib_r.at[0, :, at], tile_ss.at[n], tile_rs.at[n], tensor=x * 2 + (1 - c)
        )

    def ring_copy(way, part):
        return remote(
            ring_s.at[way, part],
            ring_r.at[way, part],
            ring_ss.at[way, part],
            ring_rs.at[way, part],
            tensor=(right, left)[way],
        )

    def half_rows(part, put):
        @pl.loop(0, half // 32)
        def _(n):
            put(span(part * half + n * 32, 32), span(n * 32, 32))

    def send_hop(n):
        at = span(n * TILE, TILE)
        sib_tile(n).wait_recv()
        for way in range(2):
            part = slice(way * half, (way + 1) * half)
            hop_s[way, :, at] = (hold[0, part, at] + sib_r[0, part, at].astype(F32)).astype(BF)
            hop_copy(way, n).start()

    def sum_ring(way, part):
        def put(at, to):
            value = hold[1 - way, at] + sib_r[1 + way, at].astype(F32)
            if way == part:
                value = value + hop_r[way, to].astype(F32)
            ring_s[way, part, to] = value.astype(BF)

        half_rows(part, put)

    def part_copy(kind, k):
        to = (t + k) % TENSOR
        return remote(
            part_s.at[kind, to],
            part_r.at[kind, k],
            part_ss.at[kind, k - 1],
            part_rs.at[kind, k - 1],
            tensor=to,
        )

    def gath_copy(kind, k):
        to = (t + k) % TENSOR
        held = ranks.at[kind, t]
        return remote(held, held, gath_ss.at[kind, k - 1], gath_rs.at[kind, k - 1], tensor=to)

    def served(ref, i, j):
        return ref[i, j].reshape(RING * 64, width)

    def send_parts(kind, make):
        @pl.loop(0, 4)
        def _(q):
            value = make(q // 2, q % 2).astype(BF)
            for piece in range(2):
                block = 2 * q + piece
                part_s[kind, block] = value[piece * 128 : (piece + 1) * 128]
                k = (block - t + TENSOR) % TENSOR

                @pl.when(k > 0)
                def _():
                    part_copy(kind, k).start()

        part_r[kind, 0] = part_s[kind, t]

    def sum_parts(kind, scale):
        @pl.loop(1, TENSOR)
        def _(k):
            part_copy(kind, k).wait_recv()

        total = part_r[kind, 0].astype(F32)
        for k in range(1, TENSOR):
            total = total + part_r[kind, k].astype(F32)
        ranks[kind, t] = (total if scale is None else total * scale).astype(BF)

        @pl.loop(1, TENSOR)
        def _(k):
            gath_copy(kind, k).start()

    def gathered(kind):
        @pl.loop(1, TENSOR)
        def _(k):
            held = ranks.at[kind, (t + TENSOR - k) % TENSOR]
            remote(held, held, gath_ss.at[kind, k - 1], gath_rs.at[kind, k - 1], tensor=t).wait_recv()

    def rank_rows(kind, i, j):
        return ranks[kind, pl.ds(i * 4 + j * 2, 2)].reshape(RING * 64, ranks.shape[3])

    for i in range(2):
        w_copy(jnp.int32(i)).wait()

    @pl.loop(0, tiles)
    def _(n):
        at = span(n * TILE, TILE)
        sib_s[0, :, at] = mm(xs[...], wbuf[0, :, at]).astype(BF)
        sib_tile(n).start()
        hold[0, :, at] = mm(xs[...], wbuf[1, :, at])

        @pl.when(n > 0)
        def _():
            send_hop(n - 1)

    for i in range(2):
        w_copy(jnp.int32(i + W_SLOTS)).start()
    send_hop(jnp.int32(tiles - 1))

    @pl.loop(1, 4)
    def _(j):
        w_copy(2 * j).wait()

        @pl.when(j == 2)
        def _():
            for n in range(tiles):
                sib_tile(n).wait_send()

        @pl.when(j == 3)
        def _():
            sib_copy(1).wait_send()

        @pl.loop(0, tiles)
        def _(n):
            at = span(n * TILE, TILE)
            sib_s[j % 2, :, at] = mm(xs[...], wbuf[(2 * j) % W_SLOTS, :, at]).astype(BF)

        sib_copy(j).start()

        @pl.when(2 * j + W_SLOTS < 8)
        def _():
            w_copy(2 * j + W_SLOTS).start()

        @pl.when(j == 2)
        def _():
            fac_wait(1, others[1:])
            fac_relay(1).start()
            for m in range(4, len(MESSAGES)):
                c_copy(m).start()

        w_copy(2 * j + 1).wait()

        @pl.loop(0, tiles)
        def _(n):
            at = span(n * TILE, TILE)
            hold[jnp.where(j == 3, 2, j % 2), :, at] = mm(xs[...], wbuf[(2 * j + 1) % W_SLOTS, :, at])

        @pl.when(2 * j + 1 + W_SLOTS < 8)
        def _():
            w_copy(2 * j + 1 + W_SLOTS).start()

        @pl.when(j == 1)
        def _():
            fac_wait(0, others[:1])

            @pl.loop(0, 2)
            def _(h):
                for m in range(len(MESSAGES)):
                    x_copy(h, m).wait_recv()

            send_parts(0, lambda i, k: mm(served(x_r, i, k), fa[i, k]))

        @pl.when(j == 2)
        def _():
            sum_parts(0, None)
            for way in range(2):
                sib_copy(1 + way).wait_recv()
                sum_ring(way, 1 - way)
                ring_copy(way, 1 - way).start()

    def ad_copy(m):
        message = MESSAGES[m]
        dy, dz = lane_move(*message)
        return remote(
            ad_s.at[lane_place(*message)],
            ad_r.at[message],
            ad_ss.at[m],
            ad_rs.at[m],
            dp=near(-dy, -dz),
        )

    fac_wait(1, others[:1])
    gathered(0)

    @pl.loop(0, 4)
    def _(q):
        i, j = q // 2, q % 2
        value = mm(rank_rows(0, i, j), fb[i, j]) * factor_at(owner_of(i, j), width)
        ad_s[i, j] = value.astype(BF).reshape(RING, 64, width)

    for m in range(len(MESSAGES)):
        ad_copy(m).start()
    ad_r[BOTH, BOTH] = ad_s[:, :, 0]

    for m in range(len(MESSAGES)):
        c_copy(m).wait_recv()
    send_parts(
        1,
        lambda i, j: lax.dot_general(
            served(c_r, i, j), fb[i, j], (((1,), (1,)), ((), ())), preferred_element_type=F32
        ),
    )

    def g_copy(n, which):
        dy = jnp.where(which == 0, -ahead * (1 - n), jnp.where(which == 1, ahead, 0))
        dz = jnp.where(which == 0, -ahead, jnp.where(which == 1, 0, ahead))
        return remote(
            g_s.at[n, which],
            g_r.at[n, which],
            g_ss.at[n, which],
            g_rs.at[n, which],
            dp=near(dy, dz),
        )

    def gradient(n, kind, row_ref):
        @pl.loop(0, 4)
        def _(which):
            i = jnp.where((which == 1) | (which == 3), odd, 1 - odd)
            j = jnp.where(which >= 2, odd, 1 - odd)
            turned = rank_rows(kind, i, j).astype(F32).T.astype(BF)
            value = mm(turned, served(row_ref, i, j)) * (1.0 / seq_len)
            if n == 1:
                value = value * factor_at(owner_of(i, j), width)
            g_own[n] = value
            g_s[n, which] = value.astype(BF)
            if n == 1:

                @pl.when(which == 1)
                def _():
                    g_mid[...] = value

            @pl.when((which == 0) | (which == 2) | ((which == 1) & (n == 0)))
            def _():
                g_copy(n, which).start()

    def pass_gradient():
        g_copy(1, 0).wait_recv()

        @pl.loop(0, g_mid.shape[0] // 32)
        def _(k):
            at = span(k * 32, 32)
            g_s[1, 1, at] = (g_mid[at] + g_r[1, 0, at].astype(F32)).astype(BF)

        g_copy(1, 1).start()

    gradient(1, 0, c_r)

    @pl.loop(0, rows // 64)
    def _(n):
        row = iota((64, 128), 0) + n * 64
        mine = jnp.where(slot_l == (row // seq_len).astype(F32), lane_l, 0.0)
        place = jnp.sum(mine, 1, keepdims=True) * seq_len + (row % seq_len).astype(F32)[:, :1]
        slot_hot[span(n * 64, 64), :] = jnp.where(
            iota((64, 2 * rows), 1).astype(F32) == place, 1.0, 0.0
        ).astype(BF)

    for way in range(2):
        for n in range(tiles):
            hop_copy(way, n).wait_recv()
        sum_ring(way, way)
    sum_parts(1, factor_at(owner_of(t // 4, (t // 2) % 2), ranks.shape[3]))
    for way in range(2):
        ring_copy(way, way).start()
    gathered(1)
    gradient(0, 1, x_r)
    pass_gradient()

    sib_copy(3).wait_recv()
    for m in range(len(MESSAGES)):
        ad_copy(m).wait_recv()

    @pl.loop(0, tiles)
    def _(n):
        at = span(n * TILE, TILE)
        back = ad_r[:, :, :, at].reshape(2 * rows, TILE)
        hold[2, :, at] = hold[2, :, at] + sib_r[3, :, at].astype(F32) + mm(slot_hot[...], back)

    for way in range(2):
        for part in range(2):
            ring_copy(way, part).wait_recv()

    for part in range(2):

        def put(at, to):
            out_v[at] = (
                hold[2, at] + ring_r[0, part, to].astype(F32) + ring_r[1, part, to].astype(F32)
            ).astype(BF)

        half_rows(part, put)
    stores = [pltpu.make_async_copy(out_v, out_ref, out_sem.at[2])]
    stores[0].start()

    for n, g_ref in ((1, gb_ref), (0, ga_ref)):

        @pl.loop(n, 3)
        def _(which):
            g_copy(n, which).wait_recv()

        @pl.loop(0, g_own.shape[1] // 32)
        def _(k):
            at = span(k * 32, 32)
            total = g_own[n, at]
            for which in range(n, 3):
                total = total + g_r[n, which, at].astype(F32)
            g_own[n, at] = total

        stores.append(pltpu.make_async_copy(g_own.at[n], g_ref, out_sem.at[n]))
        stores[-1].start()

    for k in range(DP - 1):
        facts_copy(k).wait_send()
        tok_copy(0, k).wait_send()
        tok_copy(1, k).wait_send()

    for n in range(2):
        for axis in range(2):
            fac_copy(axis, n).wait_send()
        fac_relay(n).wait_send()
    for m in range(len(MESSAGES)):
        for h in range(2):
            x_copy(h, m).wait_send()
        c_copy(m).wait_send()
        ad_copy(m).wait_send()
    for j in (2, 3):
        sib_copy(j).wait_send()
    for way in range(2):
        for n in range(tiles):
            hop_copy(way, n).wait_send()
        for part in range(2):
            ring_copy(way, part).wait_send()
    for kind in range(2):

        @pl.loop(1, TENSOR)
        def _(k):
            part_copy(kind, k).wait_send()
            gath_copy(kind, k).wait_send()

        @pl.loop(0, 3)
        def _(which):
            g_copy(kind, which).wait_send()

    for store in stores:
        store.wait()


def finish(out_ref, gb_ref, ga_ref, out_to, gb_to, ga_to, out_v, gb_v, ga_v, turned_v, sem):
    names = ((ga_ref, ga_v, turned_v, ga_to), (gb_ref, gb_v, gb_v, gb_to), (out_ref, out_v, out_v, out_to))
    loads = [pltpu.make_async_copy(src, held, sem.at[0, n]) for n, (src, held, _, _) in enumerate(names)]
    stores = [pltpu.make_async_copy(held, dst, sem.at[1, n]) for n, (_, _, held, dst) in enumerate(names)]
    for load in loads:
        load.start()
    loads[0].wait()
    turned_v[...] = ga_v[...].T
    stores[0].start()
    for n in (1, 2):
        loads[n].wait()
        stores[n].start()
    for store in stores:
        store.wait()


def on_device(
    tokens,
    destinations,
    counts,
    sequence_job_ids,
    job_owner_slot,
    rank_per_job,
    weight,
    input_factor_table,
    output_factor_table,
    cotangent,
):
    slot_count, seq_len, width = tokens.shape
    max_rank = input_factor_table.shape[2]
    rows = slot_count * seq_len
    anywhere = pl.BlockSpec(memory_space=pl.ANY)
    smem = pl.BlockSpec(memory_space=pltpu.SMEM)
    dma = pltpu.SemaphoreType.DMA
    served = (2, 2, RING, 64, width)
    lanes = (RING, RING, 64, width)
    out, ga, gb = pl.pallas_call(
        kernel,
        out_shape=(
            jax.ShapeDtypeStruct((rows, width), BF),
            jax.ShapeDtypeStruct((max_rank, width), F32),
            jax.ShapeDtypeStruct((max_rank, width), F32),
        ),
        in_specs=[smem] * 5 + [anywhere] * 5,
        out_specs=(anywhere,) * 3,
        scratch_shapes=[
            pltpu.VMEM(tokens.shape, BF),
            pltpu.VMEM((rows, width), BF),
            pltpu.VMEM(input_factor_table.shape, BF),
            pltpu.VMEM(output_factor_table.shape, BF),
            pltpu.VMEM((rows, width), BF),
            pltpu.VMEM((DP, seq_len, width), BF),
            pltpu.VMEM((DP, seq_len, width), BF),
            pltpu.SMEM((DP,), jnp.int32),
            pltpu.VMEM((DP, 8, 128), jnp.int32),
            pltpu.VMEM((DP, 8, 128), jnp.int32),
            pltpu.VMEM((rows, rows), BF),
            pltpu.VMEM((2 * rows, rows), BF),
            pltpu.VMEM((2 * rows, rows), BF),
            pltpu.VMEM((rows, 2 * rows), BF),
            pltpu.VMEM((rows, width), BF),
            pltpu.VMEM(lanes, BF),
            pltpu.VMEM(served, BF),
            pltpu.VMEM(lanes, BF),
            pltpu.VMEM(served, BF),
            pltpu.VMEM((2, 2, width, max_rank), BF),
            pltpu.VMEM((2, 2, max_rank, width), BF),
            pltpu.VMEM((W_SLOTS, width, width), BF),
            pltpu.VMEM((2, rows, width), BF),
            pltpu.VMEM((4, rows, width), BF),
            pltpu.VMEM((3, rows, width), F32),
            pltpu.VMEM((2, rows // 2, width), BF),
            pltpu.VMEM((2, rows // 2, width), BF),
            pltpu.VMEM((2, 2, rows // 2, width), BF),
            pltpu.VMEM((2, 2, rows // 2, width), BF),
            pltpu.VMEM((2, TENSOR, 128, max_rank), BF),
            pltpu.VMEM((2, TENSOR, 128, max_rank), BF),
            pltpu.VMEM((2, TENSOR, 128, max_rank), BF),
            pltpu.VMEM(served, BF),
            pltpu.VMEM(lanes, BF),
            pltpu.VMEM((2, max_rank, width), F32),
            pltpu.VMEM((max_rank, width), F32),
            pltpu.VMEM((2, 4, max_rank, width), BF),
            pltpu.VMEM((2, 3, max_rank, width), BF),
            dma((4,)),
            dma((3,)),
            dma((W_SLOTS,)),
            dma((DP - 1,)),
            dma((DP - 1,)),
            dma((2, DP - 1)),
            dma((2, DP - 1)),
            dma((3, 2)),
            dma((2, 2, 2)),
            dma((8,)),
            dma((8,)),
            dma((2, 8)),
            dma((2, 8)),
            dma((2,)),
            dma((4,)),
            dma((4,)),
            dma((4,)),
            dma((2, 4)),
            dma((2, 4)),
            dma((2, 2)),
            dma((2, 2)),
            dma((2, TENSOR - 1)),
            dma((2, TENSOR - 1)),
            dma((2, TENSOR - 1)),
            dma((2, TENSOR - 1)),
            dma((8,)),
            dma((8,)),
            dma((2, 3)),
            dma((2, 3)),
        ],
        compiler_params=pltpu.CompilerParams(
            collective_id=0, has_side_effects=True, vmem_limit_bytes=58 * 2**20
        ),
    )(
        destinations,
        counts,
        sequence_job_ids,
        job_owner_slot,
        rank_per_job,
        tokens,
        cotangent.reshape(rows, width),
        input_factor_table,
        output_factor_table,
        weight,
    )
    out, gb, ga = pl.pallas_call(
        finish,
        out_shape=(
            jax.ShapeDtypeStruct((rows, width), BF),
            jax.ShapeDtypeStruct((max_rank, width), F32),
            jax.ShapeDtypeStruct((width, max_rank), F32),
        ),
        in_specs=[anywhere] * 3,
        out_specs=(anywhere,) * 3,
        scratch_shapes=[
            pltpu.VMEM((rows, width), BF),
            pltpu.VMEM((max_rank, width), F32),
            pltpu.VMEM((max_rank, width), F32),
            pltpu.VMEM((width, max_rank), F32),
            dma((2, 3)),
        ],
    )(out, gb, ga)
    return out.reshape(slot_count, seq_len, width), ga[None], gb[None]


def solution(mesh):
    in_specs = (
        P("dp", None, "tensor"),
        P("dp"),
        P("dp"),
        P("dp"),
        P(),
        P(),
        P("tensor", None),
        P("dp", "tensor", None),
        P("dp", None, "tensor"),
        P("dp", None, "tensor"),
    )
    out_specs = (P("dp", None, "tensor"), P("dp", "tensor", None), P("dp", None, "tensor"))
    return jax.shard_map(
        on_device, mesh=mesh, in_specs=in_specs, out_specs=out_specs, check_vma=False
    )
```

```python
import jax
import jax.numpy as jnp
from jax import lax
from jax.experimental import pallas as pl
from jax.experimental.pallas import tpu as pltpu
from jax.sharding import PartitionSpec as P

BF = jnp.bfloat16
F32 = jnp.float32
RING = 4
DP = RING * RING
TENSOR = 2 * RING
TILE = 256
W_SLOTS = 3
MOVE, PLACE = (0, 0, -1, 1), (0, 1, 1, 0)
BOTH = slice(0, 2)
MESSAGES = ((2, BOTH), (BOTH, 2), (3, BOTH), (BOTH, 3), (2, 2), (3, 3), (2, 3), (3, 2))
NEIGHBOURS = ((0, 1), (1, 0), (0, 3), (3, 0), (1, 1), (3, 3), (1, 3), (3, 1))
OTHERS = NEIGHBOURS + ((0, 2), (2, 0), (2, 1), (1, 2), (2, 3), (3, 2), (2, 2))


def mm(a, b):
    return jnp.dot(a, b, preferred_element_type=F32)


def kernel(
    dest_ref,
    count_ref,
    job_ref,
    owner_ref,
    rank_ref,
    tok_ref,
    cot_ref,
    a_ref,
    b_ref,
    w_ref,
    out_ref,
    ga_ref,
    gb_ref,
    tok_v,
    cot_v,
    a_v,
    b_v,
    out_v,
    tok_s,
    tok_r,
    source,
    facts_s,
    facts_r,
    place_hot,
    x_hot,
    c_hot,
    slot_hot,
    xs,
    x_s,
    x_r,
    c_s,
    c_r,
    fa,
    fb,
    wbuf,
    sib_s,
    sib_r,
    hold,
    hop_s,
    hop_r,
    ring_s,
    ring_r,
    part_s,
    part_r,
    ranks,
    ad_s,
    ad_r,
    g_own,
    g_mid,
    g_s,
    g_r,
    in_sem,
    out_sem,
    w_sem,
    facts_ss,
    facts_rs,
    tok_ss,
    tok_rs,
    fac_ss,
    fac_rs,
    c_ss,
    c_rs,
    x_ss,
    x_rs,
    sib_ss,
    sib_rs,
    tile_ss,
    tile_rs,
    hop_ss,
    hop_rs,
    ring_ss,
    ring_rs,
    part_ss,
    part_rs,
    gath_ss,
    gath_rs,
    ad_ss,
    ad_rs,
    g_ss,
    g_rs,
):
    seq_len, width = tok_ref.shape[1:]
    rows = DP * seq_len
    half = rows // 2
    me = lax.axis_index("dp")
    t = lax.axis_index("tensor")
    y, z = me // RING, me % RING
    x, c = t // 2, t % 2
    odd = (y + z) % 2
    ahead = 1 - 2 * odd
    others = ((1 - odd, 1 - odd), (odd, 1 - odd), (1 - odd, odd))
    tiles = width // TILE
    wide_half = width // 2

    def remote(src, dst, send, recv, **where):
        return pltpu.make_async_remote_copy(
            src_ref=src,
            dst_ref=dst,
            send_sem=send,
            recv_sem=recv,
            device_id=where,
            device_id_type=pl.DeviceIdType.MESH,
        )

    def iota(shape, axis):
        return lax.broadcasted_iota(jnp.int32, shape, axis)

    def near(dy, dz):
        return (y + dy + RING) % RING * RING + (z + dz + RING) % RING

    def owner_of(i, j):
        first, second = (y - i + RING) % RING, (z - j + RING) % RING
        shift = (first + second) % 2
        return (first + shift) % RING * RING + (second + shift) % RING

    def rank_at(owner):
        total = jnp.int32(0)
        for j in range(DP):
            total = total + jnp.where(owner_ref[j] == owner, rank_ref[j], 0)
        return total

    def factor_at(owner, columns):
        return 32.0 / jnp.full((1, columns), rank_at(owner).astype(F32), F32)

    def span(start, size):
        return pl.ds(pl.multiple_of(start, size), size)

    loads = [
        pltpu.make_async_copy(src, dst, in_sem.at[n])
        for n, (src, dst) in enumerate(((tok_ref, tok_v), (a_ref, a_v), (b_ref, b_v), (cot_ref, cot_v)))
    ]
    for load in loads:
        load.start()

    barrier = pltpu.get_barrier_semaphore()

    @pl.loop(1, DP)
    def _(k):
        pl.semaphore_signal(
            barrier, inc=1, device_id={"dp": (me + k) % DP}, device_id_type=pl.DeviceIdType.MESH
        )

    @pl.loop(1, TENSOR)
    def _(k):
        pl.semaphore_signal(
            barrier, inc=1, device_id={"tensor": (t + k) % TENSOR}, device_id_type=pl.DeviceIdType.MESH
        )

    def w_copy(i):
        j = i // 2
        block = (x + jnp.where(j == 0, 2, jnp.where(j == 1, 1, jnp.where(j == 2, 3, 0)))) % RING * 2
        block = block + (c + 1 - i % 2) % 2
        return pltpu.make_async_copy(
            w_ref.at[:, span(block * width, width)], wbuf.at[i % W_SLOTS], w_sem.at[i % W_SLOTS]
        )

    for i in range(W_SLOTS):
        w_copy(jnp.int32(i)).start()

    def chosen(to):
        index = jnp.int32(0)
        for i in range(DP):
            index = jnp.where(lax.shift_right_logical(dest_ref[i], 4) == to, i, index)
        return index

    @pl.loop(0, DP)
    def _(to):
        index = chosen(to)
        source[to] = index
        owner = owner_ref[job_ref[index]]
        oy, oz = lax.shift_right_logical(owner, 2), owner & 3
        shift = (oy + oz) & 1
        dy, dz = (to // RING + RING - oy + shift) & 3, (to % RING + RING - oz + shift) & 3
        base = (dy * RING + dz) * 2
        row = iota((8, 128), 0)
        facts_s[to] = jnp.where(
            row == 0, dest_ref[index] & 15, jnp.where(row == 1, count_ref[index], base)
        )

    facts_r[me] = facts_s[me]
    loads[0].wait()

    @pl.loop(0, DP)
    def _(to):
        tok_s[to] = tok_v[source[to]]

    tok_r[me] = tok_s[me]

    pl.semaphore_wait(barrier, DP - 1 + TENSOR - 1)

    def facts_copy(k):
        to = near(*OTHERS[k])
        return remote(facts_s.at[to], facts_r.at[me], facts_ss.at[k], facts_rs.at[k], dp=to)

    def tok_copy(h, k):
        to, columns = near(*OTHERS[k]), span(h * wide_half, wide_half)
        return remote(
            tok_s.at[to, :, columns],
            tok_r.at[me, :, columns],
            tok_ss.at[h, k],
            tok_rs.at[h, k],
            dp=to,
        )

    def fac_copy(axis, n):
        table = (fa, fb)[n]
        there = ((1 - odd, odd), (odd, 1 - odd))[axis]
        to = (near(ahead, 0), near(0, ahead))[axis]
        return remote(
            table.at[odd, odd], table.at[there], fac_ss.at[axis, n], fac_rs.at[there + (n,)], dp=to
        )

    def fac_wait(n, which):
        for there in which:
            held = (fa, fb)[n].at[there]
            remote(held, held, fac_ss.at[0, n], fac_rs.at[there + (n,)], dp=me).wait_recv()

    def fac_relay(n):
        table = (fa, fb)[n]
        here = ((odd, 1 - odd), (1 - odd, odd))[n]
        to = (near(0, -ahead), near(-ahead, 0))[n]
        return remote(table.at[here], table.at[odd, odd], fac_ss.at[2, n], fac_rs.at[odd, odd, n], dp=to)

    for k in range(DP - 1):
        facts_copy(k).start()

    @pl.loop(0, 2)
    def _(h):
        for k in range(DP - 1):
            tok_copy(h, k).start()

    my_rank = rank_at(me)
    loads[1].wait()

    @pl.loop(0, width // 128)
    def _(n):
        at = span(n * 128, 128)
        kept = iota((128, a_v.shape[2]), 1) < my_rank
        fa[odd, odd, at, :] = jnp.where(kept, a_v[0, at, :].astype(F32), 0.0).astype(BF)

    for axis in range(2):
        fac_copy(axis, 0).start()
    loads[2].wait()

    @pl.loop(0, width // 128)
    def _(n):
        at = span(n * 128, 128)
        kept = iota((b_v.shape[1], 128), 0) < my_rank
        fb[odd, odd, :, at] = jnp.where(kept, b_v[0, :, at].astype(F32), 0.0).astype(BF)

    for k in range(DP - 1):
        facts_copy(k).wait_recv()

    slot_c = facts_r[:, 0, :].astype(F32)
    live_c = facts_r[:, 1, :].astype(F32)
    base_c = facts_r[:, 2, :].astype(F32)
    square = (DP, 128)
    diagonal = iota(square, 0) == iota(square, 1)
    slot_l = jnp.sum(jnp.where(diagonal, slot_c, 0.0), 0, keepdims=True)
    base_l = jnp.sum(jnp.where(diagonal, base_c, 0.0), 0, keepdims=True)
    earlier = (base_l == base_c) & (slot_l < slot_c) & (iota(square, 1) < DP)
    turn_c = jnp.sum(jnp.where(earlier, 1.0, 0.0), 1, keepdims=True)
    lane_c = base_c + turn_c
    lane_l = jnp.sum(jnp.where(diagonal, lane_c, 0.0), 0, keepdims=True)
    wide = (DP, rows)
    seq_of = iota(wide, 1) // seq_len
    slot_1, live_1, lane_1 = slot_c[:, :1], live_c[:, :1], lane_c[:, :1]
    in_slot = slot_1 == seq_of.astype(F32)
    in_order = iota(wide, 0) == seq_of
    position = (iota((1, rows), 1) % seq_len).astype(F32)

    def spread(where, value):
        return jnp.sum(jnp.where(where, value, 0.0), 0, keepdims=True)

    live = position < spread(in_order, live_1)
    c_row = spread(in_slot, lane_1) * seq_len + position
    x_row = jnp.where(live, spread(in_order, lane_1) * seq_len + position, -1.0)
    slot_row = jnp.where(live, spread(in_order, slot_1) * seq_len + position, -1.0)

    def build(hot, wanted):
        @pl.loop(0, hot.shape[0] // 64)
        def _(n):
            row = (iota((64, rows), 0) + n * 64).astype(F32)
            hot[span(n * 64, 64), :] = jnp.where(row == wanted, 1.0, 0.0).astype(BF)

    build(x_hot, x_row)
    build(place_hot, slot_row)

    lane_shape = (RING, RING, 2 * seq_len)

    def lane_place(dy, dz):
        row = PLACE[dy] if dy != BOTH else BOTH
        column = PLACE[dz] if dz != BOTH else BOTH
        return row, column, (dy != BOTH) * 2 + (dz != BOTH)

    def lane_move(dy, dz):
        return (MOVE[dy] if dy != BOTH else 0, MOVE[dz] if dz != BOTH else 0)

    def x_copy(h, m):
        message, columns = MESSAGES[m], span(h * wide_half, wide_half)
        return remote(
            x_s.at[message + (slice(None), columns)],
            x_r.at[lane_place(*message) + (slice(None), columns)],
            x_ss.at[h, m],
            x_rs.at[h, m],
            dp=near(*lane_move(*message)),
        )

    def c_copy(m):
        message = MESSAGES[m]
        return remote(
            c_s.at[message],
            c_r.at[lane_place(*message)],
            c_ss.at[m],
            c_rs.at[m],
            dp=near(*lane_move(*message)),
        )

    @pl.loop(0, 2)
    def _(h):
        for k in range(DP - 1):
            tok_copy(h, k).wait_recv()

        @pl.loop(0, tiles // 2)
        def _(n):
            at = span(h * wide_half + n * TILE, TILE)
            landed = tok_r[:, :, at].reshape(rows, TILE)
            x_s[:, :, :, at] = mm(x_hot[...], landed).astype(BF).reshape(lane_shape + (TILE,))

        for m in range(len(MESSAGES)):
            x_copy(h, m).start()

        @pl.loop(0, tiles // 2)
        def _(n):
            at = span(h * wide_half + n * TILE, TILE)
            xs[:, at] = mm(place_hot[...], tok_r[:, :, at].reshape(rows, TILE)).astype(BF)

    for axis in range(2):
        fac_copy(axis, 1).start()
    build(c_hot, c_row)
    loads[3].wait()

    @pl.loop(0, tiles)
    def _(n):
        at = span(n * TILE, TILE)
        c_s[:, :, :, at] = mm(c_hot[...], cot_v[:, at]).astype(BF).reshape(lane_shape + (TILE,))

    fac_wait(0, others[1:])
    fac_relay(0).start()
    for m in range(len(MESSAGES)):
        c_copy(m).start()
    x_r[:, :, 0] = x_s[BOTH, BOTH]
    c_r[:, :, 0] = c_s[BOTH, BOTH]

    def sib_copy(j):
        return remote(
            sib_s.at[j % 2], sib_r.at[j], sib_ss.at[j % 2], sib_rs.at[j], tensor=x * 2 + (1 - c)
        )

    right, left = ((x + 1) % RING) * 2 + c, ((x + 3) % RING) * 2 + c

    def hop_copy(way, n):
        at = span(n * TILE, TILE)
        return remote(
            hop_s.at[way, :, at],
            hop_r.at[way, :, at],
            hop_ss.at[way, n],
            hop_rs.at[way, n],
            tensor=(right, left)[way],
        )

    def sib_tile(n):
        at = span(n * TILE, TILE)
        return remote(
            sib_s.at[0, :, at], sib_r.at[0, :, at], tile_ss.at[n], tile_rs.at[n], tensor=x * 2 + (1 - c)
        )

    def ring_copy(way, part):
        return remote(
            ring_s.at[way, part],
            ring_r.at[way, part],
            ring_ss.at[way, part],
            ring_rs.at[way, part],
            tensor=(right, left)[way],
        )

    def half_rows(part, put):
        @pl.loop(0, half // 32)
        def _(n):
            put(span(part * half + n * 32, 32), span(n * 32, 32))

    def send_hop(n):
        at = span(n * TILE, TILE)
        sib_tile(n).wait_recv()
        for way in range(2):
            part = slice(way * half, (way + 1) * half)
            hop_s[way, :, at] = (hold[0, part, at] + sib_r[0, part, at].astype(F32)).astype(BF)
            hop_copy(way, n).start()

    def sum_ring(way, part):
        def put(at, to):
            value = hold[1 - way, at] + sib_r[1 + way, at].astype(F32)
            if way == part:
                value = value + hop_r[way, to].astype(F32)
            ring_s[way, part, to] = value.astype(BF)

        half_rows(part, put)

    def part_copy(kind, k):
        to = (t + k) % TENSOR
        return remote(
            part_s.at[kind, to],
            part_r.at[kind, k],
            part_ss.at[kind, k - 1],
            part_rs.at[kind, k - 1],
            tensor=to,
        )

    def gath_copy(kind, k):
        to = (t + k) % TENSOR
        held = ranks.at[kind, t]
        return remote(held, held, gath_ss.at[kind, k - 1], gath_rs.at[kind, k - 1], tensor=to)

    def served(ref, i, j):
        return ref[i, j].reshape(RING * 64, width)

    def send_parts(kind, make):
        @pl.loop(0, 4)
        def _(q):
            value = make(q // 2, q % 2).astype(BF)
            for piece in range(2):
                block = 2 * q + piece
                part_s[kind, block] = value[piece * 128 : (piece + 1) * 128]
                k = (block - t + TENSOR) % TENSOR

                @pl.when(k > 0)
                def _():
                    part_copy(kind, k).start()

        part_r[kind, 0] = part_s[kind, t]

    def sum_parts(kind, scale):
        @pl.loop(1, TENSOR)
        def _(k):
            part_copy(kind, k).wait_recv()

        total = part_r[kind, 0].astype(F32)
        for k in range(1, TENSOR):
            total = total + part_r[kind, k].astype(F32)
        ranks[kind, t] = (total if scale is None else total * scale).astype(BF)

        @pl.loop(1, TENSOR)
        def _(k):
            gath_copy(kind, k).start()

    def gathered(kind):
        @pl.loop(1, TENSOR)
        def _(k):
            held = ranks.at[kind, (t + TENSOR - k) % TENSOR]
            remote(held, held, gath_ss.at[kind, k - 1], gath_rs.at[kind, k - 1], tensor=t).wait_recv()

    def rank_rows(kind, i, j):
        return ranks[kind, pl.ds(i * 4 + j * 2, 2)].reshape(RING * 64, ranks.shape[3])

    for i in range(2):
        w_copy(jnp.int32(i)).wait()

    @pl.loop(0, tiles)
    def _(n):
        at = span(n * TILE, TILE)
        sib_s[0, :, at] = mm(xs[...], wbuf[0, :, at]).astype(BF)
        sib_tile(n).start()
        hold[0, :, at] = mm(xs[...], wbuf[1, :, at])

        @pl.when(n > 0)
        def _():
            send_hop(n - 1)

    for i in range(2):
        w_copy(jnp.int32(i + W_SLOTS)).start()
    send_hop(jnp.int32(tiles - 1))

    @pl.loop(1, 4)
    def _(j):
        w_copy(2 * j).wait()

        @pl.when(j == 2)
        def _():
            for n in range(tiles):
                sib_tile(n).wait_send()

        @pl.when(j == 3)
        def _():
            sib_copy(1).wait_send()

        @pl.loop(0, tiles)
        def _(n):
            at = span(n * TILE, TILE)
            sib_s[j % 2, :, at] = mm(xs[...], wbuf[(2 * j) % W_SLOTS, :, at]).astype(BF)

        sib_copy(j).start()

        @pl.when(2 * j + W_SLOTS < 8)
        def _():
            w_copy(2 * j + W_SLOTS).start()

        w_copy(2 * j + 1).wait()

        @pl.loop(0, tiles)
        def _(n):
            at = span(n * TILE, TILE)
            hold[jnp.where(j == 3, 2, j % 2), :, at] = mm(xs[...], wbuf[(2 * j + 1) % W_SLOTS, :, at])

        @pl.when(2 * j + 1 + W_SLOTS < 8)
        def _():
            w_copy(2 * j + 1 + W_SLOTS).start()

        @pl.when(j == 1)
        def _():
            fac_wait(0, others[:1])

            @pl.loop(0, 2)
            def _(h):
                for m in range(len(MESSAGES)):
                    x_copy(h, m).wait_recv()

            send_parts(0, lambda i, k: mm(served(x_r, i, k), fa[i, k]))
            fac_wait(1, others[1:])
            fac_relay(1).start()

        @pl.when(j == 2)
        def _():
            sum_parts(0, None)
            for way in range(2):
                sib_copy(1 + way).wait_recv()
                sum_ring(way, 1 - way)
                ring_copy(way, 1 - way).start()

    def ad_copy(m):
        message = MESSAGES[m]
        dy, dz = lane_move(*message)
        return remote(
            ad_s.at[lane_place(*message)],
            ad_r.at[message],
            ad_ss.at[m],
            ad_rs.at[m],
            dp=near(-dy, -dz),
        )

    fac_wait(1, others[:1])
    gathered(0)

    @pl.loop(0, 4)
    def _(q):
        i, j = q // 2, q % 2
        value = mm(rank_rows(0, i, j), fb[i, j]) * factor_at(owner_of(i, j), width)
        ad_s[i, j] = value.astype(BF).reshape(RING, 64, width)

    for m in range(len(MESSAGES)):
        ad_copy(m).start()
    ad_r[BOTH, BOTH] = ad_s[:, :, 0]

    for m in range(len(MESSAGES)):
        c_copy(m).wait_recv()
    send_parts(
        1,
        lambda i, j: lax.dot_general(
            served(c_r, i, j), fb[i, j], (((1,), (1,)), ((), ())), preferred_element_type=F32
        ),
    )

    def g_copy(n, which):
        dy = jnp.where(which == 0, -ahead * (1 - n), jnp.where(which == 1, ahead, 0))
        dz = jnp.where(which == 0, -ahead, jnp.where(which == 1, 0, ahead))
        return remote(
            g_s.at[n, which],
            g_r.at[n, which],
            g_ss.at[n, which],
            g_rs.at[n, which],
            dp=near(dy, dz),
        )

    def gradient(n, kind, row_ref):
        @pl.loop(0, 4)
        def _(which):
            i = jnp.where((which == 1) | (which == 3), odd, 1 - odd)
            j = jnp.where(which >= 2, odd, 1 - odd)
            turned = rank_rows(kind, i, j).astype(F32).T.astype(BF)
            value = mm(turned, served(row_ref, i, j)) * (1.0 / seq_len)
            if n == 1:
                value = value * factor_at(owner_of(i, j), width)
            g_own[n] = value
            g_s[n, which] = value.astype(BF)
            if n == 1:

                @pl.when(which == 1)
                def _():
                    g_mid[...] = value

            @pl.when((which == 0) | (which == 2) | ((which == 1) & (n == 0)))
            def _():
                g_copy(n, which).start()

    def pass_gradient():
        g_copy(1, 0).wait_recv()

        @pl.loop(0, g_mid.shape[0] // 32)
        def _(k):
            at = span(k * 32, 32)
            g_s[1, 1, at] = (g_mid[at] + g_r[1, 0, at].astype(F32)).astype(BF)

        g_copy(1, 1).start()

    gradient(1, 0, c_r)

    @pl.loop(0, rows // 64)
    def _(n):
        row = iota((64, 128), 0) + n * 64
        mine = jnp.where(slot_l == (row // seq_len).astype(F32), lane_l, 0.0)
        place = jnp.sum(mine, 1, keepdims=True) * seq_len + (row % seq_len).astype(F32)[:, :1]
        slot_hot[span(n * 64, 64), :] = jnp.where(
            iota((64, 2 * rows), 1).astype(F32) == place, 1.0, 0.0
        ).astype(BF)

    for way in range(2):
        for n in range(tiles):
            hop_copy(way, n).wait_recv()
        sum_ring(way, way)
    sum_parts(1, factor_at(owner_of(t // 4, (t // 2) % 2), ranks.shape[3]))
    for way in range(2):
        ring_copy(way, way).start()
    gathered(1)
    gradient(0, 1, x_r)
    pass_gradient()

    sib_copy(3).wait_recv()
    for m in range(len(MESSAGES)):
        ad_copy(m).wait_recv()

    @pl.loop(0, tiles)
    def _(n):
        at = span(n * TILE, TILE)
        back = ad_r[:, :, :, at].reshape(2 * rows, TILE)
        hold[2, :, at] = hold[2, :, at] + sib_r[3, :, at].astype(F32) + mm(slot_hot[...], back)

    for way in range(2):
        for part in range(2):
            ring_copy(way, part).wait_recv()

    for part in range(2):

        def put(at, to):
            out_v[at] = (
                hold[2, at] + ring_r[0, part, to].astype(F32) + ring_r[1, part, to].astype(F32)
            ).astype(BF)

        half_rows(part, put)
    stores = [pltpu.make_async_copy(out_v, out_ref, out_sem.at[2])]
    stores[0].start()

    for n, g_ref in ((1, gb_ref), (0, ga_ref)):

        @pl.loop(n, 3)
        def _(which):
            g_copy(n, which).wait_recv()

        @pl.loop(0, g_own.shape[1] // 32)
        def _(k):
            at = span(k * 32, 32)
            total = g_own[n, at]
            for which in range(n, 3):
                total = total + g_r[n, which, at].astype(F32)
            g_own[n, at] = total

        stores.append(pltpu.make_async_copy(g_own.at[n], g_ref, out_sem.at[n]))
        stores[-1].start()

    for k in range(DP - 1):
        facts_copy(k).wait_send()
        tok_copy(0, k).wait_send()
        tok_copy(1, k).wait_send()

    for n in range(2):
        for axis in range(2):
            fac_copy(axis, n).wait_send()
        fac_relay(n).wait_send()
    for m in range(len(MESSAGES)):
        for h in range(2):
            x_copy(h, m).wait_send()
        c_copy(m).wait_send()
        ad_copy(m).wait_send()
    for j in (2, 3):
        sib_copy(j).wait_send()
    for way in range(2):
        for n in range(tiles):
            hop_copy(way, n).wait_send()
        for part in range(2):
            ring_copy(way, part).wait_send()
    for kind in range(2):

        @pl.loop(1, TENSOR)
        def _(k):
            part_copy(kind, k).wait_send()
            gath_copy(kind, k).wait_send()

        @pl.loop(0, 3)
        def _(which):
            g_copy(kind, which).wait_send()

    for store in stores:
        store.wait()


def finish(out_ref, gb_ref, ga_ref, out_to, gb_to, ga_to, out_v, gb_v, ga_v, turned_v, sem):
    names = ((ga_ref, ga_v, turned_v, ga_to), (gb_ref, gb_v, gb_v, gb_to), (out_ref, out_v, out_v, out_to))
    loads = [pltpu.make_async_copy(src, held, sem.at[0, n]) for n, (src, held, _, _) in enumerate(names)]
    stores = [pltpu.make_async_copy(held, dst, sem.at[1, n]) for n, (_, _, held, dst) in enumerate(names)]
    for load in loads:
        load.start()
    loads[0].wait()
    turned_v[...] = ga_v[...].T
    stores[0].start()
    for n in (1, 2):
        loads[n].wait()
        stores[n].start()
    for store in stores:
        store.wait()


def on_device(
    tokens,
    destinations,
    counts,
    sequence_job_ids,
    job_owner_slot,
    rank_per_job,
    weight,
    input_factor_table,
    output_factor_table,
    cotangent,
):
    slot_count, seq_len, width = tokens.shape
    max_rank = input_factor_table.shape[2]
    rows = slot_count * seq_len
    anywhere = pl.BlockSpec(memory_space=pl.ANY)
    smem = pl.BlockSpec(memory_space=pltpu.SMEM)
    dma = pltpu.SemaphoreType.DMA
    served = (2, 2, RING, 64, width)
    lanes = (RING, RING, 64, width)
    out, ga, gb = pl.pallas_call(
        kernel,
        out_shape=(
            jax.ShapeDtypeStruct((rows, width), BF),
            jax.ShapeDtypeStruct((max_rank, width), F32),
            jax.ShapeDtypeStruct((max_rank, width), F32),
        ),
        in_specs=[smem] * 5 + [anywhere] * 5,
        out_specs=(anywhere,) * 3,
        scratch_shapes=[
            pltpu.VMEM(tokens.shape, BF),
            pltpu.VMEM((rows, width), BF),
            pltpu.VMEM(input_factor_table.shape, BF),
            pltpu.VMEM(output_factor_table.shape, BF),
            pltpu.VMEM((rows, width), BF),
            pltpu.VMEM((DP, seq_len, width), BF),
            pltpu.VMEM((DP, seq_len, width), BF),
            pltpu.SMEM((DP,), jnp.int32),
            pltpu.VMEM((DP, 8, 128), jnp.int32),
            pltpu.VMEM((DP, 8, 128), jnp.int32),
            pltpu.VMEM((rows, rows), BF),
            pltpu.VMEM((2 * rows, rows), BF),
            pltpu.VMEM((2 * rows, rows), BF),
            pltpu.VMEM((rows, 2 * rows), BF),
            pltpu.VMEM((rows, width), BF),
            pltpu.VMEM(lanes, BF),
            pltpu.VMEM(served, BF),
            pltpu.VMEM(lanes, BF),
            pltpu.VMEM(served, BF),
            pltpu.VMEM((2, 2, width, max_rank), BF),
            pltpu.VMEM((2, 2, max_rank, width), BF),
            pltpu.VMEM((W_SLOTS, width, width), BF),
            pltpu.VMEM((2, rows, width), BF),
            pltpu.VMEM((4, rows, width), BF),
            pltpu.VMEM((3, rows, width), F32),
            pltpu.VMEM((2, rows // 2, width), BF),
            pltpu.VMEM((2, rows // 2, width), BF),
            pltpu.VMEM((2, 2, rows // 2, width), BF),
            pltpu.VMEM((2, 2, rows // 2, width), BF),
            pltpu.VMEM((2, TENSOR, 128, max_rank), BF),
            pltpu.VMEM((2, TENSOR, 128, max_rank), BF),
            pltpu.VMEM((2, TENSOR, 128, max_rank), BF),
            pltpu.VMEM(served, BF),
            pltpu.VMEM(lanes, BF),
            pltpu.VMEM((2, max_rank, width), F32),
            pltpu.VMEM((max_rank, width), F32),
            pltpu.VMEM((2, 4, max_rank, width), BF),
            pltpu.VMEM((2, 3, max_rank, width), BF),
            dma((4,)),
            dma((3,)),
            dma((W_SLOTS,)),
            dma((DP - 1,)),
            dma((DP - 1,)),
            dma((2, DP - 1)),
            dma((2, DP - 1)),
            dma((3, 2)),
            dma((2, 2, 2)),
            dma((8,)),
            dma((8,)),
            dma((2, 8)),
            dma((2, 8)),
            dma((2,)),
            dma((4,)),
            dma((4,)),
            dma((4,)),
            dma((2, 4)),
            dma((2, 4)),
            dma((2, 2)),
            dma((2, 2)),
            dma((2, TENSOR - 1)),
            dma((2, TENSOR - 1)),
            dma((2, TENSOR - 1)),
            dma((2, TENSOR - 1)),
            dma((8,)),
            dma((8,)),
            dma((2, 3)),
            dma((2, 3)),
        ],
        compiler_params=pltpu.CompilerParams(
            collective_id=0, has_side_effects=True, vmem_limit_bytes=58 * 2**20
        ),
    )(
        destinations,
        counts,
        sequence_job_ids,
        job_owner_slot,
        rank_per_job,
        tokens,
        cotangent.reshape(rows, width),
        input_factor_table,
        output_factor_table,
        weight,
    )
    out, gb, ga = pl.pallas_call(
        finish,
        out_shape=(
            jax.ShapeDtypeStruct((rows, width), BF),
            jax.ShapeDtypeStruct((max_rank, width), F32),
            jax.ShapeDtypeStruct((width, max_rank), F32),
        ),
        in_specs=[anywhere] * 3,
        out_specs=(anywhere,) * 3,
        scratch_shapes=[
            pltpu.VMEM((rows, width), BF),
            pltpu.VMEM((max_rank, width), F32),
            pltpu.VMEM((max_rank, width), F32),
            pltpu.VMEM((width, max_rank), F32),
            dma((2, 3)),
        ],
    )(out, gb, ga)
    return out.reshape(slot_count, seq_len, width), ga[None], gb[None]


def solution(mesh):
    in_specs = (
        P("dp", None, "tensor"),
        P("dp"),
        P("dp"),
        P("dp"),
        P(),
        P(),
        P("tensor", None),
        P("dp", "tensor", None),
        P("dp", None, "tensor"),
        P("dp", None, "tensor"),
    )
    out_specs = (P("dp", None, "tensor"), P("dp", "tensor", None), P("dp", None, "tensor"))
    return jax.shard_map(
        on_device, mesh=mesh, in_specs=in_specs, out_specs=out_specs, check_vma=False
    )
```
